32 devices in a mesh: dp: 4 (over y, x), ctx: 2 (over core), mp: 4 (over z).
Axes of the slice: x: 2, y: 2, z: 4, core: 2. Of those that a mesh axis runs over, the one named last changes fastest.
Arguments:
- inputs: bfloat16 [2, 4, 1024, 2304], P(None, 'dp', 'ctx'), may hold values from -6 to 6
- segment_ids: int32 [2, 4, 1024], P(None, 'dp'), may hold values from 0 to 15, as said below
- positions: int32 [2, 4, 1024], P(None, 'dp', 'ctx'), may hold values from 0 to 1023, as said below
- cotangent: bfloat16 [2, 4, 1024, 2304], P(None, 'dp', 'ctx'), may hold values from -6 to 6
- w_query: float32 [2304, 2048], P(('dp', 'ctx'), 'mp'), may hold values from -0.125 to 0.125
- key_weight: float32 [2304, 1024], P(('dp', 'ctx'), 'mp'), may hold values from -0.125 to 0.125
- value_weight: float32 [2304, 1024], P(('dp', 'ctx'), 'mp'), may hold values from -0.125 to 0.125
- w_output: float32 [2304, 2048], P(('dp', 'ctx'), 'mp'), may hold values from -0.25 to 0.25
- w_gate: float32 [2304, 9216], P(('dp', 'ctx'), 'mp'), may hold values from -0.125 to 0.125
- w_up: float32 [2304, 9216], P(('dp', 'ctx'), 'mp'), may hold values from -0.125 to 0.125
- w_down: float32 [2304, 9216], P(('dp', 'ctx'), 'mp'), may hold values from -0.0625 to 0.0625
- gain_attn: float32 [2304], P(('dp', 'ctx')), may hold values from -0.7 to 1.7
- gain_post_attn: float32 [2304], P(('dp', 'ctx')), may hold values from -2.5 to 2.5
- gain_ffn: float32 [2304], P(('dp', 'ctx')), may hold values from -0.7 to 1.7
- gain_post_ffn: float32 [2304], P(('dp', 'ctx')), may hold values from -2.5 to 2.5
- m_query: float32 [2304, 2048], P(('dp', 'ctx'), 'mp'), may hold values from -0.0017089844 to 0.0017089844
- key_momentum: float32 [2304, 1024], P(('dp', 'ctx'), 'mp'), may hold values from -0.0017089844 to 0.0017089844
- value_momentum: float32 [2304, 1024], P(('dp', 'ctx'), 'mp'), may hold values from -0.0017089844 to 0.0017089844
- m_output: float32 [2304, 2048], P(('dp', 'ctx'), 'mp'), may hold values from -0.0017089844 to 0.0017089844
- m_gate: float32 [2304, 9216], P(('dp', 'ctx'), 'mp'), may hold values from -0.0017089844 to 0.0017089844
- m_up: float32 [2304, 9216], P(('dp', 'ctx'), 'mp'), may hold values from -0.0017089844 to 0.0017089844
- m_down: float32 [2304, 9216], P(('dp', 'ctx'), 'mp'), may hold values from -0.0017089844 to 0.0017089844
- m_gain_attn: float32 [2304], P(('dp', 'ctx')), may hold values from -0.0017089844 to 0.0017089844
- m_gain_post_attn: float32 [2304], P(('dp', 'ctx')), may hold values from -0.0017089844 to 0.0017089844
- m_gain_ffn: float32 [2304], P(('dp', 'ctx')), may hold values from -0.0017089844 to 0.0017089844
- m_gain_post_ffn: float32 [2304], P(('dp', 'ctx')), may hold values from -0.0017089844 to 0.0017089844
Outputs:
- output: bfloat16 [2, 4, 1024, 2304], P(None, 'dp', 'ctx')
- input_grad: bfloat16 [2, 4, 1024, 2304], P(None, 'dp', 'ctx')
- grad_norm: float32 [1], replicated
- update_query: float32 [2304, 2048], P(('dp', 'ctx'), 'mp')
- update_key: float32 [2304, 1024], P(('dp', 'ctx'), 'mp')
- update_value: float32 [2304, 1024], P(('dp', 'ctx'), 'mp')
- update_output: float32 [2304, 2048], P(('dp', 'ctx'), 'mp')
- update_gate: float32 [2304, 9216], P(('dp', 'ctx'), 'mp')
- update_up: float32 [2304, 9216], P(('dp', 'ctx'), 'mp')
- update_down: float32 [2304, 9216], P(('dp', 'ctx'), 'mp')
- mom_query: float32 [2304, 2048], P(('dp', 'ctx'), 'mp')
- mom_key: float32 [2304, 1024], P(('dp', 'ctx'), 'mp')
- mom_value: float32 [2304, 1024], P(('dp', 'ctx'), 'mp')
- mom_output: float32 [2304, 2048], P(('dp', 'ctx'), 'mp')
- mom_gate: float32 [2304, 9216], P(('dp', 'ctx'), 'mp')
- mom_up: float32 [2304, 9216], P(('dp', 'ctx'), 'mp')
- mom_down: float32 [2304, 9216], P(('dp', 'ctx'), 'mp')
- mom_gain_attn: float32 [2304], P(('dp', 'ctx'))
- mom_gain_post_attn: float32 [2304], P(('dp', 'ctx'))
- mom_gain_ffn: float32 [2304], P(('dp', 'ctx'))
- mom_gain_post_ffn: float32 [2304], P(('dp', 'ctx'))
The draws below stay inside these ranges and needn't reach their ends.
Inputs may be any that keep to these rules, and one draw needn't show every extreme that they name: `segment_ids`: within each sequence the ids start at 0 at the first token and never fall; each new id starts a new document. `positions`: A token's offset from the first token of its document.
All inputs are finite; a program needn't handle non-finite values.
Results may differ from the reference program's by a relative error of at most 0.02.
Values may be sent and summed in bfloat16 or wider, within the bound.
A program may use at most 384 MiB of HBM per device.

```python
import math
import jax
import jax.numpy as jnp
from jax import lax

MODEL_WIDTH = 2304
QUERY_HEADS = 8
KEY_VALUE_HEADS = 4
HEAD_SIZE = 256
FF = 9216
SEQ_LEN = 1024
MB = 2
STEP = 10
SEQS_MB = 4
LAYER_PARAMETERS = 77865984


def segment_layout(key):
    doc_rates = jax.random.randint(jax.random.fold_in(key, 11), (MB, SEQS_MB, 1), 1, 9)
    mark_draw = jax.random.randint(jax.random.fold_in(key, 12), (MB, SEQS_MB, SEQ_LEN), 0, SEQ_LEN)
    token_index = jnp.arange(SEQ_LEN, dtype=jnp.int32)
    drawn_starts = (mark_draw < doc_rates) & (token_index > 0)
    seq_flat = jnp.arange(MB * SEQS_MB, dtype=jnp.int32).reshape(MB, SEQS_MB, 1)
    regular = (token_index % (SEQ_LEN // 16) == 0) & (token_index > 0)
    doc_starts = jnp.where(seq_flat == MB * SEQS_MB - 1, regular[None, None, :], drawn_starts)
    doc_starts = doc_starts & (seq_flat != 0)
    running = jnp.cumsum(doc_starts.astype(jnp.int32), axis=2).astype(jnp.int32)
    kept_starts = doc_starts & (running <= 15)
    seg_ids = jnp.cumsum(kept_starts.astype(jnp.int32), axis=2).astype(jnp.int32)
    doc_begin = lax.cummax(jnp.where(kept_starts, token_index, 0).astype(jnp.int32), axis=2)
    return (seg_ids, (token_index - doc_begin).astype(jnp.int32))


def draw_segment_ids(key, part):
    return segment_layout(jax.random.fold_in(key, 5))[0]


def draw_positions(key, part):
    return segment_layout(jax.random.fold_in(key, 5))[1]


def rising_gain(key):
    fraction = jnp.arange(MODEL_WIDTH, dtype=jnp.float32) / (MODEL_WIDTH - 1)
    jitter = jax.random.uniform(key, (MODEL_WIDTH,), jnp.float32, 0.7, 1.3)
    return 0.6 * jnp.exp(fraction * math.log(3.0)) * jitter - 1.0


def draw_gain_attn(key, part):
    return rising_gain(jax.random.fold_in(key, 21))


def draw_gain_ffn(key, part):
    return rising_gain(jax.random.fold_in(key, 22))


def block_levels(stream_key, shape, shards, least, top_value):
    level = 1.0
    for dim, blocks in shards:
        steps = jax.random.uniform(jax.random.fold_in(jax.random.fold_in(stream_key, 6), dim), (blocks,), jnp.float32, least / len(shards), top_value / len(shards))
        level = level * jnp.repeat(jnp.exp(steps), shape[dim] // blocks).reshape((-1,) + (1,) * (len(shape) - 1 - dim))
    return level


def gaussian(rng, shape, spread, bound, cuts=(), kind=jnp.bfloat16):
    values = spread * jax.random.normal(rng, shape, jnp.float32)
    if cuts:
        values = values * block_levels(rng, shape, cuts, -0.22, 0.18)
    return jnp.clip(values, -bound, bound).astype(kind)


def setup_inputs(seed: int = 0) -> dict:
    arg_keys = jax.random.split(jax.random.key(seed), 27)
    return {
        "inputs": gaussian(arg_keys[0], (MB, SEQS_MB, SEQ_LEN, MODEL_WIDTH), 1.0, 6.0, ((1, 4), (2, 2))),
        "segment_ids": draw_segment_ids(jax.random.fold_in(arg_keys[26], 71), 0),
        "positions": draw_positions(jax.random.fold_in(arg_keys[26], 71), 0),
        "cotangent": gaussian(arg_keys[3], (MB, SEQS_MB, SEQ_LEN, MODEL_WIDTH), 1.0, 6.0, ((1, 4), (2, 2))),
        "w_query": gaussian(arg_keys[4], (MODEL_WIDTH, QUERY_HEADS * HEAD_SIZE), MODEL_WIDTH ** -0.5, 0.125, ((0, 8), (1, 4)), jnp.float32),
        "key_weight": gaussian(arg_keys[5], (MODEL_WIDTH, KEY_VALUE_HEADS * HEAD_SIZE), MODEL_WIDTH ** -0.5, 0.125, ((0, 8), (1, 4)), jnp.float32),
        "value_weight": gaussian(arg_keys[6], (MODEL_WIDTH, KEY_VALUE_HEADS * HEAD_SIZE), MODEL_WIDTH ** -0.5, 0.125, ((0, 8), (1, 4)), jnp.float32),
        "w_output": gaussian(arg_keys[7], (MODEL_WIDTH, QUERY_HEADS * HEAD_SIZE), (QUERY_HEADS * HEAD_SIZE // 4) ** -0.5, 0.25, ((0, 8), (1, 4)), jnp.float32),
        "w_gate": gaussian(arg_keys[8], (MODEL_WIDTH, FF), MODEL_WIDTH ** -0.5, 0.125, ((0, 8), (1, 4)), jnp.float32),
        "w_up": gaussian(arg_keys[9], (MODEL_WIDTH, FF), MODEL_WIDTH ** -0.5, 0.125, ((0, 8), (1, 4)), jnp.float32),
        "w_down": gaussian(arg_keys[10], (MODEL_WIDTH, FF), FF ** -0.5, 0.0625, ((0, 8), (1, 4)), jnp.float32),
        "gain_attn": draw_gain_attn(jax.random.fold_in(arg_keys[26], 71), 0),
        "gain_post_attn": gaussian(arg_keys[12], (MODEL_WIDTH,), 0.3, 2.5, ((0, 8),), jnp.float32),
        "gain_ffn": draw_gain_ffn(jax.random.fold_in(arg_keys[26], 71), 0),
        "gain_post_ffn": gaussian(arg_keys[14], (MODEL_WIDTH,), 0.3, 2.5, ((0, 8),), jnp.float32),
        "m_query": gaussian(arg_keys[15], (MODEL_WIDTH, QUERY_HEADS * HEAD_SIZE), (LAYER_PARAMETERS ** -0.5), 0.0017089844, ((0, 8), (1, 4)), jnp.float32),
        "key_momentum": gaussian(arg_keys[16], (MODEL_WIDTH, KEY_VALUE_HEADS * HEAD_SIZE), (LAYER_PARAMETERS ** -0.5), 0.0017089844, ((0, 8), (1, 4)), jnp.float32),
        "value_momentum": gaussian(arg_keys[17], (MODEL_WIDTH, KEY_VALUE_HEADS * HEAD_SIZE), (LAYER_PARAMETERS ** -0.5), 0.0017089844, ((0, 8), (1, 4)), jnp.float32),
        "m_output": gaussian(arg_keys[18], (MODEL_WIDTH, QUERY_HEADS * HEAD_SIZE), (LAYER_PARAMETERS ** -0.5), 0.0017089844, ((0, 8), (1, 4)), jnp.float32),
        "m_gate": gaussian(arg_keys[19], (MODEL_WIDTH, FF), (LAYER_PARAMETERS ** -0.5), 0.0017089844, ((0, 8), (1, 4)), jnp.float32),
        "m_up": gaussian(arg_keys[20], (MODEL_WIDTH, FF), (LAYER_PARAMETERS ** -0.5), 0.0017089844, ((0, 8), (1, 4)), jnp.float32),
        "m_down": gaussian(arg_keys[21], (MODEL_WIDTH, FF), (LAYER_PARAMETERS ** -0.5), 0.0017089844, ((0, 8), (1, 4)), jnp.float32),
        "m_gain_attn": gaussian(arg_keys[22], (MODEL_WIDTH,), (LAYER_PARAMETERS ** -0.5), 0.0017089844, ((0, 8),), jnp.float32),
        "m_gain_post_attn": gaussian(arg_keys[23], (MODEL_WIDTH,), (LAYER_PARAMETERS ** -0.5), 0.0017089844, ((0, 8),), jnp.float32),
        "m_gain_ffn": gaussian(arg_keys[24], (MODEL_WIDTH,), (LAYER_PARAMETERS ** -0.5), 0.0017089844, ((0, 8),), jnp.float32),
        "m_gain_post_ffn": gaussian(arg_keys[25], (MODEL_WIDTH,), (LAYER_PARAMETERS ** -0.5), 0.0017089844, ((0, 8),), jnp.float32),
    }


@jax.custom_vjp
def lower_precision(v):
    return lax.optimization_barrier(v.astype(jnp.bfloat16)).astype(jnp.float32)

@jax.custom_vjp
def low_back(v):
    return v

def low_keep(v):
    return (lower_precision(v), None)

def low_pass(kept, grad):
    return (grad,)

def back_keep(v):
    return (v, None)

def back_low(kept, grad):
    return (lower_precision(grad),)
lower_precision.defvjp(low_keep, low_pass)
low_back.defvjp(back_keep, back_low)
epsilon = 1e-06
softcap = 50.0
decay_steps = 1000.0
base_rate = 1.0
highest = lax.Precision.HIGHEST

def round_pair(value_rows):
    return lower_precision(low_back(value_rows))

def rms_scale(value_rows, gain_vec):
    inverse = lax.rsqrt(lax.optimization_barrier(jnp.mean(value_rows * value_rows, axis=-1, keepdims=True)) + epsilon)
    return value_rows * inverse * (1.0 + gain_vec)

def rotary_embedding(vectors, token_position):
    half_dim = vectors.shape[-1] // 2
    frequency = jnp.exp(jnp.arange(half_dim, dtype=jnp.float32) * (-2.0 * math.log(10000.0) / vectors.shape[-1]))
    angles = token_position.astype(jnp.float32)[..., None, None] * frequency
    cosine = jnp.cos(angles)
    sine_part = jnp.sin(angles)
    first_half = vectors[..., :half_dim]
    second = vectors[..., half_dim:]
    return jnp.concatenate([first_half * cosine - second * sine_part, second * cosine + first_half * sine_part], axis=-1)

def soft_probs(raw_scores, allowed):
    capped = softcap * jnp.tanh(raw_scores / softcap)
    masked = jnp.where(allowed, capped, -1e+30)
    return jax.nn.softmax(masked, axis=-1)

def layer(activity, seg_ids, token_position, weights):
    w_query, key_weight, value_weight, w_output, w_gate, w_up, w_down, gain_attn, gain_post_attn, gain_ffn, gain_post_ffn = weights
    head_groups = activity.shape[0]
    token_length = activity.shape[1]
    attn_in = lower_precision(rms_scale(activity, lower_precision(gain_attn)))
    query_proj = low_back(jnp.einsum('gld,de->gle', attn_in, lower_precision(w_query), precision=highest))
    key_projected = low_back(jnp.einsum('gld,de->gle', attn_in, lower_precision(key_weight), precision=highest))
    value_projected = jnp.einsum('gld,de->gle', attn_in, lower_precision(value_weight), precision=highest)
    query_rows = lower_precision(rotary_embedding(query_proj.reshape(head_groups, token_length, QUERY_HEADS, HEAD_SIZE), token_position))
    key_row_block = lower_precision(rotary_embedding(key_projected.reshape(head_groups, token_length, KEY_VALUE_HEADS, HEAD_SIZE), token_position))
    value_rows = round_pair(value_projected.reshape(head_groups, token_length, KEY_VALUE_HEADS, HEAD_SIZE))
    grouped_heads = query_rows.reshape(head_groups, token_length, KEY_VALUE_HEADS, QUERY_HEADS // KEY_VALUE_HEADS, HEAD_SIZE)
    raw_scores = low_back(jnp.einsum('gqkrd,gskd->gkrqs', grouped_heads, key_row_block, precision=highest) * HEAD_SIZE ** (-0.5))
    token_index = jnp.arange(token_length)
    allowed = (token_index[:, None] >= token_index[None, :])[None] & (seg_ids[:, :, None] == seg_ids[:, None, :])
    attn_probs = lower_precision(soft_probs(raw_scores, allowed[:, None, None]))
    heads_out = round_pair(jnp.einsum('gkrqs,gskd->gqkrd', attn_probs, value_rows, precision=highest)).reshape(head_groups, token_length, QUERY_HEADS * HEAD_SIZE)
    attn_out = low_back(jnp.einsum('gle,de->gld', heads_out, lower_precision(w_output), precision=highest))
    middle = activity + rms_scale(attn_out, lower_precision(gain_post_attn))
    ffn_in = lower_precision(rms_scale(middle, lower_precision(gain_ffn)))
    gate_pre = low_back(jnp.einsum('gld,df->glf', ffn_in, lower_precision(w_gate), precision=highest))
    up_pre = low_back(jnp.einsum('gld,df->glf', ffn_in, lower_precision(w_up), precision=highest))
    hidden = lower_precision(jax.nn.gelu(gate_pre, approximate=True) * up_pre)
    ffn_out = low_back(jnp.einsum('glf,df->gld', hidden, lower_precision(w_down), precision=highest))
    return middle + rms_scale(ffn_out, lower_precision(gain_post_ffn))

def reference(inputs, segment_ids, positions, cotangent, w_query, key_weight, value_weight, w_output, w_gate, w_up, w_down, gain_attn, gain_post_attn, gain_ffn, gain_post_ffn, m_query, key_momentum, value_momentum, m_output, m_gate, m_up, m_down, m_gain_attn, m_gain_post_attn, m_gain_ffn, m_gain_post_ffn):
    params = (w_query, key_weight, value_weight, w_output, w_gate, w_up, w_down, gain_attn, gain_post_attn, gain_ffn, gain_post_ffn)
    moments = (m_query, key_momentum, value_momentum, m_output, m_gate, m_up, m_down, m_gain_attn, m_gain_post_attn, m_gain_ffn, m_gain_post_ffn)
    seq_total = MB * SEQS_MB
    per_group = math.gcd(seq_total, max(1, 4096 // SEQ_LEN))
    blocks = seq_total // per_group
    stacked = (inputs.astype(jnp.float32).reshape(blocks, per_group, SEQ_LEN, MODEL_WIDTH), segment_ids.reshape(blocks, per_group, SEQ_LEN), positions.reshape(blocks, per_group, SEQ_LEN), cotangent.astype(jnp.float32).reshape(blocks, per_group, SEQ_LEN, MODEL_WIDTH))

    def one_block(running, pieces):
        block_in, block_seg, block_pos, block_cot = pieces
        result, pullback = jax.vjp(lambda activity, weights: layer(activity, block_seg, block_pos, weights), block_in, params)
        grad_in, grad_params = pullback(block_cot)
        running = tuple((summed_part + extra_part for summed_part, extra_part in zip(running, grad_params)))
        return (running, (result.astype(jnp.bfloat16), grad_in.astype(jnp.bfloat16)))
    zero_grads = tuple((jnp.zeros_like(weight_arr) for weight_arr in params))
    all_grads, (outputs, input_grads) = lax.scan(one_block, zero_grads, stacked)
    square_sum = sum((jnp.sum(grad_arr * grad_arr) for grad_arr in all_grads))
    grad_norm = jnp.sqrt(square_sum)
    factor = 1.0 / jnp.maximum(grad_norm, 1.0)
    rate_now = base_rate / math.sqrt(1.0 + STEP / decay_steps)
    new_moments = tuple((0.5 * moment + 0.5 * factor * grad_arr for moment, grad_arr in zip(moments, all_grads)))
    changes = tuple((-rate_now * (new_moment + 0.01 * weight_arr) for weight_arr, new_moment in zip(params[:7], new_moments[:7])))
    final_out = outputs.reshape(MB, SEQS_MB, SEQ_LEN, MODEL_WIDTH)
    final_grad = input_grads.reshape(MB, SEQS_MB, SEQ_LEN, MODEL_WIDTH)
    return (final_out, final_grad, grad_norm.reshape(1), changes[0], changes[1], changes[2], changes[3], changes[4], changes[5], changes[6], new_moments[0], new_moments[1], new_moments[2], new_moments[3], new_moments[4], new_moments[5], new_moments[6], new_moments[7], new_moments[8], new_moments[9], new_moments[10])
```

```python
import math

import jax
import jax.numpy as jnp
from jax import lax
from jax.sharding import PartitionSpec as P

HEAD = 256
STEP = 10
EPS = 1e-06
CAP = 50.0
RATE = 1.0 / math.sqrt(1.0 + STEP / 1000.0)
SCALE = HEAD ** (-0.5)
BF = jnp.bfloat16
F32 = jnp.float32


def flip(axis, size, mask):
    return dict(axis_name=axis, perm=[(i, i ^ mask) for i in range(size)])


def after(value, other):
    return lax.optimization_barrier((value, other))[0]


def gather_rows(own, sizes, wait):
    dp, ctx = sizes["dp"], sizes["ctx"]
    rows, cols = own.shape
    if wait is not None:
        own = after(own, wait)
    if dp != 4:
        out = lax.all_gather(own, ("dp", "ctx"), axis=0, tiled=True)
        return out, own
    me = lax.axis_index("dp")
    half = rows // 2 // 16 * 16
    from_x = lax.ppermute(own, **flip("dp", dp, 1))
    from_y = lax.ppermute(own, **flip("dp", dp, 2))
    far_top = lax.ppermute(from_y[:half], **flip("dp", dp, 1))
    far_low = lax.ppermute(from_x[half:], **flip("dp", dp, 2))
    mine = jnp.zeros((dp, rows, cols), own.dtype)
    mine = lax.dynamic_update_slice(mine, own[None], (me, 0, 0))
    mine = lax.dynamic_update_slice(mine, from_x[None], (me ^ 1, 0, 0))
    mine = lax.dynamic_update_slice(mine, from_y[None], (me ^ 2, 0, 0))
    mine = lax.dynamic_update_slice(mine, far_top[None], (me ^ 3, 0, 0))
    mine = lax.dynamic_update_slice(mine, far_low[None], (me ^ 3, half, 0))
    if ctx == 2:
        other = lax.ppermute(mine, **flip("ctx", ctx, 1))
        core = lax.axis_index("ctx")
        out = jnp.zeros((dp, ctx, rows, cols), own.dtype)
        out = lax.dynamic_update_slice(out, mine[:, None], (0, core, 0, 0))
        out = lax.dynamic_update_slice(out, other[:, None], (0, 1 - core, 0, 0))
    else:
        out = lax.all_gather(mine, "ctx", axis=1)
    return out.reshape(dp * ctx * rows, cols), from_x


def scatter_rows(full, sizes, wait):
    dp, ctx = sizes["dp"], sizes["ctx"]
    full = full.astype(BF)
    if wait is not None:
        full = after(full, wait)
    rows = full.shape[0] // (dp * ctx)
    cols = full.shape[1]
    if dp != 4:
        out = lax.psum_scatter(full, ("dp", "ctx"), scatter_dimension=0, tiled=True)
        return out.astype(F32), out
    blocks = full.reshape(dp, ctx, rows, cols)
    if ctx == 2:
        core = lax.axis_index("ctx")
        send = lax.dynamic_index_in_dim(blocks, 1 - core, 1, keepdims=False)
        keep = lax.dynamic_index_in_dim(blocks, core, 1, keepdims=False)
        got = lax.ppermute(send, **flip("ctx", ctx, 1))
    else:
        keep = lax.psum_scatter(blocks, "ctx", scatter_dimension=1, tiled=False)
        got = None
    me = lax.axis_index("dp")
    half = rows // 2 // 16 * 16

    def part(mask, low, high):
        size = (1, high - low, cols)
        piece = lax.dynamic_slice(keep, (me ^ mask, low, 0), size)[0].astype(F32)
        if got is not None:
            piece = piece + lax.dynamic_slice(got, (me ^ mask, low, 0), size)[0].astype(F32)
        return piece

    far_top = lax.ppermute(part(3, 0, half).astype(BF), **flip("dp", dp, 1))
    far_low = lax.ppermute(part(3, half, rows).astype(BF), **flip("dp", dp, 2))
    to_y = jnp.concatenate([part(2, 0, half) + far_top.astype(F32), part(2, half, rows)])
    to_x = jnp.concatenate([part(1, 0, half), part(1, half, rows) + far_low.astype(F32)])
    by_y = lax.ppermute(to_y.astype(BF), **flip("dp", dp, 2))
    by_x = lax.ppermute(to_x.astype(BF), **flip("dp", dp, 1))
    total = part(0, 0, rows) + by_x.astype(F32) + by_y.astype(F32)
    return total, far_top


def sum_mp(part, sizes):
    if sizes["mp"] != 4:
        return lax.psum(part, "mp")
    place = lax.axis_index("mp")
    inner = (place == 1) | (place == 2)
    near = lax.ppermute(part, "mp", [(0, 1), (3, 2)])
    pair = (part.astype(F32) + near.astype(F32)).astype(BF)
    across = lax.ppermute(pair, "mp", [(1, 2), (2, 1)])
    total = (pair.astype(F32) + across.astype(F32)).astype(BF)
    back = lax.ppermute(total, "mp", [(1, 0), (2, 3)])
    return jnp.where(inner, total, back)


def sum_small(value, axes, sizes):
    for axis in axes:
        size = sizes[axis]
        step = 1
        while step < size:
            value = value + lax.ppermute(value, **flip(axis, size, step))
            step *= 2
    return value


def swap_ctx(local, sizes):
    if sizes["ctx"] != 2:
        return lax.all_gather(local, "ctx", axis=0, tiled=True)
    other = lax.ppermute(local, **flip("ctx", 2, 1))
    first = lax.axis_index("ctx") == 0
    return jnp.concatenate([jnp.where(first, local, other), jnp.where(first, other, local)])


def scatter_ctx(full, sizes):
    if sizes["ctx"] != 2:
        return lax.psum_scatter(full.astype(BF), "ctx", scatter_dimension=0, tiled=True).astype(F32)
    core = lax.axis_index("ctx")
    rows = full.shape[0] // 2
    send = lax.dynamic_slice_in_dim(full, (1 - core) * rows, rows).astype(BF)
    keep = lax.dynamic_slice_in_dim(full, core * rows, rows)
    return keep.astype(BF).astype(F32) + lax.ppermute(send, **flip("ctx", 2, 1)).astype(F32)


def dot(a, b):
    return lax.dot_general(a, b, (((1,), (0,)), ((), ())), preferred_element_type=F32)


def dot_t(a, b):
    return lax.dot_general(a, b, (((1,), (1,)), ((), ())), preferred_element_type=F32)


def t_dot(a, b):
    return lax.dot_general(a, b, (((0,), (0,)), ((), ())), preferred_element_type=F32)


def inverse_rms(v):
    return lax.rsqrt(jnp.mean(v * v, axis=-1, keepdims=True) + EPS)


def norm_back(v, r, gain, dy):
    scaled = (1.0 + gain) * dy
    mean = jnp.mean(scaled * v, axis=-1, keepdims=True)
    return r * scaled - v * (r * r * r) * mean, jnp.sum(v * r * dy, axis=0)


def rotate(v, cosine, sine):
    a, b = v[:, : HEAD // 2], v[:, HEAD // 2 :]
    return jnp.concatenate([a * cosine - b * sine, b * cosine + a * sine], axis=1)


GELU_C = math.sqrt(2.0 / math.pi)


def gelu_parts(u):
    tanh = jnp.tanh(GELU_C * (u + 0.044715 * u * u * u))
    value = 0.5 * u * (1.0 + tanh)
    slope = 0.5 * (1.0 + tanh) + 0.5 * u * (1.0 - tanh * tanh) * GELU_C * (
        1.0 + 3.0 * 0.044715 * u * u
    )
    return value, slope


def attend(queries, keys, values, allowed):
    raw = dot_t(queries, keys) * SCALE
    tanh = jnp.tanh(raw / CAP)
    heads = queries.shape[0] // allowed.shape[0]
    mask = jnp.concatenate([allowed] * heads, axis=0)
    weight = jnp.where(mask, jnp.exp(CAP * tanh), 0.0)
    probs = weight / jnp.sum(weight, axis=1, keepdims=True)
    out = dot(probs.astype(BF), values).astype(BF)
    return out, (probs, tanh)


def attend_back(saved, queries, keys, values, d_out):
    probs, tanh = saved
    d_probs = dot_t(d_out, values)
    inner = jnp.sum(probs * d_probs, axis=1, keepdims=True)
    d_raw = (probs * (d_probs - inner) * (1.0 - tanh * tanh)).astype(BF)
    d_queries = dot(d_raw, keys) * SCALE
    d_keys = t_dot(d_raw, queries) * SCALE
    d_values = t_dot(probs.astype(BF), d_out)
    return d_queries, d_keys, d_values


def per_device(
    sizes,
    inputs,
    segment_ids,
    positions,
    cotangent,
    *params,
):
    masters, moments = params[:11], params[11:]
    batches, seqs, tokens, width = inputs.shape
    assert seqs == 1
    full_len = segment_ids.shape[2]
    q_cols, k_cols = masters[0].shape[1], masters[1].shape[1]
    heads = q_cols // HEAD
    assert k_cols == HEAD
    cuts = 2 if tokens >= 512 else 1
    unit = tokens // cuts

    low = [w.astype(BF) for w in masters[:7]]
    qkv_own = jnp.concatenate(low[:3], axis=1)
    gains_own = jnp.stack([g.astype(BF) for g in masters[7:]], axis=1)
    gains = lax.all_gather(gains_own, ("dp", "ctx"), axis=0, tiled=True).astype(F32)
    gain_one, gain_two, gain_three, gain_four = [gains[:, i] for i in range(4)]
    w_qkv, mark = gather_rows(qkv_own, sizes, None)
    w_out, mark = gather_rows(low[3], sizes, mark)
    w_gate, mark = gather_rows(low[4], sizes, mark)
    w_up, mark = gather_rows(low[5], sizes, mark)
    w_down, mark = gather_rows(low[6], sizes, mark)

    start = lax.axis_index("ctx") * tokens
    causal = (start + jnp.arange(tokens))[:, None] >= jnp.arange(full_len)[None, :]
    frequency = jnp.exp(
        jnp.arange(HEAD // 2, dtype=F32) * (-2.0 * math.log(10000.0) / HEAD)
    )

    state = []
    for mb in range(batches):
        x = inputs[mb, 0].astype(F32)
        r_one = inverse_rms(x)
        attn_in = (x * r_one * (1.0 + gain_one)).astype(BF)
        angles = positions[mb, 0].astype(F32)[:, None] * frequency
        cosine, sine = jnp.cos(angles), jnp.sin(angles)
        seg = segment_ids[mb, 0]
        seg_local = lax.dynamic_slice_in_dim(seg, start, tokens)
        allowed = causal & (seg_local[:, None] == seg[None, :])
        proj = dot(attn_in, w_qkv)
        queries = jnp.concatenate(
            [rotate(proj[:, h * HEAD : (h + 1) * HEAD], cosine, sine) for h in range(heads)]
        ).astype(BF)
        keys = rotate(proj[:, q_cols : q_cols + HEAD], cosine, sine).astype(BF)
        values = proj[:, q_cols + HEAD :].astype(BF)
        both = swap_ctx(jnp.concatenate([keys, values], axis=1), sizes)
        keys_all, values_all = both[:, :HEAD], both[:, HEAD:]
        out, saved = attend(queries, keys_all, values_all, allowed)
        heads_out = jnp.concatenate(jnp.split(out, heads, axis=0), axis=1)
        state.append(
            dict(
                x=x, r_one=r_one, attn_in=attn_in, cosine=cosine, sine=sine, queries=queries,
                keys=keys_all, values=values_all, saved=saved, heads_out=heads_out,
            )
        )

    units = [(mb, cut) for mb in range(batches) for cut in range(cuts)]
    work = []
    for mb, cut in units:
        rows = slice(cut * unit, (cut + 1) * unit)
        part = dot_t(state[mb]["heads_out"][rows], w_out).astype(BF)
        work.append(dict(rows=rows, mb=mb, attn_low=sum_mp(part, sizes)))
    for w in work:
        attn = w["attn_low"].astype(F32)
        r_two = inverse_rms(attn)
        mid = state[w["mb"]]["x"][w["rows"]] + attn * r_two * (1.0 + gain_two)
        r_three = inverse_rms(mid)
        ffn_in = (mid * r_three * (1.0 + gain_three)).astype(BF)
        gate, up = dot(ffn_in, w_gate), dot(ffn_in, w_up)
        value, slope = gelu_parts(gate)
        hidden = (value * up).astype(BF)
        part = dot_t(hidden, w_down).astype(BF)
        w.update(
            mid=mid, r_two=r_two, r_three=r_three, ffn_in=ffn_in, gate=gate, up=up, hidden=hidden,
            ffn_low=sum_mp(part, sizes),
        )
    for w in work:
        ffn = w["ffn_low"].astype(F32)
        r_four = inverse_rms(ffn)
        grad = cotangent[w["mb"], 0][w["rows"]].astype(F32)
        w["output"] = (w["mid"] + ffn * r_four * (1.0 + gain_four)).astype(BF)
        d_ffn, w["g_four"] = norm_back(ffn, r_four, gain_four, grad)
        d_ffn = d_ffn.astype(BF)
        d_hidden = dot(d_ffn, w_down)
        value, slope = gelu_parts(w["gate"])
        d_gate = (d_hidden * w["up"] * slope).astype(BF)
        d_up = (d_hidden * value).astype(BF)
        part = (dot_t(d_gate, w_gate) + dot_t(d_up, w_up)).astype(BF)
        w.update(grad=grad, d_ffn=d_ffn, d_gate=d_gate, d_up=d_up, d_in_low=sum_mp(part, sizes))
    for w in work:
        d_in = w["d_in_low"].astype(F32)
        back, w["g_three"] = norm_back(w["mid"], w["r_three"], gain_three, d_in)
        d_mid = w["grad"] + back
        attn = w["attn_low"].astype(F32)
        d_attn, w["g_two"] = norm_back(attn, w["r_two"], gain_two, d_mid)
        d_attn = d_attn.astype(BF)
        w.update(d_mid=d_mid, d_attn=d_attn, d_heads=dot(d_attn, w_out).astype(BF))

    def rows_of(key):
        return jnp.concatenate([w[key] for w in work])

    ffn_in = rows_of("ffn_in")
    g_down = t_dot(rows_of("d_ffn"), rows_of("hidden"))
    g_gate = t_dot(ffn_in, rows_of("d_gate"))
    g_up = t_dot(ffn_in, rows_of("d_up"))
    s_down, mark = scatter_rows(g_down, sizes, None)
    s_gate, mark = scatter_rows(g_gate, sizes, mark)
    s_up, mark = scatter_rows(g_up, sizes, mark)

    for mb in range(batches):
        s = state[mb]
        d_heads = jnp.concatenate([w["d_heads"] for w in work if w["mb"] == mb])
        d_out = jnp.concatenate(jnp.split(d_heads, heads, axis=1))
        d_queries, d_keys, d_values = attend_back(
            s["saved"], s["queries"], s["keys"], s["values"], d_out
        )
        d_kv = scatter_ctx(jnp.concatenate([d_keys, d_values], axis=1), sizes)
        pieces = [rotate(q, s["cosine"], -s["sine"]) for q in jnp.split(d_queries, heads)]
        pieces += [rotate(d_kv[:, :HEAD], s["cosine"], -s["sine"]), d_kv[:, HEAD:]]
        s["d_proj"] = jnp.concatenate(pieces, axis=1).astype(BF)
    for w in work:
        part = dot_t(state[w["mb"]]["d_proj"][w["rows"]], w_qkv).astype(BF)
        w["d_attn_in"] = sum_mp(part, sizes)

    g_out = t_dot(rows_of("d_attn"), jnp.concatenate([s["heads_out"] for s in state]))
    g_qkv = t_dot(
        jnp.concatenate([s["attn_in"] for s in state]),
        jnp.concatenate([s["d_proj"] for s in state]),
    )
    s_out, mark = scatter_rows(g_out, sizes, mark)
    s_qkv, mark = scatter_rows(g_qkv, sizes, mark)

    for w in work:
        s = state[w["mb"]]
        back, w["g_one"] = norm_back(
            s["x"][w["rows"]], s["r_one"][w["rows"]], gain_one, w["d_attn_in"].astype(F32)
        )
        w["input_grad"] = (w["d_mid"] + back).astype(BF)

    gain_grads = jnp.stack(
        [sum(w[key] for w in work) for key in ("g_one", "g_two", "g_three", "g_four")]
    )
    gain_grads = sum_small(gain_grads, ("ctx", "dp"), sizes)
    summed = (
        s_qkv[:, :q_cols], s_qkv[:, q_cols : q_cols + k_cols], s_qkv[:, q_cols + k_cols :],
        s_out, s_gate, s_up, s_down,
    )
    weight_sq = sum(jnp.sum(g * g) for g in (s_qkv, s_out, s_gate, s_up, s_down))
    weight_sq = sum_small(weight_sq.reshape(1, 1), ("ctx", "dp", "mp"), sizes)[0, 0]
    norm_value = jnp.sqrt(weight_sq + jnp.sum(gain_grads * gain_grads))
    factor = 1.0 / jnp.maximum(norm_value, 1.0)
    own = masters[7].shape[0]
    place = (lax.axis_index("dp") * sizes["ctx"] + lax.axis_index("ctx")) * own
    own_gains = lax.dynamic_slice_in_dim(gain_grads, place, own, 1)
    summed += tuple(own_gains[i] for i in range(4))
    new_moments = tuple(0.5 * m + 0.5 * factor * g for m, g in zip(moments, summed))
    changes = tuple(-RATE * (m + 0.01 * w) for w, m in zip(masters[:7], new_moments[:7]))

    def whole(key):
        return rows_of(key).reshape(inputs.shape)

    return (
        whole("output"), whole("input_grad"), norm_value.reshape(1), *changes, *new_moments
    )


def solution(mesh):
    sizes = dict(mesh.shape)
    weight, vector = P(("dp", "ctx"), "mp"), P(("dp", "ctx"))
    params = (weight,) * 7 + (vector,) * 4
    data = P(None, "dp", "ctx", None)

    def run(*args):
        return per_device(sizes, *args)

    return jax.shard_map(
        run,
        mesh=mesh,
        in_specs=(data, P(None, "dp", None), P(None, "dp", "ctx"), data) + params + params,
        out_specs=(data, data, P()) + (weight,) * 7 + params,
        check_vma=False,
    )
```

```python
import math

import jax
import jax.numpy as jnp
from jax import lax
from jax.experimental import pallas as pl
from jax.experimental.pallas import tpu as pltpu
from jax.sharding import PartitionSpec as P

HEAD = 256
STEP = 10
EPS = 1e-06
CAP = 50.0
RATE = 1.0 / math.sqrt(1.0 + STEP / 1000.0)
SCALE = HEAD ** (-0.5)
BF = jnp.bfloat16
F32 = jnp.float32


def flip(axis, size, mask):
    return dict(axis_name=axis, perm=[(i, i ^ mask) for i in range(size)])


def after(value, other):
    return lax.optimization_barrier((value, other))[0]


def gather_rows(own, sizes, wait):
    dp, ctx = sizes["dp"], sizes["ctx"]
    rows, cols = own.shape
    if wait is not None:
        own = after(own, wait)
    if dp != 4:
        out = lax.all_gather(own, ("dp", "ctx"), axis=0, tiled=True)
        return out, own
    me = lax.axis_index("dp")
    half = rows // 2 // 16 * 16
    from_x = lax.ppermute(own, **flip("dp", dp, 1))
    from_y = lax.ppermute(own, **flip("dp", dp, 2))
    far_top = lax.ppermute(from_y[:half], **flip("dp", dp, 1))
    far_low = lax.ppermute(from_x[half:], **flip("dp", dp, 2))
    mine = jnp.zeros((dp, rows, cols), own.dtype)
    mine = lax.dynamic_update_slice(mine, own[None], (me, 0, 0))
    mine = lax.dynamic_update_slice(mine, from_x[None], (me ^ 1, 0, 0))
    mine = lax.dynamic_update_slice(mine, from_y[None], (me ^ 2, 0, 0))
    mine = lax.dynamic_update_slice(mine, far_top[None], (me ^ 3, 0, 0))
    mine = lax.dynamic_update_slice(mine, far_low[None], (me ^ 3, half, 0))
    if ctx == 2:
        other = lax.ppermute(mine, **flip("ctx", ctx, 1))
        core = lax.axis_index("ctx")
        out = jnp.zeros((dp, ctx, rows, cols), own.dtype)
        out = lax.dynamic_update_slice(out, mine[:, None], (0, core, 0, 0))
        out = lax.dynamic_update_slice(out, other[:, None], (0, 1 - core, 0, 0))
    else:
        out = lax.all_gather(mine, "ctx", axis=1)
    return out.reshape(dp * ctx * rows, cols), from_x


def scatter_rows(full, sizes, wait):
    dp, ctx = sizes["dp"], sizes["ctx"]
    full = full.astype(BF)
    if wait is not None:
        full = after(full, wait)
    rows = full.shape[0] // (dp * ctx)
    cols = full.shape[1]
    if dp != 4:
        out = lax.psum_scatter(full, ("dp", "ctx"), scatter_dimension=0, tiled=True)
        return out.astype(F32), out
    blocks = full.reshape(dp, ctx, rows, cols)
    if ctx == 2:
        core = lax.axis_index("ctx")
        send = lax.dynamic_index_in_dim(blocks, 1 - core, 1, keepdims=False)
        keep = lax.dynamic_index_in_dim(blocks, core, 1, keepdims=False)
        got = lax.ppermute(send, **flip("ctx", ctx, 1))
    else:
        keep = lax.psum_scatter(blocks, "ctx", scatter_dimension=1, tiled=False)
        got = None
    me = lax.axis_index("dp")
    half = rows // 2 // 16 * 16

    def part(mask, low, high):
        size = (1, high - low, cols)
        piece = lax.dynamic_slice(keep, (me ^ mask, low, 0), size)[0].astype(F32)
        if got is not None:
            piece = piece + lax.dynamic_slice(got, (me ^ mask, low, 0), size)[0].astype(F32)
        return piece

    far_top = lax.ppermute(part(3, 0, half).astype(BF), **flip("dp", dp, 1))
    far_low = lax.ppermute(part(3, half, rows).astype(BF), **flip("dp", dp, 2))
    to_y = jnp.concatenate([part(2, 0, half) + far_top.astype(F32), part(2, half, rows)])
    to_x = jnp.concatenate([part(1, 0, half), part(1, half, rows) + far_low.astype(F32)])
    by_y = lax.ppermute(to_y.astype(BF), **flip("dp", dp, 2))
    by_x = lax.ppermute(to_x.astype(BF), **flip("dp", dp, 1))
    total = part(0, 0, rows) + by_x.astype(F32) + by_y.astype(F32)
    return total, far_top


def sum_mp(part, sizes):
    if sizes["mp"] != 4:
        return lax.psum(part, "mp")
    place = lax.axis_index("mp")
    inner = (place == 1) | (place == 2)
    near = lax.ppermute(part, "mp", [(0, 1), (3, 2)])
    pair = (part.astype(F32) + near.astype(F32)).astype(BF)
    across = lax.ppermute(pair, "mp", [(1, 2), (2, 1)])
    total = (pair.astype(F32) + across.astype(F32)).astype(BF)
    back = lax.ppermute(total, "mp", [(1, 0), (2, 3)])
    return jnp.where(inner, total, back)


def sum_small(value, axes, sizes):
    for axis in axes:
        size = sizes[axis]
        step = 1
        while step < size:
            value = value + lax.ppermute(value, **flip(axis, size, step))
            step *= 2
    return value


def swap_ctx(local, sizes):
    if sizes["ctx"] != 2:
        return lax.all_gather(local, "ctx", axis=0, tiled=True)
    other = lax.ppermute(local, **flip("ctx", 2, 1))
    first = lax.axis_index("ctx") == 0
    return jnp.concatenate([jnp.where(first, local, other), jnp.where(first, other, local)])


def scatter_ctx(full, sizes):
    if sizes["ctx"] != 2:
        return lax.psum_scatter(full.astype(BF), "ctx", scatter_dimension=0, tiled=True).astype(F32)
    core = lax.axis_index("ctx")
    rows = full.shape[0] // 2
    send = lax.dynamic_slice_in_dim(full, (1 - core) * rows, rows).astype(BF)
    keep = lax.dynamic_slice_in_dim(full, core * rows, rows)
    return keep.astype(BF).astype(F32) + lax.ppermute(send, **flip("ctx", 2, 1)).astype(F32)


def dot(a, b):
    return lax.dot_general(a, b, (((1,), (0,)), ((), ())), preferred_element_type=F32)


def dot_t(a, b):
    return lax.dot_general(a, b, (((1,), (1,)), ((), ())), preferred_element_type=F32)


def t_dot(a, b):
    return lax.dot_general(a, b, (((0,), (0,)), ((), ())), preferred_element_type=F32)


def inverse_rms(v):
    return lax.rsqrt(jnp.mean(v * v, axis=-1, keepdims=True) + EPS)


def norm_back(v, r, gain, dy):
    scaled = (1.0 + gain) * dy
    mean = jnp.mean(scaled * v, axis=-1, keepdims=True)
    return r * scaled - v * (r * r * r) * mean, jnp.sum(v * r * dy, axis=0)


def rotate(v, cosine, sine):
    a, b = v[:, : HEAD // 2], v[:, HEAD // 2 :]
    return jnp.concatenate([a * cosine - b * sine, b * cosine + a * sine], axis=1)


GELU_C = math.sqrt(2.0 / math.pi)


def gelu_parts(u):
    tanh = jnp.tanh(GELU_C * (u + 0.044715 * u * u * u))
    value = 0.5 * u * (1.0 + tanh)
    slope = 0.5 * (1.0 + tanh) + 0.5 * u * (1.0 - tanh * tanh) * GELU_C * (
        1.0 + 3.0 * 0.044715 * u * u
    )
    return value, slope


def attend(queries, keys, values, allowed):
    raw = dot_t(queries, keys) * SCALE
    tanh = jnp.tanh(raw / CAP)
    heads = queries.shape[0] // allowed.shape[0]
    mask = jnp.concatenate([allowed] * heads, axis=0)
    weight = jnp.where(mask, jnp.exp(CAP * tanh), 0.0)
    probs = weight / jnp.sum(weight, axis=1, keepdims=True)
    out = dot(probs.astype(BF), values).astype(BF)
    return out, (probs, tanh)


def attend_back(saved, queries, keys, values, d_out):
    probs, tanh = saved
    d_probs = dot_t(d_out, values)
    inner = jnp.sum(probs * d_probs, axis=1, keepdims=True)
    d_raw = (probs * (d_probs - inner) * (1.0 - tanh * tanh)).astype(BF)
    d_queries = dot(d_raw, keys) * SCALE
    d_keys = t_dot(d_raw, queries) * SCALE
    d_values = t_dot(probs.astype(BF), d_out)
    return d_queries, d_keys, d_values


MESH = pl.DeviceIdType.MESH
UNIT = 256
TILE = 256


def ffn_kernel(
    heads_ref, scale_ref, x_hbm, cot_hbm, w_out_hbm, own_hbm,
    out_hbm, ffn_in_hbm, hidden_hbm, d_ffn_hbm, d_gate_hbm, d_up_hbm, d_attn_hbm, d_heads_hbm,
    d_mid_hbm, gain_ref, attn_hbm, slope_hbm, value_hbm,
    weights, w_out, send, near, across, total, xb, cb, ab, act, stage, d_mid, d_heads,
    line_send, line_recv, credit, local, ag_send, ag_recv, ag_local,
):
    dp, core, z = lax.axis_index("dp"), lax.axis_index("ctx"), lax.axis_index("mp")
    width, units = xb.shape[1], weights.shape[2]
    rows_own = own_hbm.shape[1]
    half = rows_own // 2
    inner = (z == 1) | (z == 2)
    outer = (z == 0) | (z == 3)
    x_peer, y_peer = (dp ^ 1, core, z), (dp ^ 2, core, z)
    core_peer = (dp, 1 - core, z)
    near_peer = (dp, core, z ^ 1)
    far_peer = (dp, core, 3 - z)

    barrier = pltpu.get_barrier_semaphore()
    for peer in (x_peer, y_peer, core_peer, near_peer, far_peer):
        pl.semaphore_signal(barrier, inc=1, device_id=peer, device_id_type=MESH)
    pl.semaphore_wait(barrier, 5)

    def block(mask, other=False, low=0, size=rows_own):
        owner = (dp ^ mask) * 2 + ((1 - core) if other else core)
        return pl.ds(pl.multiple_of(owner * rows_own + low, 16), size)

    def gather(w, name, recv=False):
        table = {
            "x": (0, block(0), x_peer, block(1)),
            "y": (1, block(0), y_peer, block(2)),
            "top": (2, block(2, False, 0, half), x_peer, block(3, False, 0, half)),
            "low": (3, block(1, False, half, half), y_peer, block(3, False, half, half)),
            "own_c": (4, block(0), core_peer, block(0, True)),
            "x_c": (5, block(1), core_peer, block(1, True)),
            "y_c": (6, block(2), core_peer, block(2, True)),
            "top_c": (7, block(3, False, 0, half), core_peer, block(3, True, 0, half)),
            "low_c": (8, block(3, False, half, half), core_peer, block(3, True, half, half)),
        }
        index, out_rows, peer, in_rows = table[name]
        rows = in_rows if recv else out_rows
        src = own_hbm.at[w] if name in ("x", "y", "own_c") else weights.at[w, rows]
        return pltpu.make_async_remote_copy(
            src_ref=src, dst_ref=weights.at[w, rows], send_sem=ag_send.at[w, index],
            recv_sem=ag_recv.at[w, index], device_id=peer, device_id_type=MESH,
        )

    def own_copy(w):
        return pltpu.make_async_copy(own_hbm.at[w], weights.at[w, block(0)], ag_local.at[w])

    def gather_first(w):
        for name in ("x", "y", "own_c"):
            gather(w, name).start()
        own_copy(w).start()

    def gather_second(w):
        gather(w, "x", True).wait_recv()
        gather(w, "low").start()
        gather(w, "x_c").start()
        gather(w, "y", True).wait_recv()
        gather(w, "top").start()
        gather(w, "y_c").start()

    def gather_third(w):
        for name in ("top", "low"):
            gather(w, name, True).wait_recv()
            gather(w, name + "_c").start()

    def gather_end(w):
        for name in ("own_c", "x_c", "y_c", "top_c", "low_c"):
            gather(w, name, True).wait_recv()
        own_copy(w).wait()
        for name in ("x", "y", "top", "low", "own_c", "x_c", "y_c", "top_c", "low_c"):
            gather(w, name).wait_send()

    def hop(kind, i):
        src = (send.at[i % 3], send.at[i % 3], total.at[i % 4])[kind]
        dst = (near.at[i % 3], across.at[i % 2], total.at[i % 4])[kind]
        return pltpu.make_async_remote_copy(
            src_ref=src, dst_ref=dst, send_sem=line_send.at[kind, i % 4],
            recv_sem=line_recv.at[kind, i % 4],
            device_id=far_peer if kind == 1 else near_peer, device_id_type=MESH,
        )

    def add_rows(dst, a, b):
        @pl.loop(0, UNIT // 16)
        def _(r):
            rows = pl.ds(pl.multiple_of(r * 16, 16), 16)
            dst[rows] = (a[rows].astype(F32) + b[rows].astype(F32)).astype(BF)

    def boundary(k, up=True, cross=True, back=True, done=True):
        @pl.when(outer)
        def _():
            if done:
                hop(2, k - 3).wait_recv()
            if cross:
                hop(0, k - 1).wait_send()
            if up:
                hop(0, k).start()

        @pl.when(inner)
        def _():
            if cross:
                i = k - 1
                hop(0, i).wait_recv()
                add_rows(send.at[i % 3], send.at[i % 3], near.at[i % 3])
                if isinstance(i, int):
                    if i >= 2:
                        pl.semaphore_wait(credit, 1)
                else:
                    pl.semaphore_wait(credit, 1)
                hop(1, i).start()
            if back:
                i = k - 2
                hop(1, i).wait_recv()
                hop(1, i).wait_send()
                add_rows(total.at[i % 4], send.at[i % 3], across.at[i % 2])
                if not isinstance(i, int) or i < 10:
                    pl.semaphore_signal(credit, inc=1, device_id=far_peer, device_id_type=MESH)
                hop(2, i).start()
            if done:
                hop(2, k - 3).wait_send()

    def rows_of(u):
        return pl.ds(pl.multiple_of(u * UNIT, UNIT), UNIT)

    def load(ref, u, dst, sem):
        return pltpu.make_async_copy(ref.at[rows_of(u)], dst, local.at[sem])

    def store(src, ref, u, sem):
        return pltpu.make_async_copy(src, ref.at[rows_of(u)], local.at[sem])

    def tile(n):
        return pl.ds(pl.multiple_of(n * TILE, TILE), TILE)

    def each_rows(body):
        @pl.loop(0, UNIT // 16)
        def _(r):
            body(pl.ds(pl.multiple_of(r * 16, 16), 16))

    def scale(i):
        return scale_ref[i : i + 1]

    def add_gain(index, v):
        gain_ref[index] += v[:8] + v[8:]

    def project_out(u, k):
        dst = send.at[k % 3]

        @pl.loop(0, width // TILE)
        def _(n):
            dst[:, tile(n)] = dot_t(heads_ref[rows_of(u)], w_out[tile(n)]).astype(BF)

    def middle(rows, u4):
        attn = total[u4, rows].astype(F32) if u4 is not None else ab[rows].astype(F32)
        r_two = inverse_rms(attn)
        return attn, r_two, xb[rows].astype(F32) + attn * r_two * scale(1)

    def forward(u, k):
        load(x_hbm, u, xb, 0).start()
        store(total.at[u], attn_hbm, u, 1).start()
        load(x_hbm, u, xb, 0).wait()

        def body(rows):
            _, _, mid = middle(rows, u)
            act[rows] = (mid * inverse_rms(mid) * scale(2)).astype(BF)

        each_rows(body)
        store(act, ffn_in_hbm, u, 2).start()

        @pl.loop(0, units // TILE)
        def _(f):
            gate = dot(act[...], weights[0, :, tile(f)])
            up = dot(act[...], weights[1, :, tile(f)])
            value, slope = gelu_parts(gate)
            stage[0, :, tile(f)] = (value * up).astype(BF)
            stage[1, :, tile(f)] = (slope * up).astype(BF)
            stage[2, :, tile(f)] = value.astype(BF)

        saves = ((0, hidden_hbm), (1, slope_hbm), (2, value_hbm))
        for i, ref in saves:
            store(stage.at[i], ref, u, 3 + i).start()
        dst = send.at[k % 3]

        @pl.loop(0, width // TILE)
        def _(n):
            dst[:, tile(n)] = dot_t(stage[0], weights[2, tile(n)]).astype(BF)

        for i, ref in saves:
            store(stage.at[i], ref, u, 3 + i).wait()
        store(total.at[u], attn_hbm, u, 1).wait()
        store(act, ffn_in_hbm, u, 2).wait()

    def backward(u, k):
        loads = (
            load(x_hbm, u, xb, 0), load(attn_hbm, u, ab, 1), load(cot_hbm, u, cb, 2),
            load(slope_hbm, u, stage.at[1], 4), load(value_hbm, u, stage.at[2], 5),
        )
        for copy in loads:
            copy.start()
        for copy in loads:
            copy.wait()

        def body(rows):
            _, _, mid = middle(rows, None)
            ffn = total[u, rows].astype(F32)
            r = inverse_rms(ffn)
            dy = cb[rows].astype(F32)
            xb[rows] = (mid + ffn * r * scale(3)).astype(BF)
            scaled = scale(3) * dy
            mean = jnp.mean(scaled * ffn, axis=-1, keepdims=True)
            act[rows] = (r * scaled - ffn * (r * r * r) * mean).astype(BF)
            add_gain(2, ffn * r * dy)

        each_rows(body)
        store(xb, out_hbm, u, 0).start()
        store(act, d_ffn_hbm, u, 1).start()

        @pl.loop(0, units // TILE)
        def _(f):
            d_hidden = dot(act[...], weights[2, :, tile(f)])
            stage[1, :, tile(f)] = (d_hidden * stage[1, :, tile(f)].astype(F32)).astype(BF)
            stage[2, :, tile(f)] = (d_hidden * stage[2, :, tile(f)].astype(F32)).astype(BF)

        store(stage.at[1], d_gate_hbm, u, 4).start()
        store(stage.at[2], d_up_hbm, u, 5).start()
        dst = send.at[k % 3]

        @pl.loop(0, width // TILE)
        def _(n):
            part = dot_t(stage[1], weights[0, tile(n)]) + dot_t(stage[2], weights[1, tile(n)])
            dst[:, tile(n)] = part.astype(BF)

        store(xb, out_hbm, u, 0).wait()
        store(act, d_ffn_hbm, u, 1).wait()
        store(stage.at[1], d_gate_hbm, u, 4).wait()
        store(stage.at[2], d_up_hbm, u, 5).wait()

    def last(u):
        loads = (load(x_hbm, u, xb, 0), load(attn_hbm, u, ab, 1), load(cot_hbm, u, cb, 2))
        for copy in loads:
            copy.start()
        for copy in loads:
            copy.wait()

        def body(rows):
            attn, r_two, mid = middle(rows, None)
            r = inverse_rms(mid)
            dy = total[u, rows].astype(F32)
            scaled = scale(2) * dy
            mean = jnp.mean(scaled * mid, axis=-1, keepdims=True)
            grad = cb[rows].astype(F32) + r * scaled - mid * (r * r * r) * mean
            add_gain(1, mid * r * dy)
            d_mid[rows] = grad
            scaled = scale(1) * grad
            mean = jnp.mean(scaled * attn, axis=-1, keepdims=True)
            act[rows] = (r_two * scaled - attn * (r_two * r_two * r_two) * mean).astype(BF)
            add_gain(0, attn * r_two * grad)

        each_rows(body)
        store(d_mid, d_mid_hbm, u, 0).start()
        store(act, d_attn_hbm, u, 1).start()
        for h in range(w_out.shape[1] // TILE):
            columns = slice(h * TILE, (h + 1) * TILE)
            d_heads[:, columns] = dot(act[...], w_out[:, columns]).astype(BF)
        store(d_heads, d_heads_hbm, u, 2).start()
        store(d_mid, d_mid_hbm, u, 0).wait()
        store(act, d_attn_hbm, u, 1).wait()
        store(d_heads, d_heads_hbm, u, 2).wait()

    gather_first(0)
    pltpu.make_async_copy(w_out_hbm, w_out, local.at[0]).start()
    gain_ref[...] = jnp.zeros_like(gain_ref)
    pltpu.make_async_copy(w_out_hbm, w_out, local.at[0]).wait()
    project_out(0, 0)
    boundary(0, cross=False, back=False, done=False)
    project_out(1, 1)
    project_out(2, 2)
    boundary(1, back=False, done=False)
    gather_second(0)
    gather_first(1)
    boundary(2, done=False)
    project_out(3, 3)
    gather_third(0)
    gather_second(1)
    gather_first(2)
    boundary(3)
    gather_third(1)
    gather_second(2)
    gather_third(2)
    for w in range(3):
        gather_end(w)
    forward(0, 4)

    @pl.loop(4, 7)
    def _(k):
        boundary(k)
        forward(k - 3, k + 1)

    @pl.loop(7, 11)
    def _(k):
        boundary(k)
        backward(k - 7, k + 1)

    for k in (11, 12, 13, 14):
        boundary(k, up=k < 12, cross=k < 13, back=k < 14)
        last(k - 11)


def ffn_call(heads_out, scales, x, cot, w_out, own):
    tokens, width = x.shape
    units = own.shape[2]
    assert tokens == 4 * UNIT
    full = jax.ShapeDtypeStruct((tokens, width), BF)
    wide = jax.ShapeDtypeStruct((tokens, units), BF)
    outs = (
        full, full, wide, full, wide, wide, full,
        jax.ShapeDtypeStruct((tokens, w_out.shape[1]), BF),
        jax.ShapeDtypeStruct((tokens, width), F32),
        jax.ShapeDtypeStruct((3, 8, width), F32),
        full, wide, wide,
    )
    anywhere, vmem = pl.BlockSpec(memory_space=pl.ANY), pl.BlockSpec(memory_space=pltpu.VMEM)
    dma = pltpu.SemaphoreType.DMA
    return pl.pallas_call(
        ffn_kernel,
        out_shape=outs,
        in_specs=[vmem, vmem, anywhere, anywhere, anywhere, anywhere],
        out_specs=[anywhere] * 9 + [vmem] + [anywhere] * 3,
        scratch_shapes=[
            pltpu.VMEM((3, width, units), BF),
            pltpu.VMEM(w_out.shape, BF),
            pltpu.VMEM((3, UNIT, width), BF),
            pltpu.VMEM((3, UNIT, width), BF),
            pltpu.VMEM((2, UNIT, width), BF),
            pltpu.VMEM((4, UNIT, width), BF),
            pltpu.VMEM((UNIT, width), BF),
            pltpu.VMEM((UNIT, width), BF),
            pltpu.VMEM((UNIT, width), BF),
            pltpu.VMEM((UNIT, width), BF),
            pltpu.VMEM((3, UNIT, units), BF),
            pltpu.VMEM((UNIT, width), F32),
            pltpu.VMEM((UNIT, w_out.shape[1]), BF),
            dma((3, 4)),
            dma((3, 4)),
            pltpu.SemaphoreType.REGULAR,
            dma((6,)),
            dma((3, 9)),
            dma((3, 9)),
            dma((3,)),
        ],
        compiler_params=pltpu.CompilerParams(
            collective_id=1, has_side_effects=True, vmem_limit_bytes=60 * 2**20
        ),
        name="ffn",
    )(heads_out, scales, x, cot, w_out, own)


def fast_device(
    sizes,
    inputs,
    segment_ids,
    positions,
    cotangent,
    *params,
):
    masters, moments = params[:11], params[11:]
    batches, seqs, tokens, width = inputs.shape
    assert seqs == 1
    full_len = segment_ids.shape[2]
    q_cols, k_cols = masters[0].shape[1], masters[1].shape[1]
    heads = q_cols // HEAD
    assert k_cols == HEAD
    cuts = 2 if tokens >= 512 else 1
    unit = tokens // cuts

    low = [w.astype(BF) for w in masters[:7]]
    qkv_own = jnp.concatenate(low[:3], axis=1)
    gains_own = jnp.stack([g.astype(BF) for g in masters[7:]], axis=1)
    gains = lax.all_gather(gains_own, ("dp", "ctx"), axis=0, tiled=True).astype(F32)
    gain_one, gain_two, gain_three, gain_four = [gains[:, i] for i in range(4)]
    w_qkv, mark = gather_rows(qkv_own, sizes, None)
    w_out, mark = gather_rows(low[3], sizes, mark)

    start = lax.axis_index("ctx") * tokens
    causal = (start + jnp.arange(tokens))[:, None] >= jnp.arange(full_len)[None, :]
    frequency = jnp.exp(
        jnp.arange(HEAD // 2, dtype=F32) * (-2.0 * math.log(10000.0) / HEAD)
    )

    state = []
    for mb in range(batches):
        x = inputs[mb, 0].astype(F32)
        r_one = inverse_rms(x)
        attn_in = (x * r_one * (1.0 + gain_one)).astype(BF)
        angles = positions[mb, 0].astype(F32)[:, None] * frequency
        cosine, sine = jnp.cos(angles), jnp.sin(angles)
        seg = segment_ids[mb, 0]
        seg_local = lax.dynamic_slice_in_dim(seg, start, tokens)
        allowed = causal & (seg_local[:, None] == seg[None, :])
        proj = dot(attn_in, w_qkv)
        queries = jnp.concatenate(
            [rotate(proj[:, h * HEAD : (h + 1) * HEAD], cosine, sine) for h in range(heads)]
        ).astype(BF)
        keys = rotate(proj[:, q_cols : q_cols + HEAD], cosine, sine).astype(BF)
        values = proj[:, q_cols + HEAD :].astype(BF)
        both = swap_ctx(jnp.concatenate([keys, values], axis=1), sizes)
        keys_all, values_all = both[:, :HEAD], both[:, HEAD:]
        out, saved = attend(queries, keys_all, values_all, allowed)
        heads_out = jnp.concatenate(jnp.split(out, heads, axis=0), axis=1)
        state.append(
            dict(
                x=x, r_one=r_one, attn_in=attn_in, cosine=cosine, sine=sine, queries=queries,
                keys=keys_all, values=values_all, saved=saved, heads_out=heads_out,
            )
        )

    flat = (batches * tokens, width)
    heads_all = jnp.concatenate([s["heads_out"] for s in state])
    outs = ffn_call(
        heads_all, (1.0 + gains).T, inputs.reshape(flat), cotangent.reshape(flat), w_out,
        jnp.stack(low[4:]),
    )
    output, ffn_in, hidden, d_ffn, d_gate, d_up, d_attn, d_heads_all, d_mid, gain_parts = outs[:10]
    units = [(mb, cut) for mb in range(batches) for cut in range(cuts)]
    work = []
    for i, (mb, cut) in enumerate(units):
        work.append(dict(rows=slice(cut * unit, (cut + 1) * unit), mb=mb, all=slice(i * unit, (i + 1) * unit)))

    g_down = t_dot(d_ffn, hidden)
    g_gate = t_dot(ffn_in, d_gate)
    g_up = t_dot(ffn_in, d_up)
    s_down, mark = scatter_rows(g_down, sizes, None)
    s_gate, mark = scatter_rows(g_gate, sizes, mark)
    s_up, mark = scatter_rows(g_up, sizes, mark)

    for mb in range(batches):
        s = state[mb]
        d_heads = d_heads_all[mb * tokens : (mb + 1) * tokens]
        d_out = jnp.concatenate(jnp.split(d_heads, heads, axis=1))
        d_queries, d_keys, d_values = attend_back(
            s["saved"], s["queries"], s["keys"], s["values"], d_out
        )
        d_kv = scatter_ctx(jnp.concatenate([d_keys, d_values], axis=1), sizes)
        pieces = [rotate(q, s["cosine"], -s["sine"]) for q in jnp.split(d_queries, heads)]
        pieces += [rotate(d_kv[:, :HEAD], s["cosine"], -s["sine"]), d_kv[:, HEAD:]]
        s["d_proj"] = jnp.concatenate(pieces, axis=1).astype(BF)
    for w in work:
        part = dot_t(state[w["mb"]]["d_proj"][w["rows"]], w_qkv).astype(BF)
        w["d_attn_in"] = sum_mp(part, sizes)

    g_out = t_dot(d_attn, heads_all)
    g_qkv = t_dot(
        jnp.concatenate([s["attn_in"] for s in state]),
        jnp.concatenate([s["d_proj"] for s in state]),
    )
    s_out, mark = scatter_rows(g_out, sizes, mark)
    s_qkv, mark = scatter_rows(g_qkv, sizes, mark)

    for w in work:
        s = state[w["mb"]]
        back, w["g_one"] = norm_back(
            s["x"][w["rows"]], s["r_one"][w["rows"]], gain_one, w["d_attn_in"].astype(F32)
        )
        w["input_grad"] = (d_mid[w["all"]] + back).astype(BF)

    gain_grads = jnp.concatenate(
        [sum(w["g_one"] for w in work)[None], jnp.sum(gain_parts, axis=1)]
    )
    gain_grads = sum_small(gain_grads, ("ctx", "dp"), sizes)
    summed = (
        s_qkv[:, :q_cols], s_qkv[:, q_cols : q_cols + k_cols], s_qkv[:, q_cols + k_cols :],
        s_out, s_gate, s_up, s_down,
    )
    weight_sq = sum(jnp.sum(g * g) for g in (s_qkv, s_out, s_gate, s_up, s_down))
    weight_sq = sum_small(weight_sq.reshape(1, 1), ("ctx", "dp", "mp"), sizes)[0, 0]
    norm_value = jnp.sqrt(weight_sq + jnp.sum(gain_grads * gain_grads))
    factor = 1.0 / jnp.maximum(norm_value, 1.0)
    own = masters[7].shape[0]
    place = (lax.axis_index("dp") * sizes["ctx"] + lax.axis_index("ctx")) * own
    own_gains = lax.dynamic_slice_in_dim(gain_grads, place, own, 1)
    summed += tuple(own_gains[i] for i in range(4))
    new_moments = tuple(0.5 * m + 0.5 * factor * g for m, g in zip(moments, summed))
    changes = tuple(-RATE * (m + 0.01 * w) for w, m in zip(masters[:7], new_moments[:7]))

    return (
        output.reshape(inputs.shape),
        jnp.concatenate([w["input_grad"] for w in work]).reshape(inputs.shape), norm_value.reshape(1), *changes, *new_moments
    )


def per_device(
    sizes,
    inputs,
    segment_ids,
    positions,
    cotangent,
    *params,
):
    masters, moments = params[:11], params[11:]
    batches, seqs, tokens, width = inputs.shape
    assert seqs == 1
    full_len = segment_ids.shape[2]
    q_cols, k_cols = masters[0].shape[1], masters[1].shape[1]
    heads = q_cols // HEAD
    assert k_cols == HEAD
    cuts = 2 if tokens >= 512 else 1
    unit = tokens // cuts

    low = [w.astype(BF) for w in masters[:7]]
    qkv_own = jnp.concatenate(low[:3], axis=1)
    gains_own = jnp.stack([g.astype(BF) for g in masters[7:]], axis=1)
    gains = lax.all_gather(gains_own, ("dp", "ctx"), axis=0, tiled=True).astype(F32)
    gain_one, gain_two, gain_three, gain_four = [gains[:, i] for i in range(4)]
    w_qkv, mark = gather_rows(qkv_own, sizes, None)
    w_out, mark = gather_rows(low[3], sizes, mark)
    w_gate, mark = gather_rows(low[4], sizes, mark)
    w_up, mark = gather_rows(low[5], sizes, mark)
    w_down, mark = gather_rows(low[6], sizes, mark)

    start = lax.axis_index("ctx") * tokens
    causal = (start + jnp.arange(tokens))[:, None] >= jnp.arange(full_len)[None, :]
    frequency = jnp.exp(
        jnp.arange(HEAD // 2, dtype=F32) * (-2.0 * math.log(10000.0) / HEAD)
    )

    state = []
    for mb in range(batches):
        x = inputs[mb, 0].astype(F32)
        r_one = inverse_rms(x)
        attn_in = (x * r_one * (1.0 + gain_one)).astype(BF)
        angles = positions[mb, 0].astype(F32)[:, None] * frequency
        cosine, sine = jnp.cos(angles), jnp.sin(angles)
        seg = segment_ids[mb, 0]
        seg_local = lax.dynamic_slice_in_dim(seg, start, tokens)
        allowed = causal & (seg_local[:, None] == seg[None, :])
        proj = dot(attn_in, w_qkv)
        queries = jnp.concatenate(
            [rotate(proj[:, h * HEAD : (h + 1) * HEAD], cosine, sine) for h in range(heads)]
        ).astype(BF)
        keys = rotate(proj[:, q_cols : q_cols + HEAD], cosine, sine).astype(BF)
        values = proj[:, q_cols + HEAD :].astype(BF)
        both = swap_ctx(jnp.concatenate([keys, values], axis=1), sizes)
        keys_all, values_all = both[:, :HEAD], both[:, HEAD:]
        out, saved = attend(queries, keys_all, values_all, allowed)
        heads_out = jnp.concatenate(jnp.split(out, heads, axis=0), axis=1)
        state.append(
            dict(
                x=x, r_one=r_one, attn_in=attn_in, cosine=cosine, sine=sine, queries=queries,
                keys=keys_all, values=values_all, saved=saved, heads_out=heads_out,
            )
        )

    units = [(mb, cut) for mb in range(batches) for cut in range(cuts)]
    work = []
    for mb, cut in units:
        rows = slice(cut * unit, (cut + 1) * unit)
        part = dot_t(state[mb]["heads_out"][rows], w_out).astype(BF)
        work.append(dict(rows=rows, mb=mb, attn_low=sum_mp(part, sizes)))
    for w in work:
        attn = w["attn_low"].astype(F32)
        r_two = inverse_rms(attn)
        mid = state[w["mb"]]["x"][w["rows"]] + attn * r_two * (1.0 + gain_two)
        r_three = inverse_rms(mid)
        ffn_in = (mid * r_three * (1.0 + gain_three)).astype(BF)
        gate, up = dot(ffn_in, w_gate), dot(ffn_in, w_up)
        value, slope = gelu_parts(gate)
        hidden = (value * up).astype(BF)
        part = dot_t(hidden, w_down).astype(BF)
        w.update(
            mid=mid, r_two=r_two, r_three=r_three, ffn_in=ffn_in, gate=gate, up=up, hidden=hidden,
            ffn_low=sum_mp(part, sizes),
        )
    for w in work:
        ffn = w["ffn_low"].astype(F32)
        r_four = inverse_rms(ffn)
        grad = cotangent[w["mb"], 0][w["rows"]].astype(F32)
        w["output"] = (w["mid"] + ffn * r_four * (1.0 + gain_four)).astype(BF)
        d_ffn, w["g_four"] = norm_back(ffn, r_four, gain_four, grad)
        d_ffn = d_ffn.astype(BF)
        d_hidden = dot(d_ffn, w_down)
        value, slope = gelu_parts(w["gate"])
        d_gate = (d_hidden * w["up"] * slope).astype(BF)
        d_up = (d_hidden * value).astype(BF)
        part = (dot_t(d_gate, w_gate) + dot_t(d_up, w_up)).astype(BF)
        w.update(grad=grad, d_ffn=d_ffn, d_gate=d_gate, d_up=d_up, d_in_low=sum_mp(part, sizes))
    for w in work:
        d_in = w["d_in_low"].astype(F32)
        back, w["g_three"] = norm_back(w["mid"], w["r_three"], gain_three, d_in)
        d_mid = w["grad"] + back
        attn = w["attn_low"].astype(F32)
        d_attn, w["g_two"] = norm_back(attn, w["r_two"], gain_two, d_mid)
        d_attn = d_attn.astype(BF)
        w.update(d_mid=d_mid, d_attn=d_attn, d_heads=dot(d_attn, w_out).astype(BF))

    def rows_of(key):
        return jnp.concatenate([w[key] for w in work])

    ffn_in = rows_of("ffn_in")
    g_down = t_dot(rows_of("d_ffn"), rows_of("hidden"))
    g_gate = t_dot(ffn_in, rows_of("d_gate"))
    g_up = t_dot(ffn_in, rows_of("d_up"))
    s_down, mark = scatter_rows(g_down, sizes, None)
    s_gate, mark = scatter_rows(g_gate, sizes, mark)
    s_up, mark = scatter_rows(g_up, sizes, mark)

    for mb in range(batches):
        s = state[mb]
        d_heads = jnp.concatenate([w["d_heads"] for w in work if w["mb"] == mb])
        d_out = jnp.concatenate(jnp.split(d_heads, heads, axis=1))
        d_queries, d_keys, d_values = attend_back(
            s["saved"], s["queries"], s["keys"], s["values"], d_out
        )
        d_kv = scatter_ctx(jnp.concatenate([d_keys, d_values], axis=1), sizes)
        pieces = [rotate(q, s["cosine"], -s["sine"]) for q in jnp.split(d_queries, heads)]
        pieces += [rotate(d_kv[:, :HEAD], s["cosine"], -s["sine"]), d_kv[:, HEAD:]]
        s["d_proj"] = jnp.concatenate(pieces, axis=1).astype(BF)
    for w in work:
        part = dot_t(state[w["mb"]]["d_proj"][w["rows"]], w_qkv).astype(BF)
        w["d_attn_in"] = sum_mp(part, sizes)

    g_out = t_dot(rows_of("d_attn"), jnp.concatenate([s["heads_out"] for s in state]))
    g_qkv = t_dot(
        jnp.concatenate([s["attn_in"] for s in state]),
        jnp.concatenate([s["d_proj"] for s in state]),
    )
    s_out, mark = scatter_rows(g_out, sizes, mark)
    s_qkv, mark = scatter_rows(g_qkv, sizes, mark)

    for w in work:
        s = state[w["mb"]]
        back, w["g_one"] = norm_back(
            s["x"][w["rows"]], s["r_one"][w["rows"]], gain_one, w["d_attn_in"].astype(F32)
        )
        w["input_grad"] = (w["d_mid"] + back).astype(BF)

    gain_grads = jnp.stack(
        [sum(w[key] for w in work) for key in ("g_one", "g_two", "g_three", "g_four")]
    )
    gain_grads = sum_small(gain_grads, ("ctx", "dp"), sizes)
    summed = (
        s_qkv[:, :q_cols], s_qkv[:, q_cols : q_cols + k_cols], s_qkv[:, q_cols + k_cols :],
        s_out, s_gate, s_up, s_down,
    )
    weight_sq = sum(jnp.sum(g * g) for g in (s_qkv, s_out, s_gate, s_up, s_down))
    weight_sq = sum_small(weight_sq.reshape(1, 1), ("ctx", "dp", "mp"), sizes)[0, 0]
    norm_value = jnp.sqrt(weight_sq + jnp.sum(gain_grads * gain_grads))
    factor = 1.0 / jnp.maximum(norm_value, 1.0)
    own = masters[7].shape[0]
    place = (lax.axis_index("dp") * sizes["ctx"] + lax.axis_index("ctx")) * own
    own_gains = lax.dynamic_slice_in_dim(gain_grads, place, own, 1)
    summed += tuple(own_gains[i] for i in range(4))
    new_moments = tuple(0.5 * m + 0.5 * factor * g for m, g in zip(moments, summed))
    changes = tuple(-RATE * (m + 0.01 * w) for w, m in zip(masters[:7], new_moments[:7]))

    def whole(key):
        return rows_of(key).reshape(inputs.shape)

    return (
        whole("output"), whole("input_grad"), norm_value.reshape(1), *changes, *new_moments
    )


def solution(mesh):
    sizes = dict(mesh.shape)
    weight, vector = P(("dp", "ctx"), "mp"), P(("dp", "ctx"))
    params = (weight,) * 7 + (vector,) * 4
    data = P(None, "dp", "ctx", None)

    def run(*args):
        batches, _, tokens, _ = args[0].shape
        fast = sizes == dict(dp=4, ctx=2, mp=4) and batches == 2 and tokens == 2 * UNIT
        return (fast_device if fast else per_device)(sizes, *args)

    return jax.shard_map(
        run,
        mesh=mesh,
        in_specs=(data, P(None, "dp", None), P(None, "dp", "ctx"), data) + params + params,
        out_specs=(data, data, P()) + (weight,) * 7 + params,
        check_vma=False,
    )
```

```python
import math

import jax
import jax.numpy as jnp
from jax import lax
from jax.experimental import pallas as pl
from jax.experimental.pallas import tpu as pltpu
from jax.sharding import PartitionSpec as P

HEAD = 256
STEP = 10
EPS = 1e-06
CAP = 50.0
RATE = 1.0 / math.sqrt(1.0 + STEP / 1000.0)
SCALE = HEAD ** (-0.5)
BF = jnp.bfloat16
F32 = jnp.float32


def flip(axis, size, mask):
    return dict(axis_name=axis, perm=[(i, i ^ mask) for i in range(size)])


def after(value, other):
    return lax.optimization_barrier((value, other))[0]


def gather_rows(own, sizes, wait):
    dp, ctx = sizes["dp"], sizes["ctx"]
    rows, cols = own.shape
    if wait is not None:
        own = after(own, wait)
    if dp != 4:
        out = lax.all_gather(own, ("dp", "ctx"), axis=0, tiled=True)
        return out, own
    me = lax.axis_index("dp")
    half = rows // 2 // 16 * 16
    from_x = lax.ppermute(own, **flip("dp", dp, 1))
    from_y = lax.ppermute(own, **flip("dp", dp, 2))
    far_top = lax.ppermute(from_y[:half], **flip("dp", dp, 1))
    far_low = lax.ppermute(from_x[half:], **flip("dp", dp, 2))
    mine = jnp.zeros((dp, rows, cols), own.dtype)
    mine = lax.dynamic_update_slice(mine, own[None], (me, 0, 0))
    mine = lax.dynamic_update_slice(mine, from_x[None], (me ^ 1, 0, 0))
    mine = lax.dynamic_update_slice(mine, from_y[None], (me ^ 2, 0, 0))
    mine = lax.dynamic_update_slice(mine, far_top[None], (me ^ 3, 0, 0))
    mine = lax.dynamic_update_slice(mine, far_low[None], (me ^ 3, half, 0))
    if ctx == 2:
        other = lax.ppermute(mine, **flip("ctx", ctx, 1))
        core = lax.axis_index("ctx")
        out = jnp.zeros((dp, ctx, rows, cols), own.dtype)
        out = lax.dynamic_update_slice(out, mine[:, None], (0, core, 0, 0))
        out = lax.dynamic_update_slice(out, other[:, None], (0, 1 - core, 0, 0))
    else:
        out = lax.all_gather(mine, "ctx", axis=1)
    return out.reshape(dp * ctx * rows, cols), from_x


def scatter_rows(full, sizes, wait):
    dp, ctx = sizes["dp"], sizes["ctx"]
    full = full.astype(BF)
    if wait is not None:
        full = after(full, wait)
    rows = full.shape[0] // (dp * ctx)
    cols = full.shape[1]
    if dp != 4:
        out = lax.psum_scatter(full, ("dp", "ctx"), scatter_dimension=0, tiled=True)
        return out.astype(F32), out
    blocks = full.reshape(dp, ctx, rows, cols)
    if ctx == 2:
        core = lax.axis_index("ctx")
        send = lax.dynamic_index_in_dim(blocks, 1 - core, 1, keepdims=False)
        keep = lax.dynamic_index_in_dim(blocks, core, 1, keepdims=False)
        got = lax.ppermute(send, **flip("ctx", ctx, 1))
    else:
        keep = lax.psum_scatter(blocks, "ctx", scatter_dimension=1, tiled=False)
        got = None
    me = lax.axis_index("dp")
    half = rows // 2 // 16 * 16

    def part(mask, low, high):
        size = (1, high - low, cols)
        piece = lax.dynamic_slice(keep, (me ^ mask, low, 0), size)[0].astype(F32)
        if got is not None:
            piece = piece + lax.dynamic_slice(got, (me ^ mask, low, 0), size)[0].astype(F32)
        return piece

    far_top = lax.ppermute(part(3, 0, half).astype(BF), **flip("dp", dp, 1))
    far_low = lax.ppermute(part(3, half, rows).astype(BF), **flip("dp", dp, 2))
    to_y = jnp.concatenate([part(2, 0, half) + far_top.astype(F32), part(2, half, rows)])
    to_x = jnp.concatenate([part(1, 0, half), part(1, half, rows) + far_low.astype(F32)])
    by_y = lax.ppermute(to_y.astype(BF), **flip("dp", dp, 2))
    by_x = lax.ppermute(to_x.astype(BF), **flip("dp", dp, 1))
    total = part(0, 0, rows) + by_x.astype(F32) + by_y.astype(F32)
    return total, far_top


def sum_mp(part, sizes):
    if sizes["mp"] != 4:
        return lax.psum(part, "mp")
    place = lax.axis_index("mp")
    inner = (place == 1) | (place == 2)
    near = lax.ppermute(part, "mp", [(0, 1), (3, 2)])
    pair = (part.astype(F32) + near.astype(F32)).astype(BF)
    across = lax.ppermute(pair, "mp", [(1, 2), (2, 1)])
    total = (pair.astype(F32) + across.astype(F32)).astype(BF)
    back = lax.ppermute(total, "mp", [(1, 0), (2, 3)])
    return jnp.where(inner, total, back)


def sum_small(value, axes, sizes):
    for axis in axes:
        size = sizes[axis]
        step = 1
        while step < size:
            value = value + lax.ppermute(value, **flip(axis, size, step))
            step *= 2
    return value


def swap_ctx(local, sizes):
    if sizes["ctx"] != 2:
        return lax.all_gather(local, "ctx", axis=0, tiled=True)
    other = lax.ppermute(local, **flip("ctx", 2, 1))
    first = lax.axis_index("ctx") == 0
    return jnp.concatenate([jnp.where(first, local, other), jnp.where(first, other, local)])


def scatter_ctx(full, sizes):
    if sizes["ctx"] != 2:
        return lax.psum_scatter(full.astype(BF), "ctx", scatter_dimension=0, tiled=True).astype(F32)
    core = lax.axis_index("ctx")
    rows = full.shape[0] // 2
    send = lax.dynamic_slice_in_dim(full, (1 - core) * rows, rows).astype(BF)
    keep = lax.dynamic_slice_in_dim(full, core * rows, rows)
    return keep.astype(BF).astype(F32) + lax.ppermute(send, **flip("ctx", 2, 1)).astype(F32)


def dot(a, b):
    return lax.dot_general(a, b, (((1,), (0,)), ((), ())), preferred_element_type=F32)


def dot_t(a, b):
    return lax.dot_general(a, b, (((1,), (1,)), ((), ())), preferred_element_type=F32)


def t_dot(a, b):
    return lax.dot_general(a, b, (((0,), (0,)), ((), ())), preferred_element_type=F32)


def inverse_rms(v):
    return lax.rsqrt(jnp.mean(v * v, axis=-1, keepdims=True) + EPS)


def norm_back(v, r, gain, dy):
    scaled = (1.0 + gain) * dy
    mean = jnp.mean(scaled * v, axis=-1, keepdims=True)
    return r * scaled - v * (r * r * r) * mean, jnp.sum(v * r * dy, axis=0)


def rotate(v, cosine, sine):
    a, b = v[:, : HEAD // 2], v[:, HEAD // 2 :]
    return jnp.concatenate([a * cosine - b * sine, b * cosine + a * sine], axis=1)


GELU_C = math.sqrt(2.0 / math.pi)


def gelu_parts(u):
    tanh = jnp.tanh(GELU_C * (u + 0.044715 * u * u * u))
    value = 0.5 * u * (1.0 + tanh)
    slope = 0.5 * (1.0 + tanh) + 0.5 * u * (1.0 - tanh * tanh) * GELU_C * (
        1.0 + 3.0 * 0.044715 * u * u
    )
    return value, slope


def attend(queries, keys, values, allowed):
    raw = dot_t(queries, keys) * SCALE
    tanh = jnp.tanh(raw / CAP)
    heads = queries.shape[0] // allowed.shape[0]
    mask = jnp.concatenate([allowed] * heads, axis=0)
    weight = jnp.where(mask, jnp.exp(CAP * tanh), 0.0)
    probs = weight / jnp.sum(weight, axis=1, keepdims=True)
    out = dot(probs.astype(BF), values).astype(BF)
    return out, (probs, tanh)


def attend_back(saved, queries, keys, values, d_out):
    probs, tanh = saved
    d_probs = dot_t(d_out, values)
    inner = jnp.sum(probs * d_probs, axis=1, keepdims=True)
    d_raw = (probs * (d_probs - inner) * (1.0 - tanh * tanh)).astype(BF)
    d_queries = dot(d_raw, keys) * SCALE
    d_keys = t_dot(d_raw, queries) * SCALE
    d_values = t_dot(probs.astype(BF), d_out)
    return d_queries, d_keys, d_values


MESH = pl.DeviceIdType.MESH
UNIT = 256
TILE = 256


def ffn_kernel(
    heads_ref, scale_ref, x_hbm, cot_hbm, w_out_hbm, own_hbm,
    out_hbm, ffn_in_hbm, hidden_hbm, d_ffn_hbm, d_gate_hbm, d_up_hbm, d_attn_hbm, d_heads_hbm,
    d_mid_hbm, gain_ref, attn_hbm, slope_hbm, value_hbm,
    weights, w_out, send, near, across, total, xb, cb, ab, act, act_t, stage, d_heads,
    line_send, line_recv, credit, local, ag_send, ag_recv, ag_local,
):
    dp, core, z = lax.axis_index("dp"), lax.axis_index("ctx"), lax.axis_index("mp")
    width, units = xb.shape[1], weights.shape[2]
    rows_own = own_hbm.shape[1]
    half = rows_own // 2
    inner = (z == 1) | (z == 2)
    outer = (z == 0) | (z == 3)
    x_peer, y_peer = (dp ^ 1, core, z), (dp ^ 2, core, z)
    core_peer = (dp, 1 - core, z)
    near_peer = (dp, core, z ^ 1)
    far_peer = (dp, core, 3 - z)

    barrier = pltpu.get_barrier_semaphore()
    for peer in (x_peer, y_peer, core_peer, near_peer, far_peer):
        pl.semaphore_signal(barrier, inc=1, device_id=peer, device_id_type=MESH)
    pl.semaphore_wait(barrier, 5)

    def block(mask, other=False, low=0, size=rows_own):
        owner = (dp ^ mask) * 2 + ((1 - core) if other else core)
        return pl.ds(pl.multiple_of(owner * rows_own + low, 16), size)

    def gather(w, name, recv=False):
        table = {
            "x": (0, block(0), x_peer, block(1)),
            "y": (1, block(0), y_peer, block(2)),
            "top": (2, block(2, False, 0, half), x_peer, block(3, False, 0, half)),
            "low": (3, block(1, False, half, half), y_peer, block(3, False, half, half)),
            "own_c": (4, block(0), core_peer, block(0, True)),
            "x_c": (5, block(1), core_peer, block(1, True)),
            "y_c": (6, block(2), core_peer, block(2, True)),
            "top_c": (7, block(3, False, 0, half), core_peer, block(3, True, 0, half)),
            "low_c": (8, block(3, False, half, half), core_peer, block(3, True, half, half)),
        }
        index, out_rows, peer, in_rows = table[name]
        rows = in_rows if recv else out_rows
        src = own_hbm.at[w] if name in ("x", "y", "own_c") else weights.at[w, rows]
        return pltpu.make_async_remote_copy(
            src_ref=src, dst_ref=weights.at[w, rows], send_sem=ag_send.at[w, index],
            recv_sem=ag_recv.at[w, index], device_id=peer, device_id_type=MESH,
        )

    def own_copy(w):
        return pltpu.make_async_copy(own_hbm.at[w], weights.at[w, block(0)], ag_local.at[w])

    def gather_first(w):
        for name in ("x", "y", "own_c"):
            gather(w, name).start()
        own_copy(w).start()

    def gather_second(w):
        gather(w, "x", True).wait_recv()
        gather(w, "low").start()
        gather(w, "x_c").start()
        gather(w, "y", True).wait_recv()
        gather(w, "top").start()
        gather(w, "y_c").start()

    def gather_third(w):
        for name in ("top", "low"):
            gather(w, name, True).wait_recv()
            gather(w, name + "_c").start()

    def gather_end(w):
        for name in ("own_c", "x_c", "y_c", "top_c", "low_c"):
            gather(w, name, True).wait_recv()
        own_copy(w).wait()
        for name in ("x", "y", "top", "low", "own_c", "x_c", "y_c", "top_c", "low_c"):
            gather(w, name).wait_send()

    def hop(kind, i):
        src = (send.at[i % 3], send.at[i % 3], total.at[i % 4])[kind]
        dst = (near.at[i % 3], across.at[i % 2], total.at[i % 4])[kind]
        return pltpu.make_async_remote_copy(
            src_ref=src, dst_ref=dst, send_sem=line_send.at[kind, i % 4],
            recv_sem=line_recv.at[kind, i % 4],
            device_id=far_peer if kind == 1 else near_peer, device_id_type=MESH,
        )

    def add_rows(dst, a, b):
        @pl.loop(0, UNIT // 16)
        def _(r):
            rows = pl.ds(pl.multiple_of(r * 16, 16), 16)
            dst[rows] = (a[rows].astype(F32) + b[rows].astype(F32)).astype(BF)

    def boundary(k, up=True, cross=True, back=True, done=True):
        @pl.when(outer)
        def _():
            if done:
                hop(2, k - 3).wait_recv()
            if cross:
                hop(0, k - 1).wait_send()
            if up:
                hop(0, k).start()

        @pl.when(inner)
        def _():
            if cross:
                i = k - 1
                hop(0, i).wait_recv()
                add_rows(send.at[i % 3], send.at[i % 3], near.at[i % 3])
                if isinstance(i, int):
                    if i >= 2:
                        pl.semaphore_wait(credit, 1)
                else:
                    pl.semaphore_wait(credit, 1)
                hop(1, i).start()
            if back:
                i = k - 2
                hop(1, i).wait_recv()
                hop(1, i).wait_send()
                add_rows(total.at[i % 4], send.at[i % 3], across.at[i % 2])
                if not isinstance(i, int) or i < 10:
                    pl.semaphore_signal(credit, inc=1, device_id=far_peer, device_id_type=MESH)
                hop(2, i).start()
            if done:
                hop(2, k - 3).wait_send()

    def rows_of(u):
        return pl.ds(pl.multiple_of(u * UNIT, UNIT), UNIT)

    def load(ref, u, dst, sem):
        return pltpu.make_async_copy(ref.at[rows_of(u)], dst, local.at[sem])

    def store(src, ref, u, sem):
        return pltpu.make_async_copy(src, ref.at[rows_of(u)], local.at[sem])

    def store_t(ref, u, sem):
        return pltpu.make_async_copy(act_t, ref.at[:, rows_of(u)], local.at[sem])

    def turn():
        @pl.loop(0, width // TILE)
        def _(n):
            act_t[tile(n)] = act[:, tile(n)].T

    def tile(n):
        return pl.ds(pl.multiple_of(n * TILE, TILE), TILE)

    def each_rows(body):
        @pl.loop(0, UNIT // 16)
        def _(r):
            body(pl.ds(pl.multiple_of(r * 16, 16), 16))

    def scale(i):
        return scale_ref[i : i + 1]

    def add_gain(index, v):
        gain_ref[index] += v[:8] + v[8:]

    def project_out(u, k):
        dst = send.at[k % 3]

        @pl.loop(0, width // TILE)
        def _(n):
            dst[:, tile(n)] = dot_t(heads_ref[rows_of(u)], w_out[tile(n)]).astype(BF)

    def middle(rows, u4):
        attn = total[u4, rows].astype(F32) if u4 is not None else ab[rows].astype(F32)
        r_two = inverse_rms(attn)
        return attn, r_two, xb[rows].astype(F32) + attn * r_two * scale(1)

    def forward(u, k):
        load(x_hbm, u, xb, 0).start()
        store(total.at[u], attn_hbm, u, 1).start()
        load(x_hbm, u, xb, 0).wait()

        def body(rows):
            _, _, mid = middle(rows, u)
            act[rows] = (mid * inverse_rms(mid) * scale(2)).astype(BF)

        each_rows(body)
        turn()
        store_t(ffn_in_hbm, u, 2).start()

        @pl.loop(0, units // TILE)
        def _(f):
            gate = dot(act[...], weights[0, :, tile(f)])
            up = dot(act[...], weights[1, :, tile(f)])
            value, slope = gelu_parts(gate)
            stage[0, :, tile(f)] = (value * up).astype(BF)
            stage[1, :, tile(f)] = (slope * up).astype(BF)
            stage[2, :, tile(f)] = value.astype(BF)

        saves = ((0, hidden_hbm), (1, slope_hbm), (2, value_hbm))
        for i, ref in saves:
            store(stage.at[i], ref, u, 3 + i).start()
        dst = send.at[k % 3]

        @pl.loop(0, width // TILE)
        def _(n):
            dst[:, tile(n)] = dot_t(stage[0], weights[2, tile(n)]).astype(BF)

        for i, ref in saves:
            store(stage.at[i], ref, u, 3 + i).wait()
        store(total.at[u], attn_hbm, u, 1).wait()
        store_t(ffn_in_hbm, u, 2).wait()

    def backward(u, k):
        loads = (
            load(x_hbm, u, xb, 0), load(attn_hbm, u, ab, 1), load(cot_hbm, u, cb, 2),
            load(slope_hbm, u, stage.at[1], 4), load(value_hbm, u, stage.at[2], 5),
        )
        for copy in loads:
            copy.start()
        for copy in loads:
            copy.wait()

        def body(rows):
            _, _, mid = middle(rows, None)
            ffn = total[u, rows].astype(F32)
            r = inverse_rms(ffn)
            dy = cb[rows].astype(F32)
            xb[rows] = (mid + ffn * r * scale(3)).astype(BF)
            scaled = scale(3) * dy
            mean = jnp.mean(scaled * ffn, axis=-1, keepdims=True)
            act[rows] = (r * scaled - ffn * (r * r * r) * mean).astype(BF)
            add_gain(2, ffn * r * dy)

        each_rows(body)
        store(xb, out_hbm, u, 0).start()
        turn()
        store_t(d_ffn_hbm, u, 1).start()

        @pl.loop(0, units // TILE)
        def _(f):
            d_hidden = dot(act[...], weights[2, :, tile(f)])
            stage[1, :, tile(f)] = (d_hidden * stage[1, :, tile(f)].astype(F32)).astype(BF)
            stage[2, :, tile(f)] = (d_hidden * stage[2, :, tile(f)].astype(F32)).astype(BF)

        store(stage.at[1], d_gate_hbm, u, 4).start()
        store(stage.at[2], d_up_hbm, u, 5).start()
        dst = send.at[k % 3]

        @pl.loop(0, width // TILE)
        def _(n):
            part = dot_t(stage[1], weights[0, tile(n)]) + dot_t(stage[2], weights[1, tile(n)])
            dst[:, tile(n)] = part.astype(BF)

        store(xb, out_hbm, u, 0).wait()
        store_t(d_ffn_hbm, u, 1).wait()
        store(stage.at[1], d_gate_hbm, u, 4).wait()
        store(stage.at[2], d_up_hbm, u, 5).wait()

    def last(u):
        loads = (load(x_hbm, u, xb, 0), load(attn_hbm, u, ab, 1), load(cot_hbm, u, cb, 2))
        for copy in loads:
            copy.start()
        for copy in loads:
            copy.wait()

        def body(rows):
            attn, r_two, mid = middle(rows, None)
            r = inverse_rms(mid)
            dy = total[u, rows].astype(F32)
            scaled = scale(2) * dy
            mean = jnp.mean(scaled * mid, axis=-1, keepdims=True)
            grad = cb[rows].astype(F32) + r * scaled - mid * (r * r * r) * mean
            add_gain(1, mid * r * dy)
            cb[rows] = grad.astype(BF)
            scaled = scale(1) * grad
            mean = jnp.mean(scaled * attn, axis=-1, keepdims=True)
            act[rows] = (r_two * scaled - attn * (r_two * r_two * r_two) * mean).astype(BF)
            add_gain(0, attn * r_two * grad)

        each_rows(body)
        store(cb, d_mid_hbm, u, 0).start()
        turn()
        store_t(d_attn_hbm, u, 1).start()
        for h in range(w_out.shape[1] // TILE):
            columns = slice(h * TILE, (h + 1) * TILE)
            d_heads[:, columns] = dot(act[...], w_out[:, columns]).astype(BF)
        store(d_heads, d_heads_hbm, u, 2).start()
        store(cb, d_mid_hbm, u, 0).wait()
        store_t(d_attn_hbm, u, 1).wait()
        store(d_heads, d_heads_hbm, u, 2).wait()

    gather_first(0)
    pltpu.make_async_copy(w_out_hbm, w_out, local.at[0]).start()
    gain_ref[...] = jnp.zeros_like(gain_ref)
    pltpu.make_async_copy(w_out_hbm, w_out, local.at[0]).wait()
    project_out(0, 0)
    boundary(0, cross=False, back=False, done=False)
    project_out(1, 1)
    project_out(2, 2)
    boundary(1, back=False, done=False)
    gather_second(0)
    gather_first(1)
    boundary(2, done=False)
    project_out(3, 3)
    gather_third(0)
    gather_second(1)
    gather_first(2)
    boundary(3)
    gather_third(1)
    gather_second(2)
    gather_third(2)
    for w in range(3):
        gather_end(w)
    forward(0, 4)

    @pl.loop(4, 7)
    def _(k):
        boundary(k)
        forward(k - 3, k + 1)

    @pl.loop(7, 11)
    def _(k):
        boundary(k)
        backward(k - 7, k + 1)

    for k in (11, 12, 13, 14):
        boundary(k, up=k < 12, cross=k < 13, back=k < 14)
        last(k - 11)


def ffn_call(heads_out, scales, x, cot, w_out, own):
    tokens, width = x.shape
    units = own.shape[2]
    assert tokens == 4 * UNIT
    full = jax.ShapeDtypeStruct((tokens, width), BF)
    wide = jax.ShapeDtypeStruct((tokens, units), BF)
    flipped = jax.ShapeDtypeStruct((width, tokens), BF)
    outs = (
        full, flipped, wide, flipped, wide, wide, flipped,
        jax.ShapeDtypeStruct((tokens, w_out.shape[1]), BF),
        full,
        jax.ShapeDtypeStruct((3, 8, width), F32),
        full, wide, wide,
    )
    anywhere, vmem = pl.BlockSpec(memory_space=pl.ANY), pl.BlockSpec(memory_space=pltpu.VMEM)
    dma = pltpu.SemaphoreType.DMA
    return pl.pallas_call(
        ffn_kernel,
        out_shape=outs,
        in_specs=[vmem, vmem, anywhere, anywhere, anywhere, anywhere],
        out_specs=[anywhere] * 9 + [vmem] + [anywhere] * 3,
        scratch_shapes=[
            pltpu.VMEM((3, width, units), BF),
            pltpu.VMEM(w_out.shape, BF),
            pltpu.VMEM((3, UNIT, width), BF),
            pltpu.VMEM((3, UNIT, width), BF),
            pltpu.VMEM((2, UNIT, width), BF),
            pltpu.VMEM((4, UNIT, width), BF),
            pltpu.VMEM((UNIT, width), BF),
            pltpu.VMEM((UNIT, width), BF),
            pltpu.VMEM((UNIT, width), BF),
            pltpu.VMEM((UNIT, width), BF),
            pltpu.VMEM((width, UNIT), BF),
            pltpu.VMEM((3, UNIT, units), BF),
            pltpu.VMEM((UNIT, w_out.shape[1]), BF),
            dma((3, 4)),
            dma((3, 4)),
            pltpu.SemaphoreType.REGULAR,
            dma((6,)),
            dma((3, 9)),
            dma((3, 9)),
            dma((3,)),
        ],
        compiler_params=pltpu.CompilerParams(
            collective_id=1, has_side_effects=True, vmem_limit_bytes=60 * 2**20
        ),
        name="ffn",
    )(heads_out, scales, x, cot, w_out, own)


def grad_kernel(
    seg_row, seg_col, cosine, sine, scale_ref, x_hbm, d_mid_hbm, q_hbm, k_hbm, v_hbm, d_heads_hbm, w_qkv_hbm,
    d_ffn_t, hidden_hbm, ffn_in_t, d_gate_hbm, d_up_hbm, d_attn_t, heads_hbm, attn_in_t,
    in_grad_hbm, own_hbm, by_x_hbm, by_y_hbm, gain_ref, core_hbm, far_hbm,
    w_qkv, left, right, core_out, sums, arrived, own_sum,
    queries, keys, values, d_out, d_proj, d_keys, d_values, kv_out, kv_in,
    send, near, across, total, xb, mb_buf,
    line_send, line_recv, kv_sem, local, load_sem, rs_send, rs_recv, rs_local, own_sem,
):
    dp, core, z = lax.axis_index("dp"), lax.axis_index("ctx"), lax.axis_index("mp")
    width = xb.shape[1]
    rows_own = own_hbm.shape[1]
    half = rows_own // 2
    tokens = 2 * UNIT
    inner = (z == 1) | (z == 2)
    outer = (z == 0) | (z == 3)
    x_peer, y_peer = (dp ^ 1, core, z), (dp ^ 2, core, z)
    core_peer = (dp, 1 - core, z)
    near_peer = (dp, core, z ^ 1)
    far_peer = (dp, core, 3 - z)

    barrier = pltpu.get_barrier_semaphore()
    for peer in (x_peer, y_peer, core_peer, near_peer, far_peer):
        pl.semaphore_signal(barrier, inc=1, device_id=peer, device_id_type=MESH)

    def tile(n):
        return pl.ds(pl.multiple_of(n * TILE, TILE), TILE)

    def remote(src, dst, sems, index, peer):
        return pltpu.make_async_remote_copy(
            src_ref=src, dst_ref=dst, send_sem=sems[0].at[index], recv_sem=sems[1].at[index],
            device_id=peer, device_id_type=MESH,
        )

    jobs = (
        (d_ffn_t, hidden_hbm), (ffn_in_t, d_gate_hbm), (ffn_in_t, d_up_hbm),
        (d_attn_t, heads_hbm), (attn_in_t, None),
    )

    def columns(i):
        return (w_qkv.shape[1] if i == 4 else jobs[i][1].shape[1])

    def operands(i):
        pair = []
        if i != 2:
            pair.append(pltpu.make_async_copy(jobs[i][0], left, rs_local.at[0]))
        if i != 4:
            pair.append(pltpu.make_async_copy(jobs[i][1], right.at[:, : columns(i)], rs_local.at[1]))
        return pair

    def core_copy(i, m):
        n = columns(i)
        return remote(
            core_out.at[m % 2, :, :n], core_hbm.at[i, m, :, :n], (rs_send, rs_recv), (i, m), core_peer
        )

    def arrive(i, m):
        n = columns(i)
        return pltpu.make_async_copy(core_hbm.at[i, m, :, :n], arrived.at[m % 2, :, :n], rs_local.at[2 + m % 2])

    def far_copy(i, way):
        n = columns(i)
        rows = slice(0, half) if way == 0 else slice(half, rows_own)
        return remote(
            sums.at[i % 2, 2, rows, :n], far_hbm.at[i, rows, :n], (rs_send, rs_recv), (i, 4 + way),
            (x_peer, y_peer)[way],
        )

    def final_copy(i, way):
        n = columns(i)
        dst = (by_x_hbm, by_y_hbm)[way]
        return remote(
            sums.at[i % 2, way, :, :n], dst.at[i, :, :n], (rs_send, rs_recv), (i, 6 + way),
            (x_peer, y_peer)[way],
        )

    def own_store(i):
        n = columns(i)
        return pltpu.make_async_copy(own_sum.at[:, :n], own_hbm.at[i, :, :n], own_sem.at[0])

    def block_rows(mask, other):
        owner = (dp ^ mask) * 2 + ((1 - core) if other else core)
        return pl.ds(pl.multiple_of(owner * rows_own, 16), rows_own)

    def scatter_start(i):
        for copy in operands(i):
            copy.wait()
        source = d_proj if i == 4 else right
        steps = columns(i) // TILE

        for m in (3, 2, 1, 0):
            if m < 2:
                core_copy(i, m + 2).wait_send()
            elif i > 0:
                core_copy(i - 1, m - 2).wait_send()

            @pl.loop(0, steps)
            def _(n):
                core_out[m % 2, :, tile(n)] = dot(left[block_rows(m, True)], source[:, tile(n)]).astype(BF)

            core_copy(i, m).start()
        if i > 1:
            for way in (0, 1):
                far_copy(i - 2, way).wait_send()
                final_copy(i - 2, way).wait_send()
        if i > 0:
            own_store(i - 1).wait()
        core_copy(i, 3).wait_recv()
        arrive(i, 3).start()
        for m in (3, 2, 1, 0):
            if m:
                core_copy(i, m - 1).wait_recv()
                arrive(i, m - 1).start()
            arrive(i, m).wait()

            @pl.loop(0, steps)
            def _(n):
                part = dot(left[block_rows(m, False)], source[:, tile(n)])
                part = part + arrived[m % 2, :, tile(n)].astype(F32)
                if m:
                    sums[i % 2, m - 1, :, tile(n)] = part.astype(BF)
                else:
                    own_sum[:, tile(n)] = part

            if m == 3:
                far_copy(i, 0).start()
                far_copy(i, 1).start()
        own_store(i).start()
        if i + 1 < len(jobs):
            for copy in operands(i + 1):
                copy.start()

    def scatter_end(i):
        n = columns(i)
        for way in (0, 1):
            far_copy(i, way).wait_recv()
        copy = pltpu.make_async_copy(far_hbm.at[i, :, :n], arrived.at[0, :, :n], rs_local.at[4])
        copy.start()
        copy.wait()
        for way in (1, 0):
            base = 0 if way == 1 else half

            @pl.loop(0, half // 16)
            def _(r):
                rows = pl.ds(pl.multiple_of(base + r * 16, 16), 16)
                total_rows = sums[i % 2, way, rows, :n].astype(F32) + arrived[0, rows, :n].astype(F32)
                sums[i % 2, way, rows, :n] = total_rows.astype(BF)

            final_copy(i, way).start()

    def hop(kind, i):
        src = (send.at[i % 3], send.at[i % 3], total.at[i])[kind]
        dst = (near.at[i % 3], across.at[i], total.at[i])[kind]
        peer = far_peer if kind == 1 else near_peer
        return remote(src, dst, (line_send, line_recv), (kind, i), peer)

    def add_rows(dst, a, b):
        @pl.loop(0, UNIT // 16)
        def _(r):
            rows = pl.ds(pl.multiple_of(r * 16, 16), 16)
            dst[rows] = (a[rows].astype(F32) + b[rows].astype(F32)).astype(BF)

    def boundary(k):
        @pl.when(outer)
        def _():
            if 0 <= k - 3 < 4:
                hop(2, k - 3).wait_recv()
            if 0 <= k - 1 < 4:
                hop(0, k - 1).wait_send()
            if k < 4:
                hop(0, k).start()

        @pl.when(inner)
        def _():
            if 0 <= k - 1 < 4:
                i = k - 1
                hop(0, i).wait_recv()
                add_rows(send.at[i % 3], send.at[i % 3], near.at[i % 3])
                hop(1, i).start()
            if 0 <= k - 2 < 4:
                i = k - 2
                hop(1, i).wait_recv()
                hop(1, i).wait_send()
                add_rows(total.at[i], send.at[i % 3], across.at[i])
                hop(2, i).start()
            if 0 <= k - 3 < 4:
                hop(2, k - 3).wait_send()

    def attention_loads(mb):
        head_rows = [
            pltpu.make_async_copy(
                d_heads_hbm.at[pl.ds(mb * tokens, tokens), pl.ds(h * HEAD, HEAD)], d_out.at[h], load_sem.at[3 + h]
            )
            for h in range(2)
        ]
        return head_rows + [
            pltpu.make_async_copy(ref.at[mb], dst, load_sem.at[j])
            for j, (ref, dst) in enumerate(((q_hbm, queries), (k_hbm, keys), (v_hbm, values)))
        ]

    def unrotate(v, rows):
        a, b = v[:, : HEAD // 2], v[:, HEAD // 2 :]
        c, s = cosine[rows], sine[rows]
        return jnp.concatenate([a * c + b * s, b * c - a * s], axis=1)

    def kv_copy(mb):
        return remote(kv_out, kv_in.at[mb], (kv_sem.at[0], kv_sem.at[1]), (mb,), core_peer)

    def attention_back(mb):
        for copy in attention_loads(mb):
            copy.wait()
        d_keys[...] = jnp.zeros_like(d_keys)
        d_values[...] = jnp.zeros_like(d_values)
        length = keys.shape[0]
        for h in range(2):

            @pl.loop(0, tokens // UNIT)
            def _(b):
                rows = pl.ds(pl.multiple_of(b * UNIT, UNIT), UNIT)
                query, grad = queries[h, rows], d_out[h, rows]
                first = core * tokens + b * UNIT
                key_at = lax.broadcasted_iota(jnp.int32, (length, UNIT), 0)
                query_at = lax.broadcasted_iota(jnp.int32, (length, UNIT), 1) + first
                same = seg_col[mb] == seg_row[mb, :, rows]
                tanh = jnp.tanh(dot_t(keys[...], query) * (SCALE / CAP))
                weight = jnp.where((key_at <= query_at) & same, jnp.exp(CAP * tanh), 0.0)
                probs = weight * (1.0 / jnp.sum(weight, axis=0, keepdims=True))
                d_probs = dot_t(values[...], grad)
                mean = jnp.sum(probs * d_probs, axis=0, keepdims=True)
                d_raw = (probs * (d_probs - mean) * (1.0 - tanh * tanh)).astype(BF)
                d_values[...] += dot(probs.astype(BF), grad)
                d_keys[...] += dot(d_raw, query)
                d_query = t_dot(d_raw, keys[...]) * SCALE
                place = pl.ds(pl.multiple_of(mb * tokens + b * UNIT, UNIT), UNIT)
                d_proj[place, h * HEAD : (h + 1) * HEAD] = unrotate(d_query, place).astype(BF)

        theirs = pl.ds(pl.multiple_of((1 - core) * tokens, UNIT), tokens)
        mine = pl.ds(pl.multiple_of(core * tokens, UNIT), tokens)
        if mb:
            kv_copy(mb - 1).wait_send()
        kv_out[:, :HEAD] = (d_keys[theirs] * SCALE).astype(BF)
        kv_out[:, HEAD:] = d_values[theirs].astype(BF)
        kv_copy(mb).start()
        kv_copy(mb).wait_recv()
        place = pl.ds(mb * tokens, tokens)
        d_key = d_keys[mine] * SCALE + kv_in[mb, :, :HEAD].astype(F32)
        d_value = d_values[mine] + kv_in[mb, :, HEAD:].astype(F32)
        d_proj[place, 2 * HEAD : 3 * HEAD] = unrotate(d_key, place).astype(BF)
        d_proj[place, 3 * HEAD :] = d_value.astype(BF)

    def project(u):
        @pl.loop(0, width // TILE)
        def _(n):
            send[u % 3, :, tile(n)] = dot_t(d_proj[u * UNIT : (u + 1) * UNIT], w_qkv[tile(n)]).astype(BF)

    def last_loads(u):
        rows = pl.ds(u * UNIT, UNIT)
        return (
            pltpu.make_async_copy(x_hbm.at[rows], xb, local.at[0]),
            pltpu.make_async_copy(d_mid_hbm.at[rows], mb_buf, local.at[1]),
        )

    def last(u):
        for copy in last_loads(u):
            copy.wait()

        @pl.loop(0, UNIT // 16)
        def _(r):
            rows = pl.ds(pl.multiple_of(r * 16, 16), 16)
            x = xb[rows].astype(F32)
            r_one = inverse_rms(x)
            dy = total[u, rows].astype(F32)
            scaled = scale_ref[0:1] * dy
            mean = jnp.mean(scaled * x, axis=-1, keepdims=True)
            back = r_one * scaled - x * (r_one * r_one * r_one) * mean
            mb_buf[rows] = (mb_buf[rows].astype(F32) + back).astype(BF)
            part = x * r_one * dy
            gain_ref[...] += part[:8] + part[8:]

        store = pltpu.make_async_copy(mb_buf, in_grad_hbm.at[pl.ds(u * UNIT, UNIT)], local.at[2])
        store.start()
        store.wait()
        if u < 3:
            for copy in last_loads(u + 1):
                copy.start()

    qkv_copy = pltpu.make_async_copy(w_qkv_hbm, w_qkv, local.at[2])
    for copy in (*attention_loads(0), qkv_copy, *operands(0), *last_loads(0)):
        copy.start()
    gain_ref[...] = jnp.zeros_like(gain_ref)
    pl.semaphore_wait(barrier, 5)
    attention_back(0)
    for copy in attention_loads(1):
        copy.start()
    qkv_copy.wait()
    project(0)
    boundary(0)
    scatter_start(0)
    project(1)
    boundary(1)
    attention_back(1)
    scatter_end(0)
    project(2)
    boundary(2)
    project(3)
    scatter_start(1)
    boundary(3)
    scatter_end(1)
    last(0)
    scatter_start(2)
    boundary(4)
    last(1)
    scatter_end(2)
    scatter_start(4 - 1)
    boundary(5)
    last(2)
    scatter_end(3)
    scatter_start(4)
    boundary(6)
    last(3)
    scatter_end(4)
    kv_copy(1).wait_send()
    own_store(4).wait()
    for m in range(2):
        core_copy(4, m).wait_send()
    for i in range(5):
        for way in (0, 1):
            if i > 2:
                far_copy(i, way).wait_send()
                final_copy(i, way).wait_send()
            final_copy(i, way).wait_recv()


def grad_call(seg_row, seg_col, cosine, sine, scales, arrays):
    x, w_qkv = arrays[0], arrays[6]
    tokens, width = x.shape
    rows = width // 8
    wide = arrays[8].shape[1]
    full = jax.ShapeDtypeStruct((tokens, width), BF)
    part = jax.ShapeDtypeStruct((5, rows, wide), BF)
    outs = (
        full,
        jax.ShapeDtypeStruct((5, rows, wide), F32),
        part,
        part,
        jax.ShapeDtypeStruct((8, width), F32),
        jax.ShapeDtypeStruct((5, 4, rows, wide), BF),
        part,
    )
    anywhere, vmem = pl.BlockSpec(memory_space=pl.ANY), pl.BlockSpec(memory_space=pltpu.VMEM)
    dma = pltpu.SemaphoreType.DMA
    half, length = tokens // 2, tokens
    return pl.pallas_call(
        grad_kernel,
        out_shape=outs,
        in_specs=[vmem] * 5 + [anywhere] * 15,
        out_specs=[anywhere] * 4 + [vmem] + [anywhere] * 2,
        scratch_shapes=[
            pltpu.VMEM(w_qkv.shape, BF),
            pltpu.VMEM((width, tokens), BF),
            pltpu.VMEM((tokens, wide), BF),
            pltpu.VMEM((2, rows, wide), BF),
            pltpu.VMEM((2, 3, rows, wide), BF),
            pltpu.VMEM((2, rows, wide), BF),
            pltpu.VMEM((rows, wide), F32),
            pltpu.VMEM((2, half, HEAD), BF),
            pltpu.VMEM((length, HEAD), BF),
            pltpu.VMEM((length, HEAD), BF),
            pltpu.VMEM((2, half, HEAD), BF),
            pltpu.VMEM((tokens, 4 * HEAD), BF),
            pltpu.VMEM((length, HEAD), F32),
            pltpu.VMEM((length, HEAD), F32),
            pltpu.VMEM((half, 2 * HEAD), BF),
            pltpu.VMEM((2, half, 2 * HEAD), BF),
            pltpu.VMEM((3, UNIT, width), BF),
            pltpu.VMEM((3, UNIT, width), BF),
            pltpu.VMEM((4, UNIT, width), BF),
            pltpu.VMEM((4, UNIT, width), BF),
            pltpu.VMEM((UNIT, width), BF),
            pltpu.VMEM((UNIT, width), BF),
            dma((3, 4)),
            dma((3, 4)),
            dma((2, 2)),
            dma((3,)),
            dma((5,)),
            dma((5, 8)),
            dma((5, 8)),
            dma((5,)),
            dma((1,)),
        ],
        compiler_params=pltpu.CompilerParams(
            collective_id=2, has_side_effects=True, vmem_limit_bytes=63 * 10**6
        ),
        name="grads",
    )(seg_row, seg_col, cosine, sine, scales, *arrays)


def fast_device(
    sizes,
    inputs,
    segment_ids,
    positions,
    cotangent,
    *params,
):
    masters, moments = params[:11], params[11:]
    batches, seqs, tokens, width = inputs.shape
    assert seqs == 1
    full_len = segment_ids.shape[2]
    q_cols, k_cols = masters[0].shape[1], masters[1].shape[1]
    heads = q_cols // HEAD
    width_ff = masters[4].shape[1]
    assert k_cols == HEAD

    low = [w.astype(BF) for w in masters[:7]]
    qkv_own = jnp.concatenate(low[:3], axis=1)
    gains_own = jnp.stack([g.astype(BF) for g in masters[7:]], axis=1)
    gains = lax.all_gather(gains_own, ("dp", "ctx"), axis=0, tiled=True).astype(F32)
    gain_one, gain_two, gain_three, gain_four = [gains[:, i] for i in range(4)]
    w_qkv, mark = gather_rows(qkv_own, sizes, None)
    w_out, mark = gather_rows(low[3], sizes, mark)

    start = lax.axis_index("ctx") * tokens
    causal = (start + jnp.arange(tokens))[:, None] >= jnp.arange(full_len)[None, :]
    frequency = jnp.exp(
        jnp.arange(HEAD // 2, dtype=F32) * (-2.0 * math.log(10000.0) / HEAD)
    )

    state = []
    for mb in range(batches):
        x = inputs[mb, 0].astype(F32)
        r_one = inverse_rms(x)
        attn_in = (x * r_one * (1.0 + gain_one)).astype(BF)
        angles = positions[mb, 0].astype(F32)[:, None] * frequency
        cosine, sine = jnp.cos(angles), jnp.sin(angles)
        seg = segment_ids[mb, 0]
        seg_local = lax.dynamic_slice_in_dim(seg, start, tokens)
        allowed = causal & (seg_local[:, None] == seg[None, :])
        proj = dot(attn_in, w_qkv)
        queries = jnp.concatenate(
            [rotate(proj[:, h * HEAD : (h + 1) * HEAD], cosine, sine) for h in range(heads)]
        ).astype(BF)
        keys = rotate(proj[:, q_cols : q_cols + HEAD], cosine, sine).astype(BF)
        values = proj[:, q_cols + HEAD :].astype(BF)
        both = swap_ctx(jnp.concatenate([keys, values], axis=1), sizes)
        keys_all, values_all = both[:, :HEAD], both[:, HEAD:]
        out, saved = attend(queries, keys_all, values_all, allowed)
        heads_out = jnp.concatenate(jnp.split(out, heads, axis=0), axis=1)
        state.append(
            dict(
                x=x, r_one=r_one, attn_in=attn_in, cosine=cosine, sine=sine, queries=queries,
                keys=keys_all, values=values_all, saved=saved, heads_out=heads_out,
            )
        )

    flat = (batches * tokens, width)
    heads_all = jnp.concatenate([s["heads_out"] for s in state])
    outs = ffn_call(
        heads_all, (1.0 + gains).T, inputs.reshape(flat), cotangent.reshape(flat), w_out,
        jnp.stack(low[4:]),
    )
    output, ffn_in_t, hidden, d_ffn_t, d_gate, d_up, d_attn_t, d_heads, d_mid, gain_parts = outs[:10]

    def batch(key):
        return jnp.stack([s[key] for s in state])

    def tokens_of(key):
        return jnp.concatenate([s[key] for s in state])

    seg_all = segment_ids[:, 0]
    seg_row = lax.dynamic_slice_in_dim(seg_all, start, tokens, 1)[:, None]
    outs = grad_call(
        seg_row, seg_all[:, :, None], tokens_of("cosine"), tokens_of("sine"), (1.0 + gains).T,
        (
            inputs.reshape(flat), d_mid, batch("queries").reshape(batches, heads, tokens, HEAD),
            batch("keys"), batch("values"), d_heads, w_qkv, d_ffn_t, hidden, ffn_in_t, d_gate, d_up,
            d_attn_t, heads_all, tokens_of("attn_in").T,
        ),
    )
    input_grad, own_sum, by_x, by_y, gain_part = outs[:5]

    def final_sum(i, cols):
        picked = [v[i, :, :cols].astype(F32) for v in (own_sum, by_x, by_y)]
        return picked[0] + picked[1] + picked[2]

    qkv_cols = w_qkv.shape[1]
    s_down, s_gate, s_up = [final_sum(i, width_ff) for i in range(3)]
    s_out, s_qkv = final_sum(3, q_cols), final_sum(4, qkv_cols)
    gain_grads = jnp.concatenate([jnp.sum(gain_part, axis=0)[None], jnp.sum(gain_parts, axis=1)])
    gain_grads = sum_small(gain_grads, ("ctx", "dp"), sizes)
    summed = (
        s_qkv[:, :q_cols], s_qkv[:, q_cols : q_cols + k_cols], s_qkv[:, q_cols + k_cols :],
        s_out, s_gate, s_up, s_down,
    )
    weight_sq = sum(jnp.sum(g * g) for g in (s_qkv, s_out, s_gate, s_up, s_down))
    weight_sq = sum_small(weight_sq.reshape(1, 1), ("ctx", "dp", "mp"), sizes)[0, 0]
    norm_value = jnp.sqrt(weight_sq + jnp.sum(gain_grads * gain_grads))
    factor = 1.0 / jnp.maximum(norm_value, 1.0)
    own = masters[7].shape[0]
    place = (lax.axis_index("dp") * sizes["ctx"] + lax.axis_index("ctx")) * own
    own_gains = lax.dynamic_slice_in_dim(gain_grads, place, own, 1)
    summed += tuple(own_gains[i] for i in range(4))
    new_moments = tuple(0.5 * m + 0.5 * factor * g for m, g in zip(moments, summed))
    changes = tuple(-RATE * (m + 0.01 * w) for w, m in zip(masters[:7], new_moments[:7]))

    return (
        output.reshape(inputs.shape),
        input_grad.reshape(inputs.shape), norm_value.reshape(1), *changes, *new_moments
    )


def per_device(
    sizes,
    inputs,
    segment_ids,
    positions,
    cotangent,
    *params,
):
    masters, moments = params[:11], params[11:]
    batches, seqs, tokens, width = inputs.shape
    assert seqs == 1
    full_len = segment_ids.shape[2]
    q_cols, k_cols = masters[0].shape[1], masters[1].shape[1]
    heads = q_cols // HEAD
    assert k_cols == HEAD
    cuts = 2 if tokens >= 512 else 1
    unit = tokens // cuts

    low = [w.astype(BF) for w in masters[:7]]
    qkv_own = jnp.concatenate(low[:3], axis=1)
    gains_own = jnp.stack([g.astype(BF) for g in masters[7:]], axis=1)
    gains = lax.all_gather(gains_own, ("dp", "ctx"), axis=0, tiled=True).astype(F32)
    gain_one, gain_two, gain_three, gain_four = [gains[:, i] for i in range(4)]
    w_qkv, mark = gather_rows(qkv_own, sizes, None)
    w_out, mark = gather_rows(low[3], sizes, mark)
    w_gate, mark = gather_rows(low[4], sizes, mark)
    w_up, mark = gather_rows(low[5], sizes, mark)
    w_down, mark = gather_rows(low[6], sizes, mark)

    start = lax.axis_index("ctx") * tokens
    causal = (start + jnp.arange(tokens))[:, None] >= jnp.arange(full_len)[None, :]
    frequency = jnp.exp(
        jnp.arange(HEAD // 2, dtype=F32) * (-2.0 * math.log(10000.0) / HEAD)
    )

    state = []
    for mb in range(batches):
        x = inputs[mb, 0].astype(F32)
        r_one = inverse_rms(x)
        attn_in = (x * r_one * (1.0 + gain_one)).astype(BF)
        angles = positions[mb, 0].astype(F32)[:, None] * frequency
        cosine, sine = jnp.cos(angles), jnp.sin(angles)
        seg = segment_ids[mb, 0]
        seg_local = lax.dynamic_slice_in_dim(seg, start, tokens)
        allowed = causal & (seg_local[:, None] == seg[None, :])
        proj = dot(attn_in, w_qkv)
        queries = jnp.concatenate(
            [rotate(proj[:, h * HEAD : (h + 1) * HEAD], cosine, sine) for h in range(heads)]
        ).astype(BF)
        keys = rotate(proj[:, q_cols : q_cols + HEAD], cosine, sine).astype(BF)
        values = proj[:, q_cols + HEAD :].astype(BF)
        both = swap_ctx(jnp.concatenate([keys, values], axis=1), sizes)
        keys_all, values_all = both[:, :HEAD], both[:, HEAD:]
        out, saved = attend(queries, keys_all, values_all, allowed)
        heads_out = jnp.concatenate(jnp.split(out, heads, axis=0), axis=1)
        state.append(
            dict(
                x=x, r_one=r_one, attn_in=attn_in, cosine=cosine, sine=sine, queries=queries,
                keys=keys_all, values=values_all, saved=saved, heads_out=heads_out,
            )
        )

    units = [(mb, cut) for mb in range(batches) for cut in range(cuts)]
    work = []
    for mb, cut in units:
        rows = slice(cut * unit, (cut + 1) * unit)
        part = dot_t(state[mb]["heads_out"][rows], w_out).astype(BF)
        work.append(dict(rows=rows, mb=mb, attn_low=sum_mp(part, sizes)))
    for w in work:
        attn = w["attn_low"].astype(F32)
        r_two = inverse_rms(attn)
        mid = state[w["mb"]]["x"][w["rows"]] + attn * r_two * (1.0 + gain_two)
        r_three = inverse_rms(mid)
        ffn_in = (mid * r_three * (1.0 + gain_three)).astype(BF)
        gate, up = dot(ffn_in, w_gate), dot(ffn_in, w_up)
        value, slope = gelu_parts(gate)
        hidden = (value * up).astype(BF)
        part = dot_t(hidden, w_down).astype(BF)
        w.update(
            mid=mid, r_two=r_two, r_three=r_three, ffn_in=ffn_in, gate=gate, up=up, hidden=hidden,
            ffn_low=sum_mp(part, sizes),
        )
    for w in work:
        ffn = w["ffn_low"].astype(F32)
        r_four = inverse_rms(ffn)
        grad = cotangent[w["mb"], 0][w["rows"]].astype(F32)
        w["output"] = (w["mid"] + ffn * r_four * (1.0 + gain_four)).astype(BF)
        d_ffn, w["g_four"] = norm_back(ffn, r_four, gain_four, grad)
        d_ffn = d_ffn.astype(BF)
        d_hidden = dot(d_ffn, w_down)
        value, slope = gelu_parts(w["gate"])
        d_gate = (d_hidden * w["up"] * slope).astype(BF)
        d_up = (d_hidden * value).astype(BF)
        part = (dot_t(d_gate, w_gate) + dot_t(d_up, w_up)).astype(BF)
        w.update(grad=grad, d_ffn=d_ffn, d_gate=d_gate, d_up=d_up, d_in_low=sum_mp(part, sizes))
    for w in work:
        d_in = w["d_in_low"].astype(F32)
        back, w["g_three"] = norm_back(w["mid"], w["r_three"], gain_three, d_in)
        d_mid = w["grad"] + back
        attn = w["attn_low"].astype(F32)
        d_attn, w["g_two"] = norm_back(attn, w["r_two"], gain_two, d_mid)
        d_attn = d_attn.astype(BF)
        w.update(d_mid=d_mid, d_attn=d_attn, d_heads=dot(d_attn, w_out).astype(BF))

    def rows_of(key):
        return jnp.concatenate([w[key] for w in work])

    ffn_in = rows_of("ffn_in")
    g_down = t_dot(rows_of("d_ffn"), rows_of("hidden"))
    g_gate = t_dot(ffn_in, rows_of("d_gate"))
    g_up = t_dot(ffn_in, rows_of("d_up"))
    s_down, mark = scatter_rows(g_down, sizes, None)
    s_gate, mark = scatter_rows(g_gate, sizes, mark)
    s_up, mark = scatter_rows(g_up, sizes, mark)

    for mb in range(batches):
        s = state[mb]
        d_heads = jnp.concatenate([w["d_heads"] for w in work if w["mb"] == mb])
        d_out = jnp.concatenate(jnp.split(d_heads, heads, axis=1))
        d_queries, d_keys, d_values = attend_back(
            s["saved"], s["queries"], s["keys"], s["values"], d_out
        )
        d_kv = scatter_ctx(jnp.concatenate([d_keys, d_values], axis=1), sizes)
        pieces = [rotate(q, s["cosine"], -s["sine"]) for q in jnp.split(d_queries, heads)]
        pieces += [rotate(d_kv[:, :HEAD], s["cosine"], -s["sine"]), d_kv[:, HEAD:]]
        s["d_proj"] = jnp.concatenate(pieces, axis=1).astype(BF)
    for w in work:
        part = dot_t(state[w["mb"]]["d_proj"][w["rows"]], w_qkv).astype(BF)
        w["d_attn_in"] = sum_mp(part, sizes)

    g_out = t_dot(rows_of("d_attn"), jnp.concatenate([s["heads_out"] for s in state]))
    g_qkv = t_dot(
        jnp.concatenate([s["attn_in"] for s in state]),
        jnp.concatenate([s["d_proj"] for s in state]),
    )
    s_out, mark = scatter_rows(g_out, sizes, mark)
    s_qkv, mark = scatter_rows(g_qkv, sizes, mark)

    for w in work:
        s = state[w["mb"]]
        back, w["g_one"] = norm_back(
            s["x"][w["rows"]], s["r_one"][w["rows"]], gain_one, w["d_attn_in"].astype(F32)
        )
        w["input_grad"] = (w["d_mid"] + back).astype(BF)

    gain_grads = jnp.stack(
        [sum(w[key] for w in work) for key in ("g_one", "g_two", "g_three", "g_four")]
    )
    gain_grads = sum_small(gain_grads, ("ctx", "dp"), sizes)
    summed = (
        s_qkv[:, :q_cols], s_qkv[:, q_cols : q_cols + k_cols], s_qkv[:, q_cols + k_cols :],
        s_out, s_gate, s_up, s_down,
    )
    weight_sq = sum(jnp.sum(g * g) for g in (s_qkv, s_out, s_gate, s_up, s_down))
    weight_sq = sum_small(weight_sq.reshape(1, 1), ("ctx", "dp", "mp"), sizes)[0, 0]
    norm_value = jnp.sqrt(weight_sq + jnp.sum(gain_grads * gain_grads))
    factor = 1.0 / jnp.maximum(norm_value, 1.0)
    own = masters[7].shape[0]
    place = (lax.axis_index("dp") * sizes["ctx"] + lax.axis_index("ctx")) * own
    own_gains = lax.dynamic_slice_in_dim(gain_grads, place, own, 1)
    summed += tuple(own_gains[i] for i in range(4))
    new_moments = tuple(0.5 * m + 0.5 * factor * g for m, g in zip(moments, summed))
    changes = tuple(-RATE * (m + 0.01 * w) for w, m in zip(masters[:7], new_moments[:7]))

    def whole(key):
        return rows_of(key).reshape(inputs.shape)

    return (
        whole("output"), whole("input_grad"), norm_value.reshape(1), *changes, *new_moments
    )


def solution(mesh):
    sizes = dict(mesh.shape)
    weight, vector = P(("dp", "ctx"), "mp"), P(("dp", "ctx"))
    params = (weight,) * 7 + (vector,) * 4
    data = P(None, "dp", "ctx", None)

    def run(*args):
        batches, _, tokens, _ = args[0].shape
        fast = sizes == dict(dp=4, ctx=2, mp=4) and batches == 2 and tokens == 2 * UNIT
        return (fast_device if fast else per_device)(sizes, *args)

    return jax.shard_map(
        run,
        mesh=mesh,
        in_specs=(data, P(None, "dp", None), P(None, "dp", "ctx"), data) + params + params,
        out_specs=(data, data, P()) + (weight,) * 7 + params,
        check_vma=False,
    )
```

```python
import math

import jax
import jax.numpy as jnp
from jax import lax
from jax.experimental import pallas as pl
from jax.experimental.pallas import tpu as pltpu
from jax.sharding import PartitionSpec as P

HEAD = 256
STEP = 10
EPS = 1e-06
CAP = 50.0
RATE = 1.0 / math.sqrt(1.0 + STEP / 1000.0)
SCALE = HEAD ** (-0.5)
BF = jnp.bfloat16
F32 = jnp.float32


def flip(axis, size, mask):
    return dict(axis_name=axis, perm=[(i, i ^ mask) for i in range(size)])


def after(value, other):
    return lax.optimization_barrier((value, other))[0]


def gather_rows(own, sizes, wait):
    dp, ctx = sizes["dp"], sizes["ctx"]
    rows, cols = own.shape
    if wait is not None:
        own = after(own, wait)
    if dp != 4:
        out = lax.all_gather(own, ("dp", "ctx"), axis=0, tiled=True)
        return out, own
    me = lax.axis_index("dp")
    half = rows // 2 // 16 * 16
    from_x = lax.ppermute(own, **flip("dp", dp, 1))
    from_y = lax.ppermute(own, **flip("dp", dp, 2))
    far_top = lax.ppermute(from_y[:half], **flip("dp", dp, 1))
    far_low = lax.ppermute(from_x[half:], **flip("dp", dp, 2))
    mine = jnp.zeros((dp, rows, cols), own.dtype)
    mine = lax.dynamic_update_slice(mine, own[None], (me, 0, 0))
    mine = lax.dynamic_update_slice(mine, from_x[None], (me ^ 1, 0, 0))
    mine = lax.dynamic_update_slice(mine, from_y[None], (me ^ 2, 0, 0))
    mine = lax.dynamic_update_slice(mine, far_top[None], (me ^ 3, 0, 0))
    mine = lax.dynamic_update_slice(mine, far_low[None], (me ^ 3, half, 0))
    if ctx == 2:
        other = lax.ppermute(mine, **flip("ctx", ctx, 1))
        core = lax.axis_index("ctx")
        out = jnp.zeros((dp, ctx, rows, cols), own.dtype)
        out = lax.dynamic_update_slice(out, mine[:, None], (0, core, 0, 0))
        out = lax.dynamic_update_slice(out, other[:, None], (0, 1 - core, 0, 0))
    else:
        out = lax.all_gather(mine, "ctx", axis=1)
    return out.reshape(dp * ctx * rows, cols), from_x


def scatter_rows(full, sizes, wait):
    dp, ctx = sizes["dp"], sizes["ctx"]
    full = full.astype(BF)
    if wait is not None:
        full = after(full, wait)
    rows = full.shape[0] // (dp * ctx)
    cols = full.shape[1]
    if dp != 4:
        out = lax.psum_scatter(full, ("dp", "ctx"), scatter_dimension=0, tiled=True)
        return out.astype(F32), out
    blocks = full.reshape(dp, ctx, rows, cols)
    if ctx == 2:
        core = lax.axis_index("ctx")
        send = lax.dynamic_index_in_dim(blocks, 1 - core, 1, keepdims=False)
        keep = lax.dynamic_index_in_dim(blocks, core, 1, keepdims=False)
        got = lax.ppermute(send, **flip("ctx", ctx, 1))
    else:
        keep = lax.psum_scatter(blocks, "ctx", scatter_dimension=1, tiled=False)
        got = None
    me = lax.axis_index("dp")
    half = rows // 2 // 16 * 16

    def part(mask, low, high):
        size = (1, high - low, cols)
        piece = lax.dynamic_slice(keep, (me ^ mask, low, 0), size)[0].astype(F32)
        if got is not None:
            piece = piece + lax.dynamic_slice(got, (me ^ mask, low, 0), size)[0].astype(F32)
        return piece

    far_top = lax.ppermute(part(3, 0, half).astype(BF), **flip("dp", dp, 1))
    far_low = lax.ppermute(part(3, half, rows).astype(BF), **flip("dp", dp, 2))
    to_y = jnp.concatenate([part(2, 0, half) + far_top.astype(F32), part(2, half, rows)])
    to_x = jnp.concatenate([part(1, 0, half), part(1, half, rows) + far_low.astype(F32)])
    by_y = lax.ppermute(to_y.astype(BF), **flip("dp", dp, 2))
    by_x = lax.ppermute(to_x.astype(BF), **flip("dp", dp, 1))
    total = part(0, 0, rows) + by_x.astype(F32) + by_y.astype(F32)
    return total, far_top


def sum_mp(part, sizes):
    if sizes["mp"] != 4:
        return lax.psum(part, "mp")
    place = lax.axis_index("mp")
    inner = (place == 1) | (place == 2)
    near = lax.ppermute(part, "mp", [(0, 1), (3, 2)])
    pair = (part.astype(F32) + near.astype(F32)).astype(BF)
    across = lax.ppermute(pair, "mp", [(1, 2), (2, 1)])
    total = (pair.astype(F32) + across.astype(F32)).astype(BF)
    back = lax.ppermute(total, "mp", [(1, 0), (2, 3)])
    return jnp.where(inner, total, back)


def sum_small(value, axes, sizes):
    for axis in axes:
        size = sizes[axis]
        step = 1
        while step < size:
            value = value + lax.ppermute(value, **flip(axis, size, step))
            step *= 2
    return value


def swap_ctx(local, sizes):
    if sizes["ctx"] != 2:
        return lax.all_gather(local, "ctx", axis=0, tiled=True)
    other = lax.ppermute(local, **flip("ctx", 2, 1))
    first = lax.axis_index("ctx") == 0
    return jnp.concatenate([jnp.where(first, local, other), jnp.where(first, other, local)])


def scatter_ctx(full, sizes):
    if sizes["ctx"] != 2:
        return lax.psum_scatter(full.astype(BF), "ctx", scatter_dimension=0, tiled=True).astype(F32)
    core = lax.axis_index("ctx")
    rows = full.shape[0] // 2
    send = lax.dynamic_slice_in_dim(full, (1 - core) * rows, rows).astype(BF)
    keep = lax.dynamic_slice_in_dim(full, core * rows, rows)
    return keep.astype(BF).astype(F32) + lax.ppermute(send, **flip("ctx", 2, 1)).astype(F32)


def dot(a, b):
    return lax.dot_general(a, b, (((1,), (0,)), ((), ())), preferred_element_type=F32)


def dot_t(a, b):
    return lax.dot_general(a, b, (((1,), (1,)), ((), ())), preferred_element_type=F32)


def t_dot(a, b):
    return lax.dot_general(a, b, (((0,), (0,)), ((), ())), preferred_element_type=F32)


def inverse_rms(v):
    return lax.rsqrt(jnp.mean(v * v, axis=-1, keepdims=True) + EPS)


def norm_back(v, r, gain, dy):
    scaled = (1.0 + gain) * dy
    mean = jnp.mean(scaled * v, axis=-1, keepdims=True)
    return r * scaled - v * (r * r * r) * mean, jnp.sum(v * r * dy, axis=0)


def rotate(v, cosine, sine):
    a, b = v[:, : HEAD // 2], v[:, HEAD // 2 :]
    return jnp.concatenate([a * cosine - b * sine, b * cosine + a * sine], axis=1)


GELU_C = math.sqrt(2.0 / math.pi)


def gelu_parts(u):
    tanh = jnp.tanh(GELU_C * (u + 0.044715 * u * u * u))
    value = 0.5 * u * (1.0 + tanh)
    slope = 0.5 * (1.0 + tanh) + 0.5 * u * (1.0 - tanh * tanh) * GELU_C * (
        1.0 + 3.0 * 0.044715 * u * u
    )
    return value, slope


def attend(queries, keys, values, allowed):
    raw = dot_t(queries, keys) * SCALE
    tanh = jnp.tanh(raw / CAP)
    heads = queries.shape[0] // allowed.shape[0]
    mask = jnp.concatenate([allowed] * heads, axis=0)
    weight = jnp.where(mask, jnp.exp(CAP * tanh), 0.0)
    probs = weight / jnp.sum(weight, axis=1, keepdims=True)
    out = dot(probs.astype(BF), values).astype(BF)
    return out, (probs, tanh)


def attend_back(saved, queries, keys, values, d_out):
    probs, tanh = saved
    d_probs = dot_t(d_out, values)
    inner = jnp.sum(probs * d_probs, axis=1, keepdims=True)
    d_raw = (probs * (d_probs - inner) * (1.0 - tanh * tanh)).astype(BF)
    d_queries = dot(d_raw, keys) * SCALE
    d_keys = t_dot(d_raw, queries) * SCALE
    d_values = t_dot(probs.astype(BF), d_out)
    return d_queries, d_keys, d_values


MESH = pl.DeviceIdType.MESH
UNIT = 256
TILE = 256


def layer_kernel(
    first_row, gains_own, cos_hbm, sin_hbm, x_hbm, cot_hbm, own_qkv, own_out, own_gate, own_up, own_down,
    out_hbm, ffn_in_hbm, hidden_hbm, d_ffn_hbm, d_gate_hbm, d_up_hbm, d_attn_hbm, d_heads_hbm,
    d_mid_hbm, gain_ref, scale_ref, attn_in_hbm, heads_hbm, pack_hbm, w_qkv_hbm, w_out_hbm,
    attn_hbm, slope_hbm, value_hbm,
    weights, w_qkv, send, near, across, total, xb, cb, ab, act, act_t, stage, d_heads, angle,
    line_send, line_recv, credit, local, ag_send, ag_recv, ag_local, gain_send, gain_recv, kv_sem,
):
    dp, core, z = lax.axis_index("dp"), lax.axis_index("ctx"), lax.axis_index("mp")
    w_out = w_qkv.at[:, : w_out_hbm.shape[1]]
    width, units = xb.shape[1], weights.shape[2]
    rows_own = own_qkv.shape[0]
    half = rows_own // 2
    inner = (z == 1) | (z == 2)
    outer = (z == 0) | (z == 3)
    x_peer, y_peer = (dp ^ 1, core, z), (dp ^ 2, core, z)
    core_peer = (dp, 1 - core, z)
    near_peer = (dp, core, z ^ 1)
    far_peer = (dp, core, 3 - z)

    barrier = pltpu.get_barrier_semaphore()
    group = [(dp ^ (m // 2), (1 - core) if m % 2 else core, z) for m in range(1, 8)]
    for peer in (*group, near_peer, far_peer):
        pl.semaphore_signal(barrier, inc=1, device_id=peer, device_id_type=MESH)

    def block(mask, other=False, low=0, size=rows_own):
        owner = (dp ^ mask) * 2 + ((1 - core) if other else core)
        return pl.ds(pl.multiple_of(owner * rows_own + low, 16), size)

    owns = (own_qkv, own_out, own_gate, own_up, own_down)
    wholes = (w_qkv, w_out_hbm, weights.at[0], weights.at[1], weights.at[2])

    def gather(w, name, recv=False):
        table = {
            "x": (0, block(0), x_peer, block(1)),
            "y": (1, block(0), y_peer, block(2)),
            "top": (2, block(2, False, 0, half), x_peer, block(3, False, 0, half)),
            "low": (3, block(1, False, half, half), y_peer, block(3, False, half, half)),
            "own_c": (4, block(0), core_peer, block(0, True)),
            "x_c": (5, block(1), core_peer, block(1, True)),
            "y_c": (6, block(2), core_peer, block(2, True)),
            "top_c": (7, block(3, False, 0, half), core_peer, block(3, True, 0, half)),
            "low_c": (8, block(3, False, half, half), core_peer, block(3, True, half, half)),
        }
        index, out_rows, peer, in_rows = table[name]
        rows = in_rows if recv else out_rows
        src = owns[w] if name in ("x", "y", "own_c") else wholes[w].at[rows]
        return pltpu.make_async_remote_copy(
            src_ref=src, dst_ref=wholes[w].at[rows], send_sem=ag_send.at[w, index],
            recv_sem=ag_recv.at[w, index], device_id=peer, device_id_type=MESH,
        )

    def own_copy(w):
        return pltpu.make_async_copy(owns[w], wholes[w].at[block(0)], ag_local.at[w])

    def gather_first(w):
        for name in ("x", "y", "own_c"):
            gather(w, name).start()
        own_copy(w).start()

    def gather_second(w):
        gather(w, "x", True).wait_recv()
        gather(w, "low").start()
        gather(w, "x_c").start()
        gather(w, "y", True).wait_recv()
        gather(w, "top").start()
        gather(w, "y_c").start()

    def gather_third(w):
        for name in ("top", "low"):
            gather(w, name, True).wait_recv()
            gather(w, name + "_c").start()

    def gather_end(w):
        for name in ("own_c", "x_c", "y_c", "top_c", "low_c"):
            gather(w, name, True).wait_recv()
        own_copy(w).wait()
        for name in ("x", "y", "top", "low", "own_c", "x_c", "y_c", "top_c", "low_c"):
            gather(w, name).wait_send()

    def hop(kind, i):
        src = (send.at[i % 3], send.at[i % 3], total.at[i % 4])[kind]
        dst = (near.at[i % 3], across.at[i % 2], total.at[i % 4])[kind]
        return pltpu.make_async_remote_copy(
            src_ref=src, dst_ref=dst, send_sem=line_send.at[kind, i % 4],
            recv_sem=line_recv.at[kind, i % 4],
            device_id=far_peer if kind == 1 else near_peer, device_id_type=MESH,
        )

    def add_rows(dst, a, b):
        @pl.loop(0, UNIT // 16)
        def _(r):
            rows = pl.ds(pl.multiple_of(r * 16, 16), 16)
            dst[rows] = (a[rows].astype(F32) + b[rows].astype(F32)).astype(BF)

    def boundary(k, up=True, cross=True, back=True, done=True):
        @pl.when(outer)
        def _():
            if done:
                hop(2, k - 3).wait_recv()
            if cross:
                hop(0, k - 1).wait_send()
            if up:
                hop(0, k).start()

        @pl.when(inner)
        def _():
            if cross:
                i = k - 1
                hop(0, i).wait_recv()
                add_rows(send.at[i % 3], send.at[i % 3], near.at[i % 3])
                if isinstance(i, int):
                    if i >= 2:
                        pl.semaphore_wait(credit, 1)
                else:
                    pl.semaphore_wait(credit, 1)
                hop(1, i).start()
            if back:
                i = k - 2
                hop(1, i).wait_recv()
                hop(1, i).wait_send()
                add_rows(total.at[i % 4], send.at[i % 3], across.at[i % 2])
                if not isinstance(i, int) or i < 10:
                    pl.semaphore_signal(credit, inc=1, device_id=far_peer, device_id_type=MESH)
                hop(2, i).start()
            if done:
                hop(2, k - 3).wait_send()

    def rows_of(u):
        return pl.ds(pl.multiple_of(u * UNIT, UNIT), UNIT)

    def load(ref, u, dst, sem):
        return pltpu.make_async_copy(ref.at[rows_of(u)], dst, local.at[sem])

    def store(src, ref, u, sem):
        return pltpu.make_async_copy(src, ref.at[rows_of(u)], local.at[sem])

    def store_t(ref, u, sem):
        return pltpu.make_async_copy(act_t, ref.at[:, rows_of(u)], local.at[sem])

    def turn(source=None):
        source = act if source is None else source

        @pl.loop(0, width // TILE)
        def _(n):
            act_t[tile(n)] = source[:, tile(n)].T

    def tile(n):
        return pl.ds(pl.multiple_of(n * TILE, TILE), TILE)

    def each_rows(body):
        @pl.loop(0, UNIT // 16)
        def _(r):
            body(pl.ds(pl.multiple_of(r * 16, 16), 16))

    def scale(i):
        return scale_ref[i : i + 1]

    def add_gain(index, v):
        gain_ref[index] += v[:8] + v[8:]

    def project_out(u, k):
        dst = send.at[k % 3]

        @pl.loop(0, width // TILE)
        def _(n):
            dst[:, tile(n)] = dot_t(act[:, 2 * HEAD * u : 2 * HEAD * (u + 1)], w_out[tile(n)]).astype(BF)

    def middle(rows, u4):
        attn = total[u4, rows].astype(F32) if u4 is not None else ab[rows].astype(F32)
        r_two = inverse_rms(attn)
        return attn, r_two, xb[rows].astype(F32) + attn * r_two * scale(1)

    def forward(u, k, ready=None):
        load(x_hbm, u, xb, 0).start()
        store(total.at[u], attn_hbm, u, 1).start()
        load(x_hbm, u, xb, 0).wait()

        def body(rows):
            _, _, mid = middle(rows, u)
            act[rows] = (mid * inverse_rms(mid) * scale(2)).astype(BF)

        each_rows(body)
        turn()
        store_t(ffn_in_hbm, u, 2).start()

        @pl.loop(0, units // TILE)
        def _(f):
            gate = dot(act[...], weights[0, :, tile(f)])
            up = dot(act[...], weights[1, :, tile(f)])
            value, slope = gelu_parts(gate)
            stage[0, :, tile(f)] = (value * up).astype(BF)
            stage[1, :, tile(f)] = (slope * up).astype(BF)
            stage[2, :, tile(f)] = value.astype(BF)

        saves = ((0, hidden_hbm), (1, slope_hbm), (2, value_hbm))
        for i, ref in saves:
            store(stage.at[i], ref, u, 3 + i).start()
        if ready is not None:
            ready()
        dst = send.at[k % 3]

        @pl.loop(0, width // TILE)
        def _(n):
            dst[:, tile(n)] = dot_t(stage[0], weights[2, tile(n)]).astype(BF)

        for i, ref in saves:
            store(stage.at[i], ref, u, 3 + i).wait()
        store(total.at[u], attn_hbm, u, 1).wait()
        store_t(ffn_in_hbm, u, 2).wait()

    def backward(u, k):
        loads = (
            load(x_hbm, u, xb, 0), load(attn_hbm, u, ab, 1), load(cot_hbm, u, cb, 2),
            load(slope_hbm, u, stage.at[1], 4), load(value_hbm, u, stage.at[2], 5),
        )
        for copy in loads:
            copy.start()
        for copy in loads:
            copy.wait()

        def body(rows):
            _, _, mid = middle(rows, None)
            ffn = total[u, rows].astype(F32)
            r = inverse_rms(ffn)
            dy = cb[rows].astype(F32)
            xb[rows] = (mid + ffn * r * scale(3)).astype(BF)
            scaled = scale(3) * dy
            mean = jnp.mean(scaled * ffn, axis=-1, keepdims=True)
            act[rows] = (r * scaled - ffn * (r * r * r) * mean).astype(BF)
            add_gain(2, ffn * r * dy)

        each_rows(body)
        store(xb, out_hbm, u, 0).start()
        turn()
        store_t(d_ffn_hbm, u, 1).start()

        @pl.loop(0, units // TILE)
        def _(f):
            d_hidden = dot(act[...], weights[2, :, tile(f)])
            stage[1, :, tile(f)] = (d_hidden * stage[1, :, tile(f)].astype(F32)).astype(BF)
            stage[2, :, tile(f)] = (d_hidden * stage[2, :, tile(f)].astype(F32)).astype(BF)

        store(stage.at[1], d_gate_hbm, u, 4).start()
        store(stage.at[2], d_up_hbm, u, 5).start()
        dst = send.at[k % 3]

        @pl.loop(0, width // TILE)
        def _(n):
            part = dot_t(stage[1], weights[0, tile(n)]) + dot_t(stage[2], weights[1, tile(n)])
            dst[:, tile(n)] = part.astype(BF)

        store(xb, out_hbm, u, 0).wait()
        store_t(d_ffn_hbm, u, 1).wait()
        store(stage.at[1], d_gate_hbm, u, 4).wait()
        store(stage.at[2], d_up_hbm, u, 5).wait()

    def last(u):
        loads = (load(x_hbm, u, xb, 0), load(attn_hbm, u, ab, 1), load(cot_hbm, u, cb, 2))
        for copy in loads:
            copy.start()
        for copy in loads:
            copy.wait()

        def body(rows):
            attn, r_two, mid = middle(rows, None)
            r = inverse_rms(mid)
            dy = total[u, rows].astype(F32)
            scaled = scale(2) * dy
            mean = jnp.mean(scaled * mid, axis=-1, keepdims=True)
            grad = cb[rows].astype(F32) + r * scaled - mid * (r * r * r) * mean
            add_gain(1, mid * r * dy)
            cb[rows] = grad.astype(BF)
            scaled = scale(1) * grad
            mean = jnp.mean(scaled * attn, axis=-1, keepdims=True)
            act[rows] = (r_two * scaled - attn * (r_two * r_two * r_two) * mean).astype(BF)
            add_gain(0, attn * r_two * grad)

        each_rows(body)
        store(cb, d_mid_hbm, u, 0).start()
        turn()
        store_t(d_attn_hbm, u, 1).start()
        for h in range(w_out.shape[1] // TILE):
            columns = slice(h * TILE, (h + 1) * TILE)
            d_heads[:, columns] = dot(act[...], w_out[:, columns]).astype(BF)
        store(d_heads, d_heads_hbm, u, 2).start()
        store(cb, d_mid_hbm, u, 0).wait()
        store_t(d_attn_hbm, u, 1).wait()
        store(d_heads, d_heads_hbm, u, 2).wait()

    def gain_copy(m, recv=False):
        peer = group[m - 1]
        owner = (peer[0] * 2 + peer[1]) if recv else (dp * 2 + core)
        return pltpu.make_async_remote_copy(
            src_ref=gains_own, dst_ref=send.at[2, pl.ds(pl.multiple_of(owner * 16, 16), 16)],
            send_sem=gain_send.at[m], recv_sem=gain_recv.at[m], device_id=peer, device_id_type=MESH,
        )

    def gains_sum():
        whole = gains_own[...].astype(F32)
        for m in range(1, 8):
            gain_copy(m, True).wait_recv()
        for m in range(1, 8):
            owner = group[m - 1][0] * 2 + group[m - 1][1]
            whole += send[2, pl.ds(pl.multiple_of(owner * 16, 16), 16)].astype(F32)
        scale_ref[...] = 1.0 + whole[:8]
        for m in range(1, 8):
            gain_copy(m).wait_send()

    loaded = (stage.at[0], stage.at[1], stage.at[2], act)

    def first_norm(u):
        load(x_hbm, u, loaded[u], u).wait()

        def body(rows):
            x = loaded[u][rows].astype(F32)
            total[u, rows] = (x * inverse_rms(x) * scale(0)).astype(BF)

        each_rows(body)

    def first_turn(u):
        if u:
            store_t(attn_in_hbm, u - 1, 4).wait()
        turn(total.at[u])
        store_t(attn_in_hbm, u, 4).start()

    def angles(u):
        rows = rows_of(u)
        return (
            pltpu.make_async_copy(cos_hbm.at[rows], angle.at[u % 2, 0], local.at[2 * (u % 2)]),
            pltpu.make_async_copy(sin_hbm.at[rows], angle.at[u % 2, 1], local.at[2 * (u % 2) + 1]),
        )

    packs = (cb, ab)

    def kv_columns(kind, peer=False):
        side = (1 - core) if peer else core
        return pl.ds(pl.multiple_of(kind * 4 * HEAD + side * 2 * HEAD, HEAD), 2 * HEAD)

    def kv_copy(mb, kind, recv=False):
        part = packs[mb].at[:, kv_columns(kind, recv)]
        return pltpu.make_async_remote_copy(
            src_ref=part, dst_ref=part, send_sem=kv_sem.at[0, mb, kind], recv_sem=kv_sem.at[1, mb, kind],
            device_id=core_peer, device_id_type=MESH,
        )

    def projections(u):
        mb, b = divmod(u, 2)
        for copy in angles(u):
            copy.wait()
        if u < 3:
            for copy in angles(u + 1):
                copy.start()
        c, s = angle[u % 2, 0], angle[u % 2, 1]
        for j in range(4):
            v = dot(total[u], w_qkv[:, j * HEAD : (j + 1) * HEAD])
            if j < 2:
                xb[:, (mb * 4 + j * 2 + b) * HEAD : (mb * 4 + j * 2 + b + 1) * HEAD] = rotate(v, c, s).astype(BF)
            else:
                place = pl.multiple_of((j - 2) * 4 * HEAD + (core * 2 + b) * HEAD, HEAD)
                packs[mb][:, pl.ds(place, HEAD)] = (rotate(v, c, s) if j == 2 else v).astype(BF)

    def attention(mb):
        for kind in (0, 1):
            kv_copy(mb, kind, True).wait_recv()

        @pl.loop(0, 4)
        def _(i):
            h, b = i // 2, i % 2
            query = xb[:, pl.ds(pl.multiple_of(mb * 4 * HEAD + i * HEAD, HEAD), HEAD)]
            lowest = first_row[mb, :, pl.ds(pl.multiple_of(b * UNIT, UNIT), UNIT)]
            query_at = lax.broadcasted_iota(jnp.int32, (UNIT, UNIT), 1) + core * 2 * UNIT + b * UNIT
            weight, length = [], 0.0
            for j in range(4):
                key_at = lax.broadcasted_iota(jnp.int32, (UNIT, UNIT), 0) + j * UNIT
                score = dot_t(packs[mb][:, j * HEAD : (j + 1) * HEAD], query) * (SCALE / CAP)
                ok = (key_at <= query_at) & (key_at >= lowest)
                weight.append(jnp.where(ok, jnp.exp(CAP * jnp.tanh(score)), 0.0))
                length = length + jnp.sum(weight[j], axis=0, keepdims=True)
            inverse = 1.0 / length
            out = 0.0
            for j in range(4):
                value = packs[mb][:, (4 + j) * HEAD : (5 + j) * HEAD]
                out = out + t_dot((weight[j] * inverse).astype(BF), value)
            place = pl.multiple_of((mb * 2 + b) * 2 * HEAD + h * HEAD, HEAD)
            act[:, pl.ds(place, HEAD)] = out.astype(BF)

    def heads_store(u):
        return pltpu.make_async_copy(
            act.at[:, 2 * HEAD * u : 2 * HEAD * (u + 1)], heads_hbm.at[rows_of(u)], local.at[u]
        )

    def pack_store(i):
        return pltpu.make_async_copy((xb, cb, ab)[i], pack_hbm.at[i], ag_local.at[5 + i])

    for u in range(4):
        load(x_hbm, u, loaded[u], u).start()
    gain_ref[...] = jnp.zeros_like(gain_ref)
    pl.semaphore_wait(barrier, 9)
    for m in range(1, 8):
        gain_copy(m).start()
    gather_first(0)
    gains_sum()
    for u in range(4):
        first_norm(u)
    for copy in angles(0):
        copy.start()
    first_turn(0)
    gather_second(0)
    first_turn(1)
    first_turn(2)
    gather_third(0)
    gather_first(1)
    first_turn(3)
    gather_end(0)
    qkv_store = pltpu.make_async_copy(w_qkv, w_qkv_hbm, local.at[5])
    qkv_store.start()
    for u in range(4):
        projections(u)
        if u % 2:
            for kind in (0, 1):
                kv_copy(u // 2, kind).start()
    gather_second(1)
    gather_first(2)
    attention(0)
    gather_third(1)
    gather_end(1)
    qkv_store.wait()
    store_t(attn_in_hbm, 3, 4).wait()
    out_load = pltpu.make_async_copy(w_out_hbm, w_out, local.at[4])
    out_load.start()
    out_load.wait()
    project_out(0, 0)
    boundary(0, cross=False, back=False, done=False)
    project_out(1, 1)
    attention(1)
    project_out(2, 2)
    for i in range(3):
        pack_store(i).start()
    for u in range(4):
        heads_store(u).start()
    gather_second(2)
    gather_first(3)
    boundary(1, back=False, done=False)
    gather_third(2)
    for kind in (0, 1):
        for mb in (0, 1):
            kv_copy(mb, kind).wait_send()
    for i in range(3):
        pack_store(i).wait()
    for u in range(4):
        heads_store(u).wait()
    boundary(2, done=False)
    project_out(3, 3)
    gather_second(3)
    gather_first(4)
    boundary(3)
    gather_third(3)
    gather_end(2)
    gather_end(3)

    def ready():
        gather_second(4)
        gather_third(4)
        gather_end(4)

    forward(0, 4, ready)

    @pl.loop(4, 7)
    def _(k):
        boundary(k)
        forward(k - 3, k + 1)

    @pl.loop(7, 11)
    def _(k):
        boundary(k)
        backward(k - 7, k + 1)

    for k in (11, 12, 13, 14):
        boundary(k, up=k < 12, cross=k < 13, back=k < 14)
        last(k - 11)


def layer_call(first_row, gains_own, cosine, sine, x, cot, owns):
    tokens, width = x.shape
    units = owns[2].shape[1]
    qkv_cols, out_cols = owns[0].shape[1], owns[1].shape[1]
    assert tokens == 4 * UNIT
    full = jax.ShapeDtypeStruct((tokens, width), BF)
    wide = jax.ShapeDtypeStruct((tokens, units), BF)
    flipped = jax.ShapeDtypeStruct((width, tokens), BF)
    heads = jax.ShapeDtypeStruct((tokens, out_cols), BF)
    outs = (
        full, flipped, wide, flipped, wide, wide, flipped, heads, full,
        jax.ShapeDtypeStruct((3, 8, width), F32),
        jax.ShapeDtypeStruct((8, width), F32),
        flipped,
        heads,
        jax.ShapeDtypeStruct((3, UNIT, width), BF),
        jax.ShapeDtypeStruct((width, qkv_cols), BF),
        jax.ShapeDtypeStruct((width, out_cols), BF),
        full, wide, wide,
    )
    anywhere, vmem = pl.BlockSpec(memory_space=pl.ANY), pl.BlockSpec(memory_space=pltpu.VMEM)
    dma = pltpu.SemaphoreType.DMA
    return pl.pallas_call(
        layer_kernel,
        out_shape=outs,
        in_specs=[vmem] * 2 + [anywhere] * 9,
        out_specs=[anywhere] * 9 + [vmem] * 2 + [anywhere] * 8,
        scratch_shapes=[
            pltpu.VMEM((3, width, units), BF),
            pltpu.VMEM((width, qkv_cols), BF),
            pltpu.VMEM((3, UNIT, width), BF),
            pltpu.VMEM((3, UNIT, width), BF),
            pltpu.VMEM((2, UNIT, width), BF),
            pltpu.VMEM((4, UNIT, width), BF),
            pltpu.VMEM((UNIT, width), BF),
            pltpu.VMEM((UNIT, width), BF),
            pltpu.VMEM((UNIT, width), BF),
            pltpu.VMEM((UNIT, width), BF),
            pltpu.VMEM((width, UNIT), BF),
            pltpu.VMEM((3, UNIT, units), BF),
            pltpu.VMEM((UNIT, out_cols), BF),
            pltpu.VMEM((2, 2, UNIT, HEAD // 2), F32),
            dma((3, 4)),
            dma((3, 4)),
            pltpu.SemaphoreType.REGULAR,
            dma((6,)),
            dma((5, 9)),
            dma((5, 9)),
            dma((8,)),
            dma((8,)),
            dma((8,)),
            dma((2, 2, 2)),
        ],
        compiler_params=pltpu.CompilerParams(
            collective_id=1, has_side_effects=True, vmem_limit_bytes=63 * 10**6
        ),
        name="layer",
    )(first_row, gains_own, cosine, sine, x, cot, *owns)


def grad_kernel(
    first_row, cosine, sine, scale_ref, x_hbm, d_mid_hbm, pack_hbm, d_heads_hbm, w_qkv_hbm,
    d_ffn_t, hidden_hbm, ffn_in_t, d_gate_hbm, d_up_hbm, d_attn_t, heads_hbm, attn_in_t,
    in_grad_hbm, own_hbm, by_x_hbm, by_y_hbm, gain_ref, core_hbm, far_hbm,
    w_qkv, left, right, core_out, sums, arrived, own_sum,
    queries, keys, values, d_out, d_proj, d_keys, d_values, kv_out, kv_in,
    send, near, across, total, xb, mb_buf,
    line_send, line_recv, kv_sem, local, load_sem, rs_send, rs_recv, rs_local, own_sem,
):
    dp, core, z = lax.axis_index("dp"), lax.axis_index("ctx"), lax.axis_index("mp")
    width = xb.shape[1]
    rows_own = own_hbm.shape[1]
    half = rows_own // 2
    tokens = 2 * UNIT
    inner = (z == 1) | (z == 2)
    outer = (z == 0) | (z == 3)
    x_peer, y_peer = (dp ^ 1, core, z), (dp ^ 2, core, z)
    core_peer = (dp, 1 - core, z)
    near_peer = (dp, core, z ^ 1)
    far_peer = (dp, core, 3 - z)

    barrier = pltpu.get_barrier_semaphore()
    for peer in (x_peer, y_peer, core_peer, near_peer, far_peer):
        pl.semaphore_signal(barrier, inc=1, device_id=peer, device_id_type=MESH)

    def tile(n):
        return pl.ds(pl.multiple_of(n * TILE, TILE), TILE)

    def remote(src, dst, sems, index, peer):
        return pltpu.make_async_remote_copy(
            src_ref=src, dst_ref=dst, send_sem=sems[0].at[index], recv_sem=sems[1].at[index],
            device_id=peer, device_id_type=MESH,
        )

    jobs = (
        (d_ffn_t, hidden_hbm), (ffn_in_t, d_gate_hbm), (ffn_in_t, d_up_hbm),
        (d_attn_t, heads_hbm), (attn_in_t, None),
    )

    def columns(i):
        return (w_qkv.shape[1] if i == 4 else jobs[i][1].shape[1])

    def operands(i):
        pair = []
        if i != 2:
            pair.append(pltpu.make_async_copy(jobs[i][0], left, rs_local.at[0]))
        if i != 4:
            pair.append(pltpu.make_async_copy(jobs[i][1], right.at[:, : columns(i)], rs_local.at[1]))
        return pair

    def core_copy(i, m):
        n = columns(i)
        return remote(
            core_out.at[m % 2, :, :n], core_hbm.at[i, m, :, :n], (rs_send, rs_recv), (i, m), core_peer
        )

    def arrive(i, m):
        n = columns(i)
        return pltpu.make_async_copy(core_hbm.at[i, m, :, :n], arrived.at[m % 2, :, :n], rs_local.at[2 + m % 2])

    def far_copy(i, way):
        n = columns(i)
        rows = slice(0, half) if way == 0 else slice(half, rows_own)
        return remote(
            sums.at[i % 2, 2, rows, :n], far_hbm.at[i, rows, :n], (rs_send, rs_recv), (i, 4 + way),
            (x_peer, y_peer)[way],
        )

    def final_copy(i, way):
        n = columns(i)
        dst = (by_x_hbm, by_y_hbm)[way]
        return remote(
            sums.at[i % 2, way, :, :n], dst.at[i, :, :n], (rs_send, rs_recv), (i, 6 + way),
            (x_peer, y_peer)[way],
        )

    def own_store(i):
        n = columns(i)
        return pltpu.make_async_copy(own_sum.at[:, :n], own_hbm.at[i, :, :n], own_sem.at[0])

    def block_rows(mask, other):
        owner = (dp ^ mask) * 2 + ((1 - core) if other else core)
        return pl.ds(pl.multiple_of(owner * rows_own, 16), rows_own)

    def scatter_start(i):
        for copy in operands(i):
            copy.wait()
        source = d_proj if i == 4 else right
        steps = columns(i) // TILE

        for m in (3, 2, 1, 0):
            if m < 2:
                core_copy(i, m + 2).wait_send()
            elif i > 0:
                core_copy(i - 1, m - 2).wait_send()

            @pl.loop(0, steps)
            def _(n):
                core_out[m % 2, :, tile(n)] = dot(left[block_rows(m, True)], source[:, tile(n)]).astype(BF)

            core_copy(i, m).start()
        if i > 1:
            for way in (0, 1):
                far_copy(i - 2, way).wait_send()
                final_copy(i - 2, way).wait_send()
        if i > 0:
            own_store(i - 1).wait()
        core_copy(i, 3).wait_recv()
        arrive(i, 3).start()
        for m in (3, 2, 1, 0):
            if m:
                core_copy(i, m - 1).wait_recv()
                arrive(i, m - 1).start()
            arrive(i, m).wait()

            @pl.loop(0, steps)
            def _(n):
                part = dot(left[block_rows(m, False)], source[:, tile(n)])
                part = part + arrived[m % 2, :, tile(n)].astype(F32)
                if m:
                    sums[i % 2, m - 1, :, tile(n)] = part.astype(BF)
                else:
                    own_sum[:, tile(n)] = part

            if m == 3:
                far_copy(i, 0).start()
                far_copy(i, 1).start()
        own_store(i).start()
        if i + 1 < len(jobs):
            for copy in operands(i + 1):
                copy.start()

    def scatter_end(i):
        n = columns(i)
        for way in (0, 1):
            far_copy(i, way).wait_recv()
        copy = pltpu.make_async_copy(far_hbm.at[i, :, :n], arrived.at[0, :, :n], rs_local.at[4])
        copy.start()
        copy.wait()
        for way in (1, 0):
            base = 0 if way == 1 else half

            @pl.loop(0, half // 16)
            def _(r):
                rows = pl.ds(pl.multiple_of(base + r * 16, 16), 16)
                total_rows = sums[i % 2, way, rows, :n].astype(F32) + arrived[0, rows, :n].astype(F32)
                sums[i % 2, way, rows, :n] = total_rows.astype(BF)

            final_copy(i, way).start()

    def hop(kind, i):
        src = (send.at[i % 3], send.at[i % 3], total.at[i])[kind]
        dst = (near.at[i % 3], across.at[i], total.at[i])[kind]
        peer = far_peer if kind == 1 else near_peer
        return remote(src, dst, (line_send, line_recv), (kind, i), peer)

    def add_rows(dst, a, b):
        @pl.loop(0, UNIT // 16)
        def _(r):
            rows = pl.ds(pl.multiple_of(r * 16, 16), 16)
            dst[rows] = (a[rows].astype(F32) + b[rows].astype(F32)).astype(BF)

    def boundary(k):
        @pl.when(outer)
        def _():
            if 0 <= k - 3 < 4:
                hop(2, k - 3).wait_recv()
            if 0 <= k - 1 < 4:
                hop(0, k - 1).wait_send()
            if k < 4:
                hop(0, k).start()

        @pl.when(inner)
        def _():
            if 0 <= k - 1 < 4:
                i = k - 1
                hop(0, i).wait_recv()
                add_rows(send.at[i % 3], send.at[i % 3], near.at[i % 3])
                hop(1, i).start()
            if 0 <= k - 2 < 4:
                i = k - 2
                hop(1, i).wait_recv()
                hop(1, i).wait_send()
                add_rows(total.at[i], send.at[i % 3], across.at[i])
                hop(2, i).start()
            if 0 <= k - 3 < 4:
                hop(2, k - 3).wait_send()

    def attention_loads(mb):
        head_rows = [
            pltpu.make_async_copy(
                d_heads_hbm.at[pl.ds(mb * tokens, tokens), pl.ds(h * HEAD, HEAD)], d_out.at[h], load_sem.at[3 + h]
            )
            for h in range(2)
        ]

        def block(i, j, dst, rows, sem):
            src = pack_hbm.at[i, :, j * HEAD : (j + 1) * HEAD]
            return pltpu.make_async_copy(src, dst.at[pl.ds(rows * UNIT, UNIT)], load_sem.at[sem])

        return (
            head_rows
            + [block(0, mb * 4 + j, queries.at[j // 2], j % 2, 5 + j) for j in range(4)]
            + [block(1 + mb, j, keys, j, 9 + j) for j in range(4)]
            + [block(1 + mb, 4 + j, values, j, 13 + j) for j in range(4)]
        )

    def unrotate(v, rows):
        a, b = v[:, : HEAD // 2], v[:, HEAD // 2 :]
        c, s = cosine[rows], sine[rows]
        return jnp.concatenate([a * c + b * s, b * c - a * s], axis=1)

    def kv_copy(mb):
        return remote(kv_out, kv_in.at[mb], (kv_sem.at[0], kv_sem.at[1]), (mb,), core_peer)

    def attention_back(mb):
        for copy in attention_loads(mb):
            copy.wait()
        d_keys[...] = jnp.zeros_like(d_keys)
        d_values[...] = jnp.zeros_like(d_values)
        length = keys.shape[0]
        for h in range(2):

            @pl.loop(0, tokens // UNIT)
            def _(b):
                rows = pl.ds(pl.multiple_of(b * UNIT, UNIT), UNIT)
                query, grad = queries[h, rows], d_out[h, rows]
                first = core * tokens + b * UNIT
                key_at = lax.broadcasted_iota(jnp.int32, (length, UNIT), 0)
                query_at = lax.broadcasted_iota(jnp.int32, (length, UNIT), 1) + first
                lowest = first_row[mb, :, rows]
                tanh = jnp.tanh(dot_t(keys[...], query) * (SCALE / CAP))
                weight = jnp.where((key_at <= query_at) & (key_at >= lowest), jnp.exp(CAP * tanh), 0.0)
                probs = weight * (1.0 / jnp.sum(weight, axis=0, keepdims=True))
                d_probs = dot_t(values[...], grad)
                mean = jnp.sum(probs * d_probs, axis=0, keepdims=True)
                d_raw = (probs * (d_probs - mean) * (1.0 - tanh * tanh)).astype(BF)
                d_values[...] += dot(probs.astype(BF), grad)
                d_keys[...] += dot(d_raw, query)
                d_query = t_dot(d_raw, keys[...]) * SCALE
                place = pl.ds(pl.multiple_of(mb * tokens + b * UNIT, UNIT), UNIT)
                d_proj[place, h * HEAD : (h + 1) * HEAD] = unrotate(d_query, place).astype(BF)

        theirs = pl.ds(pl.multiple_of((1 - core) * tokens, UNIT), tokens)
        mine = pl.ds(pl.multiple_of(core * tokens, UNIT), tokens)
        if mb:
            kv_copy(mb - 1).wait_send()
        kv_out[:, :HEAD] = (d_keys[theirs] * SCALE).astype(BF)
        kv_out[:, HEAD:] = d_values[theirs].astype(BF)
        kv_copy(mb).start()
        kv_copy(mb).wait_recv()
        place = pl.ds(mb * tokens, tokens)
        d_key = d_keys[mine] * SCALE + kv_in[mb, :, :HEAD].astype(F32)
        d_value = d_values[mine] + kv_in[mb, :, HEAD:].astype(F32)
        d_proj[place, 2 * HEAD : 3 * HEAD] = unrotate(d_key, place).astype(BF)
        d_proj[place, 3 * HEAD :] = d_value.astype(BF)

    def project(u):
        @pl.loop(0, width // TILE)
        def _(n):
            send[u % 3, :, tile(n)] = dot_t(d_proj[u * UNIT : (u + 1) * UNIT], w_qkv[tile(n)]).astype(BF)

    def last_loads(u):
        rows = pl.ds(u * UNIT, UNIT)
        return (
            pltpu.make_async_copy(x_hbm.at[rows], xb, local.at[0]),
            pltpu.make_async_copy(d_mid_hbm.at[rows], mb_buf, local.at[1]),
        )

    def last(u):
        for copy in last_loads(u):
            copy.wait()

        @pl.loop(0, UNIT // 16)
        def _(r):
            rows = pl.ds(pl.multiple_of(r * 16, 16), 16)
            x = xb[rows].astype(F32)
            r_one = inverse_rms(x)
            dy = total[u, rows].astype(F32)
            scaled = scale_ref[0:1] * dy
            mean = jnp.mean(scaled * x, axis=-1, keepdims=True)
            back = r_one * scaled - x * (r_one * r_one * r_one) * mean
            mb_buf[rows] = (mb_buf[rows].astype(F32) + back).astype(BF)
            part = x * r_one * dy
            gain_ref[...] += part[:8] + part[8:]

        store = pltpu.make_async_copy(mb_buf, in_grad_hbm.at[pl.ds(u * UNIT, UNIT)], local.at[2])
        store.start()
        store.wait()
        if u < 3:
            for copy in last_loads(u + 1):
                copy.start()

    qkv_copy = pltpu.make_async_copy(w_qkv_hbm, w_qkv, local.at[2])
    for copy in (*attention_loads(0), qkv_copy, *operands(0), *last_loads(0)):
        copy.start()
    gain_ref[...] = jnp.zeros_like(gain_ref)
    pl.semaphore_wait(barrier, 5)
    attention_back(0)
    for copy in attention_loads(1):
        copy.start()
    qkv_copy.wait()
    project(0)
    boundary(0)
    scatter_start(0)
    project(1)
    boundary(1)
    attention_back(1)
    scatter_end(0)
    project(2)
    boundary(2)
    project(3)
    scatter_start(1)
    boundary(3)
    scatter_end(1)
    last(0)
    scatter_start(2)
    boundary(4)
    last(1)
    scatter_end(2)
    scatter_start(4 - 1)
    boundary(5)
    last(2)
    scatter_end(3)
    scatter_start(4)
    boundary(6)
    last(3)
    scatter_end(4)
    kv_copy(1).wait_send()
    own_store(4).wait()
    for m in range(2):
        core_copy(4, m).wait_send()
    for i in range(5):
        for way in (0, 1):
            if i > 2:
                far_copy(i, way).wait_send()
                final_copy(i, way).wait_send()
            final_copy(i, way).wait_recv()


def grad_call(first_row, cosine, sine, scales, arrays):
    x, w_qkv = arrays[0], arrays[4]
    tokens, width = x.shape
    rows = width // 8
    wide = arrays[6].shape[1]
    full = jax.ShapeDtypeStruct((tokens, width), BF)
    part = jax.ShapeDtypeStruct((5, rows, wide), BF)
    outs = (
        full,
        jax.ShapeDtypeStruct((5, rows, wide), F32),
        part,
        part,
        jax.ShapeDtypeStruct((8, width), F32),
        jax.ShapeDtypeStruct((5, 4, rows, wide), BF),
        part,
    )
    anywhere, vmem = pl.BlockSpec(memory_space=pl.ANY), pl.BlockSpec(memory_space=pltpu.VMEM)
    dma = pltpu.SemaphoreType.DMA
    half, length = tokens // 2, tokens
    return pl.pallas_call(
        grad_kernel,
        out_shape=outs,
        in_specs=[vmem] * 4 + [anywhere] * 13,
        out_specs=[anywhere] * 4 + [vmem] + [anywhere] * 2,
        scratch_shapes=[
            pltpu.VMEM(w_qkv.shape, BF),
            pltpu.VMEM((width, tokens), BF),
            pltpu.VMEM((tokens, wide), BF),
            pltpu.VMEM((2, rows, wide), BF),
            pltpu.VMEM((2, 3, rows, wide), BF),
            pltpu.VMEM((2, rows, wide), BF),
            pltpu.VMEM((rows, wide), F32),
            pltpu.VMEM((2, half, HEAD), BF),
            pltpu.VMEM((length, HEAD), BF),
            pltpu.VMEM((length, HEAD), BF),
            pltpu.VMEM((2, half, HEAD), BF),
            pltpu.VMEM((tokens, 4 * HEAD), BF),
            pltpu.VMEM((length, HEAD), F32),
            pltpu.VMEM((length, HEAD), F32),
            pltpu.VMEM((half, 2 * HEAD), BF),
            pltpu.VMEM((2, half, 2 * HEAD), BF),
            pltpu.VMEM((3, UNIT, width), BF),
            pltpu.VMEM((3, UNIT, width), BF),
            pltpu.VMEM((4, UNIT, width), BF),
            pltpu.VMEM((4, UNIT, width), BF),
            pltpu.VMEM((UNIT, width), BF),
            pltpu.VMEM((UNIT, width), BF),
            dma((3, 4)),
            dma((3, 4)),
            dma((2, 2)),
            dma((3,)),
            dma((17,)),
            dma((5, 8)),
            dma((5, 8)),
            dma((5,)),
            dma((1,)),
        ],
        compiler_params=pltpu.CompilerParams(
            collective_id=2, has_side_effects=True, vmem_limit_bytes=63 * 10**6
        ),
        name="grads",
    )(first_row, cosine, sine, scales, *arrays)


def fast_device(
    sizes,
    inputs,
    segment_ids,
    positions,
    cotangent,
    *params,
):
    masters, moments = params[:11], params[11:]
    batches, seqs, tokens, width = inputs.shape
    assert seqs == 1
    q_cols, k_cols = masters[0].shape[1], masters[1].shape[1]
    width_ff = masters[4].shape[1]
    assert k_cols == HEAD

    own = masters[7].shape[0]
    place = (lax.axis_index("dp") * sizes["ctx"] + lax.axis_index("ctx")) * own
    low = [w.astype(BF) for w in masters[:7]]
    owns = (jnp.concatenate(low[:3], axis=1), *low[3:])
    gains_own = jnp.zeros((16, width), BF)
    gains_own = lax.dynamic_update_slice(gains_own, jnp.stack(masters[7:]).astype(BF), (0, place))
    start = lax.axis_index("ctx") * tokens
    frequency = jnp.exp(
        jnp.arange(HEAD // 2, dtype=F32) * (-2.0 * math.log(10000.0) / HEAD)
    )
    angle = positions.reshape(-1).astype(F32)[:, None] * frequency
    cosine, sine = jnp.cos(angle), jnp.sin(angle)
    first_row = (start + jnp.arange(tokens, dtype=jnp.int32))[None, None] - positions
    flat = (batches * tokens, width)
    x = inputs.reshape(flat)
    outs = layer_call(first_row, gains_own, cosine, sine, x, cotangent.reshape(flat), owns)
    (
        output, ffn_in_t, hidden, d_ffn_t, d_gate, d_up, d_attn_t, d_heads, d_mid, gain_parts, scales,
        attn_in_t, heads_out, pack, w_qkv,
    ) = outs[:15]
    outs = grad_call(
        first_row, cosine, sine, scales,
        (
            x, d_mid, pack, d_heads, w_qkv, d_ffn_t, hidden, ffn_in_t, d_gate, d_up, d_attn_t, heads_out,
            attn_in_t,
        ),
    )
    input_grad, own_sum, by_x, by_y, gain_part = outs[:5]

    def final_sum(i, cols):
        picked = [v[i, :, :cols].astype(F32) for v in (own_sum, by_x, by_y)]
        return picked[0] + picked[1] + picked[2]

    qkv_cols = w_qkv.shape[1]
    s_down, s_gate, s_up = [final_sum(i, width_ff) for i in range(3)]
    s_out, s_qkv = final_sum(3, q_cols), final_sum(4, qkv_cols)
    gain_grads = jnp.concatenate([jnp.sum(gain_part, axis=0)[None], jnp.sum(gain_parts, axis=1)])
    gain_grads = sum_small(gain_grads, ("ctx", "dp"), sizes)
    summed = (
        s_qkv[:, :q_cols], s_qkv[:, q_cols : q_cols + k_cols], s_qkv[:, q_cols + k_cols :],
        s_out, s_gate, s_up, s_down,
    )
    weight_sq = sum(jnp.sum(g * g) for g in (s_qkv, s_out, s_gate, s_up, s_down))
    weight_sq = sum_small(weight_sq.reshape(1, 1), ("ctx", "dp", "mp"), sizes)[0, 0]
    norm_value = jnp.sqrt(weight_sq + jnp.sum(gain_grads * gain_grads))
    factor = 1.0 / jnp.maximum(norm_value, 1.0)
    own_gains = lax.dynamic_slice_in_dim(gain_grads, place, own, 1)
    summed += tuple(own_gains[i] for i in range(4))
    new_moments = tuple(0.5 * m + 0.5 * factor * g for m, g in zip(moments, summed))
    changes = tuple(-RATE * (m + 0.01 * w) for w, m in zip(masters[:7], new_moments[:7]))

    return (
        output.reshape(inputs.shape),
        input_grad.reshape(inputs.shape), norm_value.reshape(1), *changes, *new_moments
    )


def per_device(
    sizes,
    inputs,
    segment_ids,
    positions,
    cotangent,
    *params,
):
    masters, moments = params[:11], params[11:]
    batches, seqs, tokens, width = inputs.shape
    assert seqs == 1
    full_len = segment_ids.shape[2]
    q_cols, k_cols = masters[0].shape[1], masters[1].shape[1]
    heads = q_cols // HEAD
    assert k_cols == HEAD
    cuts = 2 if tokens >= 512 else 1
    unit = tokens // cuts

    low = [w.astype(BF) for w in masters[:7]]
    qkv_own = jnp.concatenate(low[:3], axis=1)
    gains_own = jnp.stack([g.astype(BF) for g in masters[7:]], axis=1)
    gains = lax.all_gather(gains_own, ("dp", "ctx"), axis=0, tiled=True).astype(F32)
    gain_one, gain_two, gain_three, gain_four = [gains[:, i] for i in range(4)]
    w_qkv, mark = gather_rows(qkv_own, sizes, None)
    w_out, mark = gather_rows(low[3], sizes, mark)
    w_gate, mark = gather_rows(low[4], sizes, mark)
    w_up, mark = gather_rows(low[5], sizes, mark)
    w_down, mark = gather_rows(low[6], sizes, mark)

    start = lax.axis_index("ctx") * tokens
    causal = (start + jnp.arange(tokens))[:, None] >= jnp.arange(full_len)[None, :]
    frequency = jnp.exp(
        jnp.arange(HEAD // 2, dtype=F32) * (-2.0 * math.log(10000.0) / HEAD)
    )

    state = []
    for mb in range(batches):
        x = inputs[mb, 0].astype(F32)
        r_one = inverse_rms(x)
        attn_in = (x * r_one * (1.0 + gain_one)).astype(BF)
        angles = positions[mb, 0].astype(F32)[:, None] * frequency
        cosine, sine = jnp.cos(angles), jnp.sin(angles)
        seg = segment_ids[mb, 0]
        seg_local = lax.dynamic_slice_in_dim(seg, start, tokens)
        allowed = causal & (seg_local[:, None] == seg[None, :])
        proj = dot(attn_in, w_qkv)
        queries = jnp.concatenate(
            [rotate(proj[:, h * HEAD : (h + 1) * HEAD], cosine, sine) for h in range(heads)]
        ).astype(BF)
        keys = rotate(proj[:, q_cols : q_cols + HEAD], cosine, sine).astype(BF)
        values = proj[:, q_cols + HEAD :].astype(BF)
        both = swap_ctx(jnp.concatenate([keys, values], axis=1), sizes)
        keys_all, values_all = both[:, :HEAD], both[:, HEAD:]
        out, saved = attend(queries, keys_all, values_all, allowed)
        heads_out = jnp.concatenate(jnp.split(out, heads, axis=0), axis=1)
        state.append(
            dict(
                x=x, r_one=r_one, attn_in=attn_in, cosine=cosine, sine=sine, queries=queries,
                keys=keys_all, values=values_all, saved=saved, heads_out=heads_out,
            )
        )

    units = [(mb, cut) for mb in range(batches) for cut in range(cuts)]
    work = []
    for mb, cut in units:
        rows = slice(cut * unit, (cut + 1) * unit)
        part = dot_t(state[mb]["heads_out"][rows], w_out).astype(BF)
        work.append(dict(rows=rows, mb=mb, attn_low=sum_mp(part, sizes)))
    for w in work:
        attn = w["attn_low"].astype(F32)
        r_two = inverse_rms(attn)
        mid = state[w["mb"]]["x"][w["rows"]] + attn * r_two * (1.0 + gain_two)
        r_three = inverse_rms(mid)
        ffn_in = (mid * r_three * (1.0 + gain_three)).astype(BF)
        gate, up = dot(ffn_in, w_gate), dot(ffn_in, w_up)
        value, slope = gelu_parts(gate)
        hidden = (value * up).astype(BF)
        part = dot_t(hidden, w_down).astype(BF)
        w.update(
            mid=mid, r_two=r_two, r_three=r_three, ffn_in=ffn_in, gate=gate, up=up, hidden=hidden,
            ffn_low=sum_mp(part, sizes),
        )
    for w in work:
        ffn = w["ffn_low"].astype(F32)
        r_four = inverse_rms(ffn)
        grad = cotangent[w["mb"], 0][w["rows"]].astype(F32)
        w["output"] = (w["mid"] + ffn * r_four * (1.0 + gain_four)).astype(BF)
        d_ffn, w["g_four"] = norm_back(ffn, r_four, gain_four, grad)
        d_ffn = d_ffn.astype(BF)
        d_hidden = dot(d_ffn, w_down)
        value, slope = gelu_parts(w["gate"])
        d_gate = (d_hidden * w["up"] * slope).astype(BF)
        d_up = (d_hidden * value).astype(BF)
        part = (dot_t(d_gate, w_gate) + dot_t(d_up, w_up)).astype(BF)
        w.update(grad=grad, d_ffn=d_ffn, d_gate=d_gate, d_up=d_up, d_in_low=sum_mp(part, sizes))
    for w in work:
        d_in = w["d_in_low"].astype(F32)
        back, w["g_three"] = norm_back(w["mid"], w["r_three"], gain_three, d_in)
        d_mid = w["grad"] + back
        attn = w["attn_low"].astype(F32)
        d_attn, w["g_two"] = norm_back(attn, w["r_two"], gain_two, d_mid)
        d_attn = d_attn.astype(BF)
        w.update(d_mid=d_mid, d_attn=d_attn, d_heads=dot(d_attn, w_out).astype(BF))

    def rows_of(key):
        return jnp.concatenate([w[key] for w in work])

    ffn_in = rows_of("ffn_in")
    g_down = t_dot(rows_of("d_ffn"), rows_of("hidden"))
    g_gate = t_dot(ffn_in, rows_of("d_gate"))
    g_up = t_dot(ffn_in, rows_of("d_up"))
    s_down, mark = scatter_rows(g_down, sizes, None)
    s_gate, mark = scatter_rows(g_gate, sizes, mark)
    s_up, mark = scatter_rows(g_up, sizes, mark)

    for mb in range(batches):
        s = state[mb]
        d_heads = jnp.concatenate([w["d_heads"] for w in work if w["mb"] == mb])
        d_out = jnp.concatenate(jnp.split(d_heads, heads, axis=1))
        d_queries, d_keys, d_values = attend_back(
            s["saved"], s["queries"], s["keys"], s["values"], d_out
        )
        d_kv = scatter_ctx(jnp.concatenate([d_keys, d_values], axis=1), sizes)
        pieces = [rotate(q, s["cosine"], -s["sine"]) for q in jnp.split(d_queries, heads)]
        pieces += [rotate(d_kv[:, :HEAD], s["cosine"], -s["sine"]), d_kv[:, HEAD:]]
        s["d_proj"] = jnp.concatenate(pieces, axis=1).astype(BF)
    for w in work:
        part = dot_t(state[w["mb"]]["d_proj"][w["rows"]], w_qkv).astype(BF)
        w["d_attn_in"] = sum_mp(part, sizes)

    g_out = t_dot(rows_of("d_attn"), jnp.concatenate([s["heads_out"] for s in state]))
    g_qkv = t_dot(
        jnp.concatenate([s["attn_in"] for s in state]),
        jnp.concatenate([s["d_proj"] for s in state]),
    )
    s_out, mark = scatter_rows(g_out, sizes, mark)
    s_qkv, mark = scatter_rows(g_qkv, sizes, mark)

    for w in work:
        s = state[w["mb"]]
        back, w["g_one"] = norm_back(
            s["x"][w["rows"]], s["r_one"][w["rows"]], gain_one, w["d_attn_in"].astype(F32)
        )
        w["input_grad"] = (w["d_mid"] + back).astype(BF)

    gain_grads = jnp.stack(
        [sum(w[key] for w in work) for key in ("g_one", "g_two", "g_three", "g_four")]
    )
    gain_grads = sum_small(gain_grads, ("ctx", "dp"), sizes)
    summed = (
        s_qkv[:, :q_cols], s_qkv[:, q_cols : q_cols + k_cols], s_qkv[:, q_cols + k_cols :],
        s_out, s_gate, s_up, s_down,
    )
    weight_sq = sum(jnp.sum(g * g) for g in (s_qkv, s_out, s_gate, s_up, s_down))
    weight_sq = sum_small(weight_sq.reshape(1, 1), ("ctx", "dp", "mp"), sizes)[0, 0]
    norm_value = jnp.sqrt(weight_sq + jnp.sum(gain_grads * gain_grads))
    factor = 1.0 / jnp.maximum(norm_value, 1.0)
    own = masters[7].shape[0]
    place = (lax.axis_index("dp") * sizes["ctx"] + lax.axis_index("ctx")) * own
    own_gains = lax.dynamic_slice_in_dim(gain_grads, place, own, 1)
    summed += tuple(own_gains[i] for i in range(4))
    new_moments = tuple(0.5 * m + 0.5 * factor * g for m, g in zip(moments, summed))
    changes = tuple(-RATE * (m + 0.01 * w) for w, m in zip(masters[:7], new_moments[:7]))

    def whole(key):
        return rows_of(key).reshape(inputs.shape)

    return (
        whole("output"), whole("input_grad"), norm_value.reshape(1), *changes, *new_moments
    )


def solution(mesh):
    sizes = dict(mesh.shape)
    weight, vector = P(("dp", "ctx"), "mp"), P(("dp", "ctx"))
    params = (weight,) * 7 + (vector,) * 4
    data = P(None, "dp", "ctx", None)

    def run(*args):
        batches, _, tokens, _ = args[0].shape
        fast = sizes == dict(dp=4, ctx=2, mp=4) and batches == 2 and tokens == 2 * UNIT
        return (fast_device if fast else per_device)(sizes, *args)

    return jax.shard_map(
        run,
        mesh=mesh,
        in_specs=(data, P(None, "dp", None), P(None, "dp", "ctx"), data) + params + params,
        out_specs=(data, data, P()) + (weight,) * 7 + params,
        check_vma=False,
    )
```

```python
import math

import jax
import jax.numpy as jnp
from jax import lax
from jax.experimental import pallas as pl
from jax.experimental.pallas import tpu as pltpu
from jax.sharding import PartitionSpec as P

HEAD = 256
STEP = 10
EPS = 1e-06
CAP = 50.0
RATE = 1.0 / math.sqrt(1.0 + STEP / 1000.0)
SCALE = HEAD ** (-0.5)
BF = jnp.bfloat16
F32 = jnp.float32


def flip(axis, size, mask):
    return dict(axis_name=axis, perm=[(i, i ^ mask) for i in range(size)])


def after(value, other):
    return lax.optimization_barrier((value, other))[0]


def gather_rows(own, sizes, wait):
    dp, ctx = sizes["dp"], sizes["ctx"]
    rows, cols = own.shape
    if wait is not None:
        own = after(own, wait)
    if dp != 4:
        out = lax.all_gather(own, ("dp", "ctx"), axis=0, tiled=True)
        return out, own
    me = lax.axis_index("dp")
    half = rows // 2 // 16 * 16
    from_x = lax.ppermute(own, **flip("dp", dp, 1))
    from_y = lax.ppermute(own, **flip("dp", dp, 2))
    far_top = lax.ppermute(from_y[:half], **flip("dp", dp, 1))
    far_low = lax.ppermute(from_x[half:], **flip("dp", dp, 2))
    mine = jnp.zeros((dp, rows, cols), own.dtype)
    mine = lax.dynamic_update_slice(mine, own[None], (me, 0, 0))
    mine = lax.dynamic_update_slice(mine, from_x[None], (me ^ 1, 0, 0))
    mine = lax.dynamic_update_slice(mine, from_y[None], (me ^ 2, 0, 0))
    mine = lax.dynamic_update_slice(mine, far_top[None], (me ^ 3, 0, 0))
    mine = lax.dynamic_update_slice(mine, far_low[None], (me ^ 3, half, 0))
    if ctx == 2:
        other = lax.ppermute(mine, **flip("ctx", ctx, 1))
        core = lax.axis_index("ctx")
        out = jnp.zeros((dp, ctx, rows, cols), own.dtype)
        out = lax.dynamic_update_slice(out, mine[:, None], (0, core, 0, 0))
        out = lax.dynamic_update_slice(out, other[:, None], (0, 1 - core, 0, 0))
    else:
        out = lax.all_gather(mine, "ctx", axis=1)
    return out.reshape(dp * ctx * rows, cols), from_x


def scatter_rows(full, sizes, wait):
    dp, ctx = sizes["dp"], sizes["ctx"]
    full = full.astype(BF)
    if wait is not None:
        full = after(full, wait)
    rows = full.shape[0] // (dp * ctx)
    cols = full.shape[1]
    if dp != 4:
        out = lax.psum_scatter(full, ("dp", "ctx"), scatter_dimension=0, tiled=True)
        return out.astype(F32), out
    blocks = full.reshape(dp, ctx, rows, cols)
    if ctx == 2:
        core = lax.axis_index("ctx")
        send = lax.dynamic_index_in_dim(blocks, 1 - core, 1, keepdims=False)
        keep = lax.dynamic_index_in_dim(blocks, core, 1, keepdims=False)
        got = lax.ppermute(send, **flip("ctx", ctx, 1))
    else:
        keep = lax.psum_scatter(blocks, "ctx", scatter_dimension=1, tiled=False)
        got = None
    me = lax.axis_index("dp")
    half = rows // 2 // 16 * 16

    def part(mask, low, high):
        size = (1, high - low, cols)
        piece = lax.dynamic_slice(keep, (me ^ mask, low, 0), size)[0].astype(F32)
        if got is not None:
            piece = piece + lax.dynamic_slice(got, (me ^ mask, low, 0), size)[0].astype(F32)
        return piece

    far_top = lax.ppermute(part(3, 0, half).astype(BF), **flip("dp", dp, 1))
    far_low = lax.ppermute(part(3, half, rows).astype(BF), **flip("dp", dp, 2))
    to_y = jnp.concatenate([part(2, 0, half) + far_top.astype(F32), part(2, half, rows)])
    to_x = jnp.concatenate([part(1, 0, half), part(1, half, rows) + far_low.astype(F32)])
    by_y = lax.ppermute(to_y.astype(BF), **flip("dp", dp, 2))
    by_x = lax.ppermute(to_x.astype(BF), **flip("dp", dp, 1))
    total = part(0, 0, rows) + by_x.astype(F32) + by_y.astype(F32)
    return total, far_top


def sum_mp(part, sizes):
    if sizes["mp"] != 4:
        return lax.psum(part, "mp")
    place = lax.axis_index("mp")
    inner = (place == 1) | (place == 2)
    near = lax.ppermute(part, "mp", [(0, 1), (3, 2)])
    pair = (part.astype(F32) + near.astype(F32)).astype(BF)
    across = lax.ppermute(pair, "mp", [(1, 2), (2, 1)])
    total = (pair.astype(F32) + across.astype(F32)).astype(BF)
    back = lax.ppermute(total, "mp", [(1, 0), (2, 3)])
    return jnp.where(inner, total, back)


def sum_small(value, axes, sizes):
    for axis in axes:
        size = sizes[axis]
        step = 1
        while step < size:
            value = value + lax.ppermute(value, **flip(axis, size, step))
            step *= 2
    return value


def swap_ctx(local, sizes):
    if sizes["ctx"] != 2:
        return lax.all_gather(local, "ctx", axis=0, tiled=True)
    other = lax.ppermute(local, **flip("ctx", 2, 1))
    first = lax.axis_index("ctx") == 0
    return jnp.concatenate([jnp.where(first, local, other), jnp.where(first, other, local)])


def scatter_ctx(full, sizes):
    if sizes["ctx"] != 2:
        return lax.psum_scatter(full.astype(BF), "ctx", scatter_dimension=0, tiled=True).astype(F32)
    core = lax.axis_index("ctx")
    rows = full.shape[0] // 2
    send = lax.dynamic_slice_in_dim(full, (1 - core) * rows, rows).astype(BF)
    keep = lax.dynamic_slice_in_dim(full, core * rows, rows)
    return keep.astype(BF).astype(F32) + lax.ppermute(send, **flip("ctx", 2, 1)).astype(F32)


def dot(a, b):
    return lax.dot_general(a, b, (((1,), (0,)), ((), ())), preferred_element_type=F32)


def dot_t(a, b):
    return lax.dot_general(a, b, (((1,), (1,)), ((), ())), preferred_element_type=F32)


def t_dot(a, b):
    return lax.dot_general(a, b, (((0,), (0,)), ((), ())), preferred_element_type=F32)


def inverse_rms(v):
    return lax.rsqrt(jnp.mean(v * v, axis=-1, keepdims=True) + EPS)


def norm_back(v, r, gain, dy):
    scaled = (1.0 + gain) * dy
    mean = jnp.mean(scaled * v, axis=-1, keepdims=True)
    return r * scaled - v * (r * r * r) * mean, jnp.sum(v * r * dy, axis=0)


def rotate(v, cosine, sine):
    a, b = v[:, : HEAD // 2], v[:, HEAD // 2 :]
    return jnp.concatenate([a * cosine - b * sine, b * cosine + a * sine], axis=1)


GELU_C = math.sqrt(2.0 / math.pi)


def gelu_parts(u):
    tanh = jnp.tanh(GELU_C * (u + 0.044715 * u * u * u))
    value = 0.5 * u * (1.0 + tanh)
    slope = 0.5 * (1.0 + tanh) + 0.5 * u * (1.0 - tanh * tanh) * GELU_C * (
        1.0 + 3.0 * 0.044715 * u * u
    )
    return value, slope


def attend(queries, keys, values, allowed):
    raw = dot_t(queries, keys) * SCALE
    tanh = jnp.tanh(raw / CAP)
    heads = queries.shape[0] // allowed.shape[0]
    mask = jnp.concatenate([allowed] * heads, axis=0)
    weight = jnp.where(mask, jnp.exp(CAP * tanh), 0.0)
    probs = weight / jnp.sum(weight, axis=1, keepdims=True)
    out = dot(probs.astype(BF), values).astype(BF)
    return out, (probs, tanh)


def attend_back(saved, queries, keys, values, d_out):
    probs, tanh = saved
    d_probs = dot_t(d_out, values)
    inner = jnp.sum(probs * d_probs, axis=1, keepdims=True)
    d_raw = (probs * (d_probs - inner) * (1.0 - tanh * tanh)).astype(BF)
    d_queries = dot(d_raw, keys) * SCALE
    d_keys = t_dot(d_raw, queries) * SCALE
    d_values = t_dot(probs.astype(BF), d_out)
    return d_queries, d_keys, d_values


MESH = pl.DeviceIdType.MESH
UNIT = 256
TILE = 256


def layer_kernel(
    first_row, gains_own, cos_hbm, sin_hbm, x_hbm, cot_hbm, own_qkv, own_out, own_gate, own_up, own_down,
    out_hbm, ffn_in_hbm, hidden_hbm, d_ffn_hbm, d_gate_hbm, d_up_hbm, d_attn_hbm, d_heads_hbm,
    d_mid_hbm, gain_ref, scale_ref, attn_in_hbm, heads_hbm, pack_hbm, w_qkv_hbm, w_out_hbm,
    attn_hbm, slope_hbm, value_hbm,
    in_grad_hbm, own_hbm, by_x_hbm, by_y_hbm, core_hbm, far_hbm, kv_hbm, d_proj_hbm,
    weights, w_qkv, send, near, across, total, xb, cb, ab, act, act_t, stage, d_heads, angle,
    line_send, line_recv, credit, local, ag_send, ag_recv, ag_local, gain_send, gain_recv, kv_sem,
    load_sem, rs_send, rs_recv, rs_local, kv_back, proj_sem,
):
    dp, core, z = lax.axis_index("dp"), lax.axis_index("ctx"), lax.axis_index("mp")
    w_out = w_qkv.at[:, : w_out_hbm.shape[1]]
    width, units = xb.shape[1], weights.shape[2]
    rows_own = own_qkv.shape[0]
    half = rows_own // 2
    inner = (z == 1) | (z == 2)
    outer = (z == 0) | (z == 3)
    x_peer, y_peer = (dp ^ 1, core, z), (dp ^ 2, core, z)
    core_peer = (dp, 1 - core, z)
    near_peer = (dp, core, z ^ 1)
    far_peer = (dp, core, 3 - z)

    barrier = pltpu.get_barrier_semaphore()
    group = [(dp ^ (m // 2), (1 - core) if m % 2 else core, z) for m in range(1, 8)]
    for peer in (*group, near_peer, far_peer):
        pl.semaphore_signal(barrier, inc=1, device_id=peer, device_id_type=MESH)

    def block(mask, other=False, low=0, size=rows_own):
        owner = (dp ^ mask) * 2 + ((1 - core) if other else core)
        return pl.ds(pl.multiple_of(owner * rows_own + low, 16), size)

    owns = (own_qkv, own_out, own_gate, own_up, own_down)
    wholes = (w_qkv, w_out_hbm, weights.at[0], weights.at[1], weights.at[2])

    def gather(w, name, recv=False):
        table = {
            "x": (0, block(0), x_peer, block(1)),
            "y": (1, block(0), y_peer, block(2)),
            "top": (2, block(2, False, 0, half), x_peer, block(3, False, 0, half)),
            "low": (3, block(1, False, half, half), y_peer, block(3, False, half, half)),
            "own_c": (4, block(0), core_peer, block(0, True)),
            "x_c": (5, block(1), core_peer, block(1, True)),
            "y_c": (6, block(2), core_peer, block(2, True)),
            "top_c": (7, block(3, False, 0, half), core_peer, block(3, True, 0, half)),
            "low_c": (8, block(3, False, half, half), core_peer, block(3, True, half, half)),
        }
        index, out_rows, peer, in_rows = table[name]
        rows = in_rows if recv else out_rows
        src = owns[w] if name in ("x", "y", "own_c") else wholes[w].at[rows]
        return pltpu.make_async_remote_copy(
            src_ref=src, dst_ref=wholes[w].at[rows], send_sem=ag_send.at[w, index],
            recv_sem=ag_recv.at[w, index], device_id=peer, device_id_type=MESH,
        )

    def own_copy(w):
        return pltpu.make_async_copy(owns[w], wholes[w].at[block(0)], ag_local.at[w])

    def gather_first(w):
        for name in ("x", "y", "own_c"):
            gather(w, name).start()
        own_copy(w).start()

    def gather_second(w):
        gather(w, "x", True).wait_recv()
        gather(w, "low").start()
        gather(w, "x_c").start()
        gather(w, "y", True).wait_recv()
        gather(w, "top").start()
        gather(w, "y_c").start()

    def gather_third(w):
        for name in ("top", "low"):
            gather(w, name, True).wait_recv()
            gather(w, name + "_c").start()

    def gather_end(w):
        for name in ("own_c", "x_c", "y_c", "top_c", "low_c"):
            gather(w, name, True).wait_recv()
        own_copy(w).wait()
        for name in ("x", "y", "top", "low", "own_c", "x_c", "y_c", "top_c", "low_c"):
            gather(w, name).wait_send()

    def hop(kind, i):
        src = (send.at[i % 3], send.at[i % 3], total.at[i % 4])[kind]
        dst = (near.at[i % 3], across.at[i % 2], total.at[i % 4])[kind]
        return pltpu.make_async_remote_copy(
            src_ref=src, dst_ref=dst, send_sem=line_send.at[kind, i % 4],
            recv_sem=line_recv.at[kind, i % 4],
            device_id=far_peer if kind == 1 else near_peer, device_id_type=MESH,
        )

    def add_rows(dst, a, b):
        @pl.loop(0, UNIT // 16)
        def _(r):
            rows = pl.ds(pl.multiple_of(r * 16, 16), 16)
            dst[rows] = (a[rows].astype(F32) + b[rows].astype(F32)).astype(BF)

    def boundary(up=None, cross=None, back=None, done=None):
        @pl.when(outer)
        def _():
            if done is not None:
                hop(2, done).wait_recv()
            if cross is not None:
                hop(0, cross).wait_send()
            if up is not None:
                hop(0, up).start()

        @pl.when(inner)
        def _():
            if cross is not None:
                hop(0, cross).wait_recv()
                add_rows(send.at[cross % 3], send.at[cross % 3], near.at[cross % 3])
                if not isinstance(cross, int) or cross >= 2:
                    pl.semaphore_wait(credit, 1)
                hop(1, cross).start()
            if back is not None:
                hop(1, back).wait_recv()
                hop(1, back).wait_send()
                add_rows(total.at[back % 4], send.at[back % 3], across.at[back % 2])
                if not isinstance(back, int) or back < 14:
                    pl.semaphore_signal(credit, inc=1, device_id=far_peer, device_id_type=MESH)
                hop(2, back).start()
            if done is not None:
                hop(2, done).wait_send()

    def rows_of(u):
        return pl.ds(pl.multiple_of(u * UNIT, UNIT), UNIT)

    def load(ref, u, dst, sem):
        return pltpu.make_async_copy(ref.at[rows_of(u)], dst, local.at[sem])

    def store(src, ref, u, sem):
        return pltpu.make_async_copy(src, ref.at[rows_of(u)], local.at[sem])

    def store_t(ref, u, sem):
        return pltpu.make_async_copy(act_t, ref.at[:, rows_of(u)], local.at[sem])

    def turn(source=None):
        source = act if source is None else source

        @pl.loop(0, width // TILE)
        def _(n):
            act_t[tile(n)] = source[:, tile(n)].T

    def tile(n):
        return pl.ds(pl.multiple_of(n * TILE, TILE), TILE)

    def each_rows(body):
        @pl.loop(0, UNIT // 16)
        def _(r):
            body(pl.ds(pl.multiple_of(r * 16, 16), 16))

    def scale(i):
        return scale_ref[i : i + 1]

    def add_gain(index, v):
        gain_ref[index] += v[:8] + v[8:]

    def project_out(u, k):
        dst = send.at[k % 3]

        @pl.loop(0, width // TILE)
        def _(n):
            dst[:, tile(n)] = dot_t(act[:, 2 * HEAD * u : 2 * HEAD * (u + 1)], w_out[tile(n)]).astype(BF)

    def middle(rows, u4):
        attn = total[u4, rows].astype(F32) if u4 is not None else ab[rows].astype(F32)
        r_two = inverse_rms(attn)
        return attn, r_two, xb[rows].astype(F32) + attn * r_two * scale(1)

    def forward(u, k, ready=None):
        load(x_hbm, u, xb, 0).start()
        store(total.at[u], attn_hbm, u, 1).start()
        load(x_hbm, u, xb, 0).wait()

        def body(rows):
            _, _, mid = middle(rows, u)
            act[rows] = (mid * inverse_rms(mid) * scale(2)).astype(BF)

        each_rows(body)
        turn()
        store_t(ffn_in_hbm, u, 2).start()

        @pl.loop(0, units // TILE)
        def _(f):
            gate = dot(act[...], weights[0, :, tile(f)])
            up = dot(act[...], weights[1, :, tile(f)])
            value, slope = gelu_parts(gate)
            stage[0, :, tile(f)] = (value * up).astype(BF)
            stage[1, :, tile(f)] = (slope * up).astype(BF)
            stage[2, :, tile(f)] = value.astype(BF)

        saves = ((0, hidden_hbm), (1, slope_hbm), (2, value_hbm))
        for i, ref in saves:
            store(stage.at[i], ref, u, 3 + i).start()
        if ready is not None:
            ready()
        dst = send.at[k % 3]

        @pl.loop(0, width // TILE)
        def _(n):
            dst[:, tile(n)] = dot_t(stage[0], weights[2, tile(n)]).astype(BF)

        for i, ref in saves:
            store(stage.at[i], ref, u, 3 + i).wait()
        store(total.at[u], attn_hbm, u, 1).wait()
        store_t(ffn_in_hbm, u, 2).wait()

    def backward(u, k):
        loads = (
            load(x_hbm, u, xb, 0), load(attn_hbm, u, ab, 1), load(cot_hbm, u, cb, 2),
            load(slope_hbm, u, stage.at[1], 4), load(value_hbm, u, stage.at[2], 5),
        )
        for copy in loads:
            copy.start()
        for copy in loads:
            copy.wait()

        def body(rows):
            _, _, mid = middle(rows, None)
            ffn = total[u, rows].astype(F32)
            r = inverse_rms(ffn)
            dy = cb[rows].astype(F32)
            xb[rows] = (mid + ffn * r * scale(3)).astype(BF)
            scaled = scale(3) * dy
            mean = jnp.mean(scaled * ffn, axis=-1, keepdims=True)
            act[rows] = (r * scaled - ffn * (r * r * r) * mean).astype(BF)
            add_gain(2, ffn * r * dy)

        each_rows(body)
        store(xb, out_hbm, u, 0).start()
        turn()
        store_t(d_ffn_hbm, u, 1).start()

        @pl.loop(0, units // TILE)
        def _(f):
            d_hidden = dot(act[...], weights[2, :, tile(f)])
            stage[1, :, tile(f)] = (d_hidden * stage[1, :, tile(f)].astype(F32)).astype(BF)
            stage[2, :, tile(f)] = (d_hidden * stage[2, :, tile(f)].astype(F32)).astype(BF)

        store(stage.at[1], d_gate_hbm, u, 4).start()
        store(stage.at[2], d_up_hbm, u, 5).start()
        dst = send.at[k % 3]

        @pl.loop(0, width // TILE)
        def _(n):
            part = dot_t(stage[1], weights[0, tile(n)]) + dot_t(stage[2], weights[1, tile(n)])
            dst[:, tile(n)] = part.astype(BF)

        store(xb, out_hbm, u, 0).wait()
        store_t(d_ffn_hbm, u, 1).wait()
        store(stage.at[1], d_gate_hbm, u, 4).wait()
        store(stage.at[2], d_up_hbm, u, 5).wait()

    def last(u):
        loads = (load(x_hbm, u, xb, 0), load(attn_hbm, u, ab, 1), load(cot_hbm, u, cb, 2))
        for copy in loads:
            copy.start()
        for copy in loads:
            copy.wait()

        def body(rows):
            attn, r_two, mid = middle(rows, None)
            r = inverse_rms(mid)
            dy = total[u, rows].astype(F32)
            scaled = scale(2) * dy
            mean = jnp.mean(scaled * mid, axis=-1, keepdims=True)
            grad = cb[rows].astype(F32) + r * scaled - mid * (r * r * r) * mean
            add_gain(1, mid * r * dy)
            cb[rows] = grad.astype(BF)
            scaled = scale(1) * grad
            mean = jnp.mean(scaled * attn, axis=-1, keepdims=True)
            act[rows] = (r_two * scaled - attn * (r_two * r_two * r_two) * mean).astype(BF)
            add_gain(0, attn * r_two * grad)

        each_rows(body)
        store(cb, d_mid_hbm, u, 0).start()
        turn()
        store_t(d_attn_hbm, u, 1).start()
        for h in range(w_out.shape[1] // TILE):
            columns = slice(h * TILE, (h + 1) * TILE)
            d_heads[:, columns] = dot(act[...], w_out[:, columns]).astype(BF)
        store(d_heads, d_heads_hbm, u, 2).start()
        store(cb, d_mid_hbm, u, 0).wait()
        store_t(d_attn_hbm, u, 1).wait()
        store(d_heads, d_heads_hbm, u, 2).wait()

    def gain_copy(m, recv=False):
        peer = group[m - 1]
        owner = (peer[0] * 2 + peer[1]) if recv else (dp * 2 + core)
        return pltpu.make_async_remote_copy(
            src_ref=gains_own, dst_ref=send.at[2, pl.ds(pl.multiple_of(owner * 16, 16), 16)],
            send_sem=gain_send.at[m], recv_sem=gain_recv.at[m], device_id=peer, device_id_type=MESH,
        )

    def gains_sum():
        whole = gains_own[...].astype(F32)
        for m in range(1, 8):
            gain_copy(m, True).wait_recv()
        for m in range(1, 8):
            owner = group[m - 1][0] * 2 + group[m - 1][1]
            whole += send[2, pl.ds(pl.multiple_of(owner * 16, 16), 16)].astype(F32)
        scale_ref[...] = 1.0 + whole[:8]
        for m in range(1, 8):
            gain_copy(m).wait_send()

    loaded = (stage.at[0], stage.at[1], stage.at[2], act)

    def first_norm(u):
        load(x_hbm, u, loaded[u], u).wait()

        def body(rows):
            x = loaded[u][rows].astype(F32)
            total[u, rows] = (x * inverse_rms(x) * scale(0)).astype(BF)

        each_rows(body)

    def first_turn(u):
        if u:
            store_t(attn_in_hbm, u - 1, 4).wait()
        turn(total.at[u])
        store_t(attn_in_hbm, u, 4).start()

    def angles(u):
        rows = rows_of(u)
        return (
            pltpu.make_async_copy(cos_hbm.at[rows], angle.at[u % 2, 0], local.at[2 * (u % 2)]),
            pltpu.make_async_copy(sin_hbm.at[rows], angle.at[u % 2, 1], local.at[2 * (u % 2) + 1]),
        )

    packs = (cb, ab)

    def kv_columns(kind, peer=False):
        side = (1 - core) if peer else core
        return pl.ds(pl.multiple_of(kind * 4 * HEAD + side * 2 * HEAD, HEAD), 2 * HEAD)

    def kv_copy(mb, kind, recv=False):
        part = packs[mb].at[:, kv_columns(kind, recv)]
        return pltpu.make_async_remote_copy(
            src_ref=part, dst_ref=part, send_sem=kv_sem.at[0, mb, kind], recv_sem=kv_sem.at[1, mb, kind],
            device_id=core_peer, device_id_type=MESH,
        )

    def projections(u):
        mb, b = divmod(u, 2)
        for copy in angles(u):
            copy.wait()
        if u < 3:
            for copy in angles(u + 1):
                copy.start()
        c, s = angle[u % 2, 0], angle[u % 2, 1]
        for j in range(4):
            v = dot(total[u], w_qkv[:, j * HEAD : (j + 1) * HEAD])
            if j < 2:
                xb[:, (mb * 4 + j * 2 + b) * HEAD : (mb * 4 + j * 2 + b + 1) * HEAD] = rotate(v, c, s).astype(BF)
            else:
                place = pl.multiple_of((j - 2) * 4 * HEAD + (core * 2 + b) * HEAD, HEAD)
                packs[mb][:, pl.ds(place, HEAD)] = (rotate(v, c, s) if j == 2 else v).astype(BF)

    def attention(mb):
        for kind in (0, 1):
            kv_copy(mb, kind, True).wait_recv()

        @pl.loop(0, 4)
        def _(i):
            h, b = i // 2, i % 2
            query = xb[:, pl.ds(pl.multiple_of(mb * 4 * HEAD + i * HEAD, HEAD), HEAD)]
            lowest = first_row[mb, :, pl.ds(pl.multiple_of(b * UNIT, UNIT), UNIT)]
            query_at = lax.broadcasted_iota(jnp.int32, (UNIT, UNIT), 1) + core * 2 * UNIT + b * UNIT
            weight, length = [], 0.0
            for j in range(4):
                key_at = lax.broadcasted_iota(jnp.int32, (UNIT, UNIT), 0) + j * UNIT
                score = dot_t(packs[mb][:, j * HEAD : (j + 1) * HEAD], query) * (SCALE / CAP)
                ok = (key_at <= query_at) & (key_at >= lowest)
                weight.append(jnp.where(ok, jnp.exp(CAP * jnp.tanh(score)), 0.0))
                length = length + jnp.sum(weight[j], axis=0, keepdims=True)
            inverse = 1.0 / length
            out = 0.0
            for j in range(4):
                value = packs[mb][:, (4 + j) * HEAD : (5 + j) * HEAD]
                out = out + t_dot((weight[j] * inverse).astype(BF), value)
            place = pl.multiple_of((mb * 2 + b) * 2 * HEAD + h * HEAD, HEAD)
            act[:, pl.ds(place, HEAD)] = out.astype(BF)

    def heads_store(u):
        return pltpu.make_async_copy(
            act.at[:, 2 * HEAD * u : 2 * HEAD * (u + 1)], heads_hbm.at[rows_of(u)], local.at[u]
        )

    def pack_store(i):
        return pltpu.make_async_copy((xb, cb, ab)[i], pack_hbm.at[i], ag_local.at[5 + i])

    for u in range(4):
        load(x_hbm, u, loaded[u], u).start()
    gain_ref[...] = jnp.zeros_like(gain_ref)
    pl.semaphore_wait(barrier, 9)
    for m in range(1, 8):
        gain_copy(m).start()
    gather_first(0)
    gains_sum()
    for u in range(4):
        first_norm(u)
    for copy in angles(0):
        copy.start()
    first_turn(0)
    gather_second(0)
    first_turn(1)
    first_turn(2)
    gather_third(0)
    gather_first(1)
    first_turn(3)
    gather_end(0)
    qkv_store = pltpu.make_async_copy(w_qkv, w_qkv_hbm, local.at[5])
    qkv_store.start()
    for u in range(4):
        projections(u)
        if u % 2:
            for kind in (0, 1):
                kv_copy(u // 2, kind).start()
    gather_second(1)
    gather_first(2)
    attention(0)
    gather_third(1)
    gather_end(1)
    qkv_store.wait()
    store_t(attn_in_hbm, 3, 4).wait()
    out_load = pltpu.make_async_copy(w_out_hbm, w_out, local.at[4])
    out_load.start()
    out_load.wait()
    project_out(0, 0)
    boundary(0)
    project_out(1, 1)
    attention(1)
    project_out(2, 2)
    for i in range(3):
        pack_store(i).start()
    for u in range(4):
        heads_store(u).start()
    gather_second(2)
    gather_first(3)
    boundary(1, 0)
    gather_third(2)
    for kind in (0, 1):
        for mb in (0, 1):
            kv_copy(mb, kind).wait_send()
    for i in range(3):
        pack_store(i).wait()
    for u in range(4):
        heads_store(u).wait()
    boundary(2, 1, 0)
    project_out(3, 3)
    gather_second(3)
    gather_first(4)
    boundary(3, 2, 1, 0)
    gather_third(3)
    gather_end(2)
    gather_end(3)

    def ready():
        gather_second(4)
        gather_third(4)
        gather_end(4)

    forward(0, 4, ready)

    @pl.loop(4, 7)
    def _(k):
        boundary(k, k - 1, k - 2, k - 3)
        forward(k - 3, k + 1)

    @pl.loop(7, 11)
    def _(k):
        boundary(k, k - 1, k - 2, k - 3)
        backward(k - 7, k + 1)

    left, w_back = weights.at[0, :, : 4 * UNIT], weights.at[0, :, 4 * UNIT : 8 * UNIT]
    queries = weights.at[0, : 4 * UNIT, 8 * UNIT :]
    d_out = weights.at[0, 4 * UNIT : 8 * UNIT, 8 * UNIT :]
    right = weights.at[1, : 4 * UNIT]
    jobs = (
        (d_ffn_hbm, hidden_hbm), (ffn_in_hbm, d_gate_hbm), (ffn_in_hbm, d_up_hbm),
        (d_attn_hbm, heads_hbm), (attn_in_hbm, d_proj_hbm),
    )

    def columns(i):
        return jobs[i][1].shape[1]

    def core_out(m):
        low = 4 * UNIT + (m % 2) * rows_own
        return weights.at[1, low : low + rows_own]

    def arrived(m):
        low = 4 * UNIT + (2 + m % 2) * rows_own
        return weights.at[1, low : low + rows_own]

    def sums(i, m):
        low = ((i % 2) * 3 + m - 1) * rows_own
        return weights.at[2, low : low + rows_own]

    packed = weights.at[2, 6 * rows_own : 6 * rows_own + UNIT]
    own_sum = weights.at[2, 6 * rows_own + UNIT : 7 * rows_own + UNIT]

    def remote(src, dst, index, peer):
        return pltpu.make_async_remote_copy(
            src_ref=src, dst_ref=dst, send_sem=rs_send.at[index], recv_sem=rs_recv.at[index],
            device_id=peer, device_id_type=MESH,
        )

    def operands(i):
        pair = [pltpu.make_async_copy(jobs[i][1], right.at[:, : columns(i)], rs_local.at[1])]
        if i != 2:
            pair.append(pltpu.make_async_copy(jobs[i][0], left, rs_local.at[0]))
        return pair

    def core_copy(i, m):
        n = columns(i)
        return remote(core_out(m).at[:, :n], core_hbm.at[i, m, :, :n], (i, m), core_peer)

    def arrive(i, m):
        n = columns(i)
        return pltpu.make_async_copy(core_hbm.at[i, m, :, :n], arrived(m).at[:, :n], rs_local.at[2 + m % 2])

    def far_copy(i, way):
        n = columns(i)
        rows = slice(0, half) if way == 0 else slice(half, rows_own)
        peer = (x_peer, y_peer)[way]
        return remote(sums(i, 3).at[rows, :n], far_hbm.at[i, rows, :n], (i, 4 + way), peer)

    def final_copy(i, way):
        n = columns(i)
        dst = (by_x_hbm, by_y_hbm)[way]
        peer = (x_peer, y_peer)[way]
        return remote(sums(i, way + 1).at[:, :n], dst.at[i, :, :n], (i, 6 + way), peer)

    def own_store(i):
        n = columns(i)
        return pltpu.make_async_copy(own_sum.at[:, :n], own_hbm.at[i, :, :n], rs_local.at[5])

    def block_rows(mask, other):
        owner = (dp ^ mask) * 2 + ((1 - core) if other else core)
        return pl.ds(pl.multiple_of(owner * rows_own, 16), rows_own)

    def scatter_start(i):
        for copy in operands(i):
            copy.wait()
        steps = columns(i) // TILE

        for m in (3, 2, 1, 0):
            if m < 2:
                core_copy(i, m + 2).wait_send()
            elif i > 0:
                core_copy(i - 1, m - 2).wait_send()
            dst = core_out(m)

            @pl.loop(0, steps)
            def _(n):
                dst[:, tile(n)] = dot(left[block_rows(m, True)], right[:, tile(n)]).astype(BF)

            core_copy(i, m).start()
        if i > 1:
            for way in (0, 1):
                far_copy(i - 2, way).wait_send()
                final_copy(i - 2, way).wait_send()
        if i > 0:
            own_store(i - 1).wait()
        core_copy(i, 3).wait_recv()
        arrive(i, 3).start()
        for m in (3, 2, 1, 0):
            if m:
                core_copy(i, m - 1).wait_recv()
                arrive(i, m - 1).start()
            arrive(i, m).wait()
            dst, extra = (sums(i, m) if m else own_sum), arrived(m)

            @pl.loop(0, steps)
            def _(n):
                part = dot(left[block_rows(m, False)], right[:, tile(n)])
                dst[:, tile(n)] = (part + extra[:, tile(n)].astype(F32)).astype(BF)

            if m == 3:
                far_copy(i, 0).start()
                far_copy(i, 1).start()
        own_store(i).start()

    def operands_start(i):
        for copy in operands(i):
            copy.start()

    def scatter_end(i):
        n = columns(i)
        for way in (0, 1):
            far_copy(i, way).wait_recv()
        added = arrived(0)
        copy = pltpu.make_async_copy(far_hbm.at[i, :, :n], added.at[:, :n], rs_local.at[4])
        copy.start()
        copy.wait()
        for way in (1, 0):
            base = 0 if way == 1 else half
            dst = sums(i, way + 1)

            @pl.loop(0, half // 16)
            def _(r):
                rows = pl.ds(pl.multiple_of(base + r * 16, 16), 16)
                dst[rows, :n] = (dst[rows, :n].astype(F32) + added[rows, :n].astype(F32)).astype(BF)

            final_copy(i, way).start()

    def back_loads(mb):
        copies = [pltpu.make_async_copy(pack_hbm.at[1 + mb], packed, load_sem.at[8])]
        for i in range(4):
            h, b = divmod(i, 2)
            rows = pl.ds(i * UNIT, UNIT)
            query = pack_hbm.at[0, :, (mb * 4 + i) * HEAD : (mb * 4 + i + 1) * HEAD]
            grad = d_heads_hbm.at[pl.ds((2 * mb + b) * UNIT, UNIT), h * HEAD : (h + 1) * HEAD]
            copies.append(pltpu.make_async_copy(query, queries.at[rows], load_sem.at[i]))
            copies.append(pltpu.make_async_copy(grad, d_out.at[rows], load_sem.at[4 + i]))
        return [*copies, *angles(2 * mb), *angles(2 * mb + 1)]

    def unrotate(v, b):
        c, s = angle[b, 0], angle[b, 1]
        v, w = v[:, : HEAD // 2], v[:, HEAD // 2 :]
        return jnp.concatenate([v * c + w * s, w * c - v * s], axis=1)

    def kv_out(mb):
        return pltpu.make_async_remote_copy(
            src_ref=act_t.at[: 4 * UNIT], dst_ref=kv_hbm.at[mb], send_sem=kv_back.at[0, mb],
            recv_sem=kv_back.at[1, mb], device_id=core_peer, device_id_type=MESH,
        )

    def proj_store(u):
        part = stage.at[u // 2, :, (u % 2) * 4 * HEAD : (u % 2 + 1) * 4 * HEAD]
        return pltpu.make_async_copy(part, d_proj_hbm.at[rows_of(u)], proj_sem.at[u])

    def attention_back(mb):
        for copy in back_loads(mb):
            copy.start()
        for copy in back_loads(mb):
            copy.wait()
        d_scores, weights_of = (xb, ab), (act, cb)

        @pl.loop(0, 4)
        def _(i):
            h, b = i // 2, i % 2
            rows = pl.ds(pl.multiple_of(i * UNIT, UNIT), UNIT)
            query, grad = queries[rows], d_out[rows]
            lowest = first_row[mb, :, pl.ds(pl.multiple_of(b * UNIT, UNIT), UNIT)]
            query_at = lax.broadcasted_iota(jnp.int32, (UNIT, UNIT), 1) + core * 2 * UNIT + b * UNIT
            tanh, weight, d_probs, length, mean = [], [], [], 0.0, 0.0
            for j in range(4):
                key_at = lax.broadcasted_iota(jnp.int32, (UNIT, UNIT), 0) + j * UNIT
                ok = (key_at <= query_at) & (key_at >= lowest)
                score = dot_t(packed[:, j * HEAD : (j + 1) * HEAD], query) * (SCALE / CAP)
                tanh.append(jnp.tanh(score))
                weight.append(jnp.where(ok, jnp.exp(CAP * tanh[j]), 0.0))
                d_probs.append(dot_t(packed[:, (4 + j) * HEAD : (5 + j) * HEAD], grad))
                length = length + jnp.sum(weight[j], axis=0, keepdims=True)
                mean = mean + jnp.sum(weight[j] * d_probs[j], axis=0, keepdims=True)
            inverse = 1.0 / length
            mean = mean * inverse
            d_query = 0.0
            for j in range(4):
                probs = weight[j] * inverse
                d_raw = (probs * (d_probs[j] - mean) * (1.0 - tanh[j] * tanh[j])).astype(BF)
                place = pl.ds(pl.multiple_of((j % 2) * 4 * HEAD + i * HEAD, HEAD), HEAD)
                d_scores[j // 2][:, place] = d_raw
                weights_of[j // 2][:, place] = probs.astype(BF)
                d_query = d_query + t_dot(d_raw, packed[:, j * HEAD : (j + 1) * HEAD])
            place = pl.ds(pl.multiple_of(b * 4 * HEAD + h * HEAD, HEAD), HEAD)
            stage[mb, :, place] = unrotate(d_query * SCALE, b).astype(BF)

        def block_grads(j):
            place = slice((j % 2) * 4 * HEAD, (j % 2 + 1) * 4 * HEAD)
            d_key = dot(d_scores[j // 2][:, place], queries[...]) * SCALE
            return d_key, dot(weights_of[j // 2][:, place], d_out[...])

        for side in (0, 1):

            @pl.when(core == side)
            def _():
                for t in (0, 1):
                    d_key, d_value = block_grads((1 - side) * 2 + t)
                    act_t[t * UNIT : (t + 1) * UNIT] = d_key.astype(BF)
                    act_t[(2 + t) * UNIT : (3 + t) * UNIT] = d_value.astype(BF)

        kv_out(mb).start()
        kv_out(mb).wait_recv()
        copy = pltpu.make_async_copy(kv_hbm.at[mb], act_t.at[4 * UNIT : 8 * UNIT], rs_local.at[6])
        copy.start()
        copy.wait()
        for side in (0, 1):

            @pl.when(core == side)
            def _():
                for t in (0, 1):
                    d_key, d_value = block_grads(side * 2 + t)
                    d_key = d_key + act_t[(4 + t) * UNIT : (5 + t) * UNIT].astype(F32)
                    d_value = d_value + act_t[(6 + t) * UNIT : (7 + t) * UNIT].astype(F32)
                    low = t * 4 * HEAD
                    stage[mb, :, low + 2 * HEAD : low + 3 * HEAD] = unrotate(d_key, t).astype(BF)
                    stage[mb, :, low + 3 * HEAD : low + 4 * HEAD] = d_value.astype(BF)

        proj_store(2 * mb).start()
        proj_store(2 * mb + 1).start()
        kv_out(mb).wait_send()

    def project_back(u):
        dst = send.at[(12 + u) % 3]
        low = (u % 2) * 4 * HEAD

        @pl.loop(0, width // TILE)
        def _(n):
            dst[:, tile(n)] = dot_t(stage[u // 2, :, low : low + 4 * HEAD], w_back[tile(n)]).astype(BF)

    def first_back(u):
        loads = (load(x_hbm, u, xb, 0), load(d_mid_hbm, u, ab, 1))
        for copy in loads:
            copy.start()
        for copy in loads:
            copy.wait()

        def body(rows):
            x = xb[rows].astype(F32)
            r_one = inverse_rms(x)
            dy = total[u, rows].astype(F32)
            scaled = scale(0) * dy
            mean = jnp.mean(scaled * x, axis=-1, keepdims=True)
            back = r_one * scaled - x * (r_one * r_one * r_one) * mean
            ab[rows] = (ab[rows].astype(F32) + back).astype(BF)
            add_gain(3, x * r_one * dy)

        each_rows(body)
        store(ab, in_grad_hbm, u, 2).start()
        store(ab, in_grad_hbm, u, 2).wait()

    w_load = pltpu.make_async_copy(w_qkv_hbm, w_back, rs_local.at[7])
    operands_start(0)
    w_load.start()
    boundary(11, 10, 9, 8)
    scatter_start(0)
    operands_start(1)
    last(0)
    boundary(None, 11, 10, 9)
    scatter_end(0)
    last(1)
    attention_back(0)
    w_load.wait()
    project_back(0)
    boundary(12, None, 11, 10)
    project_back(1)
    last(2)
    scatter_start(1)
    operands_start(2)
    boundary(13, 12, None, 11)
    scatter_end(1)
    last(3)
    attention_back(1)
    project_back(2)
    boundary(14, 13, 12)
    project_back(3)
    scatter_start(2)
    operands_start(3)
    boundary(15, 14, 13, 12)
    scatter_end(2)
    first_back(0)
    scatter_start(3)
    for u in range(4):
        proj_store(u).wait()
    operands_start(4)
    boundary(None, 15, 14, 13)
    scatter_end(3)
    scatter_start(4)
    first_back(1)
    boundary(None, None, 15, 14)
    scatter_end(4)
    first_back(2)
    boundary(None, None, None, 15)
    first_back(3)
    own_store(4).wait()
    for m in range(2):
        core_copy(4, m).wait_send()
    for i in range(5):
        for way in (0, 1):
            if i > 2:
                far_copy(i, way).wait_send()
                final_copy(i, way).wait_send()
            final_copy(i, way).wait_recv()


def layer_call(first_row, gains_own, cosine, sine, x, cot, owns):
    tokens, width = x.shape
    units = owns[2].shape[1]
    qkv_cols, out_cols = owns[0].shape[1], owns[1].shape[1]
    assert tokens == 4 * UNIT
    full = jax.ShapeDtypeStruct((tokens, width), BF)
    wide = jax.ShapeDtypeStruct((tokens, units), BF)
    flipped = jax.ShapeDtypeStruct((width, tokens), BF)
    rows = owns[0].shape[0]
    part = jax.ShapeDtypeStruct((5, rows, units), BF)
    heads = jax.ShapeDtypeStruct((tokens, out_cols), BF)
    outs = (
        full, flipped, wide, flipped, wide, wide, flipped, heads, full,
        jax.ShapeDtypeStruct((4, 8, width), F32),
        jax.ShapeDtypeStruct((8, width), F32),
        flipped,
        heads,
        jax.ShapeDtypeStruct((3, UNIT, width), BF),
        jax.ShapeDtypeStruct((width, qkv_cols), BF),
        jax.ShapeDtypeStruct((width, out_cols), BF),
        full, wide, wide,
        full, part, part, part,
        jax.ShapeDtypeStruct((5, 4, rows, units), BF),
        part,
        jax.ShapeDtypeStruct((2, tokens, HEAD), BF),
        jax.ShapeDtypeStruct((tokens, qkv_cols), BF),
    )
    anywhere, vmem = pl.BlockSpec(memory_space=pl.ANY), pl.BlockSpec(memory_space=pltpu.VMEM)
    dma = pltpu.SemaphoreType.DMA
    return pl.pallas_call(
        layer_kernel,
        out_shape=outs,
        in_specs=[vmem] * 2 + [anywhere] * 9,
        out_specs=[anywhere] * 9 + [vmem] * 2 + [anywhere] * 16,
        scratch_shapes=[
            pltpu.VMEM((3, width, units), BF),
            pltpu.VMEM((width, qkv_cols), BF),
            pltpu.VMEM((3, UNIT, width), BF),
            pltpu.VMEM((3, UNIT, width), BF),
            pltpu.VMEM((2, UNIT, width), BF),
            pltpu.VMEM((4, UNIT, width), BF),
            pltpu.VMEM((UNIT, width), BF),
            pltpu.VMEM((UNIT, width), BF),
            pltpu.VMEM((UNIT, width), BF),
            pltpu.VMEM((UNIT, width), BF),
            pltpu.VMEM((width, UNIT), BF),
            pltpu.VMEM((3, UNIT, units), BF),
            pltpu.VMEM((UNIT, out_cols), BF),
            pltpu.VMEM((2, 2, UNIT, HEAD // 2), F32),
            dma((3, 4)),
            dma((3, 4)),
            pltpu.SemaphoreType.REGULAR,
            dma((6,)),
            dma((5, 9)),
            dma((5, 9)),
            dma((8,)),
            dma((8,)),
            dma((8,)),
            dma((2, 2, 2)),
            dma((9,)),
            dma((5, 8)),
            dma((5, 8)),
            dma((8,)),
            dma((2, 2)),
            dma((4,)),
        ],
        compiler_params=pltpu.CompilerParams(
            collective_id=1, has_side_effects=True, vmem_limit_bytes=63 * 2**20
        ),
        name="layer",
    )(first_row, gains_own, cosine, sine, x, cot, *owns)


def fast_device(
    sizes,
    inputs,
    segment_ids,
    positions,
    cotangent,
    *params,
):
    masters, moments = params[:11], params[11:]
    batches, seqs, tokens, width = inputs.shape
    assert seqs == 1
    q_cols, k_cols = masters[0].shape[1], masters[1].shape[1]
    width_ff = masters[4].shape[1]
    assert k_cols == HEAD

    own = masters[7].shape[0]
    place = (lax.axis_index("dp") * sizes["ctx"] + lax.axis_index("ctx")) * own
    low = [w.astype(BF) for w in masters[:7]]
    owns = (jnp.concatenate(low[:3], axis=1), *low[3:])
    gains_own = jnp.zeros((16, width), BF)
    gains_own = lax.dynamic_update_slice(gains_own, jnp.stack(masters[7:]).astype(BF), (0, place))
    start = lax.axis_index("ctx") * tokens
    frequency = jnp.exp(
        jnp.arange(HEAD // 2, dtype=F32) * (-2.0 * math.log(10000.0) / HEAD)
    )
    angle = positions.reshape(-1).astype(F32)[:, None] * frequency
    cosine, sine = jnp.cos(angle), jnp.sin(angle)
    first_row = (start + jnp.arange(tokens, dtype=jnp.int32))[None, None] - positions
    flat = (batches * tokens, width)
    x = inputs.reshape(flat)
    outs = layer_call(first_row, gains_own, cosine, sine, x, cotangent.reshape(flat), owns)
    output, gain_parts = outs[0], outs[9]
    input_grad, own_sum, by_x, by_y = outs[19:23]

    def final_sum(i, cols):
        picked = [v[i, :, :cols].astype(F32) for v in (own_sum, by_x, by_y)]
        return picked[0] + picked[1] + picked[2]

    qkv_cols = owns[0].shape[1]
    s_down, s_gate, s_up = [final_sum(i, width_ff) for i in range(3)]
    s_out, s_qkv = final_sum(3, q_cols), final_sum(4, qkv_cols)
    gain_grads = jnp.sum(gain_parts, axis=1)
    gain_grads = sum_small(gain_grads, ("ctx", "dp"), sizes)
    summed = (
        s_qkv[:, :q_cols], s_qkv[:, q_cols : q_cols + k_cols], s_qkv[:, q_cols + k_cols :],
        s_out, s_gate, s_up, s_down,
    )
    weight_sq = sum(jnp.sum(g * g) for g in (s_qkv, s_out, s_gate, s_up, s_down))
    weight_sq = sum_small(weight_sq.reshape(1, 1), ("ctx", "dp", "mp"), sizes)[0, 0]
    norm_value = jnp.sqrt(weight_sq + jnp.sum(gain_grads * gain_grads))
    factor = 1.0 / jnp.maximum(norm_value, 1.0)
    own_gains = lax.dynamic_slice_in_dim(gain_grads, place, own, 1)
    summed += tuple(own_gains[i] for i in (3, 0, 1, 2))
    new_moments = tuple(0.5 * m + 0.5 * factor * g for m, g in zip(moments, summed))
    changes = tuple(-RATE * (m + 0.01 * w) for w, m in zip(masters[:7], new_moments[:7]))

    return (
        output.reshape(inputs.shape),
        input_grad.reshape(inputs.shape), norm_value.reshape(1), *changes, *new_moments
    )


def per_device(
    sizes,
    inputs,
    segment_ids,
    positions,
    cotangent,
    *params,
):
    masters, moments = params[:11], params[11:]
    batches, seqs, tokens, width = inputs.shape
    assert seqs == 1
    full_len = segment_ids.shape[2]
    q_cols, k_cols = masters[0].shape[1], masters[1].shape[1]
    heads = q_cols // HEAD
    assert k_cols == HEAD
    cuts = 2 if tokens >= 512 else 1
    unit = tokens // cuts

    low = [w.astype(BF) for w in masters[:7]]
    qkv_own = jnp.concatenate(low[:3], axis=1)
    gains_own = jnp.stack([g.astype(BF) for g in masters[7:]], axis=1)
    gains = lax.all_gather(gains_own, ("dp", "ctx"), axis=0, tiled=True).astype(F32)
    gain_one, gain_two, gain_three, gain_four = [gains[:, i] for i in range(4)]
    w_qkv, mark = gather_rows(qkv_own, sizes, None)
    w_out, mark = gather_rows(low[3], sizes, mark)
    w_gate, mark = gather_rows(low[4], sizes, mark)
    w_up, mark = gather_rows(low[5], sizes, mark)
    w_down, mark = gather_rows(low[6], sizes, mark)

    start = lax.axis_index("ctx") * tokens
    causal = (start + jnp.arange(tokens))[:, None] >= jnp.arange(full_len)[None, :]
    frequency = jnp.exp(
        jnp.arange(HEAD // 2, dtype=F32) * (-2.0 * math.log(10000.0) / HEAD)
    )

    state = []
    for mb in range(batches):
        x = inputs[mb, 0].astype(F32)
        r_one = inverse_rms(x)
        attn_in = (x * r_one * (1.0 + gain_one)).astype(BF)
        angles = positions[mb, 0].astype(F32)[:, None] * frequency
        cosine, sine = jnp.cos(angles), jnp.sin(angles)
        seg = segment_ids[mb, 0]
        seg_local = lax.dynamic_slice_in_dim(seg, start, tokens)
        allowed = causal & (seg_local[:, None] == seg[None, :])
        proj = dot(attn_in, w_qkv)
        queries = jnp.concatenate(
            [rotate(proj[:, h * HEAD : (h + 1) * HEAD], cosine, sine) for h in range(heads)]
        ).astype(BF)
        keys = rotate(proj[:, q_cols : q_cols + HEAD], cosine, sine).astype(BF)
        values = proj[:, q_cols + HEAD :].astype(BF)
        both = swap_ctx(jnp.concatenate([keys, values], axis=1), sizes)
        keys_all, values_all = both[:, :HEAD], both[:, HEAD:]
        out, saved = attend(queries, keys_all, values_all, allowed)
        heads_out = jnp.concatenate(jnp.split(out, heads, axis=0), axis=1)
        state.append(
            dict(
                x=x, r_one=r_one, attn_in=attn_in, cosine=cosine, sine=sine, queries=queries,
                keys=keys_all, values=values_all, saved=saved, heads_out=heads_out,
            )
        )

    units = [(mb, cut) for mb in range(batches) for cut in range(cuts)]
    work = []
    for mb, cut in units:
        rows = slice(cut * unit, (cut + 1) * unit)
        part = dot_t(state[mb]["heads_out"][rows], w_out).astype(BF)
        work.append(dict(rows=rows, mb=mb, attn_low=sum_mp(part, sizes)))
    for w in work:
        attn = w["attn_low"].astype(F32)
        r_two = inverse_rms(attn)
        mid = state[w["mb"]]["x"][w["rows"]] + attn * r_two * (1.0 + gain_two)
        r_three = inverse_rms(mid)
        ffn_in = (mid * r_three * (1.0 + gain_three)).astype(BF)
        gate, up = dot(ffn_in, w_gate), dot(ffn_in, w_up)
        value, slope = gelu_parts(gate)
        hidden = (value * up).astype(BF)
        part = dot_t(hidden, w_down).astype(BF)
        w.update(
            mid=mid, r_two=r_two, r_three=r_three, ffn_in=ffn_in, gate=gate, up=up, hidden=hidden,
            ffn_low=sum_mp(part, sizes),
        )
    for w in work:
        ffn = w["ffn_low"].astype(F32)
        r_four = inverse_rms(ffn)
        grad = cotangent[w["mb"], 0][w["rows"]].astype(F32)
        w["output"] = (w["mid"] + ffn * r_four * (1.0 + gain_four)).astype(BF)
        d_ffn, w["g_four"] = norm_back(ffn, r_four, gain_four, grad)
        d_ffn = d_ffn.astype(BF)
        d_hidden = dot(d_ffn, w_down)
        value, slope = gelu_parts(w["gate"])
        d_gate = (d_hidden * w["up"] * slope).astype(BF)
        d_up = (d_hidden * value).astype(BF)
        part = (dot_t(d_gate, w_gate) + dot_t(d_up, w_up)).astype(BF)
        w.update(grad=grad, d_ffn=d_ffn, d_gate=d_gate, d_up=d_up, d_in_low=sum_mp(part, sizes))
    for w in work:
        d_in = w["d_in_low"].astype(F32)
        back, w["g_three"] = norm_back(w["mid"], w["r_three"], gain_three, d_in)
        d_mid = w["grad"] + back
        attn = w["attn_low"].astype(F32)
        d_attn, w["g_two"] = norm_back(attn, w["r_two"], gain_two, d_mid)
        d_attn = d_attn.astype(BF)
        w.update(d_mid=d_mid, d_attn=d_attn, d_heads=dot(d_attn, w_out).astype(BF))

    def rows_of(key):
        return jnp.concatenate([w[key] for w in work])

    ffn_in = rows_of("ffn_in")
    g_down = t_dot(rows_of("d_ffn"), rows_of("hidden"))
    g_gate = t_dot(ffn_in, rows_of("d_gate"))
    g_up = t_dot(ffn_in, rows_of("d_up"))
    s_down, mark = scatter_rows(g_down, sizes, None)
    s_gate, mark = scatter_rows(g_gate, sizes, mark)
    s_up, mark = scatter_rows(g_up, sizes, mark)

    for mb in range(batches):
        s = state[mb]
        d_heads = jnp.concatenate([w["d_heads"] for w in work if w["mb"] == mb])
        d_out = jnp.concatenate(jnp.split(d_heads, heads, axis=1))
        d_queries, d_keys, d_values = attend_back(
            s["saved"], s["queries"], s["keys"], s["values"], d_out
        )
        d_kv = scatter_ctx(jnp.concatenate([d_keys, d_values], axis=1), sizes)
        pieces = [rotate(q, s["cosine"], -s["sine"]) for q in jnp.split(d_queries, heads)]
        pieces += [rotate(d_kv[:, :HEAD], s["cosine"], -s["sine"]), d_kv[:, HEAD:]]
        s["d_proj"] = jnp.concatenate(pieces, axis=1).astype(BF)
    for w in work:
        part = dot_t(state[w["mb"]]["d_proj"][w["rows"]], w_qkv).astype(BF)
        w["d_attn_in"] = sum_mp(part, sizes)

    g_out = t_dot(rows_of("d_attn"), jnp.concatenate([s["heads_out"] for s in state]))
    g_qkv = t_dot(
        jnp.concatenate([s["attn_in"] for s in state]),
        jnp.concatenate([s["d_proj"] for s in state]),
    )
    s_out, mark = scatter_rows(g_out, sizes, mark)
    s_qkv, mark = scatter_rows(g_qkv, sizes, mark)

    for w in work:
        s = state[w["mb"]]
        back, w["g_one"] = norm_back(
            s["x"][w["rows"]], s["r_one"][w["rows"]], gain_one, w["d_attn_in"].astype(F32)
        )
        w["input_grad"] = (w["d_mid"] + back).astype(BF)

    gain_grads = jnp.stack(
        [sum(w[key] for w in work) for key in ("g_one", "g_two", "g_three", "g_four")]
    )
    gain_grads = sum_small(gain_grads, ("ctx", "dp"), sizes)
    summed = (
        s_qkv[:, :q_cols], s_qkv[:, q_cols : q_cols + k_cols], s_qkv[:, q_cols + k_cols :],
        s_out, s_gate, s_up, s_down,
    )
    weight_sq = sum(jnp.sum(g * g) for g in (s_qkv, s_out, s_gate, s_up, s_down))
    weight_sq = sum_small(weight_sq.reshape(1, 1), ("ctx", "dp", "mp"), sizes)[0, 0]
    norm_value = jnp.sqrt(weight_sq + jnp.sum(gain_grads * gain_grads))
    factor = 1.0 / jnp.maximum(norm_value, 1.0)
    own = masters[7].shape[0]
    place = (lax.axis_index("dp") * sizes["ctx"] + lax.axis_index("ctx")) * own
    own_gains = lax.dynamic_slice_in_dim(gain_grads, place, own, 1)
    summed += tuple(own_gains[i] for i in range(4))
    new_moments = tuple(0.5 * m + 0.5 * factor * g for m, g in zip(moments, summed))
    changes = tuple(-RATE * (m + 0.01 * w) for w, m in zip(masters[:7], new_moments[:7]))

    def whole(key):
        return rows_of(key).reshape(inputs.shape)

    return (
        whole("output"), whole("input_grad"), norm_value.reshape(1), *changes, *new_moments
    )


def solution(mesh):
    sizes = dict(mesh.shape)
    weight, vector = P(("dp", "ctx"), "mp"), P(("dp", "ctx"))
    params = (weight,) * 7 + (vector,) * 4
    data = P(None, "dp", "ctx", None)

    def run(*args):
        batches, _, tokens, _ = args[0].shape
        fast = sizes == dict(dp=4, ctx=2, mp=4) and batches == 2 and tokens == 2 * UNIT
        return (fast_device if fast else per_device)(sizes, *args)

    return jax.shard_map(
        run,
        mesh=mesh,
        in_specs=(data, P(None, "dp", None), P(None, "dp", "ctx"), data) + params + params,
        out_specs=(data, data, P()) + (weight,) * 7 + params,
        check_vma=False,
    )
```

```python
import math

import jax
import jax.numpy as jnp
from jax import lax
from jax.experimental import pallas as pl
from jax.experimental.pallas import tpu as pltpu
from jax.sharding import PartitionSpec as P

HEAD = 256
STEP = 10
EPS = 1e-06
CAP = 50.0
RATE = 1.0 / math.sqrt(1.0 + STEP / 1000.0)
SCALE = HEAD ** (-0.5)
BF = jnp.bfloat16
F32 = jnp.float32


def flip(axis, size, mask):
    return dict(axis_name=axis, perm=[(i, i ^ mask) for i in range(size)])


def after(value, other):
    return lax.optimization_barrier((value, other))[0]


def gather_rows(own, sizes, wait):
    dp, ctx = sizes["dp"], sizes["ctx"]
    rows, cols = own.shape
    if wait is not None:
        own = after(own, wait)
    if dp != 4:
        out = lax.all_gather(own, ("dp", "ctx"), axis=0, tiled=True)
        return out, own
    me = lax.axis_index("dp")
    half = rows // 2 // 16 * 16
    from_x = lax.ppermute(own, **flip("dp", dp, 1))
    from_y = lax.ppermute(own, **flip("dp", dp, 2))
    far_top = lax.ppermute(from_y[:half], **flip("dp", dp, 1))
    far_low = lax.ppermute(from_x[half:], **flip("dp", dp, 2))
    mine = jnp.zeros((dp, rows, cols), own.dtype)
    mine = lax.dynamic_update_slice(mine, own[None], (me, 0, 0))
    mine = lax.dynamic_update_slice(mine, from_x[None], (me ^ 1, 0, 0))
    mine = lax.dynamic_update_slice(mine, from_y[None], (me ^ 2, 0, 0))
    mine = lax.dynamic_update_slice(mine, far_top[None], (me ^ 3, 0, 0))
    mine = lax.dynamic_update_slice(mine, far_low[None], (me ^ 3, half, 0))
    if ctx == 2:
        other = lax.ppermute(mine, **flip("ctx", ctx, 1))
        core = lax.axis_index("ctx")
        out = jnp.zeros((dp, ctx, rows, cols), own.dtype)
        out = lax.dynamic_update_slice(out, mine[:, None], (0, core, 0, 0))
        out = lax.dynamic_update_slice(out, other[:, None], (0, 1 - core, 0, 0))
    else:
        out = lax.all_gather(mine, "ctx", axis=1)
    return out.reshape(dp * ctx * rows, cols), from_x


def scatter_rows(full, sizes, wait):
    dp, ctx = sizes["dp"], sizes["ctx"]
    full = full.astype(BF)
    if wait is not None:
        full = after(full, wait)
    rows = full.shape[0] // (dp * ctx)
    cols = full.shape[1]
    if dp != 4:
        out = lax.psum_scatter(full, ("dp", "ctx"), scatter_dimension=0, tiled=True)
        return out.astype(F32), out
    blocks = full.reshape(dp, ctx, rows, cols)
    if ctx == 2:
        core = lax.axis_index("ctx")
        send = lax.dynamic_index_in_dim(blocks, 1 - core, 1, keepdims=False)
        keep = lax.dynamic_index_in_dim(blocks, core, 1, keepdims=False)
        got = lax.ppermute(send, **flip("ctx", ctx, 1))
    else:
        keep = lax.psum_scatter(blocks, "ctx", scatter_dimension=1, tiled=False)
        got = None
    me = lax.axis_index("dp")
    half = rows // 2 // 16 * 16

    def part(mask, low, high):
        size = (1, high - low, cols)
        piece = lax.dynamic_slice(keep, (me ^ mask, low, 0), size)[0].astype(F32)
        if got is not None:
            piece = piece + lax.dynamic_slice(got, (me ^ mask, low, 0), size)[0].astype(F32)
        return piece

    far_top = lax.ppermute(part(3, 0, half).astype(BF), **flip("dp", dp, 1))
    far_low = lax.ppermute(part(3, half, rows).astype(BF), **flip("dp", dp, 2))
    to_y = jnp.concatenate([part(2, 0, half) + far_top.astype(F32), part(2, half, rows)])
    to_x = jnp.concatenate([part(1, 0, half), part(1, half, rows) + far_low.astype(F32)])
    by_y = lax.ppermute(to_y.astype(BF), **flip("dp", dp, 2))
    by_x = lax.ppermute(to_x.astype(BF), **flip("dp", dp, 1))
    total = part(0, 0, rows) + by_x.astype(F32) + by_y.astype(F32)
    return total, far_top


def sum_mp(part, sizes):
    if sizes["mp"] != 4:
        return lax.psum(part, "mp")
    place = lax.axis_index("mp")
    inner = (place == 1) | (place == 2)
    near = lax.ppermute(part, "mp", [(0, 1), (3, 2)])
    pair = (part.astype(F32) + near.astype(F32)).astype(BF)
    across = lax.ppermute(pair, "mp", [(1, 2), (2, 1)])
    total = (pair.astype(F32) + across.astype(F32)).astype(BF)
    back = lax.ppermute(total, "mp", [(1, 0), (2, 3)])
    return jnp.where(inner, total, back)


def sum_small(value, axes, sizes):
    for axis in axes:
        size = sizes[axis]
        step = 1
        while step < size:
            value = value + lax.ppermute(value, **flip(axis, size, step))
            step *= 2
    return value


def swap_ctx(local, sizes):
    if sizes["ctx"] != 2:
        return lax.all_gather(local, "ctx", axis=0, tiled=True)
    other = lax.ppermute(local, **flip("ctx", 2, 1))
    first = lax.axis_index("ctx") == 0
    return jnp.concatenate([jnp.where(first, local, other), jnp.where(first, other, local)])


def scatter_ctx(full, sizes):
    if sizes["ctx"] != 2:
        return lax.psum_scatter(full.astype(BF), "ctx", scatter_dimension=0, tiled=True).astype(F32)
    core = lax.axis_index("ctx")
    rows = full.shape[0] // 2
    send = lax.dynamic_slice_in_dim(full, (1 - core) * rows, rows).astype(BF)
    keep = lax.dynamic_slice_in_dim(full, core * rows, rows)
    return keep.astype(BF).astype(F32) + lax.ppermute(send, **flip("ctx", 2, 1)).astype(F32)


def dot(a, b):
    return lax.dot_general(a, b, (((1,), (0,)), ((), ())), preferred_element_type=F32)


def dot_t(a, b):
    return lax.dot_general(a, b, (((1,), (1,)), ((), ())), preferred_element_type=F32)


def t_dot(a, b):
    return lax.dot_general(a, b, (((0,), (0,)), ((), ())), preferred_element_type=F32)


def inverse_rms(v):
    return lax.rsqrt(jnp.mean(v * v, axis=-1, keepdims=True) + EPS)


def norm_back(v, r, gain, dy):
    scaled = (1.0 + gain) * dy
    mean = jnp.mean(scaled * v, axis=-1, keepdims=True)
    return r * scaled - v * (r * r * r) * mean, jnp.sum(v * r * dy, axis=0)


def rotate(v, cosine, sine):
    a, b = v[:, : HEAD // 2], v[:, HEAD // 2 :]
    return jnp.concatenate([a * cosine - b * sine, b * cosine + a * sine], axis=1)


GELU_C = math.sqrt(2.0 / math.pi)


def gelu_parts(u):
    tanh = jnp.tanh(GELU_C * (u + 0.044715 * u * u * u))
    value = 0.5 * u * (1.0 + tanh)
    slope = 0.5 * (1.0 + tanh) + 0.5 * u * (1.0 - tanh * tanh) * GELU_C * (
        1.0 + 3.0 * 0.044715 * u * u
    )
    return value, slope


def attend(queries, keys, values, allowed):
    raw = dot_t(queries, keys) * SCALE
    tanh = jnp.tanh(raw / CAP)
    heads = queries.shape[0] // allowed.shape[0]
    mask = jnp.concatenate([allowed] * heads, axis=0)
    weight = jnp.where(mask, jnp.exp(CAP * tanh), 0.0)
    probs = weight / jnp.sum(weight, axis=1, keepdims=True)
    out = dot(probs.astype(BF), values).astype(BF)
    return out, (probs, tanh)


def attend_back(saved, queries, keys, values, d_out):
    probs, tanh = saved
    d_probs = dot_t(d_out, values)
    inner = jnp.sum(probs * d_probs, axis=1, keepdims=True)
    d_raw = (probs * (d_probs - inner) * (1.0 - tanh * tanh)).astype(BF)
    d_queries = dot(d_raw, keys) * SCALE
    d_keys = t_dot(d_raw, queries) * SCALE
    d_values = t_dot(probs.astype(BF), d_out)
    return d_queries, d_keys, d_values


MESH = pl.DeviceIdType.MESH
UNIT = 256
TILE = 256


def layer_kernel(
    first_row, gains_own, cos_hbm, sin_hbm, x_hbm, cot_hbm, own_qkv, own_out, own_gate, own_up, own_down,
    out_hbm, ffn_in_hbm, hidden_hbm, d_ffn_hbm, d_gate_hbm, d_up_hbm, d_attn_hbm, d_heads_hbm,
    d_mid_hbm, gains_out, norm_out, attn_in_hbm, heads_hbm, pack_hbm, w_qkv_hbm, w_out_hbm,
    attn_hbm, slope_hbm, value_hbm,
    in_grad_hbm, own_hbm, by_x_hbm, by_y_hbm, core_hbm, far_hbm, kv_hbm, d_proj_hbm,
    weights, w_qkv, send, near, across, total, xb, cb, ab, act, act_t, stage, d_heads, angle,
    line_send, line_recv, credit, local, ag_send, ag_recv, ag_local, gain_send, gain_recv, kv_sem,
    load_sem, rs_send, rs_recv, rs_local, kv_back, proj_sem,
    gain_ref, scale_ref, cast, squares, cast_sem, fin_sem, tail_send, tail_recv, z_send, z_recv,
):
    dp, core, z = lax.axis_index("dp"), lax.axis_index("ctx"), lax.axis_index("mp")
    w_out = w_qkv.at[:, : w_out_hbm.shape[1]]
    width, units = xb.shape[1], weights.shape[2]
    rows_own = own_qkv.shape[0]
    half = rows_own // 2
    inner = (z == 1) | (z == 2)
    outer = (z == 0) | (z == 3)
    x_peer, y_peer = (dp ^ 1, core, z), (dp ^ 2, core, z)
    core_peer = (dp, 1 - core, z)
    near_peer = (dp, core, z ^ 1)
    far_peer = (dp, core, 3 - z)

    barrier = pltpu.get_barrier_semaphore()
    group = [(dp ^ (m // 2), (1 - core) if m % 2 else core, z) for m in range(1, 8)]
    line = [(dp, core, z ^ m) for m in range(1, 4)]
    for peer in (*group, *line):
        pl.semaphore_signal(barrier, inc=1, device_id=peer, device_id_type=MESH)

    def block(mask, other=False, low=0, size=rows_own):
        owner = (dp ^ mask) * 2 + ((1 - core) if other else core)
        return pl.ds(pl.multiple_of(owner * rows_own + low, 16), size)

    owns = (own_qkv, own_out, own_gate, own_up, own_down)
    wholes = (w_qkv, w_out_hbm, weights.at[0], weights.at[1], weights.at[2])

    def gather(w, name, recv=False):
        table = {
            "x": (0, block(0), x_peer, block(1)),
            "y": (1, block(0), y_peer, block(2)),
            "top": (2, block(2, False, 0, half), x_peer, block(3, False, 0, half)),
            "low": (3, block(1, False, half, half), y_peer, block(3, False, half, half)),
            "own_c": (4, block(0), core_peer, block(0, True)),
            "x_c": (5, block(1), core_peer, block(1, True)),
            "y_c": (6, block(2), core_peer, block(2, True)),
            "top_c": (7, block(3, False, 0, half), core_peer, block(3, True, 0, half)),
            "low_c": (8, block(3, False, half, half), core_peer, block(3, True, half, half)),
        }
        index, out_rows, peer, in_rows = table[name]
        rows = in_rows if recv else out_rows
        direct = w < 2 and name in ("x", "y", "own_c")
        src = owns[w] if direct else wholes[w].at[rows]
        return pltpu.make_async_remote_copy(
            src_ref=src, dst_ref=wholes[w].at[rows], send_sem=ag_send.at[w, index],
            recv_sem=ag_recv.at[w, index], device_id=peer, device_id_type=MESH,
        )

    def own_copy(w):
        return pltpu.make_async_copy(owns[w], wholes[w].at[block(0)], ag_local.at[w])

    def round_own(w):
        size = cast.shape[1]
        steps = rows_own // size
        copies = [
            pltpu.make_async_copy(owns[w].at[pl.ds(c * size, size)], cast.at[c % 2], cast_sem.at[c % 2])
            for c in range(steps)
        ]
        copies[0].start()
        for c in range(steps):
            if c + 1 < steps:
                copies[c + 1].start()
            copies[c].wait()
            weights[w - 2, block(0, False, c * size, size)] = cast[c % 2].astype(BF)

    def gather_first(w):
        for name in ("x", "y", "own_c"):
            gather(w, name).start()
        if w < 2:
            own_copy(w).start()

    def gather_second(w):
        gather(w, "x", True).wait_recv()
        gather(w, "low").start()
        gather(w, "x_c").start()
        gather(w, "y", True).wait_recv()
        gather(w, "top").start()
        gather(w, "y_c").start()

    def gather_third(w):
        for name in ("top", "low"):
            gather(w, name, True).wait_recv()
            gather(w, name + "_c").start()

    def gather_end(w):
        for name in ("own_c", "x_c", "y_c", "top_c", "low_c"):
            gather(w, name, True).wait_recv()
        if w < 2:
            own_copy(w).wait()
        for name in ("x", "y", "top", "low", "own_c", "x_c", "y_c", "top_c", "low_c"):
            gather(w, name).wait_send()

    def hop(kind, i):
        src = (send.at[i % 3], send.at[i % 3], total.at[i % 4])[kind]
        dst = (near.at[i % 3], across.at[i % 2], total.at[i % 4])[kind]
        return pltpu.make_async_remote_copy(
            src_ref=src, dst_ref=dst, send_sem=line_send.at[kind, i % 4],
            recv_sem=line_recv.at[kind, i % 4],
            device_id=far_peer if kind == 1 else near_peer, device_id_type=MESH,
        )

    def add_rows(dst, a, b):
        @pl.loop(0, UNIT // 16)
        def _(r):
            rows = pl.ds(pl.multiple_of(r * 16, 16), 16)
            dst[rows] = (a[rows].astype(F32) + b[rows].astype(F32)).astype(BF)

    def boundary(up=None, cross=None, back=None, done=None):
        @pl.when(outer)
        def _():
            if done is not None:
                hop(2, done).wait_recv()
            if cross is not None:
                hop(0, cross).wait_send()
            if up is not None:
                hop(0, up).start()

        @pl.when(inner)
        def _():
            if cross is not None:
                hop(0, cross).wait_recv()
                add_rows(send.at[cross % 3], send.at[cross % 3], near.at[cross % 3])
                if not isinstance(cross, int) or cross >= 2:
                    pl.semaphore_wait(credit, 1)
                hop(1, cross).start()
            if back is not None:
                hop(1, back).wait_recv()
                hop(1, back).wait_send()
                add_rows(total.at[back % 4], send.at[back % 3], across.at[back % 2])
                if not isinstance(back, int) or back < 14:
                    pl.semaphore_signal(credit, inc=1, device_id=far_peer, device_id_type=MESH)
                hop(2, back).start()
            if done is not None:
                hop(2, done).wait_send()

    def rows_of(u):
        return pl.ds(pl.multiple_of(u * UNIT, UNIT), UNIT)

    def load(ref, u, dst, sem):
        return pltpu.make_async_copy(ref.at[rows_of(u)], dst, local.at[sem])

    def store(src, ref, u, sem):
        return pltpu.make_async_copy(src, ref.at[rows_of(u)], local.at[sem])

    def store_t(ref, u, sem):
        return pltpu.make_async_copy(act_t, ref.at[:, rows_of(u)], local.at[sem])

    def turn(source=None):
        source = act if source is None else source

        @pl.loop(0, width // TILE)
        def _(n):
            act_t[tile(n)] = source[:, tile(n)].T

    def tile(n):
        return pl.ds(pl.multiple_of(n * TILE, TILE), TILE)

    def each_rows(body):
        @pl.loop(0, UNIT // 16)
        def _(r):
            body(pl.ds(pl.multiple_of(r * 16, 16), 16))

    def scale(i):
        return scale_ref[i : i + 1]

    def add_gain(index, v):
        gain_ref[index] += v[:8] + v[8:]

    def project_out(u, k):
        dst = send.at[k % 3]

        @pl.loop(0, width // TILE)
        def _(n):
            dst[:, tile(n)] = dot_t(act[:, 2 * HEAD * u : 2 * HEAD * (u + 1)], w_out[tile(n)]).astype(BF)

    def middle(rows, u4):
        attn = total[u4, rows].astype(F32) if u4 is not None else ab[rows].astype(F32)
        r_two = inverse_rms(attn)
        return attn, r_two, xb[rows].astype(F32) + attn * r_two * scale(1)

    def forward(u, k, ready=None):
        load(x_hbm, u, xb, 0).start()
        store(total.at[u], attn_hbm, u, 1).start()
        load(x_hbm, u, xb, 0).wait()

        def body(rows):
            _, _, mid = middle(rows, u)
            act[rows] = (mid * inverse_rms(mid) * scale(2)).astype(BF)

        each_rows(body)
        turn()
        store_t(ffn_in_hbm, u, 2).start()

        @pl.loop(0, units // TILE)
        def _(f):
            gate = dot(act[...], weights[0, :, tile(f)])
            up = dot(act[...], weights[1, :, tile(f)])
            value, slope = gelu_parts(gate)
            stage[0, :, tile(f)] = (value * up).astype(BF)
            stage[1, :, tile(f)] = (slope * up).astype(BF)
            stage[2, :, tile(f)] = value.astype(BF)

        saves = ((0, hidden_hbm), (1, slope_hbm), (2, value_hbm))
        for i, ref in saves:
            store(stage.at[i], ref, u, 3 + i).start()
        if ready is not None:
            ready()
        dst = send.at[k % 3]

        @pl.loop(0, width // TILE)
        def _(n):
            dst[:, tile(n)] = dot_t(stage[0], weights[2, tile(n)]).astype(BF)

        for i, ref in saves:
            store(stage.at[i], ref, u, 3 + i).wait()
        store(total.at[u], attn_hbm, u, 1).wait()
        store_t(ffn_in_hbm, u, 2).wait()

    def backward(u, k):
        loads = (
            load(x_hbm, u, xb, 0), load(attn_hbm, u, ab, 1), load(cot_hbm, u, cb, 2),
            load(slope_hbm, u, stage.at[1], 4), load(value_hbm, u, stage.at[2], 5),
        )
        for copy in loads:
            copy.start()
        for copy in loads:
            copy.wait()

        def body(rows):
            _, _, mid = middle(rows, None)
            ffn = total[u, rows].astype(F32)
            r = inverse_rms(ffn)
            dy = cb[rows].astype(F32)
            xb[rows] = (mid + ffn * r * scale(3)).astype(BF)
            scaled = scale(3) * dy
            mean = jnp.mean(scaled * ffn, axis=-1, keepdims=True)
            act[rows] = (r * scaled - ffn * (r * r * r) * mean).astype(BF)
            add_gain(2, ffn * r * dy)

        each_rows(body)
        store(xb, out_hbm, u, 0).start()
        turn()
        store_t(d_ffn_hbm, u, 1).start()

        @pl.loop(0, units // TILE)
        def _(f):
            d_hidden = dot(act[...], weights[2, :, tile(f)])
            stage[1, :, tile(f)] = (d_hidden * stage[1, :, tile(f)].astype(F32)).astype(BF)
            stage[2, :, tile(f)] = (d_hidden * stage[2, :, tile(f)].astype(F32)).astype(BF)

        store(stage.at[1], d_gate_hbm, u, 4).start()
        store(stage.at[2], d_up_hbm, u, 5).start()
        dst = send.at[k % 3]

        @pl.loop(0, width // TILE)
        def _(n):
            part = dot_t(stage[1], weights[0, tile(n)]) + dot_t(stage[2], weights[1, tile(n)])
            dst[:, tile(n)] = part.astype(BF)

        store(xb, out_hbm, u, 0).wait()
        store_t(d_ffn_hbm, u, 1).wait()
        store(stage.at[1], d_gate_hbm, u, 4).wait()
        store(stage.at[2], d_up_hbm, u, 5).wait()

    def last_loads(u):
        return (load(x_hbm, u, xb, 0), load(attn_hbm, u, ab, 1), load(cot_hbm, u, cb, 2))

    def start_all(copies):
        for copy in copies:
            copy.start()

    def last(u):
        for copy in last_loads(u):
            copy.wait()

        def body(rows):
            attn, r_two, mid = middle(rows, None)
            r = inverse_rms(mid)
            dy = total[u, rows].astype(F32)
            scaled = scale(2) * dy
            mean = jnp.mean(scaled * mid, axis=-1, keepdims=True)
            grad = cb[rows].astype(F32) + r * scaled - mid * (r * r * r) * mean
            add_gain(1, mid * r * dy)
            cb[rows] = grad.astype(BF)
            scaled = scale(1) * grad
            mean = jnp.mean(scaled * attn, axis=-1, keepdims=True)
            act[rows] = (r_two * scaled - attn * (r_two * r_two * r_two) * mean).astype(BF)
            add_gain(0, attn * r_two * grad)

        each_rows(body)
        store(cb, d_mid_hbm, u, 0).start()
        turn()
        store_t(d_attn_hbm, u, 1).start()
        for h in range(w_out.shape[1] // TILE):
            columns = slice(h * TILE, (h + 1) * TILE)
            d_heads[:, columns] = dot(act[...], w_out[:, columns]).astype(BF)
        store(d_heads, d_heads_hbm, u, 2).start()
        store(cb, d_mid_hbm, u, 0).wait()
        store_t(d_attn_hbm, u, 1).wait()
        store(d_heads, d_heads_hbm, u, 2).wait()

    own_rows = pl.ds(pl.multiple_of((dp * 2 + core) * 16, 16), 16)

    def gain_copy(m, recv=False):
        peer = group[m - 1]
        owner = (peer[0] * 2 + peer[1]) if recv else (dp * 2 + core)
        return pltpu.make_async_remote_copy(
            src_ref=send.at[2, own_rows],
            dst_ref=send.at[2, own_rows if not recv else pl.ds(pl.multiple_of(owner * 16, 16), 16)],
            send_sem=gain_send.at[m], recv_sem=gain_recv.at[m], device_id=peer, device_id_type=MESH,
        )

    def gains_sum():
        whole = send[2, own_rows].astype(F32)
        for m in range(1, 8):
            gain_copy(m, True).wait_recv()
        for m in range(1, 8):
            owner = group[m - 1][0] * 2 + group[m - 1][1]
            whole += send[2, pl.ds(pl.multiple_of(owner * 16, 16), 16)].astype(F32)
        scale_ref[...] = 1.0 + whole[:8]
        for m in range(1, 8):
            gain_copy(m).wait_send()

    loaded = (stage.at[0], stage.at[1], stage.at[2], act)

    def first_norm(u):
        load(x_hbm, u, loaded[u], u).wait()

        def body(rows):
            x = loaded[u][rows].astype(F32)
            total[u, rows] = (x * inverse_rms(x) * scale(0)).astype(BF)

        each_rows(body)

    def first_turn(u):
        if u:
            store_t(attn_in_hbm, u - 1, 4).wait()
        turn(total.at[u])
        store_t(attn_in_hbm, u, 4).start()

    def angles(u):
        rows = rows_of(u)
        return (
            pltpu.make_async_copy(cos_hbm.at[rows], angle.at[u % 2, 0], local.at[2 * (u % 2)]),
            pltpu.make_async_copy(sin_hbm.at[rows], angle.at[u % 2, 1], local.at[2 * (u % 2) + 1]),
        )

    packs = (cb, ab)

    def kv_columns(kind, peer=False):
        side = (1 - core) if peer else core
        return pl.ds(pl.multiple_of(kind * 4 * HEAD + side * 2 * HEAD, HEAD), 2 * HEAD)

    def kv_copy(mb, kind, recv=False):
        part = packs[mb].at[:, kv_columns(kind, recv)]
        return pltpu.make_async_remote_copy(
            src_ref=part, dst_ref=part, send_sem=kv_sem.at[0, mb, kind], recv_sem=kv_sem.at[1, mb, kind],
            device_id=core_peer, device_id_type=MESH,
        )

    def projections(u):
        mb, b = divmod(u, 2)
        for copy in angles(u):
            copy.wait()
        if u < 3:
            for copy in angles(u + 1):
                copy.start()
        c, s = angle[u % 2, 0], angle[u % 2, 1]
        for j in range(4):
            v = dot(total[u], w_qkv[:, j * HEAD : (j + 1) * HEAD])
            if j < 2:
                xb[:, (mb * 4 + j * 2 + b) * HEAD : (mb * 4 + j * 2 + b + 1) * HEAD] = rotate(v, c, s).astype(BF)
            else:
                place = pl.multiple_of((j - 2) * 4 * HEAD + (core * 2 + b) * HEAD, HEAD)
                packs[mb][:, pl.ds(place, HEAD)] = (rotate(v, c, s) if j == 2 else v).astype(BF)

    def attention(mb):
        for kind in (0, 1):
            kv_copy(mb, kind, True).wait_recv()

        @pl.loop(0, 4)
        def _(i):
            h, b = i // 2, i % 2
            query = xb[:, pl.ds(pl.multiple_of(mb * 4 * HEAD + i * HEAD, HEAD), HEAD)]
            lowest = first_row[mb, :, pl.ds(pl.multiple_of(b * UNIT, UNIT), UNIT)]
            query_at = lax.broadcasted_iota(jnp.int32, (UNIT, UNIT), 1) + core * 2 * UNIT + b * UNIT
            weight, length = [], 0.0
            for j in range(4):
                key_at = lax.broadcasted_iota(jnp.int32, (UNIT, UNIT), 0) + j * UNIT
                score = dot_t(packs[mb][:, j * HEAD : (j + 1) * HEAD], query) * (SCALE / CAP)
                ok = (key_at <= query_at) & (key_at >= lowest)
                weight.append(jnp.where(ok, jnp.exp(CAP * jnp.tanh(score)), 0.0))
                length = length + jnp.sum(weight[j], axis=0, keepdims=True)
            inverse = 1.0 / length
            out = 0.0
            for j in range(4):
                value = packs[mb][:, (4 + j) * HEAD : (5 + j) * HEAD]
                out = out + t_dot((weight[j] * inverse).astype(BF), value)
            place = pl.multiple_of((mb * 2 + b) * 2 * HEAD + h * HEAD, HEAD)
            act[:, pl.ds(place, HEAD)] = out.astype(BF)

    def heads_store(u):
        return pltpu.make_async_copy(
            act.at[:, 2 * HEAD * u : 2 * HEAD * (u + 1)], heads_hbm.at[rows_of(u)], local.at[u]
        )

    def pack_store(i):
        return pltpu.make_async_copy((xb, cb, ab)[i], pack_hbm.at[i], ag_local.at[5 + i])

    for u in range(4):
        load(x_hbm, u, loaded[u], u).start()
    gain_ref[...] = jnp.zeros_like(gain_ref)
    send[2, own_rows] = gains_own[...].astype(BF)
    pl.semaphore_wait(barrier, 10)
    for m in range(1, 8):
        gain_copy(m).start()
    gather_first(0)
    gains_sum()
    for u in range(4):
        first_norm(u)
    for copy in angles(0):
        copy.start()
    first_turn(0)
    gather_second(0)
    first_turn(1)
    first_turn(2)
    gather_third(0)
    gather_first(1)
    first_turn(3)
    round_own(2)
    gather_end(0)
    qkv_store = pltpu.make_async_copy(w_qkv, w_qkv_hbm, local.at[5])
    qkv_store.start()
    for u in range(4):
        projections(u)
        if u % 2:
            for kind in (0, 1):
                kv_copy(u // 2, kind).start()
    gather_second(1)
    gather_first(2)
    attention(0)
    gather_third(1)
    gather_end(1)
    qkv_store.wait()
    store_t(attn_in_hbm, 3, 4).wait()
    out_load = pltpu.make_async_copy(w_out_hbm, w_out, local.at[4])
    out_load.start()
    out_load.wait()
    project_out(0, 0)
    boundary(0)
    project_out(1, 1)
    attention(1)
    project_out(2, 2)
    for i in range(3):
        pack_store(i).start()
    for u in range(4):
        heads_store(u).start()
    round_own(3)
    gather_second(2)
    gather_first(3)
    boundary(1, 0)
    gather_third(2)
    round_own(4)
    for kind in (0, 1):
        for mb in (0, 1):
            kv_copy(mb, kind).wait_send()
    for i in range(3):
        pack_store(i).wait()
    for u in range(4):
        heads_store(u).wait()
    boundary(2, 1, 0)
    project_out(3, 3)
    gather_second(3)
    gather_first(4)
    boundary(3, 2, 1, 0)
    gather_third(3)
    gather_end(2)
    gather_end(3)

    def ready():
        gather_second(4)
        gather_third(4)
        gather_end(4)

    forward(0, 4, ready)

    @pl.loop(4, 7)
    def _(k):
        boundary(k, k - 1, k - 2, k - 3)
        forward(k - 3, k + 1)

    @pl.loop(7, 11)
    def _(k):
        boundary(k, k - 1, k - 2, k - 3)
        backward(k - 7, k + 1)

    left, w_back = weights.at[0, :, : 4 * UNIT], weights.at[0, :, 4 * UNIT : 8 * UNIT]
    queries = weights.at[0, : 4 * UNIT, 8 * UNIT :]
    d_out = weights.at[0, 4 * UNIT : 8 * UNIT, 8 * UNIT :]
    right = weights.at[1, : 4 * UNIT]
    jobs = (
        (d_ffn_hbm, hidden_hbm), (ffn_in_hbm, d_gate_hbm), (ffn_in_hbm, d_up_hbm),
        (d_attn_hbm, heads_hbm), (attn_in_hbm, d_proj_hbm),
    )

    def columns(i):
        return jobs[i][1].shape[1]

    def core_out(m):
        low = 4 * UNIT + (m % 2) * rows_own
        return weights.at[1, low : low + rows_own]

    def arrived(m):
        low = 4 * UNIT + (2 + m % 2) * rows_own
        return weights.at[1, low : low + rows_own]

    def sums(i, m):
        low = ((i % 2) * 3 + m - 1) * rows_own
        return weights.at[2, low : low + rows_own]

    packed = weights.at[2, 6 * rows_own : 6 * rows_own + UNIT]
    own_sum = weights.at[2, 6 * rows_own + UNIT : 7 * rows_own + UNIT]

    def remote(src, dst, index, peer):
        return pltpu.make_async_remote_copy(
            src_ref=src, dst_ref=dst, send_sem=rs_send.at[index], recv_sem=rs_recv.at[index],
            device_id=peer, device_id_type=MESH,
        )

    def operands(i):
        pair = [pltpu.make_async_copy(jobs[i][1], right.at[:, : columns(i)], rs_local.at[1])]
        if i != 2:
            pair.append(pltpu.make_async_copy(jobs[i][0], left, rs_local.at[0]))
        return pair

    def core_copy(i, m):
        n = columns(i)
        return remote(core_out(m).at[:, :n], core_hbm.at[i, m, :, :n], (i, m), core_peer)

    def arrive(i, m):
        n = columns(i)
        return pltpu.make_async_copy(core_hbm.at[i, m, :, :n], arrived(m).at[:, :n], rs_local.at[2 + m % 2])

    def far_copy(i, way):
        n = columns(i)
        rows = slice(0, half) if way == 0 else slice(half, rows_own)
        peer = (x_peer, y_peer)[way]
        return remote(sums(i, 3).at[rows, :n], far_hbm.at[i, rows, :n], (i, 4 + way), peer)

    def final_copy(i, way):
        n = columns(i)
        dst = (by_x_hbm, by_y_hbm)[way]
        peer = (x_peer, y_peer)[way]
        return remote(sums(i, way + 1).at[:, :n], dst.at[i, :, :n], (i, 6 + way), peer)

    def own_store(i):
        n = columns(i)
        return pltpu.make_async_copy(own_sum.at[:, :n], own_hbm.at[i, :, :n], rs_local.at[5])

    def block_rows(mask, other):
        owner = (dp ^ mask) * 2 + ((1 - core) if other else core)
        return pl.ds(pl.multiple_of(owner * rows_own, 16), rows_own)

    def scatter_start(i):
        for copy in operands(i):
            copy.wait()
        piece = 768 if columns(i) % 768 == 0 else 512
        steps = columns(i) // piece

        def piece_at(n):
            return pl.ds(pl.multiple_of(n * piece, TILE), piece)

        for m in (3, 2, 1, 0):
            if m < 2:
                core_copy(i, m + 2).wait_send()
            elif i > 0:
                core_copy(i - 1, m - 2).wait_send()
            dst = core_out(m)

            @pl.loop(0, steps)
            def _(n):
                dst[:, piece_at(n)] = dot(left[block_rows(m, True)], right[:, piece_at(n)]).astype(BF)

            core_copy(i, m).start()
        if i > 1:
            for way in (0, 1):
                far_copy(i - 2, way).wait_send()
                final_copy(i - 2, way).wait_send()
        if i > 0:
            own_store(i - 1).wait()
        core_copy(i, 3).wait_recv()
        arrive(i, 3).start()
        for m in (3, 2, 1, 0):
            if m:
                core_copy(i, m - 1).wait_recv()
                arrive(i, m - 1).start()
            arrive(i, m).wait()
            dst, extra = (sums(i, m) if m else own_sum), arrived(m)

            @pl.loop(0, steps)
            def _(n):
                part = dot(left[block_rows(m, False)], right[:, piece_at(n)])
                dst[:, piece_at(n)] = (part + extra[:, piece_at(n)].astype(F32)).astype(BF)

            if m == 3:
                far_copy(i, 0).start()
                far_copy(i, 1).start()
        own_store(i).start()

    def operands_start(i):
        for copy in operands(i):
            copy.start()

    def scatter_end(i):
        n = columns(i)
        for way in (0, 1):
            far_copy(i, way).wait_recv()
        added = arrived(0)
        copy = pltpu.make_async_copy(far_hbm.at[i, :, :n], added.at[:, :n], rs_local.at[4])
        copy.start()
        copy.wait()
        for way in (1, 0):
            base = 0 if way == 1 else half
            dst = sums(i, way + 1)

            @pl.loop(0, half // 16)
            def _(r):
                rows = pl.ds(pl.multiple_of(base + r * 16, 16), 16)
                dst[rows, :n] = (dst[rows, :n].astype(F32) + added[rows, :n].astype(F32)).astype(BF)

            final_copy(i, way).start()

    def back_loads(mb):
        copies = [pltpu.make_async_copy(pack_hbm.at[1 + mb], packed, load_sem.at[8])]
        for i in range(4):
            h, b = divmod(i, 2)
            rows = pl.ds(i * UNIT, UNIT)
            query = pack_hbm.at[0, :, (mb * 4 + i) * HEAD : (mb * 4 + i + 1) * HEAD]
            grad = d_heads_hbm.at[pl.ds((2 * mb + b) * UNIT, UNIT), h * HEAD : (h + 1) * HEAD]
            copies.append(pltpu.make_async_copy(query, queries.at[rows], load_sem.at[i]))
            copies.append(pltpu.make_async_copy(grad, d_out.at[rows], load_sem.at[4 + i]))
        return [*copies, *angles(2 * mb), *angles(2 * mb + 1)]

    def unrotate(v, b):
        c, s = angle[b, 0], angle[b, 1]
        v, w = v[:, : HEAD // 2], v[:, HEAD // 2 :]
        return jnp.concatenate([v * c + w * s, w * c - v * s], axis=1)

    def kv_out(mb):
        return pltpu.make_async_remote_copy(
            src_ref=act_t.at[: 4 * UNIT], dst_ref=kv_hbm.at[mb], send_sem=kv_back.at[0, mb],
            recv_sem=kv_back.at[1, mb], device_id=core_peer, device_id_type=MESH,
        )

    def proj_store(u):
        part = stage.at[u // 2, :, (u % 2) * 4 * HEAD : (u % 2 + 1) * 4 * HEAD]
        return pltpu.make_async_copy(part, d_proj_hbm.at[rows_of(u)], proj_sem.at[u])

    def attention_back(mb):
        for copy in back_loads(mb):
            copy.start()
        for copy in back_loads(mb):
            copy.wait()
        d_scores, weights_of = (xb, ab), (act, cb)

        @pl.loop(0, 4)
        def _(i):
            h, b = i // 2, i % 2
            rows = pl.ds(pl.multiple_of(i * UNIT, UNIT), UNIT)
            query, grad = queries[rows], d_out[rows]
            lowest = first_row[mb, :, pl.ds(pl.multiple_of(b * UNIT, UNIT), UNIT)]
            query_at = lax.broadcasted_iota(jnp.int32, (UNIT, UNIT), 1) + core * 2 * UNIT + b * UNIT
            tanh, weight, d_probs, length, mean = [], [], [], 0.0, 0.0
            for j in range(4):
                key_at = lax.broadcasted_iota(jnp.int32, (UNIT, UNIT), 0) + j * UNIT
                ok = (key_at <= query_at) & (key_at >= lowest)
                score = dot_t(packed[:, j * HEAD : (j + 1) * HEAD], query) * (SCALE / CAP)
                tanh.append(jnp.tanh(score))
                weight.append(jnp.where(ok, jnp.exp(CAP * tanh[j]), 0.0))
                d_probs.append(dot_t(packed[:, (4 + j) * HEAD : (5 + j) * HEAD], grad))
                length = length + jnp.sum(weight[j], axis=0, keepdims=True)
                mean = mean + jnp.sum(weight[j] * d_probs[j], axis=0, keepdims=True)
            inverse = 1.0 / length
            mean = mean * inverse
            d_query = 0.0
            for j in range(4):
                probs = weight[j] * inverse
                d_raw = (probs * (d_probs[j] - mean) * (1.0 - tanh[j] * tanh[j])).astype(BF)
                place = pl.ds(pl.multiple_of((j % 2) * 4 * HEAD + i * HEAD, HEAD), HEAD)
                d_scores[j // 2][:, place] = d_raw
                weights_of[j // 2][:, place] = probs.astype(BF)
                d_query = d_query + t_dot(d_raw, packed[:, j * HEAD : (j + 1) * HEAD])
            place = pl.ds(pl.multiple_of(b * 4 * HEAD + h * HEAD, HEAD), HEAD)
            stage[mb, :, place] = unrotate(d_query * SCALE, b).astype(BF)

        def block_grads(j):
            place = slice((j % 2) * 4 * HEAD, (j % 2 + 1) * 4 * HEAD)
            d_key = dot(d_scores[j // 2][:, place], queries[...]) * SCALE
            return d_key, dot(weights_of[j // 2][:, place], d_out[...])

        for side in (0, 1):

            @pl.when(core == side)
            def _():
                for t in (0, 1):
                    d_key, d_value = block_grads((1 - side) * 2 + t)
                    act_t[t * UNIT : (t + 1) * UNIT] = d_key.astype(BF)
                    act_t[(2 + t) * UNIT : (3 + t) * UNIT] = d_value.astype(BF)

        kv_out(mb).start()
        kv_out(mb).wait_recv()
        copy = pltpu.make_async_copy(kv_hbm.at[mb], act_t.at[4 * UNIT : 8 * UNIT], rs_local.at[6])
        copy.start()
        copy.wait()
        for side in (0, 1):

            @pl.when(core == side)
            def _():
                for t in (0, 1):
                    d_key, d_value = block_grads(side * 2 + t)
                    d_key = d_key + act_t[(4 + t) * UNIT : (5 + t) * UNIT].astype(F32)
                    d_value = d_value + act_t[(6 + t) * UNIT : (7 + t) * UNIT].astype(F32)
                    low = t * 4 * HEAD
                    stage[mb, :, low + 2 * HEAD : low + 3 * HEAD] = unrotate(d_key, t).astype(BF)
                    stage[mb, :, low + 3 * HEAD : low + 4 * HEAD] = d_value.astype(BF)

        proj_store(2 * mb).start()
        proj_store(2 * mb + 1).start()
        kv_out(mb).wait_send()

    def project_back(u):
        dst = send.at[(12 + u) % 3]
        low = (u % 2) * 4 * HEAD

        @pl.loop(0, width // TILE)
        def _(n):
            dst[:, tile(n)] = dot_t(stage[u // 2, :, low : low + 4 * HEAD], w_back[tile(n)]).astype(BF)

    def first_loads(u):
        return (load(x_hbm, u, xb, 0), load(d_mid_hbm, u, ab, 1))

    def first_back(u):
        for copy in first_loads(u):
            copy.wait()

        def body(rows):
            x = xb[rows].astype(F32)
            r_one = inverse_rms(x)
            dy = total[u, rows].astype(F32)
            scaled = scale(0) * dy
            mean = jnp.mean(scaled * x, axis=-1, keepdims=True)
            back = r_one * scaled - x * (r_one * r_one * r_one) * mean
            ab[rows] = (ab[rows].astype(F32) + back).astype(BF)
            add_gain(3, x * r_one * dy)

        each_rows(body)
        store(ab, in_grad_hbm, u, 2).start()
        store(ab, in_grad_hbm, u, 2).wait()
        if u < 3:
            start_all(first_loads(u + 1))

    def finish(i):
        n = columns(i)
        for way in (0, 1):
            final_copy(i, way).wait_recv()
        for low in (0, half):
            pairs = ((own_hbm, cb), (by_x_hbm, act), (by_y_hbm, stage.at[2]))
            copies = [
                pltpu.make_async_copy(ref.at[i, low : low + half, :n], dst.at[:half, :n], fin_sem.at[j])
                for j, (ref, dst) in enumerate(pairs)
            ]
            start_all(copies)
            for copy in copies:
                copy.wait()

            @pl.loop(0, half // 16)
            def _(r):
                rows = pl.ds(pl.multiple_of(r * 16, 16), 16)
                v = cb[rows, :n].astype(F32) + act[rows, :n].astype(F32) + stage[2, rows, :n].astype(F32)
                v = v * v
                gain_ref[4, :, :n] += v[:8] + v[8:]

    table = weights.at[1, 4 * UNIT + 4 * rows_own :]

    def table_copy(m, recv=False):
        peer = group[m - 1]
        owner = (peer[0] * 2 + peer[1]) if recv else (dp * 2 + core)
        rows = pl.ds(pl.multiple_of(owner * 16, 16), 16)
        return pltpu.make_async_remote_copy(
            src_ref=table.at[own_rows], dst_ref=table.at[rows], send_sem=tail_send.at[m],
            recv_sem=tail_recv.at[m], device_id=peer, device_id_type=MESH,
        )

    def square_copy(m, recv=False):
        place = (z ^ m) if recv else z
        return pltpu.make_async_remote_copy(
            src_ref=squares.at[z], dst_ref=squares.at[place], send_sem=z_send.at[m],
            recv_sem=z_recv.at[m], device_id=line[m - 1], device_id_type=MESH,
        )

    def agree():
        rows = [jnp.sum(gain_ref[i], axis=0, keepdims=True) for i in (3, 0, 1, 2, 4)]
        high = [v.astype(BF).astype(F32) for v in rows]
        low = [v - h for v, h in zip(rows, high)]
        blank = jnp.zeros((6, rows[0].shape[1]), F32)
        table[own_rows] = jnp.concatenate([*high, *low, blank], axis=0).astype(BF)
        for m in range(1, 8):
            table_copy(m).start()
        for m in range(1, 8):
            table_copy(m, True).wait_recv()
        whole = jnp.zeros((16, rows[0].shape[1]), F32)
        for owner in range(8):
            whole = whole + table[owner * 16 : owner * 16 + 16].astype(F32)
        gains = whole[0:4] + whole[5:9]
        squares[z] = jnp.broadcast_to(jnp.sum(whole[4:5] + whole[9:10], axis=1, keepdims=True), (8, 128))
        for m in range(1, 4):
            square_copy(m).start()
        gains_out[0:4] = gains
        gains_out[4:8] = jnp.zeros_like(gains)
        gain_square = jnp.sum(jnp.sum(gains * gains, axis=1, keepdims=True), axis=0, keepdims=True)
        for m in range(1, 4):
            square_copy(m, True).wait_recv()
        norm_out[...] = jnp.sqrt(squares[0] + squares[1] + squares[2] + squares[3] + gain_square)
        for m in range(1, 8):
            table_copy(m).wait_send()
        for m in range(1, 4):
            square_copy(m).wait_send()

    w_load = pltpu.make_async_copy(w_qkv_hbm, w_back, rs_local.at[7])
    operands_start(0)
    w_load.start()
    start_all(last_loads(0))
    boundary(11, 10, 9, 8)
    scatter_start(0)
    operands_start(1)
    last(0)
    start_all(last_loads(1))
    boundary(None, 11, 10, 9)
    scatter_end(0)
    last(1)
    attention_back(0)
    start_all(last_loads(2))
    w_load.wait()
    project_back(0)
    boundary(12, None, 11, 10)
    project_back(1)
    last(2)
    start_all(last_loads(3))
    scatter_start(1)
    operands_start(2)
    boundary(13, 12, None, 11)
    scatter_end(1)
    last(3)
    attention_back(1)
    start_all(first_loads(0))
    project_back(2)
    boundary(14, 13, 12)
    project_back(3)
    scatter_start(2)
    operands_start(3)
    boundary(15, 14, 13, 12)
    scatter_end(2)
    first_back(0)
    scatter_start(3)
    for u in range(4):
        proj_store(u).wait()
    operands_start(4)
    finish(0)
    finish(1)
    boundary(None, 15, 14, 13)
    scatter_end(3)
    scatter_start(4)
    first_back(1)
    boundary(None, None, 15, 14)
    scatter_end(4)
    own_store(4).wait()
    first_back(2)
    finish(2)
    finish(3)
    boundary(None, None, None, 15)
    first_back(3)
    finish(4)
    agree()
    for m in range(2):
        core_copy(4, m).wait_send()
    for i in range(3, 5):
        for way in (0, 1):
            far_copy(i, way).wait_send()
            final_copy(i, way).wait_send()


def layer_call(first_row, gains_own, cosine, sine, x, cot, owns):
    tokens, width = x.shape
    units = owns[2].shape[1]
    qkv_cols, out_cols = owns[0].shape[1], owns[1].shape[1]
    assert tokens == 4 * UNIT
    full = jax.ShapeDtypeStruct((tokens, width), BF)
    wide = jax.ShapeDtypeStruct((tokens, units), BF)
    flipped = jax.ShapeDtypeStruct((width, tokens), BF)
    rows = owns[0].shape[0]
    part = jax.ShapeDtypeStruct((5, rows, units), BF)
    heads = jax.ShapeDtypeStruct((tokens, out_cols), BF)
    outs = (
        full, flipped, wide, flipped, wide, wide, flipped, heads, full,
        jax.ShapeDtypeStruct((8, width), F32),
        jax.ShapeDtypeStruct((8, 128), F32),
        flipped,
        heads,
        jax.ShapeDtypeStruct((3, UNIT, width), BF),
        jax.ShapeDtypeStruct((width, qkv_cols), BF),
        jax.ShapeDtypeStruct((width, out_cols), BF),
        full, wide, wide,
        full, part, part, part,
        jax.ShapeDtypeStruct((5, 4, rows, units), BF),
        part,
        jax.ShapeDtypeStruct((2, tokens, HEAD), BF),
        jax.ShapeDtypeStruct((tokens, qkv_cols), BF),
    )
    anywhere, vmem = pl.BlockSpec(memory_space=pl.ANY), pl.BlockSpec(memory_space=pltpu.VMEM)
    dma = pltpu.SemaphoreType.DMA
    return pl.pallas_call(
        layer_kernel,
        out_shape=outs,
        in_specs=[vmem] * 2 + [anywhere] * 9,
        out_specs=[anywhere] * 9 + [vmem] * 2 + [anywhere] * 16,
        scratch_shapes=[
            pltpu.VMEM((3, width, units), BF),
            pltpu.VMEM((width, qkv_cols), BF),
            pltpu.VMEM((3, UNIT, width), BF),
            pltpu.VMEM((3, UNIT, width), BF),
            pltpu.VMEM((2, UNIT, width), BF),
            pltpu.VMEM((4, UNIT, width), BF),
            pltpu.VMEM((UNIT, width), BF),
            pltpu.VMEM((UNIT, width), BF),
            pltpu.VMEM((UNIT, width), BF),
            pltpu.VMEM((UNIT, width), BF),
            pltpu.VMEM((width, UNIT), BF),
            pltpu.VMEM((3, UNIT, units), BF),
            pltpu.VMEM((UNIT, out_cols), BF),
            pltpu.VMEM((2, 2, UNIT, HEAD // 2), F32),
            dma((3, 4)),
            dma((3, 4)),
            pltpu.SemaphoreType.REGULAR,
            dma((6,)),
            dma((5, 9)),
            dma((5, 9)),
            dma((8,)),
            dma((8,)),
            dma((8,)),
            dma((2, 2, 2)),
            dma((9,)),
            dma((5, 8)),
            dma((5, 8)),
            dma((8,)),
            dma((2, 2)),
            dma((4,)),
            pltpu.VMEM((5, 8, width), F32),
            pltpu.VMEM((8, width), F32),
            pltpu.VMEM((2, 32, units), F32),
            pltpu.VMEM((4, 8, 128), F32),
            dma((2,)),
            dma((3,)),
            dma((8,)),
            dma((8,)),
            dma((4,)),
            dma((4,)),
        ],
        compiler_params=pltpu.CompilerParams(
            collective_id=1, has_side_effects=True, vmem_limit_bytes=63 * 2**20
        ),
        name="layer",
    )(first_row, gains_own, cosine, sine, x, cot, *owns)


def fast_device(
    sizes,
    inputs,
    segment_ids,
    positions,
    cotangent,
    *params,
):
    masters, moments = params[:11], params[11:]
    batches, seqs, tokens, width = inputs.shape
    assert seqs == 1
    q_cols, k_cols = masters[0].shape[1], masters[1].shape[1]
    width_ff = masters[4].shape[1]
    assert k_cols == HEAD

    own = masters[7].shape[0]
    place = (lax.axis_index("dp") * sizes["ctx"] + lax.axis_index("ctx")) * own
    low = [w.astype(BF) for w in masters[:4]]
    owns = (jnp.concatenate(low[:3], axis=1), low[3], *masters[4:7])
    gains_own = jnp.zeros((16, width), F32)
    gains_own = lax.dynamic_update_slice(gains_own, jnp.stack(masters[7:]), (0, place))
    start = lax.axis_index("ctx") * tokens
    frequency = jnp.exp(
        jnp.arange(HEAD // 2, dtype=F32) * (-2.0 * math.log(10000.0) / HEAD)
    )
    angle = positions.reshape(-1).astype(F32)[:, None] * frequency
    cosine, sine = jnp.cos(angle), jnp.sin(angle)
    first_row = (start + jnp.arange(tokens, dtype=jnp.int32))[None, None] - positions
    flat = (batches * tokens, width)
    x = inputs.reshape(flat)
    outs = layer_call(first_row, gains_own, cosine, sine, x, cotangent.reshape(flat), owns)
    output, gain_grads, norm_tile = outs[0], outs[9], outs[10]
    input_grad, own_sum, by_x, by_y = outs[19:23]

    def final_sum(i, cols):
        picked = [v[i, :, :cols].astype(F32) for v in (own_sum, by_x, by_y)]
        return picked[0] + picked[1] + picked[2]

    qkv_cols = owns[0].shape[1]
    s_down, s_gate, s_up = [final_sum(i, width_ff) for i in range(3)]
    s_out, s_qkv = final_sum(3, q_cols), final_sum(4, qkv_cols)
    summed = (
        s_qkv[:, :q_cols], s_qkv[:, q_cols : q_cols + k_cols], s_qkv[:, q_cols + k_cols :],
        s_out, s_gate, s_up, s_down,
    )
    norm_value = norm_tile[0, 0]
    factor = 1.0 / jnp.maximum(norm_value, 1.0)
    own_gains = lax.dynamic_slice_in_dim(gain_grads, place, own, 1)
    summed += tuple(own_gains[i] for i in range(4))
    new_moments = tuple(0.5 * m + 0.5 * factor * g for m, g in zip(moments, summed))
    changes = tuple(-RATE * (m + 0.01 * w) for w, m in zip(masters[:7], new_moments[:7]))

    return (
        output.reshape(inputs.shape),
        input_grad.reshape(inputs.shape), norm_value.reshape(1), *changes, *new_moments
    )


def per_device(
    sizes,
    inputs,
    segment_ids,
    positions,
    cotangent,
    *params,
):
    masters, moments = params[:11], params[11:]
    batches, seqs, tokens, width = inputs.shape
    assert seqs == 1
    full_len = segment_ids.shape[2]
    q_cols, k_cols = masters[0].shape[1], masters[1].shape[1]
    heads = q_cols // HEAD
    assert k_cols == HEAD
    cuts = 2 if tokens >= 512 else 1
    unit = tokens // cuts

    low = [w.astype(BF) for w in masters[:7]]
    qkv_own = jnp.concatenate(low[:3], axis=1)
    gains_own = jnp.stack([g.astype(BF) for g in masters[7:]], axis=1)
    gains = lax.all_gather(gains_own, ("dp", "ctx"), axis=0, tiled=True).astype(F32)
    gain_one, gain_two, gain_three, gain_four = [gains[:, i] for i in range(4)]
    w_qkv, mark = gather_rows(qkv_own, sizes, None)
    w_out, mark = gather_rows(low[3], sizes, mark)
    w_gate, mark = gather_rows(low[4], sizes, mark)
    w_up, mark = gather_rows(low[5], sizes, mark)
    w_down, mark = gather_rows(low[6], sizes, mark)

    start = lax.axis_index("ctx") * tokens
    causal = (start + jnp.arange(tokens))[:, None] >= jnp.arange(full_len)[None, :]
    frequency = jnp.exp(
        jnp.arange(HEAD // 2, dtype=F32) * (-2.0 * math.log(10000.0) / HEAD)
    )

    state = []
    for mb in range(batches):
        x = inputs[mb, 0].astype(F32)
        r_one = inverse_rms(x)
        attn_in = (x * r_one * (1.0 + gain_one)).astype(BF)
        angles = positions[mb, 0].astype(F32)[:, None] * frequency
        cosine, sine = jnp.cos(angles), jnp.sin(angles)
        seg = segment_ids[mb, 0]
        seg_local = lax.dynamic_slice_in_dim(seg, start, tokens)
        allowed = causal & (seg_local[:, None] == seg[None, :])
        proj = dot(attn_in, w_qkv)
        queries = jnp.concatenate(
            [rotate(proj[:, h * HEAD : (h + 1) * HEAD], cosine, sine) for h in range(heads)]
        ).astype(BF)
        keys = rotate(proj[:, q_cols : q_cols + HEAD], cosine, sine).astype(BF)
        values = proj[:, q_cols + HEAD :].astype(BF)
        both = swap_ctx(jnp.concatenate([keys, values], axis=1), sizes)
        keys_all, values_all = both[:, :HEAD], both[:, HEAD:]
        out, saved = attend(queries, keys_all, values_all, allowed)
        heads_out = jnp.concatenate(jnp.split(out, heads, axis=0), axis=1)
        state.append(
            dict(
                x=x, r_one=r_one, attn_in=attn_in, cosine=cosine, sine=sine, queries=queries,
                keys=keys_all, values=values_all, saved=saved, heads_out=heads_out,
            )
        )

    units = [(mb, cut) for mb in range(batches) for cut in range(cuts)]
    work = []
    for mb, cut in units:
        rows = slice(cut * unit, (cut + 1) * unit)
        part = dot_t(state[mb]["heads_out"][rows], w_out).astype(BF)
        work.append(dict(rows=rows, mb=mb, attn_low=sum_mp(part, sizes)))
    for w in work:
        attn = w["attn_low"].astype(F32)
        r_two = inverse_rms(attn)
        mid = state[w["mb"]]["x"][w["rows"]] + attn * r_two * (1.0 + gain_two)
        r_three = inverse_rms(mid)
        ffn_in = (mid * r_three * (1.0 + gain_three)).astype(BF)
        gate, up = dot(ffn_in, w_gate), dot(ffn_in, w_up)
        value, slope = gelu_parts(gate)
        hidden = (value * up).astype(BF)
        part = dot_t(hidden, w_down).astype(BF)
        w.update(
            mid=mid, r_two=r_two, r_three=r_three, ffn_in=ffn_in, gate=gate, up=up, hidden=hidden,
            ffn_low=sum_mp(part, sizes),
        )
    for w in work:
        ffn = w["ffn_low"].astype(F32)
        r_four = inverse_rms(ffn)
        grad = cotangent[w["mb"], 0][w["rows"]].astype(F32)
        w["output"] = (w["mid"] + ffn * r_four * (1.0 + gain_four)).astype(BF)
        d_ffn, w["g_four"] = norm_back(ffn, r_four, gain_four, grad)
        d_ffn = d_ffn.astype(BF)
        d_hidden = dot(d_ffn, w_down)
        value, slope = gelu_parts(w["gate"])
        d_gate = (d_hidden * w["up"] * slope).astype(BF)
        d_up = (d_hidden * value).astype(BF)
        part = (dot_t(d_gate, w_gate) + dot_t(d_up, w_up)).astype(BF)
        w.update(grad=grad, d_ffn=d_ffn, d_gate=d_gate, d_up=d_up, d_in_low=sum_mp(part, sizes))
    for w in work:
        d_in = w["d_in_low"].astype(F32)
        back, w["g_three"] = norm_back(w["mid"], w["r_three"], gain_three, d_in)
        d_mid = w["grad"] + back
        attn = w["attn_low"].astype(F32)
        d_attn, w["g_two"] = norm_back(attn, w["r_two"], gain_two, d_mid)
        d_attn = d_attn.astype(BF)
        w.update(d_mid=d_mid, d_attn=d_attn, d_heads=dot(d_attn, w_out).astype(BF))

    def rows_of(key):
        return jnp.concatenate([w[key] for w in work])

    ffn_in = rows_of("ffn_in")
    g_down = t_dot(rows_of("d_ffn"), rows_of("hidden"))
    g_gate = t_dot(ffn_in, rows_of("d_gate"))
    g_up = t_dot(ffn_in, rows_of("d_up"))
    s_down, mark = scatter_rows(g_down, sizes, None)
    s_gate, mark = scatter_rows(g_gate, sizes, mark)
    s_up, mark = scatter_rows(g_up, sizes, mark)

    for mb in range(batches):
        s = state[mb]
        d_heads = jnp.concatenate([w["d_heads"] for w in work if w["mb"] == mb])
        d_out = jnp.concatenate(jnp.split(d_heads, heads, axis=1))
        d_queries, d_keys, d_values = attend_back(
            s["saved"], s["queries"], s["keys"], s["values"], d_out
        )
        d_kv = scatter_ctx(jnp.concatenate([d_keys, d_values], axis=1), sizes)
        pieces = [rotate(q, s["cosine"], -s["sine"]) for q in jnp.split(d_queries, heads)]
        pieces += [rotate(d_kv[:, :HEAD], s["cosine"], -s["sine"]), d_kv[:, HEAD:]]
        s["d_proj"] = jnp.concatenate(pieces, axis=1).astype(BF)
    for w in work:
        part = dot_t(state[w["mb"]]["d_proj"][w["rows"]], w_qkv).astype(BF)
        w["d_attn_in"] = sum_mp(part, sizes)

    g_out = t_dot(rows_of("d_attn"), jnp.concatenate([s["heads_out"] for s in state]))
    g_qkv = t_dot(
        jnp.concatenate([s["attn_in"] for s in state]),
        jnp.concatenate([s["d_proj"] for s in state]),
    )
    s_out, mark = scatter_rows(g_out, sizes, mark)
    s_qkv, mark = scatter_rows(g_qkv, sizes, mark)

    for w in work:
        s = state[w["mb"]]
        back, w["g_one"] = norm_back(
            s["x"][w["rows"]], s["r_one"][w["rows"]], gain_one, w["d_attn_in"].astype(F32)
        )
        w["input_grad"] = (w["d_mid"] + back).astype(BF)

    gain_grads = jnp.stack(
        [sum(w[key] for w in work) for key in ("g_one", "g_two", "g_three", "g_four")]
    )
    gain_grads = sum_small(gain_grads, ("ctx", "dp"), sizes)
    summed = (
        s_qkv[:, :q_cols], s_qkv[:, q_cols : q_cols + k_cols], s_qkv[:, q_cols + k_cols :],
        s_out, s_gate, s_up, s_down,
    )
    weight_sq = sum(jnp.sum(g * g) for g in (s_qkv, s_out, s_gate, s_up, s_down))
    weight_sq = sum_small(weight_sq.reshape(1, 1), ("ctx", "dp", "mp"), sizes)[0, 0]
    norm_value = jnp.sqrt(weight_sq + jnp.sum(gain_grads * gain_grads))
    factor = 1.0 / jnp.maximum(norm_value, 1.0)
    own = masters[7].shape[0]
    place = (lax.axis_index("dp") * sizes["ctx"] + lax.axis_index("ctx")) * own
    own_gains = lax.dynamic_slice_in_dim(gain_grads, place, own, 1)
    summed += tuple(own_gains[i] for i in range(4))
    new_moments = tuple(0.5 * m + 0.5 * factor * g for m, g in zip(moments, summed))
    changes = tuple(-RATE * (m + 0.01 * w) for w, m in zip(masters[:7], new_moments[:7]))

    def whole(key):
        return rows_of(key).reshape(inputs.shape)

    return (
        whole("output"), whole("input_grad"), norm_value.reshape(1), *changes, *new_moments
    )


def solution(mesh):
    sizes = dict(mesh.shape)
    weight, vector = P(("dp", "ctx"), "mp"), P(("dp", "ctx"))
    params = (weight,) * 7 + (vector,) * 4
    data = P(None, "dp", "ctx", None)

    def run(*args):
        batches, _, tokens, _ = args[0].shape
        fast = sizes == dict(dp=4, ctx=2, mp=4) and batches == 2 and tokens == 2 * UNIT
        return (fast_device if fast else per_device)(sizes, *args)

    return jax.shard_map(
        run,
        mesh=mesh,
        in_specs=(data, P(None, "dp", None), P(None, "dp", "ctx"), data) + params + params,
        out_specs=(data, data, P()) + (weight,) * 7 + params,
        check_vma=False,
    )
```

```python
import math

import jax
import jax.numpy as jnp
from jax import lax
from jax.experimental import pallas as pl
from jax.experimental.pallas import tpu as pltpu
from jax.sharding import PartitionSpec as P

HEAD = 256
STEP = 10
EPS = 1e-06
CAP = 50.0
RATE = 1.0 / math.sqrt(1.0 + STEP / 1000.0)
SCALE = HEAD ** (-0.5)
BF = jnp.bfloat16
F32 = jnp.float32


def flip(axis, size, mask):
    return dict(axis_name=axis, perm=[(i, i ^ mask) for i in range(size)])


def after(value, other):
    return lax.optimization_barrier((value, other))[0]


def gather_rows(own, sizes, wait):
    dp, ctx = sizes["dp"], sizes["ctx"]
    rows, cols = own.shape
    if wait is not None:
        own = after(own, wait)
    if dp != 4:
        out = lax.all_gather(own, ("dp", "ctx"), axis=0, tiled=True)
        return out, own
    me = lax.axis_index("dp")
    half = rows // 2 // 16 * 16
    from_x = lax.ppermute(own, **flip("dp", dp, 1))
    from_y = lax.ppermute(own, **flip("dp", dp, 2))
    far_top = lax.ppermute(from_y[:half], **flip("dp", dp, 1))
    far_low = lax.ppermute(from_x[half:], **flip("dp", dp, 2))
    mine = jnp.zeros((dp, rows, cols), own.dtype)
    mine = lax.dynamic_update_slice(mine, own[None], (me, 0, 0))
    mine = lax.dynamic_update_slice(mine, from_x[None], (me ^ 1, 0, 0))
    mine = lax.dynamic_update_slice(mine, from_y[None], (me ^ 2, 0, 0))
    mine = lax.dynamic_update_slice(mine, far_top[None], (me ^ 3, 0, 0))
    mine = lax.dynamic_update_slice(mine, far_low[None], (me ^ 3, half, 0))
    if ctx == 2:
        other = lax.ppermute(mine, **flip("ctx", ctx, 1))
        core = lax.axis_index("ctx")
        out = jnp.zeros((dp, ctx, rows, cols), own.dtype)
        out = lax.dynamic_update_slice(out, mine[:, None], (0, core, 0, 0))
        out = lax.dynamic_update_slice(out, other[:, None], (0, 1 - core, 0, 0))
    else:
        out = lax.all_gather(mine, "ctx", axis=1)
    return out.reshape(dp * ctx * rows, cols), from_x


def scatter_rows(full, sizes, wait):
    dp, ctx = sizes["dp"], sizes["ctx"]
    full = full.astype(BF)
    if wait is not None:
        full = after(full, wait)
    rows = full.shape[0] // (dp * ctx)
    cols = full.shape[1]
    if dp != 4:
        out = lax.psum_scatter(full, ("dp", "ctx"), scatter_dimension=0, tiled=True)
        return out.astype(F32), out
    blocks = full.reshape(dp, ctx, rows, cols)
    if ctx == 2:
        core = lax.axis_index("ctx")
        send = lax.dynamic_index_in_dim(blocks, 1 - core, 1, keepdims=False)
        keep = lax.dynamic_index_in_dim(blocks, core, 1, keepdims=False)
        got = lax.ppermute(send, **flip("ctx", ctx, 1))
    else:
        keep = lax.psum_scatter(blocks, "ctx", scatter_dimension=1, tiled=False)
        got = None
    me = lax.axis_index("dp")
    half = rows // 2 // 16 * 16

    def part(mask, low, high):
        size = (1, high - low, cols)
        piece = lax.dynamic_slice(keep, (me ^ mask, low, 0), size)[0].astype(F32)
        if got is not None:
            piece = piece + lax.dynamic_slice(got, (me ^ mask, low, 0), size)[0].astype(F32)
        return piece

    far_top = lax.ppermute(part(3, 0, half).astype(BF), **flip("dp", dp, 1))
    far_low = lax.ppermute(part(3, half, rows).astype(BF), **flip("dp", dp, 2))
    to_y = jnp.concatenate([part(2, 0, half) + far_top.astype(F32), part(2, half, rows)])
    to_x = jnp.concatenate([part(1, 0, half), part(1, half, rows) + far_low.astype(F32)])
    by_y = lax.ppermute(to_y.astype(BF), **flip("dp", dp, 2))
    by_x = lax.ppermute(to_x.astype(BF), **flip("dp", dp, 1))
    total = part(0, 0, rows) + by_x.astype(F32) + by_y.astype(F32)
    return total, far_top


def sum_mp(part, sizes):
    if sizes["mp"] != 4:
        return lax.psum(part, "mp")
    place = lax.axis_index("mp")
    inner = (place == 1) | (place == 2)
    near = lax.ppermute(part, "mp", [(0, 1), (3, 2)])
    pair = (part.astype(F32) + near.astype(F32)).astype(BF)
    across = lax.ppermute(pair, "mp", [(1, 2), (2, 1)])
    total = (pair.astype(F32) + across.astype(F32)).astype(BF)
    back = lax.ppermute(total, "mp", [(1, 0), (2, 3)])
    return jnp.where(inner, total, back)


def sum_small(value, axes, sizes):
    for axis in axes:
        size = sizes[axis]
        step = 1
        while step < size:
            value = value + lax.ppermute(value, **flip(axis, size, step))
            step *= 2
    return value


def swap_ctx(local, sizes):
    if sizes["ctx"] != 2:
        return lax.all_gather(local, "ctx", axis=0, tiled=True)
    other = lax.ppermute(local, **flip("ctx", 2, 1))
    first = lax.axis_index("ctx") == 0
    return jnp.concatenate([jnp.where(first, local, other), jnp.where(first, other, local)])


def scatter_ctx(full, sizes):
    if sizes["ctx"] != 2:
        return lax.psum_scatter(full.astype(BF), "ctx", scatter_dimension=0, tiled=True).astype(F32)
    core = lax.axis_index("ctx")
    rows = full.shape[0] // 2
    send = lax.dynamic_slice_in_dim(full, (1 - core) * rows, rows).astype(BF)
    keep = lax.dynamic_slice_in_dim(full, core * rows, rows)
    return keep.astype(BF).astype(F32) + lax.ppermute(send, **flip("ctx", 2, 1)).astype(F32)


def dot(a, b):
    return lax.dot_general(a, b, (((1,), (0,)), ((), ())), preferred_element_type=F32)


def dot_t(a, b):
    return lax.dot_general(a, b, (((1,), (1,)), ((), ())), preferred_element_type=F32)


def t_dot(a, b):
    return lax.dot_general(a, b, (((0,), (0,)), ((), ())), preferred_element_type=F32)


def inverse_rms(v):
    return lax.rsqrt(jnp.mean(v * v, axis=-1, keepdims=True) + EPS)


def norm_back(v, r, gain, dy):
    scaled = (1.0 + gain) * dy
    mean = jnp.mean(scaled * v, axis=-1, keepdims=True)
    return r * scaled - v * (r * r * r) * mean, jnp.sum(v * r * dy, axis=0)


def rotate(v, cosine, sine):
    a, b = v[:, : HEAD // 2], v[:, HEAD // 2 :]
    return jnp.concatenate([a * cosine - b * sine, b * cosine + a * sine], axis=1)


GELU_C = math.sqrt(2.0 / math.pi)


def gelu_parts(u):
    tanh = jnp.tanh(GELU_C * (u + 0.044715 * u * u * u))
    value = 0.5 * u * (1.0 + tanh)
    slope = 0.5 * (1.0 + tanh) + 0.5 * u * (1.0 - tanh * tanh) * GELU_C * (
        1.0 + 3.0 * 0.044715 * u * u
    )
    return value, slope


def attend(queries, keys, values, allowed):
    raw = dot_t(queries, keys) * SCALE
    tanh = jnp.tanh(raw / CAP)
    heads = queries.shape[0] // allowed.shape[0]
    mask = jnp.concatenate([allowed] * heads, axis=0)
    weight = jnp.where(mask, jnp.exp(CAP * tanh), 0.0)
    probs = weight / jnp.sum(weight, axis=1, keepdims=True)
    out = dot(probs.astype(BF), values).astype(BF)
    return out, (probs, tanh)


def attend_back(saved, queries, keys, values, d_out):
    probs, tanh = saved
    d_probs = dot_t(d_out, values)
    inner = jnp.sum(probs * d_probs, axis=1, keepdims=True)
    d_raw = (probs * (d_probs - inner) * (1.0 - tanh * tanh)).astype(BF)
    d_queries = dot(d_raw, keys) * SCALE
    d_keys = t_dot(d_raw, queries) * SCALE
    d_values = t_dot(probs.astype(BF), d_out)
    return d_queries, d_keys, d_values


MESH = pl.DeviceIdType.MESH
UNIT = 256
TILE = 256


def layer_kernel(
    first_row, gains_own, cos_hbm, sin_hbm, x_hbm, cot_hbm, own_qkv, own_out, own_gate, own_up, own_down,
    out_hbm, ffn_in_hbm, hidden_hbm, d_ffn_hbm, d_gate_hbm, d_up_hbm, d_attn_hbm, d_heads_hbm,
    d_mid_hbm, gains_out, norm_out, attn_in_hbm, heads_hbm, pack_hbm, w_qkv_hbm, w_out_hbm,
    attn_hbm, slope_hbm, value_hbm,
    in_grad_hbm, own_hbm, by_x_hbm, by_y_hbm, core_hbm, far_hbm, kv_hbm, d_proj_hbm,
    weights, w_qkv, send, near, across, total, xb, cb, ab, act, act_t, stage, angle,
    line_send, line_recv, credit, local, ag_send, ag_recv, ag_local, gain_send, gain_recv, kv_sem,
    load_sem, rs_send, rs_recv, rs_local, kv_back, proj_sem,
    gain_ref, scale_ref, cast, squares, cast_sem, fin_sem, tail_send, tail_recv, z_send, z_recv,
):
    dp, core, z = lax.axis_index("dp"), lax.axis_index("ctx"), lax.axis_index("mp")
    w_out = w_qkv.at[:, : w_out_hbm.shape[1]]
    width, units = xb.shape[1], weights.shape[2]
    rows_own = own_qkv.shape[0]
    half = rows_own // 2
    inner = (z == 1) | (z == 2)
    outer = (z == 0) | (z == 3)
    x_peer, y_peer = (dp ^ 1, core, z), (dp ^ 2, core, z)
    core_peer = (dp, 1 - core, z)
    near_peer = (dp, core, z ^ 1)
    far_peer = (dp, core, 3 - z)

    barrier = pltpu.get_barrier_semaphore()
    group = [(dp ^ (m // 2), (1 - core) if m % 2 else core, z) for m in range(1, 8)]
    line = [(dp, core, z ^ m) for m in range(1, 4)]
    for peer in (*group, *line):
        pl.semaphore_signal(barrier, inc=1, device_id=peer, device_id_type=MESH)

    def block(mask, other=False, low=0, size=rows_own):
        owner = (dp ^ mask) * 2 + ((1 - core) if other else core)
        return pl.ds(pl.multiple_of(owner * rows_own + low, 16), size)

    owns = (own_qkv, own_out, own_gate, own_up, own_down)
    wholes = (w_qkv, w_out_hbm, weights.at[0], weights.at[1], weights.at[2])

    def gather(w, name, recv=False):
        table = {
            "x": (0, block(0), x_peer, block(1)),
            "y": (1, block(0), y_peer, block(2)),
            "top": (2, block(2, False, 0, half), x_peer, block(3, False, 0, half)),
            "low": (3, block(1, False, half, half), y_peer, block(3, False, half, half)),
            "own_c": (4, block(0), core_peer, block(0, True)),
            "x_c": (5, block(1), core_peer, block(1, True)),
            "y_c": (6, block(2), core_peer, block(2, True)),
            "top_c": (7, block(3, False, 0, half), core_peer, block(3, True, 0, half)),
            "low_c": (8, block(3, False, half, half), core_peer, block(3, True, half, half)),
        }
        index, out_rows, peer, in_rows = table[name]
        rows = in_rows if recv else out_rows
        direct = w < 2 and name in ("x", "y", "own_c")
        src = owns[w] if direct else wholes[w].at[rows]
        return pltpu.make_async_remote_copy(
            src_ref=src, dst_ref=wholes[w].at[rows], send_sem=ag_send.at[w, index],
            recv_sem=ag_recv.at[w, index], device_id=peer, device_id_type=MESH,
        )

    def own_copy(w):
        return pltpu.make_async_copy(owns[w], wholes[w].at[block(0)], ag_local.at[w])

    def round_own(w):
        size = cast.shape[1]
        steps = rows_own // size
        copies = [
            pltpu.make_async_copy(owns[w].at[pl.ds(c * size, size)], cast.at[c % 2], cast_sem.at[c % 2])
            for c in range(steps)
        ]
        copies[0].start()
        for c in range(steps):
            if c + 1 < steps:
                copies[c + 1].start()
            copies[c].wait()
            weights[w - 2, block(0, False, c * size, size)] = cast[c % 2].astype(BF)

    def gather_first(w):
        for name in ("x", "y", "own_c"):
            gather(w, name).start()
        if w < 2:
            own_copy(w).start()

    def gather_second(w):
        gather(w, "x", True).wait_recv()
        gather(w, "low").start()
        gather(w, "x_c").start()
        gather(w, "y", True).wait_recv()
        gather(w, "top").start()
        gather(w, "y_c").start()

    def gather_third(w):
        for name in ("top", "low"):
            gather(w, name, True).wait_recv()
            gather(w, name + "_c").start()

    def gather_end(w):
        for name in ("own_c", "x_c", "y_c", "top_c", "low_c"):
            gather(w, name, True).wait_recv()
        if w < 2:
            own_copy(w).wait()
        for name in ("x", "y", "top", "low", "own_c", "x_c", "y_c", "top_c", "low_c"):
            gather(w, name).wait_send()

    def hop(kind, i):
        src = (send.at[i % 3], send.at[i % 3], total.at[i % 4])[kind]
        dst = (near.at[i % 3], across.at[i % 2], total.at[i % 4])[kind]
        return pltpu.make_async_remote_copy(
            src_ref=src, dst_ref=dst, send_sem=line_send.at[kind, i % 4],
            recv_sem=line_recv.at[kind, i % 4],
            device_id=far_peer if kind == 1 else near_peer, device_id_type=MESH,
        )

    def add_rows(dst, a, b):
        @pl.loop(0, UNIT // 16, unroll=4)
        def _(r):
            rows = pl.ds(pl.multiple_of(r * 16, 16), 16)
            dst[rows] = (a[rows].astype(F32) + b[rows].astype(F32)).astype(BF)

    def boundary(up=None, cross=None, back=None, done=None):
        @pl.when(outer)
        def _():
            if done is not None:
                hop(2, done).wait_recv()
            if cross is not None:
                hop(0, cross).wait_send()
            if up is not None:
                hop(0, up).start()

        @pl.when(inner)
        def _():
            if cross is not None:
                hop(0, cross).wait_recv()
                add_rows(send.at[cross % 3], send.at[cross % 3], near.at[cross % 3])
                if not isinstance(cross, int) or cross >= 2:
                    pl.semaphore_wait(credit, 1)
                hop(1, cross).start()
            if back is not None:
                hop(1, back).wait_recv()
                hop(1, back).wait_send()
                add_rows(total.at[back % 4], send.at[back % 3], across.at[back % 2])
                if not isinstance(back, int) or back < 14:
                    pl.semaphore_signal(credit, inc=1, device_id=far_peer, device_id_type=MESH)
                hop(2, back).start()
            if done is not None:
                hop(2, done).wait_send()

    def rows_of(u):
        return pl.ds(pl.multiple_of(u * UNIT, UNIT), UNIT)

    def load(ref, u, dst, sem):
        return pltpu.make_async_copy(ref.at[rows_of(u)], dst, local.at[sem])

    def store(src, ref, u, sem):
        return pltpu.make_async_copy(src, ref.at[rows_of(u)], local.at[sem])

    def store_t(ref, u, sem):
        return pltpu.make_async_copy(act_t, ref.at[:, rows_of(u)], local.at[sem])

    def turn(source=None):
        source = act if source is None else source

        @pl.loop(0, width // TILE, unroll=3)
        def _(n):
            act_t[tile(n)] = source[:, tile(n)].T

    def tile(n):
        return pl.ds(pl.multiple_of(n * TILE, TILE), TILE)

    def each_rows(body):
        @pl.loop(0, UNIT // 16, unroll=4)
        def _(r):
            body(pl.ds(pl.multiple_of(r * 16, 16), 16))

    def scale(i):
        return scale_ref[i : i + 1]

    def add_gain(index, v):
        gain_ref[index] += v[:8] + v[8:]

    def project_out(u, k):
        dst = send.at[k % 3]

        @pl.loop(0, width // TILE, unroll=3)
        def _(n):
            dst[:, tile(n)] = dot_t(act[:, 2 * HEAD * u : 2 * HEAD * (u + 1)], w_out[tile(n)]).astype(BF)

    def middle(rows, u4):
        attn = total[u4, rows].astype(F32) if u4 is not None else ab[rows].astype(F32)
        r_two = inverse_rms(attn)
        return attn, r_two, xb[rows].astype(F32) + attn * r_two * scale(1)

    def forward(u, k, ready=None):
        load(x_hbm, u, xb, 0).start()
        store(total.at[u], attn_hbm, u, 1).start()
        load(x_hbm, u, xb, 0).wait()

        def body(rows):
            _, _, mid = middle(rows, u)
            act[rows] = (mid * inverse_rms(mid) * scale(2)).astype(BF)

        each_rows(body)
        turn()
        store_t(ffn_in_hbm, u, 2).start()

        @pl.loop(0, units // TILE, unroll=3)
        def _(f):
            gate = dot(act[...], weights[0, :, tile(f)])
            up = dot(act[...], weights[1, :, tile(f)])
            value, slope = gelu_parts(gate)
            stage[0, :, tile(f)] = (value * up).astype(BF)
            stage[1, :, tile(f)] = (slope * up).astype(BF)
            stage[2, :, tile(f)] = value.astype(BF)

        saves = ((0, hidden_hbm), (1, slope_hbm), (2, value_hbm))
        for i, ref in saves:
            store(stage.at[i], ref, u, 3 + i).start()
        if ready is not None:
            ready()
        dst = send.at[k % 3]

        @pl.loop(0, width // TILE, unroll=3)
        def _(n):
            dst[:, tile(n)] = dot_t(stage[0], weights[2, tile(n)]).astype(BF)

        for i, ref in saves:
            store(stage.at[i], ref, u, 3 + i).wait()
        store(total.at[u], attn_hbm, u, 1).wait()
        store_t(ffn_in_hbm, u, 2).wait()

    def backward(u, k):
        loads = (
            load(x_hbm, u, xb, 0), load(attn_hbm, u, ab, 1), load(cot_hbm, u, cb, 2),
            load(slope_hbm, u, stage.at[1], 4), load(value_hbm, u, stage.at[2], 5),
        )
        for copy in loads:
            copy.start()
        for copy in loads:
            copy.wait()

        def body(rows):
            _, _, mid = middle(rows, None)
            ffn = total[u, rows].astype(F32)
            r = inverse_rms(ffn)
            dy = cb[rows].astype(F32)
            xb[rows] = (mid + ffn * r * scale(3)).astype(BF)
            scaled = scale(3) * dy
            mean = jnp.mean(scaled * ffn, axis=-1, keepdims=True)
            act[rows] = (r * scaled - ffn * (r * r * r) * mean).astype(BF)
            add_gain(2, ffn * r * dy)

        each_rows(body)
        store(xb, out_hbm, u, 0).start()
        turn()
        store_t(d_ffn_hbm, u, 1).start()

        @pl.loop(0, units // TILE, unroll=3)
        def _(f):
            d_hidden = dot(act[...], weights[2, :, tile(f)])
            stage[1, :, tile(f)] = (d_hidden * stage[1, :, tile(f)].astype(F32)).astype(BF)
            stage[2, :, tile(f)] = (d_hidden * stage[2, :, tile(f)].astype(F32)).astype(BF)

        store(stage.at[1], d_gate_hbm, u, 4).start()
        store(stage.at[2], d_up_hbm, u, 5).start()
        dst = send.at[k % 3]

        @pl.loop(0, width // TILE, unroll=3)
        def _(n):
            part = dot_t(stage[1], weights[0, tile(n)]) + dot_t(stage[2], weights[1, tile(n)])
            dst[:, tile(n)] = part.astype(BF)

        store(xb, out_hbm, u, 0).wait()
        store_t(d_ffn_hbm, u, 1).wait()
        store(stage.at[1], d_gate_hbm, u, 4).wait()
        store(stage.at[2], d_up_hbm, u, 5).wait()

    d_heads = stage.at[2, :, : w_out_hbm.shape[1]]

    def last_loads(u):
        return (load(x_hbm, u, xb, 0), load(attn_hbm, u, ab, 1), load(cot_hbm, u, cb, 2))

    def start_all(copies):
        for copy in copies:
            copy.start()

    def last(u):
        for copy in last_loads(u):
            copy.wait()

        def body(rows):
            attn, r_two, mid = middle(rows, None)
            r = inverse_rms(mid)
            dy = total[u, rows].astype(F32)
            scaled = scale(2) * dy
            mean = jnp.mean(scaled * mid, axis=-1, keepdims=True)
            grad = cb[rows].astype(F32) + r * scaled - mid * (r * r * r) * mean
            add_gain(1, mid * r * dy)
            cb[rows] = grad.astype(BF)
            scaled = scale(1) * grad
            mean = jnp.mean(scaled * attn, axis=-1, keepdims=True)
            act[rows] = (r_two * scaled - attn * (r_two * r_two * r_two) * mean).astype(BF)
            add_gain(0, attn * r_two * grad)

        each_rows(body)
        store(cb, d_mid_hbm, u, 0).start()
        turn()
        store_t(d_attn_hbm, u, 1).start()
        for h in range(w_out.shape[1] // TILE):
            columns = slice(h * TILE, (h + 1) * TILE)
            d_heads[:, columns] = dot(act[...], w_out[:, columns]).astype(BF)
        store(d_heads, d_heads_hbm, u, 2).start()
        store(cb, d_mid_hbm, u, 0).wait()
        store_t(d_attn_hbm, u, 1).wait()
        store(d_heads, d_heads_hbm, u, 2).wait()

    own_rows = pl.ds(pl.multiple_of((dp * 2 + core) * 16, 16), 16)

    def gain_copy(m, recv=False):
        peer = group[m - 1]
        owner = (peer[0] * 2 + peer[1]) if recv else (dp * 2 + core)
        return pltpu.make_async_remote_copy(
            src_ref=send.at[2, own_rows],
            dst_ref=send.at[2, own_rows if not recv else pl.ds(pl.multiple_of(owner * 16, 16), 16)],
            send_sem=gain_send.at[m], recv_sem=gain_recv.at[m], device_id=peer, device_id_type=MESH,
        )

    def gains_sum():
        whole = send[2, own_rows].astype(F32)
        for m in range(1, 8):
            gain_copy(m, True).wait_recv()
        for m in range(1, 8):
            owner = group[m - 1][0] * 2 + group[m - 1][1]
            whole += send[2, pl.ds(pl.multiple_of(owner * 16, 16), 16)].astype(F32)
        scale_ref[...] = 1.0 + whole[:8]
        for m in range(1, 8):
            gain_copy(m).wait_send()

    loaded = (stage.at[0], stage.at[1], stage.at[2], act)

    def first_norm(u):
        load(x_hbm, u, loaded[u], u).wait()

        def body(rows):
            x = loaded[u][rows].astype(F32)
            total[u, rows] = (x * inverse_rms(x) * scale(0)).astype(BF)

        each_rows(body)

    def first_turn(u):
        if u:
            store_t(attn_in_hbm, u - 1, 4).wait()
        turn(total.at[u])
        store_t(attn_in_hbm, u, 4).start()

    def angles(u):
        rows = rows_of(u)
        return (
            pltpu.make_async_copy(cos_hbm.at[rows], angle.at[u % 2, 0], local.at[2 * (u % 2)]),
            pltpu.make_async_copy(sin_hbm.at[rows], angle.at[u % 2, 1], local.at[2 * (u % 2) + 1]),
        )

    packs = (cb, ab)

    def kv_columns(kind, peer=False):
        side = (1 - core) if peer else core
        return pl.ds(pl.multiple_of(kind * 4 * HEAD + side * 2 * HEAD, HEAD), 2 * HEAD)

    def kv_copy(mb, kind, recv=False):
        part = packs[mb].at[:, kv_columns(kind, recv)]
        return pltpu.make_async_remote_copy(
            src_ref=part, dst_ref=part, send_sem=kv_sem.at[0, mb, kind], recv_sem=kv_sem.at[1, mb, kind],
            device_id=core_peer, device_id_type=MESH,
        )

    def projections(u):
        mb, b = divmod(u, 2)
        for copy in angles(u):
            copy.wait()
        if u < 3:
            for copy in angles(u + 1):
                copy.start()
        c, s = angle[u % 2, 0], angle[u % 2, 1]
        for j in range(4):
            v = dot(total[u], w_qkv[:, j * HEAD : (j + 1) * HEAD])
            if j < 2:
                xb[:, (mb * 4 + j * 2 + b) * HEAD : (mb * 4 + j * 2 + b + 1) * HEAD] = rotate(v, c, s).astype(BF)
            else:
                place = pl.multiple_of((j - 2) * 4 * HEAD + (core * 2 + b) * HEAD, HEAD)
                packs[mb][:, pl.ds(place, HEAD)] = (rotate(v, c, s) if j == 2 else v).astype(BF)

    def attention(mb):
        for kind in (0, 1):
            kv_copy(mb, kind, True).wait_recv()

        @pl.loop(0, 4)
        def _(i):
            h, b = i // 2, i % 2
            query = xb[:, pl.ds(pl.multiple_of(mb * 4 * HEAD + i * HEAD, HEAD), HEAD)]
            lowest = first_row[mb, :, pl.ds(pl.multiple_of(b * UNIT, UNIT), UNIT)]
            query_at = lax.broadcasted_iota(jnp.int32, (UNIT, UNIT), 1) + core * 2 * UNIT + b * UNIT
            weight, length = [], 0.0
            for j in range(4):
                key_at = lax.broadcasted_iota(jnp.int32, (UNIT, UNIT), 0) + j * UNIT
                score = dot_t(packs[mb][:, j * HEAD : (j + 1) * HEAD], query) * (SCALE / CAP)
                ok = (key_at <= query_at) & (key_at >= lowest)
                weight.append(jnp.where(ok, jnp.exp(CAP * jnp.tanh(score)), 0.0))
                length = length + jnp.sum(weight[j], axis=0, keepdims=True)
            inverse = 1.0 / length
            out = 0.0
            for j in range(4):
                value = packs[mb][:, (4 + j) * HEAD : (5 + j) * HEAD]
                out = out + t_dot((weight[j] * inverse).astype(BF), value)
            place = pl.multiple_of((mb * 2 + b) * 2 * HEAD + h * HEAD, HEAD)
            act[:, pl.ds(place, HEAD)] = out.astype(BF)

    def heads_store(u):
        return pltpu.make_async_copy(
            act.at[:, 2 * HEAD * u : 2 * HEAD * (u + 1)], heads_hbm.at[rows_of(u)], local.at[u]
        )

    def pack_store(i):
        return pltpu.make_async_copy((xb, cb, ab)[i], pack_hbm.at[i], ag_local.at[5 + i])

    for u in range(4):
        load(x_hbm, u, loaded[u], u).start()
    gain_ref[...] = jnp.zeros_like(gain_ref)
    send[2, own_rows] = gains_own[...].astype(BF)
    pl.semaphore_wait(barrier, 10)
    for m in range(1, 8):
        gain_copy(m).start()
    gather_first(0)
    gains_sum()
    for u in range(4):
        first_norm(u)
    for copy in angles(0):
        copy.start()
    first_turn(0)
    gather_second(0)
    first_turn(1)
    first_turn(2)
    gather_third(0)
    gather_first(1)
    first_turn(3)
    round_own(2)
    gather_end(0)
    qkv_store = pltpu.make_async_copy(w_qkv, w_qkv_hbm, local.at[5])
    qkv_store.start()
    for u in range(4):
        projections(u)
        if u % 2:
            for kind in (0, 1):
                kv_copy(u // 2, kind).start()
    gather_second(1)
    gather_first(2)
    attention(0)
    gather_third(1)
    gather_end(1)
    qkv_store.wait()
    store_t(attn_in_hbm, 3, 4).wait()
    out_load = pltpu.make_async_copy(w_out_hbm, w_out, local.at[4])
    out_load.start()
    out_load.wait()
    project_out(0, 0)
    boundary(0)
    project_out(1, 1)
    attention(1)
    project_out(2, 2)
    for i in range(3):
        pack_store(i).start()
    for u in range(4):
        heads_store(u).start()
    round_own(3)
    gather_second(2)
    gather_first(3)
    boundary(1, 0)
    gather_third(2)
    round_own(4)
    for kind in (0, 1):
        for mb in (0, 1):
            kv_copy(mb, kind).wait_send()
    for i in range(3):
        pack_store(i).wait()
    for u in range(4):
        heads_store(u).wait()
    boundary(2, 1, 0)
    project_out(3, 3)
    gather_second(3)
    gather_first(4)
    boundary(3, 2, 1, 0)
    gather_third(3)
    gather_end(2)
    gather_end(3)

    def ready():
        gather_second(4)
        gather_third(4)
        gather_end(4)

    forward(0, 4, ready)

    @pl.loop(4, 7)
    def _(k):
        boundary(k, k - 1, k - 2, k - 3)
        forward(k - 3, k + 1)

    @pl.loop(7, 11)
    def _(k):
        boundary(k, k - 1, k - 2, k - 3)
        backward(k - 7, k + 1)

    left, w_back = weights.at[0, :, : 4 * UNIT], weights.at[0, :, 4 * UNIT : 8 * UNIT]
    queries = weights.at[0, : 4 * UNIT, 8 * UNIT :]
    d_out = weights.at[0, 4 * UNIT : 8 * UNIT, 8 * UNIT :]
    right = weights.at[1, : 4 * UNIT]
    jobs = (
        (d_ffn_hbm, hidden_hbm), (ffn_in_hbm, d_gate_hbm), (ffn_in_hbm, d_up_hbm),
        (d_attn_hbm, heads_hbm), (attn_in_hbm, d_proj_hbm),
    )

    def columns(i):
        return jobs[i][1].shape[1]

    def core_out(m):
        low = 4 * UNIT + (m % 2) * rows_own
        return weights.at[1, low : low + rows_own]

    def arrived(m):
        low = 4 * UNIT + (2 + m % 2) * rows_own
        return weights.at[1, low : low + rows_own]

    def sums(i, m):
        low = ((i % 2) * 3 + m - 1) * rows_own
        return weights.at[2, low : low + rows_own]

    packed = weights.at[2, 6 * rows_own : 6 * rows_own + UNIT]
    own_sum = weights.at[2, 6 * rows_own + UNIT : 7 * rows_own + UNIT]

    def remote(src, dst, index, peer):
        return pltpu.make_async_remote_copy(
            src_ref=src, dst_ref=dst, send_sem=rs_send.at[index], recv_sem=rs_recv.at[index],
            device_id=peer, device_id_type=MESH,
        )

    def operands(i):
        pair = [pltpu.make_async_copy(jobs[i][1], right.at[:, : columns(i)], rs_local.at[1])]
        if i != 2:
            pair.append(pltpu.make_async_copy(jobs[i][0], left, rs_local.at[0]))
        return pair

    def core_copy(i, m):
        n = columns(i)
        return remote(core_out(m).at[:, :n], core_hbm.at[i, m, :, :n], (i, m), core_peer)

    def arrive(i, m):
        n = columns(i)
        return pltpu.make_async_copy(core_hbm.at[i, m, :, :n], arrived(m).at[:, :n], rs_local.at[2 + m % 2])

    def far_copy(i, way):
        n = columns(i)
        rows = slice(0, half) if way == 0 else slice(half, rows_own)
        peer = (x_peer, y_peer)[way]
        return remote(sums(i, 3).at[rows, :n], far_hbm.at[i, rows, :n], (i, 4 + way), peer)

    def final_copy(i, way):
        n = columns(i)
        dst = (by_x_hbm, by_y_hbm)[way]
        peer = (x_peer, y_peer)[way]
        return remote(sums(i, way + 1).at[:, :n], dst.at[i, :, :n], (i, 6 + way), peer)

    def own_store(i):
        n = columns(i)
        return pltpu.make_async_copy(own_sum.at[:, :n], own_hbm.at[i, :, :n], rs_local.at[5])

    def block_rows(mask, other):
        owner = (dp ^ mask) * 2 + ((1 - core) if other else core)
        return pl.ds(pl.multiple_of(owner * rows_own, 16), rows_own)

    def scatter_start(i):
        for copy in operands(i):
            copy.wait()
        piece = 768 if columns(i) % 768 == 0 else 512
        steps = columns(i) // piece

        def piece_at(n):
            return pl.ds(pl.multiple_of(n * piece, TILE), piece)

        for m in (3, 2, 1, 0):
            if m < 2:
                core_copy(i, m + 2).wait_send()
            elif i > 0:
                core_copy(i - 1, m - 2).wait_send()
            dst = core_out(m)

            @pl.loop(0, steps)
            def _(n):
                dst[:, piece_at(n)] = dot(left[block_rows(m, True)], right[:, piece_at(n)]).astype(BF)

            core_copy(i, m).start()
        if i > 1:
            for way in (0, 1):
                far_copy(i - 2, way).wait_send()
                final_copy(i - 2, way).wait_send()
        if i > 0:
            own_store(i - 1).wait()
        core_copy(i, 3).wait_recv()
        arrive(i, 3).start()
        for m in (3, 2, 1, 0):
            if m:
                core_copy(i, m - 1).wait_recv()
                arrive(i, m - 1).start()
            arrive(i, m).wait()
            dst, extra = (sums(i, m) if m else own_sum), arrived(m)

            @pl.loop(0, steps)
            def _(n):
                part = dot(left[block_rows(m, False)], right[:, piece_at(n)])
                dst[:, piece_at(n)] = (part + extra[:, piece_at(n)].astype(F32)).astype(BF)

            if m == 3:
                far_copy(i, 0).start()
                far_copy(i, 1).start()
        own_store(i).start()

    def operands_start(i):
        for copy in operands(i):
            copy.start()

    def scatter_end(i):
        n = columns(i)
        for way in (0, 1):
            far_copy(i, way).wait_recv()
        added = arrived(0)
        copy = pltpu.make_async_copy(far_hbm.at[i, :, :n], added.at[:, :n], rs_local.at[4])
        copy.start()
        copy.wait()
        for way in (1, 0):
            base = 0 if way == 1 else half
            dst = sums(i, way + 1)

            @pl.loop(0, half // 16, unroll=3)
            def _(r):
                rows = pl.ds(pl.multiple_of(base + r * 16, 16), 16)
                dst[rows, :n] = (dst[rows, :n].astype(F32) + added[rows, :n].astype(F32)).astype(BF)

            final_copy(i, way).start()

    def back_loads(mb):
        copies = [pltpu.make_async_copy(pack_hbm.at[1 + mb], packed, load_sem.at[8])]
        for i in range(4):
            h, b = divmod(i, 2)
            rows = pl.ds(i * UNIT, UNIT)
            query = pack_hbm.at[0, :, (mb * 4 + i) * HEAD : (mb * 4 + i + 1) * HEAD]
            grad = d_heads_hbm.at[pl.ds((2 * mb + b) * UNIT, UNIT), h * HEAD : (h + 1) * HEAD]
            copies.append(pltpu.make_async_copy(query, queries.at[rows], load_sem.at[i]))
            copies.append(pltpu.make_async_copy(grad, d_out.at[rows], load_sem.at[4 + i]))
        return [*copies, *angles(2 * mb), *angles(2 * mb + 1)]

    def unrotate(v, b):
        c, s = angle[b, 0], angle[b, 1]
        v, w = v[:, : HEAD // 2], v[:, HEAD // 2 :]
        return jnp.concatenate([v * c + w * s, w * c - v * s], axis=1)

    def kv_out(mb):
        return pltpu.make_async_remote_copy(
            src_ref=act_t.at[: 4 * UNIT], dst_ref=kv_hbm.at[mb], send_sem=kv_back.at[0, mb],
            recv_sem=kv_back.at[1, mb], device_id=core_peer, device_id_type=MESH,
        )

    def proj_store(u):
        part = stage.at[u // 2, :, (u % 2) * 4 * HEAD : (u % 2 + 1) * 4 * HEAD]
        return pltpu.make_async_copy(part, d_proj_hbm.at[rows_of(u)], proj_sem.at[u])

    def attention_back(mb):
        for copy in back_loads(mb):
            copy.start()
        for copy in back_loads(mb):
            copy.wait()
        d_scores, weights_of = (xb, ab), (act, cb)

        @pl.loop(0, 4)
        def _(i):
            h, b = i // 2, i % 2
            rows = pl.ds(pl.multiple_of(i * UNIT, UNIT), UNIT)
            query, grad = queries[rows], d_out[rows]
            lowest = first_row[mb, :, pl.ds(pl.multiple_of(b * UNIT, UNIT), UNIT)]
            query_at = lax.broadcasted_iota(jnp.int32, (UNIT, UNIT), 1) + core * 2 * UNIT + b * UNIT
            tanh, weight, d_probs, length, mean = [], [], [], 0.0, 0.0
            for j in range(4):
                key_at = lax.broadcasted_iota(jnp.int32, (UNIT, UNIT), 0) + j * UNIT
                ok = (key_at <= query_at) & (key_at >= lowest)
                score = dot_t(packed[:, j * HEAD : (j + 1) * HEAD], query) * (SCALE / CAP)
                tanh.append(jnp.tanh(score))
                weight.append(jnp.where(ok, jnp.exp(CAP * tanh[j]), 0.0))
                d_probs.append(dot_t(packed[:, (4 + j) * HEAD : (5 + j) * HEAD], grad))
                length = length + jnp.sum(weight[j], axis=0, keepdims=True)
                mean = mean + jnp.sum(weight[j] * d_probs[j], axis=0, keepdims=True)
            inverse = 1.0 / length
            mean = mean * inverse
            d_query = 0.0
            for j in range(4):
                probs = weight[j] * inverse
                d_raw = (probs * (d_probs[j] - mean) * (1.0 - tanh[j] * tanh[j])).astype(BF)
                place = pl.ds(pl.multiple_of((j % 2) * 4 * HEAD + i * HEAD, HEAD), HEAD)
                d_scores[j // 2][:, place] = d_raw
                weights_of[j // 2][:, place] = probs.astype(BF)
                d_query = d_query + t_dot(d_raw, packed[:, j * HEAD : (j + 1) * HEAD])
            place = pl.ds(pl.multiple_of(b * 4 * HEAD + h * HEAD, HEAD), HEAD)
            stage[mb, :, place] = unrotate(d_query * SCALE, b).astype(BF)

        def block_grads(j):
            place = slice((j % 2) * 4 * HEAD, (j % 2 + 1) * 4 * HEAD)
            d_key = dot(d_scores[j // 2][:, place], queries[...]) * SCALE
            return d_key, dot(weights_of[j // 2][:, place], d_out[...])

        for side in (0, 1):

            @pl.when(core == side)
            def _():
                for t in (0, 1):
                    d_key, d_value = block_grads((1 - side) * 2 + t)
                    act_t[t * UNIT : (t + 1) * UNIT] = d_key.astype(BF)
                    act_t[(2 + t) * UNIT : (3 + t) * UNIT] = d_value.astype(BF)

        kv_out(mb).start()
        kv_out(mb).wait_recv()
        copy = pltpu.make_async_copy(kv_hbm.at[mb], act_t.at[4 * UNIT : 8 * UNIT], rs_local.at[6])
        copy.start()
        copy.wait()
        for side in (0, 1):

            @pl.when(core == side)
            def _():
                for t in (0, 1):
                    d_key, d_value = block_grads(side * 2 + t)
                    d_key = d_key + act_t[(4 + t) * UNIT : (5 + t) * UNIT].astype(F32)
                    d_value = d_value + act_t[(6 + t) * UNIT : (7 + t) * UNIT].astype(F32)
                    low = t * 4 * HEAD
                    stage[mb, :, low + 2 * HEAD : low + 3 * HEAD] = unrotate(d_key, t).astype(BF)
                    stage[mb, :, low + 3 * HEAD : low + 4 * HEAD] = d_value.astype(BF)

        proj_store(2 * mb).start()
        proj_store(2 * mb + 1).start()
        kv_out(mb).wait_send()

    def project_back(u):
        dst = send.at[(12 + u) % 3]
        low = (u % 2) * 4 * HEAD

        @pl.loop(0, width // TILE, unroll=3)
        def _(n):
            dst[:, tile(n)] = dot_t(stage[u // 2, :, low : low + 4 * HEAD], w_back[tile(n)]).astype(BF)

    def first_loads(u):
        return (load(x_hbm, u, xb, 0), load(d_mid_hbm, u, ab, 1))

    def first_back(u):
        for copy in first_loads(u):
            copy.wait()

        def body(rows):
            x = xb[rows].astype(F32)
            r_one = inverse_rms(x)
            dy = total[u, rows].astype(F32)
            scaled = scale(0) * dy
            mean = jnp.mean(scaled * x, axis=-1, keepdims=True)
            back = r_one * scaled - x * (r_one * r_one * r_one) * mean
            ab[rows] = (ab[rows].astype(F32) + back).astype(BF)
            add_gain(3, x * r_one * dy)

        each_rows(body)
        store(ab, in_grad_hbm, u, 2).start()
        store(ab, in_grad_hbm, u, 2).wait()
        if u < 3:
            start_all(first_loads(u + 1))

    def finish(i):
        n = columns(i)
        for way in (0, 1):
            final_copy(i, way).wait_recv()
        for low in (0, half):
            pairs = ((own_hbm, cb), (by_x_hbm, act), (by_y_hbm, stage.at[2]))
            copies = [
                pltpu.make_async_copy(ref.at[i, low : low + half, :n], dst.at[:half, :n], fin_sem.at[j])
                for j, (ref, dst) in enumerate(pairs)
            ]
            start_all(copies)
            for copy in copies:
                copy.wait()

            @pl.loop(0, half // 16, unroll=3)
            def _(r):
                rows = pl.ds(pl.multiple_of(r * 16, 16), 16)
                v = cb[rows, :n].astype(F32) + act[rows, :n].astype(F32) + stage[2, rows, :n].astype(F32)
                cb[rows, :n] = v.astype(BF)
                v = v * v
                gain_ref[4, :, :n] += v[:8] + v[8:]

            copy = pltpu.make_async_copy(cb.at[:half, :n], own_hbm.at[i, low : low + half, :n], fin_sem.at[0])
            copy.start()
            copy.wait()

    table = weights.at[1, 4 * UNIT + 4 * rows_own :]

    def table_copy(m, recv=False):
        peer = group[m - 1]
        owner = (peer[0] * 2 + peer[1]) if recv else (dp * 2 + core)
        rows = pl.ds(pl.multiple_of(owner * 16, 16), 16)
        return pltpu.make_async_remote_copy(
            src_ref=table.at[own_rows], dst_ref=table.at[rows], send_sem=tail_send.at[m],
            recv_sem=tail_recv.at[m], device_id=peer, device_id_type=MESH,
        )

    def square_copy(m, recv=False):
        place = (z ^ m) if recv else z
        return pltpu.make_async_remote_copy(
            src_ref=squares.at[z], dst_ref=squares.at[place], send_sem=z_send.at[m],
            recv_sem=z_recv.at[m], device_id=line[m - 1], device_id_type=MESH,
        )

    def agree():
        rows = [jnp.sum(gain_ref[i], axis=0, keepdims=True) for i in (3, 0, 1, 2, 4)]
        high = [v.astype(BF).astype(F32) for v in rows]
        low = [v - h for v, h in zip(rows, high)]
        blank = jnp.zeros((6, rows[0].shape[1]), F32)
        table[own_rows] = jnp.concatenate([*high, *low, blank], axis=0).astype(BF)
        for m in range(1, 8):
            table_copy(m).start()
        for m in range(1, 8):
            table_copy(m, True).wait_recv()
        whole = jnp.zeros((16, rows[0].shape[1]), F32)
        for owner in range(8):
            whole = whole + table[owner * 16 : owner * 16 + 16].astype(F32)
        gains = whole[0:4] + whole[5:9]
        squares[z] = jnp.broadcast_to(jnp.sum(whole[4:5] + whole[9:10], axis=1, keepdims=True), (8, 128))
        for m in range(1, 4):
            square_copy(m).start()
        gains_out[0:4] = gains
        gains_out[4:8] = jnp.zeros_like(gains)
        gain_square = jnp.sum(jnp.sum(gains * gains, axis=1, keepdims=True), axis=0, keepdims=True)
        for m in range(1, 4):
            square_copy(m, True).wait_recv()
        norm_out[...] = jnp.sqrt(squares[0] + squares[1] + squares[2] + squares[3] + gain_square)
        for m in range(1, 8):
            table_copy(m).wait_send()
        for m in range(1, 4):
            square_copy(m).wait_send()

    w_load = pltpu.make_async_copy(w_qkv_hbm, w_back, rs_local.at[7])
    operands_start(0)
    w_load.start()
    start_all(last_loads(0))
    boundary(11, 10, 9, 8)
    scatter_start(0)
    operands_start(1)
    last(0)
    start_all(last_loads(1))
    boundary(None, 11, 10, 9)
    last(1)
    attention_back(0)
    start_all(last_loads(2))
    w_load.wait()
    project_back(0)
    boundary(12)
    scatter_end(0)
    project_back(1)
    boundary(None, None, 11, 10)
    last(2)
    start_all(last_loads(3))
    scatter_start(1)
    operands_start(2)
    boundary(13, 12)
    boundary(None, None, None, 11)
    last(3)
    attention_back(1)
    start_all(first_loads(0))
    project_back(2)
    boundary(14)
    scatter_end(1)
    boundary(None, 13, 12)
    project_back(3)
    scatter_start(2)
    operands_start(3)
    boundary(15, 14, 13, 12)
    scatter_end(2)
    first_back(0)
    scatter_start(3)
    for u in range(4):
        proj_store(u).wait()
    operands_start(4)
    finish(0)
    finish(1)
    boundary(None, 15, 14, 13)
    scatter_end(3)
    scatter_start(4)
    first_back(1)
    boundary(None, None, 15, 14)
    scatter_end(4)
    own_store(4).wait()
    first_back(2)
    finish(2)
    finish(3)
    boundary(None, None, None, 15)
    first_back(3)
    finish(4)
    agree()
    for m in range(2):
        core_copy(4, m).wait_send()
    for i in range(3, 5):
        for way in (0, 1):
            far_copy(i, way).wait_send()
            final_copy(i, way).wait_send()


def layer_call(first_row, gains_own, cosine, sine, x, cot, owns):
    tokens, width = x.shape
    units = owns[2].shape[1]
    qkv_cols, out_cols = owns[0].shape[1], owns[1].shape[1]
    assert tokens == 4 * UNIT
    full = jax.ShapeDtypeStruct((tokens, width), BF)
    wide = jax.ShapeDtypeStruct((tokens, units), BF)
    flipped = jax.ShapeDtypeStruct((width, tokens), BF)
    rows = owns[0].shape[0]
    part = jax.ShapeDtypeStruct((5, rows, units), BF)
    heads = jax.ShapeDtypeStruct((tokens, out_cols), BF)
    outs = (
        full, flipped, wide, flipped, wide, wide, flipped, heads, full,
        jax.ShapeDtypeStruct((8, width), F32),
        jax.ShapeDtypeStruct((8, 128), F32),
        flipped,
        heads,
        jax.ShapeDtypeStruct((3, UNIT, width), BF),
        jax.ShapeDtypeStruct((width, qkv_cols), BF),
        jax.ShapeDtypeStruct((width, out_cols), BF),
        full, wide, wide,
        full, part, part, part,
        jax.ShapeDtypeStruct((5, 4, rows, units), BF),
        part,
        jax.ShapeDtypeStruct((2, tokens, HEAD), BF),
        jax.ShapeDtypeStruct((tokens, qkv_cols), BF),
    )
    anywhere, vmem = pl.BlockSpec(memory_space=pl.ANY), pl.BlockSpec(memory_space=pltpu.VMEM)
    dma = pltpu.SemaphoreType.DMA
    return pl.pallas_call(
        layer_kernel,
        out_shape=outs,
        in_specs=[vmem] * 2 + [anywhere] * 9,
        out_specs=[anywhere] * 9 + [vmem] * 2 + [anywhere] * 16,
        scratch_shapes=[
            pltpu.VMEM((3, width, units), BF),
            pltpu.VMEM((width, qkv_cols), BF),
            pltpu.VMEM((3, UNIT, width), BF),
            pltpu.VMEM((3, UNIT, width), BF),
            pltpu.VMEM((2, UNIT, width), BF),
            pltpu.VMEM((4, UNIT, width), BF),
            pltpu.VMEM((UNIT, width), BF),
            pltpu.VMEM((UNIT, width), BF),
            pltpu.VMEM((UNIT, width), BF),
            pltpu.VMEM((UNIT, width), BF),
            pltpu.VMEM((width, UNIT), BF),
            pltpu.VMEM((3, UNIT, units), BF),
            pltpu.VMEM((2, 2, UNIT, HEAD // 2), F32),
            dma((3, 4)),
            dma((3, 4)),
            pltpu.SemaphoreType.REGULAR,
            dma((6,)),
            dma((5, 9)),
            dma((5, 9)),
            dma((8,)),
            dma((8,)),
            dma((8,)),
            dma((2, 2, 2)),
            dma((9,)),
            dma((5, 8)),
            dma((5, 8)),
            dma((8,)),
            dma((2, 2)),
            dma((4,)),
            pltpu.VMEM((5, 8, width), F32),
            pltpu.VMEM((8, width), F32),
            pltpu.VMEM((2, 32, units), F32),
            pltpu.VMEM((4, 8, 128), F32),
            dma((2,)),
            dma((3,)),
            dma((8,)),
            dma((8,)),
            dma((4,)),
            dma((4,)),
        ],
        compiler_params=pltpu.CompilerParams(
            collective_id=1, has_side_effects=True, vmem_limit_bytes=63 * 2**20
        ),
        name="layer",
    )(first_row, gains_own, cosine, sine, x, cot, *owns)


def fast_device(
    sizes,
    inputs,
    segment_ids,
    positions,
    cotangent,
    *params,
):
    masters, moments = params[:11], params[11:]
    batches, seqs, tokens, width = inputs.shape
    assert seqs == 1
    q_cols, k_cols = masters[0].shape[1], masters[1].shape[1]
    width_ff = masters[4].shape[1]
    assert k_cols == HEAD

    own = masters[7].shape[0]
    place = (lax.axis_index("dp") * sizes["ctx"] + lax.axis_index("ctx")) * own
    low = [w.astype(BF) for w in masters[:4]]
    owns = (jnp.concatenate(low[:3], axis=1), low[3], *masters[4:7])
    gains_own = jnp.zeros((16, width), F32)
    gains_own = lax.dynamic_update_slice(gains_own, jnp.concatenate(masters[7:]).reshape(4, own), (0, place))
    start = lax.axis_index("ctx") * tokens
    frequency = jnp.exp(
        jnp.arange(HEAD // 2, dtype=F32) * (-2.0 * math.log(10000.0) / HEAD)
    )
    angle = positions.reshape(-1).astype(F32)[:, None] * frequency
    cosine, sine = jnp.cos(angle), jnp.sin(angle)
    first_row = (start + jnp.arange(tokens, dtype=jnp.int32))[None, None] - positions
    flat = (batches * tokens, width)
    x = inputs.reshape(flat)
    outs = layer_call(first_row, gains_own, cosine, sine, x, cotangent.reshape(flat), owns)
    output, gain_grads, norm_tile = outs[0], outs[9], outs[10]
    input_grad, grad_sum = outs[19:21]

    def final_sum(i, cols):
        return grad_sum[i, :, :cols].astype(F32)

    qkv_cols = owns[0].shape[1]
    s_down, s_gate, s_up = [final_sum(i, width_ff) for i in range(3)]
    s_out, s_qkv = final_sum(3, q_cols), final_sum(4, qkv_cols)
    summed = (
        s_qkv[:, :q_cols], s_qkv[:, q_cols : q_cols + k_cols], s_qkv[:, q_cols + k_cols :],
        s_out, s_gate, s_up, s_down,
    )
    norm_value = norm_tile[0, 0]
    factor = 1.0 / jnp.maximum(norm_value, 1.0)
    own_gains = lax.dynamic_slice_in_dim(gain_grads, place, own, 1)
    summed += tuple(own_gains[i] for i in range(4))
    new_moments = tuple(0.5 * m + 0.5 * factor * g for m, g in zip(moments, summed))
    changes = tuple(-RATE * (m + 0.01 * w) for w, m in zip(masters[:7], new_moments[:7]))

    return (
        output.reshape(inputs.shape),
        input_grad.reshape(inputs.shape), norm_value.reshape(1), *changes, *new_moments
    )


def per_device(
    sizes,
    inputs,
    segment_ids,
    positions,
    cotangent,
    *params,
):
    masters, moments = params[:11], params[11:]
    batches, seqs, tokens, width = inputs.shape
    assert seqs == 1
    full_len = segment_ids.shape[2]
    q_cols, k_cols = masters[0].shape[1], masters[1].shape[1]
    heads = q_cols // HEAD
    assert k_cols == HEAD
    cuts = 2 if tokens >= 512 else 1
    unit = tokens // cuts

    low = [w.astype(BF) for w in masters[:7]]
    qkv_own = jnp.concatenate(low[:3], axis=1)
    gains_own = jnp.stack([g.astype(BF) for g in masters[7:]], axis=1)
    gains = lax.all_gather(gains_own, ("dp", "ctx"), axis=0, tiled=True).astype(F32)
    gain_one, gain_two, gain_three, gain_four = [gains[:, i] for i in range(4)]
    w_qkv, mark = gather_rows(qkv_own, sizes, None)
    w_out, mark = gather_rows(low[3], sizes, mark)
    w_gate, mark = gather_rows(low[4], sizes, mark)
    w_up, mark = gather_rows(low[5], sizes, mark)
    w_down, mark = gather_rows(low[6], sizes, mark)

    start = lax.axis_index("ctx") * tokens
    causal = (start + jnp.arange(tokens))[:, None] >= jnp.arange(full_len)[None, :]
    frequency = jnp.exp(
        jnp.arange(HEAD // 2, dtype=F32) * (-2.0 * math.log(10000.0) / HEAD)
    )

    state = []
    for mb in range(batches):
        x = inputs[mb, 0].astype(F32)
        r_one = inverse_rms(x)
        attn_in = (x * r_one * (1.0 + gain_one)).astype(BF)
        angles = positions[mb, 0].astype(F32)[:, None] * frequency
        cosine, sine = jnp.cos(angles), jnp.sin(angles)
        seg = segment_ids[mb, 0]
        seg_local = lax.dynamic_slice_in_dim(seg, start, tokens)
        allowed = causal & (seg_local[:, None] == seg[None, :])
        proj = dot(attn_in, w_qkv)
        queries = jnp.concatenate(
            [rotate(proj[:, h * HEAD : (h + 1) * HEAD], cosine, sine) for h in range(heads)]
        ).astype(BF)
        keys = rotate(proj[:, q_cols : q_cols + HEAD], cosine, sine).astype(BF)
        values = proj[:, q_cols + HEAD :].astype(BF)
        both = swap_ctx(jnp.concatenate([keys, values], axis=1), sizes)
        keys_all, values_all = both[:, :HEAD], both[:, HEAD:]
        out, saved = attend(queries, keys_all, values_all, allowed)
        heads_out = jnp.concatenate(jnp.split(out, heads, axis=0), axis=1)
        state.append(
            dict(
                x=x, r_one=r_one, attn_in=attn_in, cosine=cosine, sine=sine, queries=queries,
                keys=keys_all, values=values_all, saved=saved, heads_out=heads_out,
            )
        )

    units = [(mb, cut) for mb in range(batches) for cut in range(cuts)]
    work = []
    for mb, cut in units:
        rows = slice(cut * unit, (cut + 1) * unit)
        part = dot_t(state[mb]["heads_out"][rows], w_out).astype(BF)
        work.append(dict(rows=rows, mb=mb, attn_low=sum_mp(part, sizes)))
    for w in work:
        attn = w["attn_low"].astype(F32)
        r_two = inverse_rms(attn)
        mid = state[w["mb"]]["x"][w["rows"]] + attn * r_two * (1.0 + gain_two)
        r_three = inverse_rms(mid)
        ffn_in = (mid * r_three * (1.0 + gain_three)).astype(BF)
        gate, up = dot(ffn_in, w_gate), dot(ffn_in, w_up)
        value, slope = gelu_parts(gate)
        hidden = (value * up).astype(BF)
        part = dot_t(hidden, w_down).astype(BF)
        w.update(
            mid=mid, r_two=r_two, r_three=r_three, ffn_in=ffn_in, gate=gate, up=up, hidden=hidden,
            ffn_low=sum_mp(part, sizes),
        )
    for w in work:
        ffn = w["ffn_low"].astype(F32)
        r_four = inverse_rms(ffn)
        grad = cotangent[w["mb"], 0][w["rows"]].astype(F32)
        w["output"] = (w["mid"] + ffn * r_four * (1.0 + gain_four)).astype(BF)
        d_ffn, w["g_four"] = norm_back(ffn, r_four, gain_four, grad)
        d_ffn = d_ffn.astype(BF)
        d_hidden = dot(d_ffn, w_down)
        value, slope = gelu_parts(w["gate"])
        d_gate = (d_hidden * w["up"] * slope).astype(BF)
        d_up = (d_hidden * value).astype(BF)
        part = (dot_t(d_gate, w_gate) + dot_t(d_up, w_up)).astype(BF)
        w.update(grad=grad, d_ffn=d_ffn, d_gate=d_gate, d_up=d_up, d_in_low=sum_mp(part, sizes))
    for w in work:
        d_in = w["d_in_low"].astype(F32)
        back, w["g_three"] = norm_back(w["mid"], w["r_three"], gain_three, d_in)
        d_mid = w["grad"] + back
        attn = w["attn_low"].astype(F32)
        d_attn, w["g_two"] = norm_back(attn, w["r_two"], gain_two, d_mid)
        d_attn = d_attn.astype(BF)
        w.update(d_mid=d_mid, d_attn=d_attn, d_heads=dot(d_attn, w_out).astype(BF))

    def rows_of(key):
        return jnp.concatenate([w[key] for w in work])

    ffn_in = rows_of("ffn_in")
    g_down = t_dot(rows_of("d_ffn"), rows_of("hidden"))
    g_gate = t_dot(ffn_in, rows_of("d_gate"))
    g_up = t_dot(ffn_in, rows_of("d_up"))
    s_down, mark = scatter_rows(g_down, sizes, None)
    s_gate, mark = scatter_rows(g_gate, sizes, mark)
    s_up, mark = scatter_rows(g_up, sizes, mark)

    for mb in range(batches):
        s = state[mb]
        d_heads = jnp.concatenate([w["d_heads"] for w in work if w["mb"] == mb])
        d_out = jnp.concatenate(jnp.split(d_heads, heads, axis=1))
        d_queries, d_keys, d_values = attend_back(
            s["saved"], s["queries"], s["keys"], s["values"], d_out
        )
        d_kv = scatter_ctx(jnp.concatenate([d_keys, d_values], axis=1), sizes)
        pieces = [rotate(q, s["cosine"], -s["sine"]) for q in jnp.split(d_queries, heads)]
        pieces += [rotate(d_kv[:, :HEAD], s["cosine"], -s["sine"]), d_kv[:, HEAD:]]
        s["d_proj"] = jnp.concatenate(pieces, axis=1).astype(BF)
    for w in work:
        part = dot_t(state[w["mb"]]["d_proj"][w["rows"]], w_qkv).astype(BF)
        w["d_attn_in"] = sum_mp(part, sizes)

    g_out = t_dot(rows_of("d_attn"), jnp.concatenate([s["heads_out"] for s in state]))
    g_qkv = t_dot(
        jnp.concatenate([s["attn_in"] for s in state]),
        jnp.concatenate([s["d_proj"] for s in state]),
    )
    s_out, mark = scatter_rows(g_out, sizes, mark)
    s_qkv, mark = scatter_rows(g_qkv, sizes, mark)

    for w in work:
        s = state[w["mb"]]
        back, w["g_one"] = norm_back(
            s["x"][w["rows"]], s["r_one"][w["rows"]], gain_one, w["d_attn_in"].astype(F32)
        )
        w["input_grad"] = (w["d_mid"] + back).astype(BF)

    gain_grads = jnp.stack(
        [sum(w[key] for w in work) for key in ("g_one", "g_two", "g_three", "g_four")]
    )
    gain_grads = sum_small(gain_grads, ("ctx", "dp"), sizes)
    summed = (
        s_qkv[:, :q_cols], s_qkv[:, q_cols : q_cols + k_cols], s_qkv[:, q_cols + k_cols :],
        s_out, s_gate, s_up, s_down,
    )
    weight_sq = sum(jnp.sum(g * g) for g in (s_qkv, s_out, s_gate, s_up, s_down))
    weight_sq = sum_small(weight_sq.reshape(1, 1), ("ctx", "dp", "mp"), sizes)[0, 0]
    norm_value = jnp.sqrt(weight_sq + jnp.sum(gain_grads * gain_grads))
    factor = 1.0 / jnp.maximum(norm_value, 1.0)
    own = masters[7].shape[0]
    place = (lax.axis_index("dp") * sizes["ctx"] + lax.axis_index("ctx")) * own
    own_gains = lax.dynamic_slice_in_dim(gain_grads, place, own, 1)
    summed += tuple(own_gains[i] for i in range(4))
    new_moments = tuple(0.5 * m + 0.5 * factor * g for m, g in zip(moments, summed))
    changes = tuple(-RATE * (m + 0.01 * w) for w, m in zip(masters[:7], new_moments[:7]))

    def whole(key):
        return rows_of(key).reshape(inputs.shape)

    return (
        whole("output"), whole("input_grad"), norm_value.reshape(1), *changes, *new_moments
    )


def solution(mesh):
    sizes = dict(mesh.shape)
    weight, vector = P(("dp", "ctx"), "mp"), P(("dp", "ctx"))
    params = (weight,) * 7 + (vector,) * 4
    data = P(None, "dp", "ctx", None)

    def run(*args):
        batches, _, tokens, _ = args[0].shape
        fast = sizes == dict(dp=4, ctx=2, mp=4) and batches == 2 and tokens == 2 * UNIT
        return (fast_device if fast else per_device)(sizes, *args)

    return jax.shard_map(
        run,
        mesh=mesh,
        in_specs=(data, P(None, "dp", None), P(None, "dp", "ctx"), data) + params + params,
        out_specs=(data, data, P()) + (weight,) * 7 + params,
        check_vma=False,
    )
```

```python
import math

import jax
import jax.numpy as jnp
from jax import lax
from jax.experimental import pallas as pl
from jax.experimental.pallas import tpu as pltpu
from jax.sharding import PartitionSpec as P

HEAD = 256
STEP = 10
EPS = 1e-06
CAP = 50.0
RATE = 1.0 / math.sqrt(1.0 + STEP / 1000.0)
SCALE = HEAD ** (-0.5)
BF = jnp.bfloat16
F32 = jnp.float32


def flip(axis, size, mask):
    return dict(axis_name=axis, perm=[(i, i ^ mask) for i in range(size)])


def after(value, other):
    return lax.optimization_barrier((value, other))[0]


def gather_rows(own, sizes, wait):
    dp, ctx = sizes["dp"], sizes["ctx"]
    rows, cols = own.shape
    if wait is not None:
        own = after(own, wait)
    if dp != 4:
        out = lax.all_gather(own, ("dp", "ctx"), axis=0, tiled=True)
        return out, own
    me = lax.axis_index("dp")
    half = rows // 2 // 16 * 16
    from_x = lax.ppermute(own, **flip("dp", dp, 1))
    from_y = lax.ppermute(own, **flip("dp", dp, 2))
    far_top = lax.ppermute(from_y[:half], **flip("dp", dp, 1))
    far_low = lax.ppermute(from_x[half:], **flip("dp", dp, 2))
    mine = jnp.zeros((dp, rows, cols), own.dtype)
    mine = lax.dynamic_update_slice(mine, own[None], (me, 0, 0))
    mine = lax.dynamic_update_slice(mine, from_x[None], (me ^ 1, 0, 0))
    mine = lax.dynamic_update_slice(mine, from_y[None], (me ^ 2, 0, 0))
    mine = lax.dynamic_update_slice(mine, far_top[None], (me ^ 3, 0, 0))
    mine = lax.dynamic_update_slice(mine, far_low[None], (me ^ 3, half, 0))
    if ctx == 2:
        other = lax.ppermute(mine, **flip("ctx", ctx, 1))
        core = lax.axis_index("ctx")
        out = jnp.zeros((dp, ctx, rows, cols), own.dtype)
        out = lax.dynamic_update_slice(out, mine[:, None], (0, core, 0, 0))
        out = lax.dynamic_update_slice(out, other[:, None], (0, 1 - core, 0, 0))
    else:
        out = lax.all_gather(mine, "ctx", axis=1)
    return out.reshape(dp * ctx * rows, cols), from_x


def scatter_rows(full, sizes, wait):
    dp, ctx = sizes["dp"], sizes["ctx"]
    full = full.astype(BF)
    if wait is not None:
        full = after(full, wait)
    rows = full.shape[0] // (dp * ctx)
    cols = full.shape[1]
    if dp != 4:
        out = lax.psum_scatter(full, ("dp", "ctx"), scatter_dimension=0, tiled=True)
        return out.astype(F32), out
    blocks = full.reshape(dp, ctx, rows, cols)
    if ctx == 2:
        core = lax.axis_index("ctx")
        send = lax.dynamic_index_in_dim(blocks, 1 - core, 1, keepdims=False)
        keep = lax.dynamic_index_in_dim(blocks, core, 1, keepdims=False)
        got = lax.ppermute(send, **flip("ctx", ctx, 1))
    else:
        keep = lax.psum_scatter(blocks, "ctx", scatter_dimension=1, tiled=False)
        got = None
    me = lax.axis_index("dp")
    half = rows // 2 // 16 * 16

    def part(mask, low, high):
        size = (1, high - low, cols)
        piece = lax.dynamic_slice(keep, (me ^ mask, low, 0), size)[0].astype(F32)
        if got is not None:
            piece = piece + lax.dynamic_slice(got, (me ^ mask, low, 0), size)[0].astype(F32)
        return piece

    far_top = lax.ppermute(part(3, 0, half).astype(BF), **flip("dp", dp, 1))
    far_low = lax.ppermute(part(3, half, rows).astype(BF), **flip("dp", dp, 2))
    to_y = jnp.concatenate([part(2, 0, half) + far_top.astype(F32), part(2, half, rows)])
    to_x = jnp.concatenate([part(1, 0, half), part(1, half, rows) + far_low.astype(F32)])
    by_y = lax.ppermute(to_y.astype(BF), **flip("dp", dp, 2))
    by_x = lax.ppermute(to_x.astype(BF), **flip("dp", dp, 1))
    total = part(0, 0, rows) + by_x.astype(F32) + by_y.astype(F32)
    return total, far_top


def sum_mp(part, sizes):
    if sizes["mp"] != 4:
        return lax.psum(part, "mp")
    place = lax.axis_index("mp")
    inner = (place == 1) | (place == 2)
    near = lax.ppermute(part, "mp", [(0, 1), (3, 2)])
    pair = (part.astype(F32) + near.astype(F32)).astype(BF)
    across = lax.ppermute(pair, "mp", [(1, 2), (2, 1)])
    total = (pair.astype(F32) + across.astype(F32)).astype(BF)
    back = lax.ppermute(total, "mp", [(1, 0), (2, 3)])
    return jnp.where(inner, total, back)


def sum_small(value, axes, sizes):
    for axis in axes:
        size = sizes[axis]
        step = 1
        while step < size:
            value = value + lax.ppermute(value, **flip(axis, size, step))
            step *= 2
    return value


def swap_ctx(local, sizes):
    if sizes["ctx"] != 2:
        return lax.all_gather(local, "ctx", axis=0, tiled=True)
    other = lax.ppermute(local, **flip("ctx", 2, 1))
    first = lax.axis_index("ctx") == 0
    return jnp.concatenate([jnp.where(first, local, other), jnp.where(first, other, local)])


def scatter_ctx(full, sizes):
    if sizes["ctx"] != 2:
        return lax.psum_scatter(full.astype(BF), "ctx", scatter_dimension=0, tiled=True).astype(F32)
    core = lax.axis_index("ctx")
    rows = full.shape[0] // 2
    send = lax.dynamic_slice_in_dim(full, (1 - core) * rows, rows).astype(BF)
    keep = lax.dynamic_slice_in_dim(full, core * rows, rows)
    return keep.astype(BF).astype(F32) + lax.ppermute(send, **flip("ctx", 2, 1)).astype(F32)


def dot(a, b):
    return lax.dot_general(a, b, (((1,), (0,)), ((), ())), preferred_element_type=F32)


def dot_t(a, b):
    return lax.dot_general(a, b, (((1,), (1,)), ((), ())), preferred_element_type=F32)


def t_dot(a, b):
    return lax.dot_general(a, b, (((0,), (0,)), ((), ())), preferred_element_type=F32)


def inverse_rms(v):
    return lax.rsqrt(jnp.mean(v * v, axis=-1, keepdims=True) + EPS)


def norm_back(v, r, gain, dy):
    scaled = (1.0 + gain) * dy
    mean = jnp.mean(scaled * v, axis=-1, keepdims=True)
    return r * scaled - v * (r * r * r) * mean, jnp.sum(v * r * dy, axis=0)


def rotate(v, cosine, sine):
    a, b = v[:, : HEAD // 2], v[:, HEAD // 2 :]
    return jnp.concatenate([a * cosine - b * sine, b * cosine + a * sine], axis=1)


GELU_C = math.sqrt(2.0 / math.pi)


def gelu_parts(u):
    tanh = jnp.tanh(GELU_C * (u + 0.044715 * u * u * u))
    value = 0.5 * u * (1.0 + tanh)
    slope = 0.5 * (1.0 + tanh) + 0.5 * u * (1.0 - tanh * tanh) * GELU_C * (
        1.0 + 3.0 * 0.044715 * u * u
    )
    return value, slope


def attend(queries, keys, values, allowed):
    raw = dot_t(queries, keys) * SCALE
    tanh = jnp.tanh(raw / CAP)
    heads = queries.shape[0] // allowed.shape[0]
    mask = jnp.concatenate([allowed] * heads, axis=0)
    weight = jnp.where(mask, jnp.exp(CAP * tanh), 0.0)
    probs = weight / jnp.sum(weight, axis=1, keepdims=True)
    out = dot(probs.astype(BF), values).astype(BF)
    return out, (probs, tanh)


def attend_back(saved, queries, keys, values, d_out):
    probs, tanh = saved
    d_probs = dot_t(d_out, values)
    inner = jnp.sum(probs * d_probs, axis=1, keepdims=True)
    d_raw = (probs * (d_probs - inner) * (1.0 - tanh * tanh)).astype(BF)
    d_queries = dot(d_raw, keys) * SCALE
    d_keys = t_dot(d_raw, queries) * SCALE
    d_values = t_dot(probs.astype(BF), d_out)
    return d_queries, d_keys, d_values


MESH = pl.DeviceIdType.MESH
UNIT = 256
TILE = 256


def layer_kernel(
    first_row, gains_own, cos_hbm, sin_hbm, x_hbm, cot_hbm, own_qkv, own_out, own_gate, own_up, own_down,
    out_hbm, ffn_in_hbm, hidden_hbm, d_ffn_hbm, d_gate_hbm, d_up_hbm, d_attn_hbm, d_heads_hbm,
    d_mid_hbm, gains_out, norm_out, attn_in_hbm, heads_hbm, pack_hbm, w_qkv_hbm, w_out_hbm,
    attn_hbm, slope_hbm, value_hbm,
    in_grad_hbm, own_hbm, by_x_hbm, by_y_hbm, core_hbm, far_hbm, kv_hbm, d_proj_hbm,
    weights, w_qkv, send, near, across, total, xb, cb, ab, act, act_t, stage, angle,
    line_send, line_recv, credit, local, ag_send, ag_recv, ag_local, gain_send, gain_recv, kv_sem,
    load_sem, rs_send, rs_recv, rs_local, kv_back, proj_sem,
    gain_ref, scale_ref, cast, squares, cast_sem, fin_sem, tail_send, tail_recv, z_send, z_recv,
):
    dp, core, z = lax.axis_index("dp"), lax.axis_index("ctx"), lax.axis_index("mp")
    w_out = w_qkv.at[:, : w_out_hbm.shape[1]]
    width, units = xb.shape[1], weights.shape[2]
    rows_own = own_qkv.shape[0]
    half = rows_own // 2
    inner = (z == 1) | (z == 2)
    outer = (z == 0) | (z == 3)
    x_peer, y_peer = (dp ^ 1, core, z), (dp ^ 2, core, z)
    core_peer = (dp, 1 - core, z)
    near_peer = (dp, core, z ^ 1)
    far_peer = (dp, core, 3 - z)

    barrier = pltpu.get_barrier_semaphore()
    group = [(dp ^ (m // 2), (1 - core) if m % 2 else core, z) for m in range(1, 8)]
    line = [(dp, core, z ^ m) for m in range(1, 4)]
    for peer in (*group, *line):
        pl.semaphore_signal(barrier, inc=1, device_id=peer, device_id_type=MESH)

    def block(mask, other=False, low=0, size=rows_own):
        owner = (dp ^ mask) * 2 + ((1 - core) if other else core)
        return pl.ds(pl.multiple_of(owner * rows_own + low, 16), size)

    owns = (own_qkv, own_out, own_gate, own_up, own_down)
    wholes = (w_qkv, w_out_hbm, weights.at[0], weights.at[1], weights.at[2])

    def gather(w, name, recv=False):
        table = {
            "x": (0, block(0), x_peer, block(1)),
            "y": (1, block(0), y_peer, block(2)),
            "top": (2, block(2, False, 0, half), x_peer, block(3, False, 0, half)),
            "low": (3, block(1, False, half, half), y_peer, block(3, False, half, half)),
            "own_c": (4, block(0), core_peer, block(0, True)),
            "x_c": (5, block(1), core_peer, block(1, True)),
            "y_c": (6, block(2), core_peer, block(2, True)),
            "top_c": (7, block(3, False, 0, half), core_peer, block(3, True, 0, half)),
            "low_c": (8, block(3, False, half, half), core_peer, block(3, True, half, half)),
        }
        index, out_rows, peer, in_rows = table[name]
        rows = in_rows if recv else out_rows
        direct = w < 2 and name in ("x", "y", "own_c")
        src = owns[w] if direct else wholes[w].at[rows]
        return pltpu.make_async_remote_copy(
            src_ref=src, dst_ref=wholes[w].at[rows], send_sem=ag_send.at[w, index],
            recv_sem=ag_recv.at[w, index], device_id=peer, device_id_type=MESH,
        )

    def own_copy(w):
        return pltpu.make_async_copy(owns[w], wholes[w].at[block(0)], ag_local.at[w])

    def round_own(w):
        size = cast.shape[1]
        steps = rows_own // size
        copies = [
            pltpu.make_async_copy(owns[w].at[pl.ds(c * size, size)], cast.at[c % 2], cast_sem.at[c % 2])
            for c in range(steps)
        ]
        copies[0].start()
        for c in range(steps):
            if c + 1 < steps:
                copies[c + 1].start()
            copies[c].wait()
            weights[w - 2, block(0, False, c * size, size)] = cast[c % 2].astype(BF)

    def gather_first(w):
        for name in ("x", "y", "own_c"):
            gather(w, name).start()
        if w < 2:
            own_copy(w).start()

    def gather_second(w):
        gather(w, "x", True).wait_recv()
        gather(w, "low").start()
        gather(w, "x_c").start()
        gather(w, "y", True).wait_recv()
        gather(w, "top").start()
        gather(w, "y_c").start()

    def gather_third(w):
        for name in ("top", "low"):
            gather(w, name, True).wait_recv()
            gather(w, name + "_c").start()

    def gather_end(w):
        for name in ("own_c", "x_c", "y_c", "top_c", "low_c"):
            gather(w, name, True).wait_recv()
        if w < 2:
            own_copy(w).wait()
        for name in ("x", "y", "top", "low", "own_c", "x_c", "y_c", "top_c", "low_c"):
            gather(w, name).wait_send()

    def hop(kind, i):
        src = (send.at[i % 3], send.at[i % 3], total.at[i % 4])[kind]
        dst = (near.at[i % 3], across.at[i % 2], total.at[i % 4])[kind]
        return pltpu.make_async_remote_copy(
            src_ref=src, dst_ref=dst, send_sem=line_send.at[kind, i % 4],
            recv_sem=line_recv.at[kind, i % 4],
            device_id=far_peer if kind == 1 else near_peer, device_id_type=MESH,
        )

    def add_rows(dst, a, b):
        @pl.loop(0, UNIT // 16, unroll=4)
        def _(r):
            rows = pl.ds(pl.multiple_of(r * 16, 16), 16)
            dst[rows] = (a[rows].astype(F32) + b[rows].astype(F32)).astype(BF)

    def boundary(up=None, cross=None, back=None, done=None):
        @pl.when(outer)
        def _():
            if done is not None:
                hop(2, done).wait_recv()
            if cross is not None:
                hop(0, cross).wait_send()
            if up is not None:
                hop(0, up).start()

        @pl.when(inner)
        def _():
            if cross is not None:
                hop(0, cross).wait_recv()
                add_rows(send.at[cross % 3], send.at[cross % 3], near.at[cross % 3])
                if not isinstance(cross, int) or cross >= 2:
                    pl.semaphore_wait(credit, 1)
                hop(1, cross).start()
            if back is not None:
                hop(1, back).wait_recv()
                hop(1, back).wait_send()
                add_rows(total.at[back % 4], send.at[back % 3], across.at[back % 2])
                if not isinstance(back, int) or back < 14:
                    pl.semaphore_signal(credit, inc=1, device_id=far_peer, device_id_type=MESH)
                hop(2, back).start()
            if done is not None:
                hop(2, done).wait_send()

    def rows_of(u):
        return pl.ds(pl.multiple_of(u * UNIT, UNIT), UNIT)

    def load(ref, u, dst, sem):
        return pltpu.make_async_copy(ref.at[rows_of(u)], dst, local.at[sem])

    def store(src, ref, u, sem):
        return pltpu.make_async_copy(src, ref.at[rows_of(u)], local.at[sem])

    def store_t(ref, u, sem):
        return pltpu.make_async_copy(act_t, ref.at[:, rows_of(u)], local.at[sem])

    def turn(source=None):
        source = act if source is None else source

        @pl.loop(0, width // TILE, unroll=3)
        def _(n):
            act_t[tile(n)] = source[:, tile(n)].T

    def tile(n):
        return pl.ds(pl.multiple_of(n * TILE, TILE), TILE)

    def each_rows(body):
        @pl.loop(0, UNIT // 16, unroll=4)
        def _(r):
            body(pl.ds(pl.multiple_of(r * 16, 16), 16))

    def scale(i):
        return scale_ref[i : i + 1]

    def add_gain(index, v):
        gain_ref[index] += v[:8] + v[8:]

    def project_out(u, k):
        dst = send.at[k % 3]

        @pl.loop(0, width // TILE, unroll=3)
        def _(n):
            dst[:, tile(n)] = dot_t(act[:, 2 * HEAD * u : 2 * HEAD * (u + 1)], w_out[tile(n)]).astype(BF)

    def middle(rows, u4):
        attn = total[u4, rows].astype(F32) if u4 is not None else ab[rows].astype(F32)
        r_two = inverse_rms(attn)
        return attn, r_two, xb[rows].astype(F32) + attn * r_two * scale(1)

    def forward(u, k, ready=None):
        load(x_hbm, u, xb, 0).start()
        store(total.at[u], attn_hbm, u, 1).start()
        load(x_hbm, u, xb, 0).wait()

        def body(rows):
            _, _, mid = middle(rows, u)
            act[rows] = (mid * inverse_rms(mid) * scale(2)).astype(BF)

        each_rows(body)
        turn()
        store_t(ffn_in_hbm, u, 2).start()

        @pl.loop(0, units // TILE, unroll=3)
        def _(f):
            gate = dot(act[...], weights[0, :, tile(f)])
            up = dot(act[...], weights[1, :, tile(f)])
            value, slope = gelu_parts(gate)
            stage[0, :, tile(f)] = (value * up).astype(BF)
            stage[1, :, tile(f)] = (slope * up).astype(BF)
            stage[2, :, tile(f)] = value.astype(BF)

        saves = ((0, hidden_hbm), (1, slope_hbm), (2, value_hbm))
        for i, ref in saves:
            store(stage.at[i], ref, u, 3 + i).start()
        if ready is not None:
            ready()
        dst = send.at[k % 3]

        @pl.loop(0, width // TILE, unroll=3)
        def _(n):
            dst[:, tile(n)] = dot_t(stage[0], weights[2, tile(n)]).astype(BF)

        for i, ref in saves:
            store(stage.at[i], ref, u, 3 + i).wait()
        store(total.at[u], attn_hbm, u, 1).wait()
        store_t(ffn_in_hbm, u, 2).wait()

    def backward(u, k):
        loads = (
            load(x_hbm, u, xb, 0), load(attn_hbm, u, ab, 1), load(cot_hbm, u, cb, 2),
            load(slope_hbm, u, stage.at[1], 4), load(value_hbm, u, stage.at[2], 5),
        )
        for copy in loads:
            copy.start()
        for copy in loads:
            copy.wait()

        def body(rows):
            _, _, mid = middle(rows, None)
            ffn = total[u, rows].astype(F32)
            r = inverse_rms(ffn)
            dy = cb[rows].astype(F32)
            xb[rows] = (mid + ffn * r * scale(3)).astype(BF)
            scaled = scale(3) * dy
            mean = jnp.mean(scaled * ffn, axis=-1, keepdims=True)
            act[rows] = (r * scaled - ffn * (r * r * r) * mean).astype(BF)
            add_gain(2, ffn * r * dy)

        each_rows(body)
        store(xb, out_hbm, u, 0).start()
        turn()
        store_t(d_ffn_hbm, u, 1).start()

        @pl.loop(0, units // TILE, unroll=3)
        def _(f):
            d_hidden = dot(act[...], weights[2, :, tile(f)])
            stage[1, :, tile(f)] = (d_hidden * stage[1, :, tile(f)].astype(F32)).astype(BF)
            stage[2, :, tile(f)] = (d_hidden * stage[2, :, tile(f)].astype(F32)).astype(BF)

        store(stage.at[1], d_gate_hbm, u, 4).start()
        store(stage.at[2], d_up_hbm, u, 5).start()
        dst = send.at[k % 3]

        @pl.loop(0, width // TILE, unroll=3)
        def _(n):
            part = dot_t(stage[1], weights[0, tile(n)]) + dot_t(stage[2], weights[1, tile(n)])
            dst[:, tile(n)] = part.astype(BF)

        store(xb, out_hbm, u, 0).wait()
        store_t(d_ffn_hbm, u, 1).wait()
        store(stage.at[1], d_gate_hbm, u, 4).wait()
        store(stage.at[2], d_up_hbm, u, 5).wait()

    d_heads = stage.at[2, :, : w_out_hbm.shape[1]]

    def last_loads(u):
        return (load(x_hbm, u, xb, 0), load(attn_hbm, u, ab, 1), load(cot_hbm, u, cb, 2))

    def start_all(copies):
        for copy in copies:
            copy.start()

    def last(u):
        for copy in last_loads(u):
            copy.wait()

        def body(rows):
            attn, r_two, mid = middle(rows, None)
            r = inverse_rms(mid)
            dy = total[u, rows].astype(F32)
            scaled = scale(2) * dy
            mean = jnp.mean(scaled * mid, axis=-1, keepdims=True)
            grad = cb[rows].astype(F32) + r * scaled - mid * (r * r * r) * mean
            add_gain(1, mid * r * dy)
            cb[rows] = grad.astype(BF)
            scaled = scale(1) * grad
            mean = jnp.mean(scaled * attn, axis=-1, keepdims=True)
            act[rows] = (r_two * scaled - attn * (r_two * r_two * r_two) * mean).astype(BF)
            add_gain(0, attn * r_two * grad)

        each_rows(body)
        store(cb, d_mid_hbm, u, 0).start()
        turn()
        store_t(d_attn_hbm, u, 1).start()
        for h in range(w_out.shape[1] // TILE):
            columns = slice(h * TILE, (h + 1) * TILE)
            d_heads[:, columns] = dot(act[...], w_out[:, columns]).astype(BF)
        store(d_heads, d_heads_hbm, u, 2).start()
        store(cb, d_mid_hbm, u, 0).wait()
        store_t(d_attn_hbm, u, 1).wait()
        store(d_heads, d_heads_hbm, u, 2).wait()

    own_rows = pl.ds(pl.multiple_of((dp * 2 + core) * 16, 16), 16)

    def gain_copy(m, recv=False):
        peer = group[m - 1]
        owner = (peer[0] * 2 + peer[1]) if recv else (dp * 2 + core)
        return pltpu.make_async_remote_copy(
            src_ref=send.at[2, own_rows],
            dst_ref=send.at[2, own_rows if not recv else pl.ds(pl.multiple_of(owner * 16, 16), 16)],
            send_sem=gain_send.at[m], recv_sem=gain_recv.at[m], device_id=peer, device_id_type=MESH,
        )

    def gains_sum():
        whole = send[2, own_rows].astype(F32)
        for m in range(1, 8):
            gain_copy(m, True).wait_recv()
        for m in range(1, 8):
            owner = group[m - 1][0] * 2 + group[m - 1][1]
            whole += send[2, pl.ds(pl.multiple_of(owner * 16, 16), 16)].astype(F32)
        scale_ref[...] = 1.0 + whole[:8]
        for m in range(1, 8):
            gain_copy(m).wait_send()

    loaded = (stage.at[0], stage.at[1], stage.at[2], act)

    def first_norm(u):
        load(x_hbm, u, loaded[u], u).wait()

        def body(rows):
            x = loaded[u][rows].astype(F32)
            total[u, rows] = (x * inverse_rms(x) * scale(0)).astype(BF)

        each_rows(body)

    def first_turn(u):
        if u:
            store_t(attn_in_hbm, u - 1, 4).wait()
        turn(total.at[u])
        store_t(attn_in_hbm, u, 4).start()

    def angles(u):
        rows = rows_of(u)
        return (
            pltpu.make_async_copy(cos_hbm.at[rows], angle.at[u % 2, 0], local.at[2 * (u % 2)]),
            pltpu.make_async_copy(sin_hbm.at[rows], angle.at[u % 2, 1], local.at[2 * (u % 2) + 1]),
        )

    packs = (cb, ab)

    def kv_columns(kind, peer=False):
        side = (1 - core) if peer else core
        return pl.ds(pl.multiple_of(kind * 4 * HEAD + side * 2 * HEAD, HEAD), 2 * HEAD)

    def kv_copy(mb, kind, recv=False):
        part = packs[mb].at[:, kv_columns(kind, recv)]
        return pltpu.make_async_remote_copy(
            src_ref=part, dst_ref=part, send_sem=kv_sem.at[0, mb, kind], recv_sem=kv_sem.at[1, mb, kind],
            device_id=core_peer, device_id_type=MESH,
        )

    def projections(u):
        mb, b = divmod(u, 2)
        for copy in angles(u):
            copy.wait()
        if u < 3:
            for copy in angles(u + 1):
                copy.start()
        c, s = angle[u % 2, 0], angle[u % 2, 1]
        for j in range(4):
            v = dot(total[u], w_qkv[:, j * HEAD : (j + 1) * HEAD])
            if j < 2:
                xb[:, (mb * 4 + j * 2 + b) * HEAD : (mb * 4 + j * 2 + b + 1) * HEAD] = rotate(v, c, s).astype(BF)
            else:
                place = pl.multiple_of((j - 2) * 4 * HEAD + (core * 2 + b) * HEAD, HEAD)
                packs[mb][:, pl.ds(place, HEAD)] = (rotate(v, c, s) if j == 2 else v).astype(BF)

    def attention(mb):
        for kind in (0, 1):
            kv_copy(mb, kind, True).wait_recv()

        @pl.loop(0, 4)
        def _(i):
            h, b = i // 2, i % 2
            query = xb[:, pl.ds(pl.multiple_of(mb * 4 * HEAD + i * HEAD, HEAD), HEAD)]
            lowest = first_row[mb, :, pl.ds(pl.multiple_of(b * UNIT, UNIT), UNIT)]
            query_at = lax.broadcasted_iota(jnp.int32, (UNIT, UNIT), 1) + core * 2 * UNIT + b * UNIT
            weight, length = [], 0.0
            for j in range(4):
                key_at = lax.broadcasted_iota(jnp.int32, (UNIT, UNIT), 0) + j * UNIT
                score = dot_t(packs[mb][:, j * HEAD : (j + 1) * HEAD], query) * (SCALE / CAP)
                ok = (key_at <= query_at) & (key_at >= lowest)
                weight.append(jnp.where(ok, jnp.exp(CAP * jnp.tanh(score)), 0.0))
                length = length + jnp.sum(weight[j], axis=0, keepdims=True)
            inverse = 1.0 / length
            out = 0.0
            for j in range(4):
                value = packs[mb][:, (4 + j) * HEAD : (5 + j) * HEAD]
                out = out + t_dot((weight[j] * inverse).astype(BF), value)
            place = pl.multiple_of((mb * 2 + b) * 2 * HEAD + h * HEAD, HEAD)
            act[:, pl.ds(place, HEAD)] = out.astype(BF)

    def heads_store(u):
        return pltpu.make_async_copy(
            act.at[:, 2 * HEAD * u : 2 * HEAD * (u + 1)], heads_hbm.at[rows_of(u)], local.at[u]
        )

    def pack_store(i):
        return pltpu.make_async_copy((xb, cb, ab)[i], pack_hbm.at[i], ag_local.at[5 + i])

    for u in range(4):
        load(x_hbm, u, loaded[u], u).start()
    gain_ref[...] = jnp.zeros_like(gain_ref)
    send[2, own_rows] = gains_own[...].astype(BF)
    pl.semaphore_wait(barrier, 10)
    for m in range(1, 8):
        gain_copy(m).start()
    gather_first(0)
    gains_sum()
    for u in range(4):
        first_norm(u)
    for copy in angles(0):
        copy.start()
    first_turn(0)
    gather_second(0)
    first_turn(1)
    first_turn(2)
    gather_third(0)
    gather_first(1)
    first_turn(3)
    round_own(2)
    gather_end(0)
    qkv_store = pltpu.make_async_copy(w_qkv, w_qkv_hbm, local.at[5])
    qkv_store.start()
    for u in range(4):
        projections(u)
        if u % 2:
            for kind in (0, 1):
                kv_copy(u // 2, kind).start()
    gather_second(1)
    gather_first(2)
    attention(0)
    gather_third(1)
    gather_end(1)
    qkv_store.wait()
    store_t(attn_in_hbm, 3, 4).wait()
    out_load = pltpu.make_async_copy(w_out_hbm, w_out, local.at[4])
    out_load.start()
    out_load.wait()
    project_out(0, 0)
    boundary(0)
    project_out(1, 1)
    attention(1)
    project_out(2, 2)
    for i in range(3):
        pack_store(i).start()
    for u in range(4):
        heads_store(u).start()
    round_own(3)
    gather_second(2)
    gather_first(3)
    boundary(1, 0)
    gather_third(2)
    round_own(4)
    for kind in (0, 1):
        for mb in (0, 1):
            kv_copy(mb, kind).wait_send()
    for i in range(3):
        pack_store(i).wait()
    for u in range(4):
        heads_store(u).wait()
    boundary(2, 1, 0)
    project_out(3, 3)
    gather_second(3)
    gather_first(4)
    boundary(3, 2, 1, 0)
    gather_third(3)
    gather_end(2)
    gather_end(3)

    def ready():
        gather_second(4)
        gather_third(4)
        gather_end(4)

    forward(0, 4, ready)

    @pl.loop(4, 7)
    def _(k):
        boundary(k, k - 1, k - 2, k - 3)
        forward(k - 3, k + 1)

    @pl.loop(7, 11)
    def _(k):
        boundary(k, k - 1, k - 2, k - 3)
        backward(k - 7, k + 1)

    left, w_back = weights.at[0, :, : 4 * UNIT], weights.at[0, :, 4 * UNIT : 8 * UNIT]
    queries = weights.at[0, : 4 * UNIT, 8 * UNIT :]
    d_out = weights.at[0, 4 * UNIT : 8 * UNIT, 8 * UNIT :]
    right = weights.at[1, : 4 * UNIT]
    jobs = (
        (d_ffn_hbm, hidden_hbm), (ffn_in_hbm, d_gate_hbm), (ffn_in_hbm, d_up_hbm),
        (d_attn_hbm, heads_hbm), (attn_in_hbm, d_proj_hbm),
    )

    def columns(i):
        return jobs[i][1].shape[1]

    def core_out(m):
        low = 4 * UNIT + (m % 2) * rows_own
        return weights.at[1, low : low + rows_own]

    def arrived(m):
        low = 4 * UNIT + (2 + m % 2) * rows_own
        return weights.at[1, low : low + rows_own]

    def sums(i, m):
        low = ((i % 2) * 3 + m - 1) * rows_own
        return weights.at[2, low : low + rows_own]

    packed = weights.at[2, 6 * rows_own : 6 * rows_own + UNIT]
    own_sum = weights.at[2, 6 * rows_own + UNIT : 7 * rows_own + UNIT]

    def remote(src, dst, index, peer):
        return pltpu.make_async_remote_copy(
            src_ref=src, dst_ref=dst, send_sem=rs_send.at[index], recv_sem=rs_recv.at[index],
            device_id=peer, device_id_type=MESH,
        )

    def operands(i):
        pair = [pltpu.make_async_copy(jobs[i][1], right.at[:, : columns(i)], rs_local.at[1])]
        if i != 2:
            pair.append(pltpu.make_async_copy(jobs[i][0], left, rs_local.at[0]))
        return pair

    def core_copy(i, m):
        n = columns(i)
        return remote(core_out(m).at[:, :n], core_hbm.at[i, m, :, :n], (i, m), core_peer)

    def arrive(i, m):
        n = columns(i)
        return pltpu.make_async_copy(core_hbm.at[i, m, :, :n], arrived(m).at[:, :n], rs_local.at[2 + m % 2])

    def far_copy(i, way):
        n = columns(i)
        rows = slice(0, half) if way == 0 else slice(half, rows_own)
        peer = (x_peer, y_peer)[way]
        return remote(sums(i, 3).at[rows, :n], far_hbm.at[i, rows, :n], (i, 4 + way), peer)

    def final_copy(i, way):
        n = columns(i)
        dst = (by_x_hbm, by_y_hbm)[way]
        peer = (x_peer, y_peer)[way]
        return remote(sums(i, way + 1).at[:, :n], dst.at[i, :, :n], (i, 6 + way), peer)

    def own_store(i):
        n = columns(i)
        return pltpu.make_async_copy(own_sum.at[:, :n], own_hbm.at[i, :, :n], rs_local.at[5])

    def block_rows(mask, other):
        owner = (dp ^ mask) * 2 + ((1 - core) if other else core)
        return pl.ds(pl.multiple_of(owner * rows_own, 16), rows_own)

    def pieces(i):
        piece = 768 if columns(i) % 768 == 0 else 512
        return columns(i) // piece, lambda n: pl.ds(pl.multiple_of(n * piece, TILE), piece)

    def scatter_theirs(i):
        for copy in operands(i):
            copy.wait()
        steps, piece_at = pieces(i)

        for m in (3, 2, 1, 0):
            if m < 2:
                core_copy(i, m + 2).wait_send()
            elif i > 0:
                core_copy(i - 1, m - 2).wait_send()
            dst = core_out(m)

            @pl.loop(0, steps)
            def _(n):
                dst[:, piece_at(n)] = dot(left[block_rows(m, True)], right[:, piece_at(n)]).astype(BF)

            core_copy(i, m).start()

    def scatter_mine(i):
        steps, piece_at = pieces(i)
        if i > 1:
            for way in (0, 1):
                far_copy(i - 2, way).wait_send()
                final_copy(i - 2, way).wait_send()
        if i > 0:
            own_store(i - 1).wait()
        core_copy(i, 3).wait_recv()
        arrive(i, 3).start()
        for m in (3, 2, 1, 0):
            if m:
                core_copy(i, m - 1).wait_recv()
                arrive(i, m - 1).start()
            arrive(i, m).wait()
            dst, extra = (sums(i, m) if m else own_sum), arrived(m)

            @pl.loop(0, steps)
            def _(n):
                part = dot(left[block_rows(m, False)], right[:, piece_at(n)])
                dst[:, piece_at(n)] = (part + extra[:, piece_at(n)].astype(F32)).astype(BF)

            if m == 3:
                far_copy(i, 0).start()
                far_copy(i, 1).start()
        own_store(i).start()

    def scatter_start(i):
        scatter_theirs(i)
        scatter_mine(i)

    def operands_start(i):
        for copy in operands(i):
            copy.start()

    def scatter_end(i):
        n = columns(i)
        for way in (0, 1):
            far_copy(i, way).wait_recv()
        added = arrived(0)
        copy = pltpu.make_async_copy(far_hbm.at[i, :, :n], added.at[:, :n], rs_local.at[4])
        copy.start()
        copy.wait()
        for way in (1, 0):
            base = 0 if way == 1 else half
            dst = sums(i, way + 1)

            @pl.loop(0, half // 16, unroll=3)
            def _(r):
                rows = pl.ds(pl.multiple_of(base + r * 16, 16), 16)
                dst[rows, :n] = (dst[rows, :n].astype(F32) + added[rows, :n].astype(F32)).astype(BF)

            final_copy(i, way).start()

    def back_loads(mb):
        copies = [pltpu.make_async_copy(pack_hbm.at[1 + mb], packed, load_sem.at[8])]
        for i in range(4):
            h, b = divmod(i, 2)
            rows = pl.ds(i * UNIT, UNIT)
            query = pack_hbm.at[0, :, (mb * 4 + i) * HEAD : (mb * 4 + i + 1) * HEAD]
            grad = d_heads_hbm.at[pl.ds((2 * mb + b) * UNIT, UNIT), h * HEAD : (h + 1) * HEAD]
            copies.append(pltpu.make_async_copy(query, queries.at[rows], load_sem.at[i]))
            copies.append(pltpu.make_async_copy(grad, d_out.at[rows], load_sem.at[4 + i]))
        return [*copies, *angles(2 * mb), *angles(2 * mb + 1)]

    def unrotate(v, b):
        c, s = angle[b, 0], angle[b, 1]
        v, w = v[:, : HEAD // 2], v[:, HEAD // 2 :]
        return jnp.concatenate([v * c + w * s, w * c - v * s], axis=1)

    def kv_out(mb):
        return pltpu.make_async_remote_copy(
            src_ref=act_t.at[: 4 * UNIT], dst_ref=kv_hbm.at[mb], send_sem=kv_back.at[0, mb],
            recv_sem=kv_back.at[1, mb], device_id=core_peer, device_id_type=MESH,
        )

    def proj_store(u):
        part = stage.at[u // 2, :, (u % 2) * 4 * HEAD : (u % 2 + 1) * 4 * HEAD]
        return pltpu.make_async_copy(part, d_proj_hbm.at[rows_of(u)], proj_sem.at[u])

    def attention_back(mb):
        for copy in back_loads(mb):
            copy.start()
        for copy in back_loads(mb):
            copy.wait()
        d_scores, weights_of = (xb, ab), (act, cb)

        @pl.loop(0, 4)
        def _(i):
            h, b = i // 2, i % 2
            rows = pl.ds(pl.multiple_of(i * UNIT, UNIT), UNIT)
            query, grad = queries[rows], d_out[rows]
            lowest = first_row[mb, :, pl.ds(pl.multiple_of(b * UNIT, UNIT), UNIT)]
            query_at = lax.broadcasted_iota(jnp.int32, (UNIT, UNIT), 1) + core * 2 * UNIT + b * UNIT
            tanh, weight, d_probs, length, mean = [], [], [], 0.0, 0.0
            for j in range(4):
                key_at = lax.broadcasted_iota(jnp.int32, (UNIT, UNIT), 0) + j * UNIT
                ok = (key_at <= query_at) & (key_at >= lowest)
                score = dot_t(packed[:, j * HEAD : (j + 1) * HEAD], query) * (SCALE / CAP)
                tanh.append(jnp.tanh(score))
                weight.append(jnp.where(ok, jnp.exp(CAP * tanh[j]), 0.0))
                d_probs.append(dot_t(packed[:, (4 + j) * HEAD : (5 + j) * HEAD], grad))
                length = length + jnp.sum(weight[j], axis=0, keepdims=True)
                mean = mean + jnp.sum(weight[j] * d_probs[j], axis=0, keepdims=True)
            inverse = 1.0 / length
            mean = mean * inverse
            d_query = 0.0
            for j in range(4):
                probs = weight[j] * inverse
                d_raw = (probs * (d_probs[j] - mean) * (1.0 - tanh[j] * tanh[j])).astype(BF)
                place = pl.ds(pl.multiple_of((j % 2) * 4 * HEAD + i * HEAD, HEAD), HEAD)
                d_scores[j // 2][:, place] = d_raw
                weights_of[j // 2][:, place] = probs.astype(BF)
                d_query = d_query + t_dot(d_raw, packed[:, j * HEAD : (j + 1) * HEAD])
            place = pl.ds(pl.multiple_of(b * 4 * HEAD + h * HEAD, HEAD), HEAD)
            stage[mb, :, place] = unrotate(d_query * SCALE, b).astype(BF)

        def block_grads(j):
            place = slice((j % 2) * 4 * HEAD, (j % 2 + 1) * 4 * HEAD)
            d_key = dot(d_scores[j // 2][:, place], queries[...]) * SCALE
            return d_key, dot(weights_of[j // 2][:, place], d_out[...])

        for side in (0, 1):

            @pl.when(core == side)
            def _():
                for t in (0, 1):
                    d_key, d_value = block_grads((1 - side) * 2 + t)
                    act_t[t * UNIT : (t + 1) * UNIT] = d_key.astype(BF)
                    act_t[(2 + t) * UNIT : (3 + t) * UNIT] = d_value.astype(BF)

        kv_out(mb).start()
        kv_out(mb).wait_recv()
        copy = pltpu.make_async_copy(kv_hbm.at[mb], act_t.at[4 * UNIT : 8 * UNIT], rs_local.at[6])
        copy.start()
        copy.wait()
        for side in (0, 1):

            @pl.when(core == side)
            def _():
                for t in (0, 1):
                    d_key, d_value = block_grads(side * 2 + t)
                    d_key = d_key + act_t[(4 + t) * UNIT : (5 + t) * UNIT].astype(F32)
                    d_value = d_value + act_t[(6 + t) * UNIT : (7 + t) * UNIT].astype(F32)
                    low = t * 4 * HEAD
                    stage[mb, :, low + 2 * HEAD : low + 3 * HEAD] = unrotate(d_key, t).astype(BF)
                    stage[mb, :, low + 3 * HEAD : low + 4 * HEAD] = d_value.astype(BF)

        proj_store(2 * mb).start()
        proj_store(2 * mb + 1).start()
        kv_out(mb).wait_send()

    def project_back(u):
        dst = send.at[(12 + u) % 3]
        low = (u % 2) * 4 * HEAD

        @pl.loop(0, width // TILE, unroll=3)
        def _(n):
            dst[:, tile(n)] = dot_t(stage[u // 2, :, low : low + 4 * HEAD], w_back[tile(n)]).astype(BF)

    def first_loads(u):
        return (load(x_hbm, u, xb, 0), load(d_mid_hbm, u, ab, 1))

    def first_back(u):
        for copy in first_loads(u):
            copy.wait()

        def body(rows):
            x = xb[rows].astype(F32)
            r_one = inverse_rms(x)
            dy = total[u, rows].astype(F32)
            scaled = scale(0) * dy
            mean = jnp.mean(scaled * x, axis=-1, keepdims=True)
            back = r_one * scaled - x * (r_one * r_one * r_one) * mean
            ab[rows] = (ab[rows].astype(F32) + back).astype(BF)
            add_gain(3, x * r_one * dy)

        each_rows(body)
        store(ab, in_grad_hbm, u, 2).start()
        store(ab, in_grad_hbm, u, 2).wait()
        if u < 3:
            start_all(first_loads(u + 1))

    def finish(i):
        n = columns(i)
        for way in (0, 1):
            final_copy(i, way).wait_recv()
        for low in (0, half):
            pairs = ((own_hbm, cb), (by_x_hbm, act), (by_y_hbm, stage.at[2]))
            copies = [
                pltpu.make_async_copy(ref.at[i, low : low + half, :n], dst.at[:half, :n], fin_sem.at[j])
                for j, (ref, dst) in enumerate(pairs)
            ]
            start_all(copies)
            for copy in copies:
                copy.wait()

            @pl.loop(0, half // 16, unroll=3)
            def _(r):
                rows = pl.ds(pl.multiple_of(r * 16, 16), 16)
                v = cb[rows, :n].astype(F32) + act[rows, :n].astype(F32) + stage[2, rows, :n].astype(F32)
                cb[rows, :n] = v.astype(BF)
                v = v * v
                gain_ref[4, :, :n] += v[:8] + v[8:]

            copy = pltpu.make_async_copy(cb.at[:half, :n], own_hbm.at[i, low : low + half, :n], fin_sem.at[0])
            copy.start()
            copy.wait()

    table = weights.at[1, 4 * UNIT + 4 * rows_own :]

    def table_copy(m, recv=False):
        peer = group[m - 1]
        owner = (peer[0] * 2 + peer[1]) if recv else (dp * 2 + core)
        rows = pl.ds(pl.multiple_of(owner * 16, 16), 16)
        return pltpu.make_async_remote_copy(
            src_ref=table.at[own_rows], dst_ref=table.at[rows], send_sem=tail_send.at[m],
            recv_sem=tail_recv.at[m], device_id=peer, device_id_type=MESH,
        )

    def square_copy(m, recv=False):
        place = (z ^ m) if recv else z
        return pltpu.make_async_remote_copy(
            src_ref=squares.at[z], dst_ref=squares.at[place], send_sem=z_send.at[m],
            recv_sem=z_recv.at[m], device_id=line[m - 1], device_id_type=MESH,
        )

    def agree():
        rows = [jnp.sum(gain_ref[i], axis=0, keepdims=True) for i in (3, 0, 1, 2, 4)]
        high = [v.astype(BF).astype(F32) for v in rows]
        low = [v - h for v, h in zip(rows, high)]
        blank = jnp.zeros((6, rows[0].shape[1]), F32)
        table[own_rows] = jnp.concatenate([*high, *low, blank], axis=0).astype(BF)
        for m in range(1, 8):
            table_copy(m).start()
        for m in range(1, 8):
            table_copy(m, True).wait_recv()
        whole = jnp.zeros((16, rows[0].shape[1]), F32)
        for owner in range(8):
            whole = whole + table[owner * 16 : owner * 16 + 16].astype(F32)
        gains = whole[0:4] + whole[5:9]
        squares[z] = jnp.broadcast_to(jnp.sum(whole[4:5] + whole[9:10], axis=1, keepdims=True), (8, 128))
        for m in range(1, 4):
            square_copy(m).start()
        gains_out[0:4] = gains
        gains_out[4:8] = jnp.zeros_like(gains)
        gain_square = jnp.sum(jnp.sum(gains * gains, axis=1, keepdims=True), axis=0, keepdims=True)
        for m in range(1, 4):
            square_copy(m, True).wait_recv()
        norm_out[...] = jnp.sqrt(squares[0] + squares[1] + squares[2] + squares[3] + gain_square)
        for m in range(1, 8):
            table_copy(m).wait_send()
        for m in range(1, 4):
            square_copy(m).wait_send()

    w_load = pltpu.make_async_copy(w_qkv_hbm, w_back, rs_local.at[7])
    operands_start(0)
    w_load.start()
    start_all(last_loads(0))
    boundary(11, 10, 9, 8)
    scatter_start(0)
    operands_start(1)
    last(0)
    start_all(last_loads(1))
    boundary(None, 11, 10, 9)
    last(1)
    scatter_end(0)
    attention_back(0)
    start_all(last_loads(2))
    w_load.wait()
    project_back(0)
    boundary(12)
    project_back(1)
    boundary(None, None, 11, 10)
    scatter_start(1)
    operands_start(2)
    last(2)
    start_all(last_loads(3))
    boundary(13, 12)
    boundary(None, None, None, 11)
    last(3)
    scatter_end(1)
    attention_back(1)
    start_all(first_loads(0))
    project_back(2)
    boundary(14)
    scatter_theirs(2)
    boundary(None, 13, 12)
    project_back(3)
    scatter_mine(2)
    operands_start(3)
    boundary(15, 14, 13, 12)
    scatter_end(2)
    scatter_start(3)
    for u in range(4):
        proj_store(u).wait()
    operands_start(4)
    first_back(0)
    finish(0)
    finish(1)
    boundary(None, 15, 14, 13)
    scatter_start(4)
    scatter_end(3)
    first_back(1)
    boundary(None, None, 15, 14)
    scatter_end(4)
    own_store(4).wait()
    first_back(2)
    finish(2)
    finish(3)
    boundary(None, None, None, 15)
    first_back(3)
    finish(4)
    agree()
    for m in range(2):
        core_copy(4, m).wait_send()
    for i in range(3, 5):
        for way in (0, 1):
            far_copy(i, way).wait_send()
            final_copy(i, way).wait_send()


def layer_call(first_row, gains_own, cosine, sine, x, cot, owns):
    tokens, width = x.shape
    units = owns[2].shape[1]
    qkv_cols, out_cols = owns[0].shape[1], owns[1].shape[1]
    assert tokens == 4 * UNIT
    full = jax.ShapeDtypeStruct((tokens, width), BF)
    wide = jax.ShapeDtypeStruct((tokens, units), BF)
    flipped = jax.ShapeDtypeStruct((width, tokens), BF)
    rows = owns[0].shape[0]
    part = jax.ShapeDtypeStruct((5, rows, units), BF)
    heads = jax.ShapeDtypeStruct((tokens, out_cols), BF)
    outs = (
        full, flipped, wide, flipped, wide, wide, flipped, heads, full,
        jax.ShapeDtypeStruct((8, width), F32),
        jax.ShapeDtypeStruct((8, 128), F32),
        flipped,
        heads,
        jax.ShapeDtypeStruct((3, UNIT, width), BF),
        jax.ShapeDtypeStruct((width, qkv_cols), BF),
        jax.ShapeDtypeStruct((width, out_cols), BF),
        full, wide, wide,
        full, part, part, part,
        jax.ShapeDtypeStruct((5, 4, rows, units), BF),
        part,
        jax.ShapeDtypeStruct((2, tokens, HEAD), BF),
        jax.ShapeDtypeStruct((tokens, qkv_cols), BF),
    )
    anywhere, vmem = pl.BlockSpec(memory_space=pl.ANY), pl.BlockSpec(memory_space=pltpu.VMEM)
    dma = pltpu.SemaphoreType.DMA
    return pl.pallas_call(
        layer_kernel,
        out_shape=outs,
        in_specs=[vmem] * 2 + [anywhere] * 9,
        out_specs=[anywhere] * 9 + [vmem] * 2 + [anywhere] * 16,
        scratch_shapes=[
            pltpu.VMEM((3, width, units), BF),
            pltpu.VMEM((width, qkv_cols), BF),
            pltpu.VMEM((3, UNIT, width), BF),
            pltpu.VMEM((3, UNIT, width), BF),
            pltpu.VMEM((2, UNIT, width), BF),
            pltpu.VMEM((4, UNIT, width), BF),
            pltpu.VMEM((UNIT, width), BF),
            pltpu.VMEM((UNIT, width), BF),
            pltpu.VMEM((UNIT, width), BF),
            pltpu.VMEM((UNIT, width), BF),
            pltpu.VMEM((width, UNIT), BF),
            pltpu.VMEM((3, UNIT, units), BF),
            pltpu.VMEM((2, 2, UNIT, HEAD // 2), F32),
            dma((3, 4)),
            dma((3, 4)),
            pltpu.SemaphoreType.REGULAR,
            dma((6,)),
            dma((5, 9)),
            dma((5, 9)),
            dma((8,)),
            dma((8,)),
            dma((8,)),
            dma((2, 2, 2)),
            dma((9,)),
            dma((5, 8)),
            dma((5, 8)),
            dma((8,)),
            dma((2, 2)),
            dma((4,)),
            pltpu.VMEM((5, 8, width), F32),
            pltpu.VMEM((8, width), F32),
            pltpu.VMEM((2, 32, units), F32),
            pltpu.VMEM((4, 8, 128), F32),
            dma((2,)),
            dma((3,)),
            dma((8,)),
            dma((8,)),
            dma((4,)),
            dma((4,)),
        ],
        compiler_params=pltpu.CompilerParams(
            collective_id=1, has_side_effects=True, vmem_limit_bytes=63 * 2**20
        ),
        name="layer",
    )(first_row, gains_own, cosine, sine, x, cot, *owns)


def fast_device(
    sizes,
    inputs,
    segment_ids,
    positions,
    cotangent,
    *params,
):
    masters, moments = params[:11], params[11:]
    batches, seqs, tokens, width = inputs.shape
    assert seqs == 1
    q_cols, k_cols = masters[0].shape[1], masters[1].shape[1]
    width_ff = masters[4].shape[1]
    assert k_cols == HEAD

    own = masters[7].shape[0]
    place = (lax.axis_index("dp") * sizes["ctx"] + lax.axis_index("ctx")) * own
    low = [w.astype(BF) for w in masters[:4]]
    owns = (jnp.concatenate(low[:3], axis=1), low[3], *masters[4:7])
    gains_own = jnp.zeros((16, width), F32)
    gains_own = lax.dynamic_update_slice(gains_own, jnp.concatenate(masters[7:]).reshape(4, own), (0, place))
    start = lax.axis_index("ctx") * tokens
    frequency = jnp.exp(
        jnp.arange(HEAD // 2, dtype=F32) * (-2.0 * math.log(10000.0) / HEAD)
    )
    angle = positions.reshape(-1).astype(F32)[:, None] * frequency
    cosine, sine = jnp.cos(angle), jnp.sin(angle)
    first_row = (start + jnp.arange(tokens, dtype=jnp.int32))[None, None] - positions
    flat = (batches * tokens, width)
    x = inputs.reshape(flat)
    outs = layer_call(first_row, gains_own, cosine, sine, x, cotangent.reshape(flat), owns)
    output, gain_grads, norm_tile = outs[0], outs[9], outs[10]
    input_grad, grad_sum = outs[19:21]

    def final_sum(i, cols):
        return grad_sum[i, :, :cols].astype(F32)

    qkv_cols = owns[0].shape[1]
    s_down, s_gate, s_up = [final_sum(i, width_ff) for i in range(3)]
    s_out, s_qkv = final_sum(3, q_cols), final_sum(4, qkv_cols)
    summed = (
        s_qkv[:, :q_cols], s_qkv[:, q_cols : q_cols + k_cols], s_qkv[:, q_cols + k_cols :],
        s_out, s_gate, s_up, s_down,
    )
    norm_value = norm_tile[0, 0]
    factor = 1.0 / jnp.maximum(norm_value, 1.0)
    own_gains = lax.dynamic_slice_in_dim(gain_grads, place, own, 1)
    summed += tuple(own_gains[i] for i in range(4))
    new_moments = tuple(0.5 * m + 0.5 * factor * g for m, g in zip(moments, summed))
    changes = tuple(-RATE * (m + 0.01 * w) for w, m in zip(masters[:7], new_moments[:7]))

    return (
        output.reshape(inputs.shape),
        input_grad.reshape(inputs.shape), norm_value.reshape(1), *changes, *new_moments
    )


def per_device(
    sizes,
    inputs,
    segment_ids,
    positions,
    cotangent,
    *params,
):
    masters, moments = params[:11], params[11:]
    batches, seqs, tokens, width = inputs.shape
    assert seqs == 1
    full_len = segment_ids.shape[2]
    q_cols, k_cols = masters[0].shape[1], masters[1].shape[1]
    heads = q_cols // HEAD
    assert k_cols == HEAD
    cuts = 2 if tokens >= 512 else 1
    unit = tokens // cuts

    low = [w.astype(BF) for w in masters[:7]]
    qkv_own = jnp.concatenate(low[:3], axis=1)
    gains_own = jnp.stack([g.astype(BF) for g in masters[7:]], axis=1)
    gains = lax.all_gather(gains_own, ("dp", "ctx"), axis=0, tiled=True).astype(F32)
    gain_one, gain_two, gain_three, gain_four = [gains[:, i] for i in range(4)]
    w_qkv, mark = gather_rows(qkv_own, sizes, None)
    w_out, mark = gather_rows(low[3], sizes, mark)
    w_gate, mark = gather_rows(low[4], sizes, mark)
    w_up, mark = gather_rows(low[5], sizes, mark)
    w_down, mark = gather_rows(low[6], sizes, mark)

    start = lax.axis_index("ctx") * tokens
    causal = (start + jnp.arange(tokens))[:, None] >= jnp.arange(full_len)[None, :]
    frequency = jnp.exp(
        jnp.arange(HEAD // 2, dtype=F32) * (-2.0 * math.log(10000.0) / HEAD)
    )

    state = []
    for mb in range(batches):
        x = inputs[mb, 0].astype(F32)
        r_one = inverse_rms(x)
        attn_in = (x * r_one * (1.0 + gain_one)).astype(BF)
        angles = positions[mb, 0].astype(F32)[:, None] * frequency
        cosine, sine = jnp.cos(angles), jnp.sin(angles)
        seg = segment_ids[mb, 0]
        seg_local = lax.dynamic_slice_in_dim(seg, start, tokens)
        allowed = causal & (seg_local[:, None] == seg[None, :])
        proj = dot(attn_in, w_qkv)
        queries = jnp.concatenate(
            [rotate(proj[:, h * HEAD : (h + 1) * HEAD], cosine, sine) for h in range(heads)]
        ).astype(BF)
        keys = rotate(proj[:, q_cols : q_cols + HEAD], cosine, sine).astype(BF)
        values = proj[:, q_cols + HEAD :].astype(BF)
        both = swap_ctx(jnp.concatenate([keys, values], axis=1), sizes)
        keys_all, values_all = both[:, :HEAD], both[:, HEAD:]
        out, saved = attend(queries, keys_all, values_all, allowed)
        heads_out = jnp.concatenate(jnp.split(out, heads, axis=0), axis=1)
        state.append(
            dict(
                x=x, r_one=r_one, attn_in=attn_in, cosine=cosine, sine=sine, queries=queries,
                keys=keys_all, values=values_all, saved=saved, heads_out=heads_out,
            )
        )

    units = [(mb, cut) for mb in range(batches) for cut in range(cuts)]
    work = []
    for mb, cut in units:
        rows = slice(cut * unit, (cut + 1) * unit)
        part = dot_t(state[mb]["heads_out"][rows], w_out).astype(BF)
        work.append(dict(rows=rows, mb=mb, attn_low=sum_mp(part, sizes)))
    for w in work:
        attn = w["attn_low"].astype(F32)
        r_two = inverse_rms(attn)
        mid = state[w["mb"]]["x"][w["rows"]] + attn * r_two * (1.0 + gain_two)
        r_three = inverse_rms(mid)
        ffn_in = (mid * r_three * (1.0 + gain_three)).astype(BF)
        gate, up = dot(ffn_in, w_gate), dot(ffn_in, w_up)
        value, slope = gelu_parts(gate)
        hidden = (value * up).astype(BF)
        part = dot_t(hidden, w_down).astype(BF)
        w.update(
            mid=mid, r_two=r_two, r_three=r_three, ffn_in=ffn_in, gate=gate, up=up, hidden=hidden,
            ffn_low=sum_mp(part, sizes),
        )
    for w in work:
        ffn = w["ffn_low"].astype(F32)
        r_four = inverse_rms(ffn)
        grad = cotangent[w["mb"], 0][w["rows"]].astype(F32)
        w["output"] = (w["mid"] + ffn * r_four * (1.0 + gain_four)).astype(BF)
        d_ffn, w["g_four"] = norm_back(ffn, r_four, gain_four, grad)
        d_ffn = d_ffn.astype(BF)
        d_hidden = dot(d_ffn, w_down)
        value, slope = gelu_parts(w["gate"])
        d_gate = (d_hidden * w["up"] * slope).astype(BF)
        d_up = (d_hidden * value).astype(BF)
        part = (dot_t(d_gate, w_gate) + dot_t(d_up, w_up)).astype(BF)
        w.update(grad=grad, d_ffn=d_ffn, d_gate=d_gate, d_up=d_up, d_in_low=sum_mp(part, sizes))
    for w in work:
        d_in = w["d_in_low"].astype(F32)
        back, w["g_three"] = norm_back(w["mid"], w["r_three"], gain_three, d_in)
        d_mid = w["grad"] + back
        attn = w["attn_low"].astype(F32)
        d_attn, w["g_two"] = norm_back(attn, w["r_two"], gain_two, d_mid)
        d_attn = d_attn.astype(BF)
        w.update(d_mid=d_mid, d_attn=d_attn, d_heads=dot(d_attn, w_out).astype(BF))

    def rows_of(key):
        return jnp.concatenate([w[key] for w in work])

    ffn_in = rows_of("ffn_in")
    g_down = t_dot(rows_of("d_ffn"), rows_of("hidden"))
    g_gate = t_dot(ffn_in, rows_of("d_gate"))
    g_up = t_dot(ffn_in, rows_of("d_up"))
    s_down, mark = scatter_rows(g_down, sizes, None)
    s_gate, mark = scatter_rows(g_gate, sizes, mark)
    s_up, mark = scatter_rows(g_up, sizes, mark)

    for mb in range(batches):
        s = state[mb]
        d_heads = jnp.concatenate([w["d_heads"] for w in work if w["mb"] == mb])
        d_out = jnp.concatenate(jnp.split(d_heads, heads, axis=1))
        d_queries, d_keys, d_values = attend_back(
            s["saved"], s["queries"], s["keys"], s["values"], d_out
        )
        d_kv = scatter_ctx(jnp.concatenate([d_keys, d_values], axis=1), sizes)
        pieces = [rotate(q, s["cosine"], -s["sine"]) for q in jnp.split(d_queries, heads)]
        pieces += [rotate(d_kv[:, :HEAD], s["cosine"], -s["sine"]), d_kv[:, HEAD:]]
        s["d_proj"] = jnp.concatenate(pieces, axis=1).astype(BF)
    for w in work:
        part = dot_t(state[w["mb"]]["d_proj"][w["rows"]], w_qkv).astype(BF)
        w["d_attn_in"] = sum_mp(part, sizes)

    g_out = t_dot(rows_of("d_attn"), jnp.concatenate([s["heads_out"] for s in state]))
    g_qkv = t_dot(
        jnp.concatenate([s["attn_in"] for s in state]),
        jnp.concatenate([s["d_proj"] for s in state]),
    )
    s_out, mark = scatter_rows(g_out, sizes, mark)
    s_qkv, mark = scatter_rows(g_qkv, sizes, mark)

    for w in work:
        s = state[w["mb"]]
        back, w["g_one"] = norm_back(
            s["x"][w["rows"]], s["r_one"][w["rows"]], gain_one, w["d_attn_in"].astype(F32)
        )
        w["input_grad"] = (w["d_mid"] + back).astype(BF)

    gain_grads = jnp.stack(
        [sum(w[key] for w in work) for key in ("g_one", "g_two", "g_three", "g_four")]
    )
    gain_grads = sum_small(gain_grads, ("ctx", "dp"), sizes)
    summed = (
        s_qkv[:, :q_cols], s_qkv[:, q_cols : q_cols + k_cols], s_qkv[:, q_cols + k_cols :],
        s_out, s_gate, s_up, s_down,
    )
    weight_sq = sum(jnp.sum(g * g) for g in (s_qkv, s_out, s_gate, s_up, s_down))
    weight_sq = sum_small(weight_sq.reshape(1, 1), ("ctx", "dp", "mp"), sizes)[0, 0]
    norm_value = jnp.sqrt(weight_sq + jnp.sum(gain_grads * gain_grads))
    factor = 1.0 / jnp.maximum(norm_value, 1.0)
    own = masters[7].shape[0]
    place = (lax.axis_index("dp") * sizes["ctx"] + lax.axis_index("ctx")) * own
    own_gains = lax.dynamic_slice_in_dim(gain_grads, place, own, 1)
    summed += tuple(own_gains[i] for i in range(4))
    new_moments = tuple(0.5 * m + 0.5 * factor * g for m, g in zip(moments, summed))
    changes = tuple(-RATE * (m + 0.01 * w) for w, m in zip(masters[:7], new_moments[:7]))

    def whole(key):
        return rows_of(key).reshape(inputs.shape)

    return (
        whole("output"), whole("input_grad"), norm_value.reshape(1), *changes, *new_moments
    )


def solution(mesh):
    sizes = dict(mesh.shape)
    weight, vector = P(("dp", "ctx"), "mp"), P(("dp", "ctx"))
    params = (weight,) * 7 + (vector,) * 4
    data = P(None, "dp", "ctx", None)

    def run(*args):
        batches, _, tokens, _ = args[0].shape
        fast = sizes == dict(dp=4, ctx=2, mp=4) and batches == 2 and tokens == 2 * UNIT
        return (fast_device if fast else per_device)(sizes, *args)

    return jax.shard_map(
        run,
        mesh=mesh,
        in_specs=(data, P(None, "dp", None), P(None, "dp", "ctx"), data) + params + params,
        out_specs=(data, data, P()) + (weight,) * 7 + params,
        check_vma=False,
    )
```
